32 devices in a mesh: space: 8 (over z, y), dp: 4 (over x, core).
Axes of the slice: x: 2, y: 2, z: 4, core: 2. Of those that a mesh axis runs over, the one named last changes fastest.
Arguments:
- features: bfloat16 [4, 32, 8, 8, 512], P('dp', 'space'), may hold values from -6 to 6
- occupancy: int32 [4, 32, 512], P('dp', 'space'), may hold values 0 or 1
- counts: int32 [4, 8], P('dp', 'space'), may hold values from 2 to 4, as said below
- send_units: int32 [4, 8, 5, 12], P('dp', 'space'), may hold values from -1 to 23, as said below
- neighbours: int32 [4, 32, 26], P('dp', 'space'), may hold values from -1 to 59, as said below
- weight: bfloat16 [1728, 64], P('dp'), may hold values from -0.15625 to 0.15625
- conv_bias: bfloat16 [64], P('dp'), may hold values from -3 to 3
- cotangent: bfloat16 [4, 32, 8, 8, 512], P('dp', 'space'), may hold values from -6 to 6
Outputs:
- block_output: bfloat16 [4, 32, 8, 8, 512], P('dp', 'space')
- grad_input: bfloat16 [4, 32, 8, 8, 512], P('dp', 'space')
- grad_weight: float32 [1728, 64], P('dp')
- grad_bias: float32 [64], P('dp')
The draws below stay inside these ranges and needn't reach their ends.
Inputs may be any that keep to these rules, and one draw needn't show every extreme that they name: `counts`: each volume has a device holding 4 bricks. `send_units`: the entry of device q at j and l is -1 or 6 times a slot below counts of q plus ((j * 12 + l) mod 6); it is -1 where device q + j - 2 does not exist; link 0 is used wherever that device exists. `neighbours`: an entry n >= 0 of a brick on device r names a unit that device r + 2 - n // 12 sends, whose face is the one the entry's offset needs (2d if o_d = 1, 2d+1 if o_d = -1, d the first dimension where o is not 0).
All inputs are finite; a program needn't handle non-finite values. No bound on the sum of `occupancy` on one device may be relied on, other than what follows from the above.
Results may differ from the reference program's by a relative error of at most 0.012.
Values may be sent and summed in bfloat16 or wider, within the bound.
No kernel may reach another device: no remote copies, remote signals or barrier semaphores. Data moves between devices by JAX's collectives and lax.ppermute only.
A program may use at most 64 MiB of HBM per device.

```python
import jax
import jax.numpy as jnp
from jax import lax

C = 64
E = 8
TAPS = 27
SLOTS = 4
REACH = 2
LINKS = 12
VOLS = 4
BRICKS = 32


def neighbour_offsets_drawn():
    return [(first - 1, second - 1, third - 1) for first in range(3) for second in range(3) for third in range(3) if (first, second, third) != (1, 1, 1)]


def needed_face(offset):
    for dimension in range(3):
        if offset[dimension] != 0:
            return 2 * dimension + (0 if offset[dimension] == 1 else 1)
    return 0


def layout(key):
    shards = BRICKS // SLOTS
    spread = 2 * REACH + 1
    base_key = jax.random.fold_in(key, 4242)
    key_list = jax.random.split(base_key, 7)
    counts = jax.random.randint(key_list[0], (VOLS, shards), SLOTS // 2, SLOTS + 1)
    fullest = jax.random.randint(key_list[1], (VOLS, 1), 0, shards)
    counts = jnp.where(jnp.arange(shards)[None, :] == fullest, SLOTS, counts).astype(jnp.int32)
    device = jnp.arange(shards)[None, :, None, None]
    offset = jnp.arange(spread)[None, None, :, None]
    link_id = jnp.arange(LINKS)[None, None, None, :]
    target = device + offset - REACH
    inside = (target >= 0) & (target < shards)
    coin_flip = jax.random.randint(key_list[2], (VOLS, shards, spread, LINKS), 0, 2)
    present = inside & ((link_id == 0) | (coin_flip == 1))
    slot_pick = jax.random.randint(key_list[3], (VOLS, shards, spread, LINKS), 0, SLOTS) % counts[:, :, None, None]
    face_id = (offset * LINKS + link_id) % 6
    send_list = jnp.where(present, slot_pick * 6 + face_id, -1).astype(jnp.int32)
    faces_needed = jnp.array([needed_face(item) for item in neighbour_offsets_drawn()], jnp.int32)
    draw_shape = (VOLS, shards, SLOTS, 26)
    column_pick = jax.random.randint(key_list[5], draw_shape, 0, spread)
    half_pick = jax.random.randint(key_list[6], draw_shape, 0, 2)
    link_pick = faces_needed[None, None, None, :] + 6 * half_pick
    link_pick = jnp.where(link_pick < LINKS, link_pick, faces_needed[None, None, None, :])
    chosen_unit = column_pick * LINKS + link_pick
    source = jnp.arange(shards)[None, :, None, None] + REACH - column_pick
    in_range = (source >= 0) & (source < shards)
    clipped = jnp.clip(source, 0, shards - 1)
    volume_ids = jnp.broadcast_to(jnp.arange(VOLS)[:, None, None, None], draw_shape)
    sent_unit = send_list[volume_ids, clipped, column_pick, link_pick]
    slot_ids = jnp.arange(SLOTS)
    dropped = (jax.random.randint(key_list[4], draw_shape, 0, 4) == 0) & (slot_ids[None, None, :, None] > 0)
    listing = jnp.where(in_range & (sent_unit >= 0) & ~dropped, chosen_unit, -1)
    return (counts, send_list, listing.reshape(VOLS, shards * SLOTS, 26).astype(jnp.int32))


def draw_counts(key, part):
    return layout(key)[0]


def draw_send_units(key, part):
    return layout(key)[1]


def draw_neighbours(key, part):
    return layout(key)[2]


def place_ends(entries, key, low, top_value):
    extent = entries.shape
    spot = [jax.random.randint(jax.random.fold_in(key, axis), (), 0, extent[axis]) for axis in range(len(extent))]
    entries = entries.at[tuple(spot)].set(low)
    longest = extent.index(max(extent))
    spot[longest] = (spot[longest] + 1) % extent[longest]
    return entries.at[tuple(spot)].set(top_value)


def steps_of(own_key, dims, cuts, low, largest):
    def one(dim, shards_of):
        draws = jax.random.uniform(jax.random.fold_in(jax.random.fold_in(own_key, 6), dim), (shards_of,), jnp.float32, low / len(cuts), largest / len(cuts))
        return jnp.repeat(jnp.exp(draws), dims[dim] // shards_of).reshape((-1,) + (1,) * (len(dims) - dim - 1))

    factor_of = one(*cuts[0])
    for cut in cuts[1:]:
        factor_of = factor_of * one(*cut)
    return factor_of


def gaussian(own_key, extent, deviation, most, cuts=(), kind=jnp.bfloat16):
    values = jax.random.normal(own_key, extent, jnp.float32) * deviation
    if len(cuts) > 0:
        values = steps_of(own_key, extent, cuts, -0.22, 0.18) * values
    return jnp.clip(values, min=-most, max=most).astype(kind)


def setup_inputs(seed: int = 0) -> dict:
    seeds = jax.random.split(jax.random.key(seed), 9)
    features = gaussian(seeds[0], (VOLS, BRICKS, E, E, E * C), 1.0, 6.0, ((0, 4), (1, 8)))
    occupancy = place_ends((jax.random.randint(seeds[1], (VOLS, BRICKS, E * E * E), 0, 2) < 1).astype(jnp.int32), jax.random.fold_in(seeds[1], 1), 0, 1)
    counts = draw_counts(jax.random.fold_in(seeds[8], 71), 0)
    send_units = draw_send_units(jax.random.fold_in(seeds[8], 71), 0)
    neighbours = draw_neighbours(jax.random.fold_in(seeds[8], 71), 0)
    weight = gaussian(seeds[5], (TAPS * C, C), (TAPS * C) ** -0.5, 0.15625, ((0, 4),))
    conv_bias = gaussian(seeds[6], (C,), 0.5, 3.0, ((0, 4),))
    cotangent = gaussian(seeds[7], (VOLS, BRICKS, E, E, E * C), 1.0, 6.0, ((0, 4), (1, 8)))
    return dict(features=features, occupancy=occupancy, counts=counts, send_units=send_units, neighbours=neighbours, weight=weight, conv_bias=conv_bias, cotangent=cotangent)


def neighbour_offsets():
    return [(first - 1, second - 1, third - 1) for first in range(3) for second in range(3) for third in range(3) if (first, second, third) != (1, 1, 1)]


def first_moving(offset):
    for dimension in range(3):
        if offset[dimension] != 0:
            return dimension
    return 0


def face_planes(values):
    brick_edge = values.shape[1]
    planes = [values[:, 0], values[:, brick_edge - 1], values[:, :, 0], values[:, :, brick_edge - 1], values[:, :, :, 0], values[:, :, :, brick_edge - 1]]
    return jnp.stack(planes, axis=1)


def rim_region(face_plane, offset, brick_edge):
    moving = first_moving(offset)
    region = face_plane
    other_dims = [dimension for dimension in range(3) if dimension != moving]
    for position, dimension in enumerate(other_dims):
        if offset[dimension] == -1:
            region = lax.slice_in_dim(region, brick_edge - 1, brick_edge, axis=position + 1)
        elif offset[dimension] == 1:
            region = lax.slice_in_dim(region, 0, 1, axis=position + 1)
    return jnp.expand_dims(region, moving + 1)


def halo_block(values, units, listing):
    brick_edge = values.shape[1]
    unit_total = units.shape[0]
    padded = jnp.pad(values, ((0, 0), (1, 1), (1, 1), (1, 1), (0, 0)))
    for offset_index, offset in enumerate(neighbour_offsets()):
        unit_index = listing[:, offset_index]
        face_plane = jnp.take(units, jnp.clip(unit_index, 0, unit_total - 1), axis=0)
        face_plane = face_plane * (unit_index >= 0).astype(face_plane.dtype)[:, None, None, None]
        region = rim_region(face_plane, offset, brick_edge)
        starts = [0] + [0 if step == -1 else (1 if step == 0 else brick_edge + 1) for step in offset] + [0]
        padded = lax.dynamic_update_slice(padded, region, starts)
    return padded


def windows(padded, brick_edge):
    return [padded[:, first:first + brick_edge, second:second + brick_edge, third:third + brick_edge, :] for first in range(3) for second in range(3) for third in range(3)]


def convolve(padded, kernels, brick_edge):
    channels = padded.shape[-1]
    result = jnp.zeros((padded.shape[0] * brick_edge ** 3, kernels.shape[-1]), jnp.float32)
    for tap_index, window in enumerate(windows(padded, brick_edge)):
        result = result + jnp.dot(window.reshape(-1, channels), kernels[tap_index], preferred_element_type=jnp.float32)
    return result.reshape(padded.shape[0], brick_edge, brick_edge, brick_edge, -1)


def weight_terms(padded, grads, brick_edge):
    channels = padded.shape[-1]
    flat_grad = grads.reshape(-1, grads.shape[-1])
    tap_terms = [lax.dot_general(window.reshape(-1, channels), flat_grad, (((0,), (0,)), ((), ())), preferred_element_type=jnp.float32) for window in windows(padded, brick_edge)]
    return jnp.concatenate(tap_terms, axis=0)


def route_units(faces_all, send_list):
    devices = faces_all.shape[0]
    spread = send_list.shape[1]
    link_count = send_list.shape[2]
    reach_span = (spread - 1) // 2
    column = jnp.arange(spread, dtype=jnp.int32)
    source = jnp.arange(devices, dtype=jnp.int32)[:, None] + reach_span - column[None, :]
    inside = (source >= 0) & (source < devices)
    clipped = jnp.clip(source, 0, devices - 1)
    chosen = send_list[clipped[:, :, None], column[None, :, None], jnp.arange(link_count, dtype=jnp.int32)[None, None, :]]
    usable = inside[:, :, None] & (chosen >= 0)
    picked = faces_all[clipped[:, :, None], jnp.clip(chosen, 0, faces_all.shape[1] - 1)]
    picked = picked * usable.astype(picked.dtype)[..., None, None, None]
    return picked.reshape(devices, spread * link_count, picked.shape[3], picked.shape[4], picked.shape[5])


def one_volume(volume_args, kernels, mirrored, bias_row):
    features, occupancy, counts, send_list, neighbours, cotangent = volume_args
    devices = counts.shape[0]
    bricks = features.shape[0]
    slot_count = bricks // devices
    brick_edge = features.shape[1]
    channels = features.shape[3] // brick_edge
    shaped = (devices, slot_count, brick_edge, brick_edge, brick_edge, channels)
    live_slot = (jnp.arange(bricks, dtype=jnp.int32) % slot_count < jnp.repeat(counts, slot_count)).astype(jnp.int32)
    active = (occupancy * live_slot[:, None]).reshape(devices, slot_count, brick_edge, brick_edge, brick_edge, 1)
    masked = features.reshape(shaped) * active.astype(features.dtype)
    listing_all = neighbours.reshape(devices, slot_count, 26)
    grad_all = cotangent.reshape(shaped)

    def faces_of(values):
        return jax.vmap(face_planes)(values).reshape(devices, slot_count * 6, brick_edge, brick_edge, channels)

    units_input = route_units(faces_of(masked), send_list)

    def forward(device_args):
        masked_dev, units_dev, listing, active_dev, grad_dev = device_args
        padded_input = halo_block(masked_dev, units_dev, listing)
        pre_activation = convolve(padded_input, kernels, brick_edge) + bias_row
        sigmoid_pre = jax.nn.sigmoid(pre_activation)
        active_full = active_dev.astype(jnp.float32)
        block_output = (pre_activation * sigmoid_pre * active_full).astype(jnp.bfloat16)
        grad_pre = (grad_dev.astype(jnp.float32) * sigmoid_pre * (1.0 + pre_activation * (1.0 - sigmoid_pre)) * active_full).astype(jnp.bfloat16)
        return block_output, grad_pre

    block_output, grad_pre = lax.map(forward, (masked, units_input, listing_all, active, grad_all))
    units_grad = route_units(faces_of(grad_pre), send_list)

    def backward(carry, device_args):
        masked_dev, units_in_dev, units_grad_dev, listing, active_dev, grad_pre_dev = device_args
        padded_input = halo_block(masked_dev, units_in_dev, listing)
        padded_grad = halo_block(grad_pre_dev, units_grad_dev, listing)
        grad_input = (convolve(padded_grad, mirrored, brick_edge) * active_dev.astype(jnp.float32)).astype(jnp.bfloat16)
        weight_grad = weight_terms(padded_input, grad_pre_dev, brick_edge)
        bias_grad = jnp.sum(grad_pre_dev.astype(jnp.float32).reshape(-1, channels), axis=0)
        return (carry[0] + weight_grad, carry[1] + bias_grad), grad_input

    start_sums = (jnp.zeros((27 * channels, channels), jnp.float32), jnp.zeros((channels,), jnp.float32))
    sums, grad_input = lax.scan(backward, start_sums, (masked, units_input, units_grad, listing_all, active, grad_pre))
    return block_output.reshape(features.shape), grad_input.reshape(features.shape), sums[0], sums[1]


def reference(features, occupancy, counts, send_units, neighbours, weight, conv_bias, cotangent):
    channels = weight.shape[1]
    kernels = weight.reshape(27, channels, channels)
    mirrored = jnp.swapaxes(kernels[::-1], 1, 2)
    bias_row = conv_bias.astype(jnp.float32)

    def per_volume(carry, volume_args):
        block_output, grad_input, weight_grad, bias_grad = one_volume(volume_args, kernels, mirrored, bias_row)
        return (carry[0] + weight_grad, carry[1] + bias_grad), (block_output, grad_input)

    start_sums = (jnp.zeros((27 * channels, channels), jnp.float32), jnp.zeros((channels,), jnp.float32))
    sums, results = lax.scan(per_volume, start_sums, (features, occupancy, counts, send_units, neighbours, cotangent))
    return results[0], results[1], sums[0], sums[1]
```

```python
import functools

import jax
import jax.numpy as jnp
from jax import lax
from jax.experimental import pallas as pl
from jax.experimental.pallas import tpu as pltpu
from jax.sharding import PartitionSpec as P

F32 = jnp.float32
BF16 = jnp.bfloat16
LANES = 128
UNIT_ROWS = 32
Z_ROWS = 64
DN_NT = (((1,), (1,)), ((), ()))
DN_NN = (((1,), (0,)), ((), ()))


def vmem():
    return pl.BlockSpec(memory_space=pltpu.VMEM)


def smem():
    return pl.BlockSpec(memory_space=pltpu.SMEM)


def offset_number(ox, oy, oz):
    flat = (ox + 1) * 9 + (oy + 1) * 3 + (oz + 1)
    return flat if flat < 13 else flat - 1


def low_half(shape):
    return lax.broadcasted_iota(jnp.int32, shape, len(shape) - 1) % LANES < 64


def chunk_rows(block):
    return [block[8 * q : 8 * q + 8] for q in range(4)]


def pack_units(values, send, outs):
    slots = values.shape[1] // 64 - 1
    low = low_half((64, LANES))
    for column, out in enumerate(outs):

        def base(link):
            unit = send[column, link]
            slot = jnp.where(unit < 0, slots, (unit * 43) >> 8)
            return pl.multiple_of(slot * 64, 64)

        for half in range(2):
            for face in range(4):
                start = base(half * 6 + face)
                if face < 2:
                    where = pl.ds(start + 56 * face, 8)
                else:
                    where = pl.ds(start + 7 * (face - 2), 8, stride=8)
                packed = jnp.concatenate([values[q, where, :] for q in range(4)], axis=0)
                at = (half * 4 + face) * UNIT_ROWS
                out[at : at + UNIT_ROWS, :] = packed.astype(BF16)
            first = values[0, pl.ds(base(half * 6 + 4), 64), :]
            last = values[3, pl.ds(base(half * 6 + 5), 64), :]
            at = 8 * UNIT_ROWS + half * Z_ROWS
            out[at : at + Z_ROWS, :] = jnp.where(low, first, last).astype(BF16)


def prepare_kernel(
    features, occupancy, counts, send, listing, weight_t, bias,
    masked_out, mask_out, rows_out, shard_out, u0, u1, u2, u3, u4, values,
):
    bricks = features.shape[0]
    live = lax.broadcasted_iota(jnp.int32, (bricks, 512), 0) < counts[0, 0]
    occ = jnp.where(live, occupancy[...], 0).astype(F32)
    row = lax.broadcasted_iota(jnp.int32, (64, 512), 0)
    col = lax.broadcasted_iota(jnp.int32, (64, 512), 1)
    same = (col >> 3) == row
    spread = jnp.concatenate(
        [jnp.where(same, occ[b : b + 1, :], 0.0) for b in range(bricks)], axis=0
    ).astype(BF16)
    z_row = lax.broadcasted_iota(jnp.int32, (512, 512), 0) & 7
    z_col = lax.broadcasted_iota(jnp.int32, (512, 512), 1) >> 6
    expand = jnp.where(z_row == z_col, 1.0, 0.0).astype(BF16)
    mask = jnp.dot(spread, expand, preferred_element_type=F32)
    mask_out[...] = mask.astype(BF16).reshape(mask_out.shape)
    value = features[...].astype(F32).reshape(bricks * 64, 512) * mask
    masked_out[...] = value.astype(BF16).reshape(masked_out.shape)
    for q in range(4):
        values[q, 0 : bricks * 64, :] = value[:, q * LANES : (q + 1) * LANES]
    values[:, bricks * 64 :, :] = jnp.zeros((4, 64, LANES), F32)
    pack_units(values, send, (u0, u1, u2, u3, u4))

    number = listing[...]
    column = (number * 43) >> 9
    link = number - column * 12
    half = (link >= 6).astype(jnp.int32)
    face = link - 6 * half
    base = column * (8 * UNIT_ROWS + 2 * Z_ROWS)
    plain = base + (half * 4 + face) * UNIT_ROWS
    paired = base + 8 * UNIT_ROWS + half * Z_ROWS
    none = 5 * (8 * UNIT_ROWS + 2 * Z_ROWS)
    rows_out[...] = jnp.where(number < 0, none, jnp.where(face < 4, plain, paired))

    shard = weight_t.shape[1]
    width = shard_out.shape[1]
    count = bias.shape[1]
    shard_out[...] = jnp.zeros(shard_out.shape, F32)
    shard_out[:, 0:shard] = weight_t[...].astype(F32)
    shard_out[0:1, shard : shard + count] = bias[...].astype(F32)


def gather_units(table, received):
    at = 0
    for part in received:
        table[at : at + part.shape[0], :] = part[...]
        at += part.shape[0]
    table[at:, :] = jnp.zeros((table.shape[0] - at, LANES), BF16)


def assemble(source, table, rows, windows, sides, walls):
    low8 = low_half((8, LANES))
    sub = lax.broadcasted_iota(jnp.int32, (8, LANES), 0)
    top, bottom = sub == 0, sub == 7

    def put(pair, xp, per_brick):
        for e in range(3):
            stacked = [
                jnp.concatenate([per_brick[0][e][i], per_brick[1][e][i]], axis=0)
                for i in range(5)
            ]
            low16 = low_half((16, LANES))
            before = [stacked[4]] + stacked[:3]
            after = stacked[1:4] + [stacked[4]]
            for q in range(4):
                windows[e, q, pair, xp, :, 0:LANES] = stacked[q].astype(BF16)
                windows[e, q, pair, xp, :, LANES:] = jnp.where(
                    low16, after[q], before[q]
                ).astype(BF16)

    def one_pair(pair, carry):
        def unit(brick, ox, oy, oz):
            return pl.multiple_of(rows[brick, offset_number(ox, oy, oz)], UNIT_ROWS)

        def plane(brick, ox, oy):
            chunks = chunk_rows(table[pl.ds(unit(brick, ox, oy, 0), UNIT_ROWS), :].astype(F32))
            after = table[pl.ds(unit(brick, ox, oy, 1), UNIT_ROWS), :].astype(F32)[0:8]
            before = table[pl.ds(unit(brick, ox, oy, -1), UNIT_ROWS), :].astype(F32)[24:32]
            return chunks + [jnp.where(low8, after, before)]

        for b2 in range(2):
            brick = pair * 2 + b2
            low64 = low_half((64, LANES))
            after = table[pl.ds(unit(brick, 0, 0, 1), Z_ROWS), :].astype(F32)
            before = table[pl.ds(unit(brick, 0, 0, -1), Z_ROWS), :].astype(F32)
            walls[b2] = jnp.where(low64, after, before)
            for side, oy in enumerate((-1, 1)):
                for i, part in enumerate(plane(brick, 0, oy)):
                    sides[b2, side, i] = part

        for ox in (-1, 1):
            per_brick = []
            for b2 in range(2):
                brick = pair * 2 + b2
                centre = plane(brick, ox, 0)
                lower = plane(brick, ox, -1)
                upper = plane(brick, ox, 1)
                per_brick.append(
                    [
                        [
                            pltpu.roll(jnp.where(bottom, l, c), 1, 0)
                            for l, c in zip(lower, centre)
                        ],
                        centre,
                        [
                            pltpu.roll(jnp.where(top, u, c), 7, 0)
                            for u, c in zip(upper, centre)
                        ],
                    ]
                )
            put(pair, 0 if ox < 0 else 9, per_brick)

        def one_x(x, carry):
            per_brick = []
            for b2 in range(2):
                brick = pair * 2 + b2
                block = source[brick, x].astype(F32)
                centre = [block[:, q * LANES : (q + 1) * LANES] for q in range(4)]
                centre.append(walls[b2, pl.ds(pl.multiple_of(x * 8, 8), 8), :])
                lower = [
                    jnp.broadcast_to(sides[b2, 0, i, pl.ds(x, 1), :], (8, LANES))
                    for i in range(5)
                ]
                upper = [
                    jnp.broadcast_to(sides[b2, 1, i, pl.ds(x, 1), :], (8, LANES))
                    for i in range(5)
                ]
                per_brick.append(
                    [
                        [jnp.where(top, l, pltpu.roll(c, 1, 0)) for l, c in zip(lower, centre)],
                        centre,
                        [
                            jnp.where(bottom, u, pltpu.roll(c, 7, 0))
                            for u, c in zip(upper, centre)
                        ],
                    ]
                )
            put(pair, x + 1, per_brick)
            return carry

        return lax.fori_loop(0, 8, one_x, carry)

    lax.fori_loop(0, windows.shape[2], one_pair, 0)


def spread_weights(gathered, flat, shifted, shard):
    for k in range(gathered.shape[0]):
        flat[:, k * shard : (k + 1) * shard] = gathered[k][:, 0:shard].astype(F32)
    total = gathered.shape[0] * shard
    flat[:, total:] = jnp.zeros((64, flat.shape[1] - total), F32)
    shifted[:, :] = pltpu.roll(flat[...], flat.shape[1] - 64, 1)


def taps_pair(flat, shifted, first):
    if first % 2 == 0:
        return flat[:, first * 64 : first * 64 + LANES]
    return shifted[:, (first - 1) * 64 : (first - 1) * 64 + LANES]


def forward_kernel(
    masked, mask, cotangent, gathered, rows, send, r0, r1, r2, r3, r4,
    block_out, grad_out, u0, u1, u2, u3, u4, *rest, shard,
):
    chunk_outs = rest[:-9]
    table, windows, sides, walls, flat, shifted, toeplitz, values, flipped = rest[-9:]
    groups = gathered.shape[0]
    bricks = masked.shape[0]
    pairs = bricks // 2
    gather_units(table, (r0, r1, r2, r3, r4))
    assemble(masked, table, rows, windows, sides, walls)
    spread_weights(gathered, flat, shifted, shard)
    low = low_half((64, LANES))
    for ae in range(9):
        one = taps_pair(flat, shifted, 3 * ae)
        two = jnp.where(low, taps_pair(flat, shifted, 3 * ae + 2), 0.0)
        late = jnp.concatenate([one, two], axis=1)
        toeplitz[ae, 64:128, :] = late.astype(BF16)
        toeplitz[ae, 0:64, :] = pltpu.roll(late, 192, 1).astype(BF16)

    lane = lax.broadcasted_iota(jnp.int32, (1, LANES), 1)
    bias_lane = shard % LANES
    bias_tile = shard - bias_lane
    count = 64 // groups
    bias_row = jnp.zeros((1, LANES), F32)
    for k in range(groups):
        tile = gathered[k][0:16, bias_tile : bias_tile + LANES].astype(F32)[0:8]
        moved = pltpu.roll(tile, (count * k - bias_lane) % LANES, 1)[0:1]
        bias_row += jnp.where((lane >= count * k) & (lane < count * (k + 1)), moved, 0.0)
    bias_row += pltpu.roll(jnp.broadcast_to(bias_row, (8, LANES)), 64, 1)[0:1]

    values[:, bricks * 64 :, :] = jnp.zeros((4, 64, LANES), F32)

    def one_chunk(q, bias_sum):
        total = jnp.zeros((pairs * LANES, LANES), F32)
        for a in range(3):
            for e in range(3):
                window = windows[e, q, :, a : a + 8].reshape(pairs * LANES, 256)
                total += lax.dot_general(
                    window, toeplitz[3 * a + e], DN_NT, preferred_element_type=F32
                )
        pre = (total + bias_row).reshape(pairs, 8, 2, 8, LANES)
        lanes = pl.ds(pl.multiple_of(q * LANES, LANES), LANES)
        for brick in range(bricks):
            p = pre[brick // 2, :, brick % 2]
            active = mask[brick, :, :, lanes].astype(F32)
            sig = jax.nn.sigmoid(p)
            block_out[brick, :, :, lanes] = (p * sig * active).astype(BF16)
            grad = (
                cotangent[brick, :, :, lanes].astype(F32)
                * sig
                * (1.0 + p * (1.0 - sig))
                * active
            ).astype(BF16)
            grad_out[brick, :, :, lanes] = grad
            wide = grad.astype(F32).reshape(64, LANES)
            values[q, brick * 64 : (brick + 1) * 64, :] = wide
            bias_sum += jnp.sum(wide.reshape(8, 8, LANES), axis=0)
        return bias_sum

    bias_sum = lax.fori_loop(0, 4, one_chunk, jnp.zeros((8, LANES), F32))
    pack_units(values, send, (u0, u1, u2, u3, u4))

    for q in range(4):
        for pair in range(pairs):
            by_x = []
            for x in range(8):
                for b2 in range(2):
                    at = (pair * 2 + b2) * 64 + x * 8
                    by_x.append(values[q, at : at + 8, :])
            flipped[q, :, pair * LANES : (pair + 1) * LANES] = jnp.transpose(
                jnp.concatenate(by_x, axis=0)
            ).astype(BF16)
    for ae in range(9):
        a, e = ae // 3, ae % 3
        total = jnp.zeros((LANES, 256), F32)
        for q in range(4):
            window = windows[e, q, :, a : a + 8].reshape(pairs * LANES, 256)
            total += jnp.dot(flipped[q], window, preferred_element_type=F32)
        flat[:, 192 * ae : 192 * ae + 256] = total[64:128] + pltpu.roll(total[0:64], 64, 1)

    width = chunk_outs[0].shape[1]
    bias_all = jnp.sum(bias_sum, axis=0, keepdims=True)
    bias_all = jnp.broadcast_to(bias_all, (8, LANES))
    bias_all = bias_all + pltpu.roll(bias_all, 64, 1)
    bias_all = pltpu.roll(bias_all, bias_lane, 1)
    row8 = lax.broadcasted_iota(jnp.int32, (8, LANES), 0)
    lane8 = lax.broadcasted_iota(jnp.int32, (8, LANES), 1)
    keep = (row8 == 0) & (lane8 >= bias_lane) & (lane8 < bias_lane + 64)
    me = lax.axis_index("dp")
    for k in range(groups):
        part = flat[:, k * shard : (k + 1) * shard]
        shifted[:, 0:shard] = part
        shifted[:, shard:width] = jnp.zeros((64, width - shard), F32)
        tile = shifted[0:8, bias_tile : bias_tile + LANES]
        shifted[0:8, bias_tile : bias_tile + LANES] = jnp.where(keep, bias_all, tile)
        block = shifted[:, 0:width].astype(BF16)
        for m in range(groups):

            @pl.when(me ^ m == k)
            def _(m=m, block=block):
                chunk_outs[m][...] = block


def backward_kernel(
    grad, mask, gathered, rows, r0, r1, r2, r3, r4, out,
    table, windows, sides, walls, flat, shifted, toeplitz, *, shard,
):
    bricks = grad.shape[0]
    pairs = bricks // 2
    gather_units(table, (r0, r1, r2, r3, r4))
    assemble(grad, table, rows, windows, sides, walls)
    spread_weights(gathered, flat, shifted, shard)
    low = low_half((64, LANES))
    for ae in range(9):
        m = 3 * (8 - ae)
        first = taps_pair(flat, shifted, m)
        second = taps_pair(flat, shifted, m + 1)
        third = taps_pair(flat, shifted, m + 2)
        toeplitz[ae, 0:64, :] = second.astype(BF16)
        toeplitz[ae, 64:128, :] = first.astype(BF16)
        toeplitz[ae, 128:192, :] = jnp.where(low, 0.0, pltpu.roll(first, 64, 1)).astype(BF16)
        toeplitz[ae, 192:256, :] = jnp.where(low, third, 0.0).astype(BF16)

    def one_chunk(q, carry):
        total = jnp.zeros((pairs * LANES, LANES), F32)
        for a in range(3):
            for e in range(3):
                window = windows[e, q, :, a : a + 8].reshape(pairs * LANES, 256)
                total += jnp.dot(window, toeplitz[3 * a + e], preferred_element_type=F32)
        total = total.reshape(pairs, 8, 2, 8, LANES)
        lanes = pl.ds(pl.multiple_of(q * LANES, LANES), LANES)
        for brick in range(bricks):
            active = mask[brick, :, :, lanes].astype(F32)
            out[brick, :, :, lanes] = (total[brick // 2, :, brick % 2] * active).astype(BF16)
        return carry

    lax.fori_loop(0, 4, one_chunk, 0)


def finish_kernel(mine, other, weight_out, bias_out):
    shard = weight_out.shape[1]
    count = bias_out.shape[1]
    total = mine[...].astype(F32) + other[...].astype(F32)
    weight_out[...] = total[:, 0:shard]
    bias_lane = shard % LANES
    bias_tile = shard - bias_lane
    tile = total[0:8, bias_tile : bias_tile + LANES]
    me = lax.axis_index("dp")
    moved = pltpu.roll(tile, 2 * LANES - bias_lane - me * count, 1)
    bias_out[...] = moved[0:1, 0:count]


def passed_along(block, axis, distance):
    devices = range(lax.axis_size(axis))
    route = [(i - distance, i) for i in devices if i - distance in devices]
    return lax.ppermute(block, axis, route)


def swapped(block, axis, bit):
    return lax.ppermute(block, axis, [(i, i ^ bit) for i in range(lax.axis_size(axis))])


def exchanged(units):
    reach = len(units) // 2
    return [
        unit if column == reach else passed_along(unit, "space", column - reach)
        for column, unit in enumerate(units)
    ]


def body(features, occupancy, counts, send_units, neighbours, weight, conv_bias, cotangent):
    grid_shape = features.shape[1:]
    bricks = grid_shape[0]
    pairs = bricks // 2
    spread = send_units.shape[2]
    shard = weight.shape[0]
    channels = weight.shape[1]
    groups = lax.axis_size("dp")
    count = conv_bias.shape[0]
    width = -(-(shard + channels) // LANES) * LANES
    unit_rows = 8 * UNIT_ROWS + 2 * Z_ROWS
    units_type = jax.ShapeDtypeStruct((unit_rows, LANES), BF16)
    grid_type = jax.ShapeDtypeStruct(grid_shape, BF16)
    send = send_units[0, 0]
    params = pltpu.CompilerParams(vmem_limit_bytes=48 * 1024 * 1024)

    masked, mask, rows, own_shard, *units = pl.pallas_call(
        prepare_kernel,
        name="prepare",
        out_shape=[
            grid_type,
            grid_type,
            jax.ShapeDtypeStruct(neighbours.shape[1:], jnp.int32),
            jax.ShapeDtypeStruct((channels, width), F32),
        ]
        + [units_type] * spread,
        in_specs=[vmem(), vmem(), smem(), smem(), vmem(), vmem(), vmem()],
        out_specs=[vmem()] * (4 + spread),
        scratch_shapes=[pltpu.VMEM((4, (bricks + 1) * 64, LANES), F32)],
        compiler_params=params,
    )(
        features[0],
        occupancy[0],
        counts,
        send,
        neighbours[0],
        weight.T,
        conv_bias.reshape(1, count),
    )

    received = exchanged(units)
    gathered = lax.all_gather(own_shard.astype(BF16), "dp", axis=0)

    table = pltpu.VMEM((spread * unit_rows + Z_ROWS, LANES), BF16)
    windows = pltpu.VMEM((3, 4, pairs, 10, 16, 256), BF16)
    sides = pltpu.VMEM((2, 2, 5, 8, LANES), F32)
    walls = pltpu.VMEM((2, 64, LANES), F32)
    flat = pltpu.VMEM((channels, 28 * 64), F32)
    block_output, grad, *rest = pl.pallas_call(
        functools.partial(forward_kernel, shard=shard),
        name="forward",
        out_shape=[grid_type, grid_type]
        + [units_type] * spread
        + [jax.ShapeDtypeStruct((channels, width), BF16)] * groups,
        in_specs=[vmem()] * 4 + [smem(), smem()] + [vmem()] * spread,
        out_specs=[vmem()] * (2 + spread + groups),
        scratch_shapes=[
            table,
            windows,
            sides,
            walls,
            flat,
            flat,
            pltpu.VMEM((9, LANES, 256), BF16),
            pltpu.VMEM((4, (bricks + 1) * 64, LANES), F32),
            pltpu.VMEM((4, LANES, pairs * LANES), BF16),
        ],
        compiler_params=params,
    )(masked, mask, cotangent[0], gathered, rows, send, *received)
    grad_units, blocks = rest[:spread], rest[spread:]

    grad_received = exchanged(grad_units)
    shares = [blocks[0]] + [swapped(blocks[m], "dp", m) for m in range(1, groups)]

    grad_input = pl.pallas_call(
        functools.partial(backward_kernel, shard=shard),
        name="backward",
        out_shape=grid_type,
        in_specs=[vmem()] * 3 + [smem()] + [vmem()] * spread,
        out_specs=vmem(),
        scratch_shapes=[
            table,
            windows,
            sides,
            walls,
            flat,
            flat,
            pltpu.VMEM((9, 256, LANES), BF16),
        ],
        compiler_params=params,
    )(grad, mask, gathered, rows, *grad_received)

    total = sum(share.astype(F32) for share in shares).astype(BF16)
    devices = lax.axis_size("space")
    bit = 1
    while 2 * bit < devices:
        total = (total.astype(F32) + swapped(total, "space", bit).astype(F32)).astype(BF16)
        bit *= 2
    weight_share, bias_share = pl.pallas_call(
        finish_kernel,
        name="finish",
        out_shape=[
            jax.ShapeDtypeStruct((channels, shard), F32),
            jax.ShapeDtypeStruct((1, count), F32),
        ],
        in_specs=[vmem()] * 2,
        out_specs=[vmem()] * 2,
        compiler_params=params,
    )(total, swapped(total, "space", bit))
    return (
        block_output[None],
        grad_input[None],
        weight_share.T,
        bias_share.reshape(count),
    )


def solution(mesh):
    placed = (
        P("dp", "space", None, None, None),
        P("dp", "space", None),
        P("dp", "space"),
        P("dp", "space", None, None),
        P("dp", "space", None),
        P("dp", None),
        P("dp"),
        P("dp", "space", None, None, None),
    )
    return jax.shard_map(
        body,
        mesh=mesh,
        in_specs=placed,
        out_specs=(
            P("dp", "space", None, None, None),
            P("dp", "space", None, None, None),
            P("dp", None),
            P("dp"),
        ),
        check_vma=False,
    )
```

```python
import functools

import jax
import jax.numpy as jnp
from jax import lax
from jax.experimental import pallas as pl
from jax.experimental.pallas import tpu as pltpu
from jax.sharding import PartitionSpec as P

F32 = jnp.float32
BF16 = jnp.bfloat16
LANES = 128
UNIT_ROWS = 32
Z_ROWS = 64
DN_NT = (((1,), (1,)), ((), ()))
DN_NN = (((1,), (0,)), ((), ()))


def vmem():
    return pl.BlockSpec(memory_space=pltpu.VMEM)


def smem():
    return pl.BlockSpec(memory_space=pltpu.SMEM)


def offset_number(ox, oy, oz):
    flat = (ox + 1) * 9 + (oy + 1) * 3 + (oz + 1)
    return flat if flat < 13 else flat - 1


def low_half(shape):
    return lax.broadcasted_iota(jnp.int32, shape, len(shape) - 1) % LANES < 64


def chunk_rows(block):
    return [block[8 * q : 8 * q + 8] for q in range(4)]


def upward(device, distance):
    return lax.rem(lax.div(device, distance), 2)


def pack_units(values, send, outs):
    slots = values.shape[1] // 64 - 1
    reach = len(outs) // 2
    low = low_half((64, LANES))
    device = lax.axis_index("space")
    for number, out in enumerate(outs):
        column = reach
        if number > 0:
            distance = (number + 1) // 2
            up = upward(device, distance) == (number + 1) % 2
            column = jnp.where(up, reach + distance, reach - distance)

        def base(link):
            unit = send[column, 0, link]
            slot = jnp.where(unit < 0, slots, (unit * 43) >> 8)
            return pl.multiple_of(slot * 64, 64)

        for half in range(2):
            for face in range(4):
                start = base(half * 6 + face)
                if face < 2:
                    where = pl.ds(start + 56 * face, 8)
                else:
                    where = pl.ds(start + 7 * (face - 2), 8, stride=8)
                packed = jnp.concatenate([values[q, where, :] for q in range(4)], axis=0)
                at = (half * 4 + face) * UNIT_ROWS
                out[at : at + UNIT_ROWS, :] = packed.astype(BF16)
            first = values[0, pl.ds(base(half * 6 + 4), 64), :]
            last = values[3, pl.ds(base(half * 6 + 5), 64), :]
            at = 8 * UNIT_ROWS + half * Z_ROWS
            out[at : at + Z_ROWS, :] = jnp.where(low, first, last).astype(BF16)


def prepare_kernel(
    features_hbm, occupancy_hbm, counts_hbm, send_hbm, listing_hbm, weight_hbm, bias_hbm,
    masked_out, mask_out, rows_out, send_out, shard_out, u0, u1, u2, u3, u4,
    values, features, occupancy, counts, listing, weight_t, bias, rows, sems,
):
    copies = [
        pltpu.make_async_copy(src, dst, sems.at[i])
        for i, (src, dst) in enumerate(
            (
                (occupancy_hbm, occupancy),
                (counts_hbm, counts),
                (features_hbm, features),
                (send_hbm, send_out),
                (listing_hbm, listing),
                (weight_hbm, weight_t),
                (bias_hbm, bias),
            )
        )
    ]
    for copy in copies:
        copy.start()
    bricks = features.shape[0]
    shard_out[...] = jnp.zeros(shard_out.shape, BF16)
    values[:, bricks * 64 :, :] = jnp.zeros((4, 64, LANES), F32)
    row = lax.broadcasted_iota(jnp.int32, (64, 512), 0)
    col = lax.broadcasted_iota(jnp.int32, (64, 512), 1)
    same = (col >> 3) == row
    z_row = lax.broadcasted_iota(jnp.int32, (512, 512), 0) & 7
    z_col = lax.broadcasted_iota(jnp.int32, (512, 512), 1) >> 6
    expand = jnp.where(z_row == z_col, 1.0, 0.0).astype(BF16)

    copies[0].wait()
    copies[1].wait()
    live = lax.broadcasted_iota(jnp.int32, (bricks, 512), 0) < counts[0, 0]
    occ = jnp.where(live, occupancy[...], 0).astype(F32)
    spread = jnp.concatenate(
        [jnp.where(same, occ[b : b + 1, :], 0.0) for b in range(bricks)], axis=0
    ).astype(BF16)
    mask = jnp.dot(spread, expand, preferred_element_type=F32)
    mask_out[...] = mask.astype(BF16).reshape(mask_out.shape)
    copies[2].wait()
    value = features[...].astype(F32).reshape(bricks * 64, 512) * mask
    masked_out[...] = value.astype(BF16).reshape(masked_out.shape)
    for q in range(4):
        values[q, 0 : bricks * 64, :] = value[:, q * LANES : (q + 1) * LANES]
    copies[3].wait()
    pack_units(values, send_out, (u0, u1, u2, u3, u4))

    copies[4].wait()
    device = lax.axis_index("space")
    number = listing[...]
    column = (number * 43) >> 9
    link = number - column * 12
    half = (link >= 6).astype(jnp.int32)
    face = link - 6 * half
    block = jnp.zeros(number.shape, jnp.int32)
    for distance in (1, 2):
        up = upward(device, distance)
        block = jnp.where(column == 2 - distance, 2 * distance - 1 + up, block)
        block = jnp.where(column == 2 + distance, 2 * distance - up, block)
    base = block * (8 * UNIT_ROWS + 2 * Z_ROWS)
    plain = base + (half * 4 + face) * UNIT_ROWS
    paired = base + 8 * UNIT_ROWS + half * Z_ROWS
    none = 5 * (8 * UNIT_ROWS + 2 * Z_ROWS)
    rows[...] = jnp.where(number < 0, none, jnp.where(face < 4, plain, paired))
    last = pltpu.make_async_copy(rows, rows_out, sems.at[len(copies)])
    last.start()

    copies[5].wait()
    copies[6].wait()
    shard = weight_t.shape[1]
    lead = shard // LANES * LANES
    count = bias.shape[1]
    shard_out[:, 0:lead] = weight_t[:, 0:lead]
    tile = jnp.concatenate(
        [weight_t[:, lead:shard].astype(F32), jnp.zeros((64, lead + LANES - shard), F32)], axis=1
    )
    offset = shard - lead
    behind = jnp.concatenate(
        [bias[...].astype(F32), jnp.zeros((1, LANES - count), F32)], axis=1
    )
    behind = pltpu.roll(jnp.broadcast_to(behind, (64, LANES)), offset, 1)
    first = lax.broadcasted_iota(jnp.int32, (64, LANES), 0) == 0
    lane = lax.broadcasted_iota(jnp.int32, (64, LANES), 1)
    behind = jnp.where(first & (lane >= offset) & (lane < offset + count), behind, 0.0)
    shard_out[:, lead : lead + LANES] = (tile + behind).astype(BF16)
    last.wait()


def gather_units(table, received):
    at = 0
    for part in received:
        table[at : at + part.shape[0], :] = part[...]
        at += part.shape[0]
    table[at:, :] = jnp.zeros((table.shape[0] - at, LANES), BF16)


def assemble(source, table, rows, windows, sides, walls):
    low8 = low_half((8, LANES))
    sub = lax.broadcasted_iota(jnp.int32, (8, LANES), 0)
    top, bottom = sub == 0, sub == 7

    def put(pair, xp, per_brick):
        for e in range(3):
            stacked = [
                jnp.concatenate([per_brick[0][e][i], per_brick[1][e][i]], axis=0)
                for i in range(5)
            ]
            low16 = low_half((16, LANES))
            before = [stacked[4]] + stacked[:3]
            after = stacked[1:4] + [stacked[4]]
            for q in range(4):
                windows[e, q, pair, xp, :, 0:LANES] = stacked[q].astype(BF16)
                windows[e, q, pair, xp, :, LANES:] = jnp.where(
                    low16, after[q], before[q]
                ).astype(BF16)

    def one_pair(pair, carry):
        def unit(brick, ox, oy, oz):
            return pl.multiple_of(rows[brick, offset_number(ox, oy, oz)], UNIT_ROWS)

        def plane(brick, ox, oy):
            chunks = chunk_rows(table[pl.ds(unit(brick, ox, oy, 0), UNIT_ROWS), :].astype(F32))
            after = table[pl.ds(unit(brick, ox, oy, 1), UNIT_ROWS), :].astype(F32)[0:8]
            before = table[pl.ds(unit(brick, ox, oy, -1), UNIT_ROWS), :].astype(F32)[24:32]
            return chunks + [jnp.where(low8, after, before)]

        for b2 in range(2):
            brick = pair * 2 + b2
            low64 = low_half((64, LANES))
            after = table[pl.ds(unit(brick, 0, 0, 1), Z_ROWS), :].astype(F32)
            before = table[pl.ds(unit(brick, 0, 0, -1), Z_ROWS), :].astype(F32)
            walls[b2] = jnp.where(low64, after, before)
            for side, oy in enumerate((-1, 1)):
                for i, part in enumerate(plane(brick, 0, oy)):
                    sides[b2, side, i] = part

        for ox in (-1, 1):
            per_brick = []
            for b2 in range(2):
                brick = pair * 2 + b2
                centre = plane(brick, ox, 0)
                lower = plane(brick, ox, -1)
                upper = plane(brick, ox, 1)
                per_brick.append(
                    [
                        [
                            pltpu.roll(jnp.where(bottom, l, c), 1, 0)
                            for l, c in zip(lower, centre)
                        ],
                        centre,
                        [
                            pltpu.roll(jnp.where(top, u, c), 7, 0)
                            for u, c in zip(upper, centre)
                        ],
                    ]
                )
            put(pair, 0 if ox < 0 else 9, per_brick)

        def one_x(x, carry):
            per_brick = []
            for b2 in range(2):
                brick = pair * 2 + b2
                block = source[brick, x].astype(F32)
                centre = [block[:, q * LANES : (q + 1) * LANES] for q in range(4)]
                centre.append(walls[b2, pl.ds(pl.multiple_of(x * 8, 8), 8), :])
                lower = [
                    jnp.broadcast_to(sides[b2, 0, i, pl.ds(x, 1), :], (8, LANES))
                    for i in range(5)
                ]
                upper = [
                    jnp.broadcast_to(sides[b2, 1, i, pl.ds(x, 1), :], (8, LANES))
                    for i in range(5)
                ]
                per_brick.append(
                    [
                        [jnp.where(top, l, pltpu.roll(c, 1, 0)) for l, c in zip(lower, centre)],
                        centre,
                        [
                            jnp.where(bottom, u, pltpu.roll(c, 7, 0))
                            for u, c in zip(upper, centre)
                        ],
                    ]
                )
            put(pair, x + 1, per_brick)
            return carry

        return lax.fori_loop(0, 8, one_x, carry)

    lax.fori_loop(0, windows.shape[2], one_pair, 0)


def weights_kernel(*refs, shard, groups):
    shards = refs[:groups]
    forward_out, backward_out, bias_out, gathered, flat, shifted = refs[groups:]
    me = lax.axis_index("dp")
    for m, part in enumerate(shards):
        gathered[m] = part[...]
    for k in range(groups):
        flat[:, k * shard : (k + 1) * shard] = gathered[me ^ k][:, 0:shard].astype(F32)
    total = groups * shard
    flat[:, total:] = jnp.zeros((64, flat.shape[1] - total), F32)
    shifted[:, :] = pltpu.roll(flat[...], flat.shape[1] - 64, 1)
    low = low_half((64, LANES))
    for ae in range(9):
        one = taps_pair(flat, shifted, 3 * ae)
        two = jnp.where(low, taps_pair(flat, shifted, 3 * ae + 2), 0.0)
        late = jnp.concatenate([one, two], axis=1)
        forward_out[ae, 64:128, :] = late.astype(BF16)
        forward_out[ae, 0:64, :] = pltpu.roll(late, 192, 1).astype(BF16)
    for ae in range(9):
        m = 3 * (8 - ae)
        first = taps_pair(flat, shifted, m)
        second = taps_pair(flat, shifted, m + 1)
        third = taps_pair(flat, shifted, m + 2)
        backward_out[ae, 0:64, :] = second.astype(BF16)
        backward_out[ae, 64:128, :] = first.astype(BF16)
        backward_out[ae, 128:192, :] = jnp.where(low, 0.0, pltpu.roll(first, 64, 1)).astype(BF16)
        backward_out[ae, 192:256, :] = jnp.where(low, third, 0.0).astype(BF16)

    lane = lax.broadcasted_iota(jnp.int32, (8, LANES), 1)
    bias_lane = shard % LANES
    bias_tile = shard - bias_lane
    count = 64 // groups
    bias_row = jnp.zeros((8, LANES), F32)
    for k in range(groups):
        tile = gathered[me ^ k][0:16, bias_tile : bias_tile + LANES].astype(F32)[0:8]
        moved = pltpu.roll(tile, (count * k - bias_lane) % LANES, 1)
        bias_row += jnp.where((lane >= count * k) & (lane < count * (k + 1)), moved, 0.0)
    bias_out[...] = bias_row + pltpu.roll(bias_row, 64, 1)


def taps_pair(flat, shifted, first):
    if first % 2 == 0:
        return flat[:, first * 64 : first * 64 + LANES]
    return shifted[:, (first - 1) * 64 : (first - 1) * 64 + LANES]


def forward_kernel(
    masked, mask, cotangent, toeplitz, bias, rows, send, r0, r1, r2, r3, r4,
    block_out, grad_out, u0, u1, u2, u3, u4, *rest, shard,
):
    chunk_outs = rest[:-8]
    table, windows, sides, walls, flat, shifted, values, flipped = rest[-8:]
    groups = len(chunk_outs)
    bricks = masked.shape[0]
    pairs = bricks // 2
    gather_units(table, (r0, r1, r2, r3, r4))
    assemble(masked, table, rows, windows, sides, walls)
    bias_lane = shard % LANES
    bias_tile = shard - bias_lane
    bias_row = bias[0:1, :]
    values[:, bricks * 64 :, :] = jnp.zeros((4, 64, LANES), F32)

    def one_chunk(q, bias_sum):
        total = jnp.zeros((pairs * LANES, LANES), F32)
        for a in range(3):
            for e in range(3):
                window = windows[e, q, :, a : a + 8].reshape(pairs * LANES, 256)
                total += lax.dot_general(
                    window, toeplitz[3 * a + e], DN_NT, preferred_element_type=F32
                )
        pre = (total + bias_row).reshape(pairs, 8, 2, 8, LANES)
        lanes = pl.ds(pl.multiple_of(q * LANES, LANES), LANES)
        for brick in range(bricks):
            p = pre[brick // 2, :, brick % 2]
            active = mask[brick, :, :, lanes].astype(F32)
            sig = jax.nn.sigmoid(p)
            block_out[brick, :, :, lanes] = (p * sig * active).astype(BF16)
            grad = (
                cotangent[brick, :, :, lanes].astype(F32)
                * sig
                * (1.0 + p * (1.0 - sig))
                * active
            ).astype(BF16)
            grad_out[brick, :, :, lanes] = grad
            wide = grad.astype(F32).reshape(64, LANES)
            values[q, brick * 64 : (brick + 1) * 64, :] = wide
            bias_sum += jnp.sum(wide.reshape(8, 8, LANES), axis=0)
        return bias_sum

    bias_sum = lax.fori_loop(0, 4, one_chunk, jnp.zeros((8, LANES), F32))
    pack_units(values, send, (u0, u1, u2, u3, u4))

    for q in range(4):
        for pair in range(pairs):
            by_x = []
            for x in range(8):
                for b2 in range(2):
                    at = (pair * 2 + b2) * 64 + x * 8
                    by_x.append(values[q, at : at + 8, :])
            flipped[q, :, pair * LANES : (pair + 1) * LANES] = jnp.transpose(
                jnp.concatenate(by_x, axis=0)
            ).astype(BF16)
    for ae in range(9):
        a, e = ae // 3, ae % 3
        total = jnp.zeros((LANES, 256), F32)
        for q in range(4):
            window = windows[e, q, :, a : a + 8].reshape(pairs * LANES, 256)
            total += jnp.dot(flipped[q], window, preferred_element_type=F32)
        flat[:, 192 * ae : 192 * ae + 256] = total[64:128] + pltpu.roll(total[0:64], 64, 1)

    width = chunk_outs[0].shape[1]
    bias_all = jnp.sum(bias_sum, axis=0, keepdims=True)
    bias_all = jnp.broadcast_to(bias_all, (8, LANES))
    bias_all = bias_all + pltpu.roll(bias_all, 64, 1)
    bias_all = pltpu.roll(bias_all, bias_lane, 1)
    row8 = lax.broadcasted_iota(jnp.int32, (8, LANES), 0)
    lane8 = lax.broadcasted_iota(jnp.int32, (8, LANES), 1)
    keep = (row8 == 0) & (lane8 >= bias_lane) & (lane8 < bias_lane + 64)
    me = lax.axis_index("dp")
    for k in range(groups):
        part = flat[:, k * shard : (k + 1) * shard]
        shifted[:, 0:shard] = part
        shifted[:, shard:width] = jnp.zeros((64, width - shard), F32)
        tile = shifted[0:8, bias_tile : bias_tile + LANES]
        shifted[0:8, bias_tile : bias_tile + LANES] = jnp.where(keep, bias_all, tile)
        block = shifted[:, 0:width].astype(BF16)
        for m in range(groups):

            @pl.when(me ^ m == k)
            def _(m=m, block=block):
                chunk_outs[m][...] = block


def backward_kernel(
    grad, mask, toeplitz, rows, r0, r1, r2, r3, r4, out, table, windows, sides, walls
):
    bricks = grad.shape[0]
    pairs = bricks // 2
    gather_units(table, (r0, r1, r2, r3, r4))
    assemble(grad, table, rows, windows, sides, walls)

    def one_chunk(q, carry):
        total = jnp.zeros((pairs * LANES, LANES), F32)
        for a in range(3):
            for e in range(3):
                window = windows[e, q, :, a : a + 8].reshape(pairs * LANES, 256)
                total += jnp.dot(window, toeplitz[3 * a + e], preferred_element_type=F32)
        total = total.reshape(pairs, 8, 2, 8, LANES)
        lanes = pl.ds(pl.multiple_of(q * LANES, LANES), LANES)
        for brick in range(bricks):
            active = mask[brick, :, :, lanes].astype(F32)
            out[brick, :, :, lanes] = (total[brick // 2, :, brick % 2] * active).astype(BF16)
        return carry

    lax.fori_loop(0, 4, one_chunk, 0)


def finish_kernel(mine, other, weight_out, bias_out):
    shard = weight_out.shape[1]
    count = bias_out.shape[1]
    total = mine[...].astype(F32) + other[...].astype(F32)
    weight_out[...] = total[:, 0:shard]
    bias_lane = shard % LANES
    bias_tile = shard - bias_lane
    tile = total[0:8, bias_tile : bias_tile + LANES]
    me = lax.axis_index("dp")
    moved = pltpu.roll(tile, 2 * LANES - bias_lane - me * count, 1)
    bias_out[...] = moved[0:1, 0:count]


def swapped(block, axis, bit):
    return lax.ppermute(block, axis, [(i, i ^ bit) for i in range(lax.axis_size(axis))])


def exchanged(units):
    devices = lax.axis_size("space")
    received = [units[0]]
    for number in range(1, len(units)):
        distance = (number + 1) // 2
        turn = (number + 1) % 2
        route = []
        for low in range(devices - distance):
            if low // distance % 2 == turn:
                route += [(low, low + distance), (low + distance, low)]
        received.append(lax.ppermute(units[number], "space", route))
    return received


def body(features, occupancy, counts, send_units, neighbours, weight, conv_bias, cotangent):
    grid_shape = features.shape[1:]
    bricks = grid_shape[0]
    pairs = bricks // 2
    spread, links = send_units.shape[2:]
    shard, channels = weight.shape
    groups = lax.axis_size("dp")
    count = conv_bias.shape[0]
    width = -(-(shard + channels) // LANES) * LANES
    unit_rows = 8 * UNIT_ROWS + 2 * Z_ROWS
    units_type = jax.ShapeDtypeStruct((unit_rows, LANES), BF16)
    grid_type = jax.ShapeDtypeStruct(grid_shape, BF16)
    shard_type = jax.ShapeDtypeStruct((channels, width), BF16)
    params = pltpu.CompilerParams(vmem_limit_bytes=48 * 1024 * 1024)
    rows_shape = neighbours.shape[1:]
    send_shape = (spread, 1, links)

    masked, mask, rows, send, own_shard, *units = pl.pallas_call(
        prepare_kernel,
        name="prepare",
        out_shape=[
            grid_type,
            grid_type,
            jax.ShapeDtypeStruct(rows_shape, jnp.int32),
            jax.ShapeDtypeStruct(send_shape, jnp.int32),
            shard_type,
        ]
        + [units_type] * spread,
        in_specs=[pl.BlockSpec(memory_space=pltpu.HBM)] * 7,
        out_specs=[vmem(), vmem(), smem(), smem(), vmem()] + [vmem()] * spread,
        scratch_shapes=[
            pltpu.VMEM((4, (bricks + 1) * 64, LANES), F32),
            pltpu.VMEM(grid_shape, BF16),
            pltpu.VMEM(occupancy.shape[1:], jnp.int32),
            pltpu.SMEM((1, 1), jnp.int32),
            pltpu.VMEM(rows_shape, jnp.int32),
            pltpu.VMEM((channels, shard), BF16),
            pltpu.VMEM((1, count), BF16),
            pltpu.VMEM(rows_shape, jnp.int32),
            pltpu.SemaphoreType.DMA((8,)),
        ],
        compiler_params=params,
    )(
        features[0],
        occupancy[0],
        counts,
        send_units.transpose(0, 2, 1, 3).reshape(send_shape),
        neighbours[0],
        weight.T,
        conv_bias.reshape(1, count),
    )

    shards = [own_shard] + [swapped(own_shard, "dp", m) for m in range(1, groups)]
    received = exchanged(units)

    flat = pltpu.VMEM((channels, 28 * 64), F32)
    band_forward, band_backward, bias = pl.pallas_call(
        functools.partial(weights_kernel, shard=shard, groups=groups),
        name="weights",
        out_shape=[
            jax.ShapeDtypeStruct((9, LANES, 256), BF16),
            jax.ShapeDtypeStruct((9, 256, LANES), BF16),
            jax.ShapeDtypeStruct((8, LANES), F32),
        ],
        in_specs=[vmem()] * groups,
        out_specs=[vmem()] * 3,
        scratch_shapes=[pltpu.VMEM((groups, channels, width), BF16), flat, flat],
        compiler_params=params,
    )(*shards)

    table = pltpu.VMEM((spread * unit_rows + Z_ROWS, LANES), BF16)
    windows = pltpu.VMEM((3, 4, pairs, 10, 16, 256), BF16)
    sides = pltpu.VMEM((2, 2, 5, 8, LANES), F32)
    walls = pltpu.VMEM((2, 64, LANES), F32)
    block_output, grad, *rest = pl.pallas_call(
        functools.partial(forward_kernel, shard=shard),
        name="forward",
        out_shape=[grid_type, grid_type] + [units_type] * spread + [shard_type] * groups,
        in_specs=[vmem()] * 5 + [smem(), smem()] + [vmem()] * spread,
        out_specs=[vmem()] * (2 + spread + groups),
        scratch_shapes=[
            table,
            windows,
            sides,
            walls,
            flat,
            flat,
            pltpu.VMEM((4, (bricks + 1) * 64, LANES), F32),
            pltpu.VMEM((4, LANES, pairs * LANES), BF16),
        ],
        compiler_params=params,
    )(masked, mask, cotangent[0], band_forward, bias, rows, send, *received)
    grad_units, blocks = rest[:spread], rest[spread:]

    shares = [blocks[0]] + [swapped(blocks[m], "dp", m) for m in range(1, groups)]
    grad_received = exchanged(grad_units)

    grad_input = pl.pallas_call(
        backward_kernel,
        name="backward",
        out_shape=grid_type,
        in_specs=[vmem()] * 3 + [smem()] + [vmem()] * spread,
        out_specs=vmem(),
        scratch_shapes=[table, windows, sides, walls],
        compiler_params=params,
    )(grad, mask, band_backward, rows, *grad_received)

    total = sum(share.astype(F32) for share in shares).astype(BF16)
    devices = lax.axis_size("space")
    bit = 1
    while 2 * bit < devices:
        total = (total.astype(F32) + swapped(total, "space", bit).astype(F32)).astype(BF16)
        bit *= 2
    weight_share, bias_share = pl.pallas_call(
        finish_kernel,
        name="finish",
        out_shape=[
            jax.ShapeDtypeStruct((channels, shard), F32),
            jax.ShapeDtypeStruct((1, count), F32),
        ],
        in_specs=[vmem()] * 2,
        out_specs=[vmem()] * 2,
        compiler_params=params,
    )(total, swapped(total, "space", bit))
    return (
        block_output[None],
        grad_input[None],
        weight_share.T,
        bias_share.reshape(count),
    )


def solution(mesh):
    placed = (
        P("dp", "space", None, None, None),
        P("dp", "space", None),
        P("dp", "space"),
        P("dp", "space", None, None),
        P("dp", "space", None),
        P("dp", None),
        P("dp"),
        P("dp", "space", None, None, None),
    )
    return jax.shard_map(
        body,
        mesh=mesh,
        in_specs=placed,
        out_specs=(
            P("dp", "space", None, None, None),
            P("dp", "space", None, None, None),
            P("dp", None),
            P("dp"),
        ),
        check_vma=False,
    )
```

```python
import functools

import jax
import jax.numpy as jnp
from jax import lax
from jax.experimental import pallas as pl
from jax.experimental.pallas import tpu as pltpu
from jax.sharding import PartitionSpec as P

F32 = jnp.float32
BF16 = jnp.bfloat16
LANES = 128
UNIT_ROWS = 32
Z_ROWS = 64
SWAPS = ((1, 0), (2, 0), (2, 1), (1, 1))
DN_NT = (((1,), (1,)), ((), ()))
DN_NN = (((1,), (0,)), ((), ()))


def vmem():
    return pl.BlockSpec(memory_space=pltpu.VMEM)


def smem():
    return pl.BlockSpec(memory_space=pltpu.SMEM)


def untouched():
    return pl.BlockSpec(memory_space=pl.ANY)


def offset_number(ox, oy, oz):
    flat = (ox + 1) * 9 + (oy + 1) * 3 + (oz + 1)
    return flat if flat < 13 else flat - 1


def low_half(shape):
    return lax.broadcasted_iota(jnp.int32, shape, len(shape) - 1) % LANES < 64


def chunk_rows(block):
    return [block[8 * q : 8 * q + 8] for q in range(4)]


def upward(device, distance):
    return lax.rem(lax.div(device, distance), 2)


def pack_units(values, send, outs):
    slots = values.shape[1] // 64 - 1
    reach = len(outs) // 2
    low = low_half((64, LANES))
    device = lax.axis_index("space")
    for number, out in enumerate(outs):
        column = reach
        if number > 0:
            distance, turn = SWAPS[number - 1]
            up = upward(device, distance) == turn
            column = jnp.where(up, reach + distance, reach - distance)

        def base(link):
            unit = send[column, 0, link]
            slot = jnp.where(unit < 0, slots, (unit * 43) >> 8)
            return pl.multiple_of(slot * 64, 64)

        for half in range(2):
            for face in range(4):
                start = base(half * 6 + face)
                if face < 2:
                    where = pl.ds(start + 56 * face, 8)
                else:
                    where = pl.ds(start + 7 * (face - 2), 8, stride=8)
                packed = jnp.concatenate([values[q, where, :] for q in range(4)], axis=0)
                at = (half * 4 + face) * UNIT_ROWS
                out[at : at + UNIT_ROWS, :] = packed.astype(BF16)
            first = values[0, pl.ds(base(half * 6 + 4), 64), :]
            last = values[3, pl.ds(base(half * 6 + 5), 64), :]
            at = 8 * UNIT_ROWS + half * Z_ROWS
            out[at : at + Z_ROWS, :] = jnp.where(low, first, last).astype(BF16)


def prepare_kernel(
    features_hbm, occupancy_hbm, send_hbm, listing_hbm, weight_hbm, bias_hbm, counts,
    masked_out, mask_out, rows_out, send_out, shard_out, u0, u1, u2, u3, u4,
    values, features, occupancy, listing, weight_t, bias, rows, sems,
):
    copies = [
        pltpu.make_async_copy(src, dst, sems.at[i])
        for i, (src, dst) in enumerate(
            (
                (occupancy_hbm, occupancy),
                (features_hbm, features),
                (send_hbm, send_out),
                (listing_hbm, listing),
                (weight_hbm, weight_t),
                (bias_hbm, bias),
            )
        )
    ]
    for copy in copies:
        copy.start()
    bricks = features.shape[0]
    shard_out[...] = jnp.zeros(shard_out.shape, BF16)
    values[:, bricks * 64 :, :] = jnp.zeros((4, 64, LANES), F32)
    row = lax.broadcasted_iota(jnp.int32, (64, 512), 0)
    col = lax.broadcasted_iota(jnp.int32, (64, 512), 1)
    same = (col >> 3) == row
    z_row = lax.broadcasted_iota(jnp.int32, (512, 512), 0) & 7
    z_col = lax.broadcasted_iota(jnp.int32, (512, 512), 1) >> 6
    expand = jnp.where(z_row == z_col, 1.0, 0.0).astype(BF16)

    copies[0].wait()
    live = lax.broadcasted_iota(jnp.int32, (bricks, 512), 0) < counts[0, 0]
    occ = jnp.where(live, occupancy[...], 0).astype(F32)
    spread = jnp.concatenate(
        [jnp.where(same, occ[b : b + 1, :], 0.0) for b in range(bricks)], axis=0
    ).astype(BF16)
    mask = jnp.dot(spread, expand, preferred_element_type=F32)
    mask_out[...] = mask.astype(BF16).reshape(mask_out.shape)
    copies[1].wait()
    value = features[...].astype(F32).reshape(bricks * 64, 512) * mask
    masked_out[...] = value.astype(BF16).reshape(masked_out.shape)
    for q in range(4):
        values[q, 0 : bricks * 64, :] = value[:, q * LANES : (q + 1) * LANES]
    copies[2].wait()
    pack_units(values, send_out, (u0, u1, u2, u3, u4))

    copies[3].wait()
    device = lax.axis_index("space")
    number = listing[...]
    column = (number * 43) >> 9
    link = number - column * 12
    half = (link >= 6).astype(jnp.int32)
    face = link - 6 * half
    block = jnp.zeros(number.shape, jnp.int32)
    for distance in (1, 2):
        up = upward(device, distance)
        even, odd = (SWAPS.index((distance, turn)) + 1 for turn in range(2))
        block = jnp.where(column == 2 - distance, jnp.where(up == 0, even, odd), block)
        block = jnp.where(column == 2 + distance, jnp.where(up == 0, odd, even), block)
    base = block * (8 * UNIT_ROWS + 2 * Z_ROWS)
    plain = base + (half * 4 + face) * UNIT_ROWS
    paired = base + 8 * UNIT_ROWS + half * Z_ROWS
    none = 5 * (8 * UNIT_ROWS + 2 * Z_ROWS)
    rows[...] = jnp.where(number < 0, none, jnp.where(face < 4, plain, paired))
    last = pltpu.make_async_copy(rows, rows_out, sems.at[len(copies)])
    last.start()

    copies[4].wait()
    copies[5].wait()
    shard = weight_t.shape[1]
    lead = shard // LANES * LANES
    count = bias.shape[1]
    shard_out[:, 0:lead] = weight_t[:, 0:lead]
    tile = jnp.concatenate(
        [weight_t[:, lead:shard].astype(F32), jnp.zeros((64, lead + LANES - shard), F32)], axis=1
    )
    offset = shard - lead
    behind = jnp.concatenate(
        [bias[...].astype(F32), jnp.zeros((1, LANES - count), F32)], axis=1
    )
    behind = pltpu.roll(jnp.broadcast_to(behind, (64, LANES)), offset, 1)
    first = lax.broadcasted_iota(jnp.int32, (64, LANES), 0) == 0
    lane = lax.broadcasted_iota(jnp.int32, (64, LANES), 1)
    behind = jnp.where(first & (lane >= offset) & (lane < offset + count), behind, 0.0)
    shard_out[:, lead : lead + LANES] = (tile + behind).astype(BF16)
    last.wait()


def gather_units(table, received):
    at = 0
    for part in received:
        table[at : at + part.shape[0], :] = part[...]
        at += part.shape[0]
    table[at:, :] = jnp.zeros((table.shape[0] - at, LANES), BF16)


def assemble(source, table, rows, windows, sides, walls):
    low8 = low_half((8, LANES))
    sub = lax.broadcasted_iota(jnp.int32, (8, LANES), 0)
    top, bottom = sub == 0, sub == 7

    def put(pair, xp, per_brick):
        for e in range(3):
            stacked = [
                jnp.concatenate([per_brick[0][e][i], per_brick[1][e][i]], axis=0)
                for i in range(5)
            ]
            low16 = low_half((16, LANES))
            before = [stacked[4]] + stacked[:3]
            after = stacked[1:4] + [stacked[4]]
            for q in range(4):
                windows[e, q, pair, xp, :, 0:LANES] = stacked[q].astype(BF16)
                windows[e, q, pair, xp, :, LANES:] = jnp.where(
                    low16, after[q], before[q]
                ).astype(BF16)

    def one_pair(pair, carry):
        def unit(brick, ox, oy, oz):
            return pl.multiple_of(rows[brick, offset_number(ox, oy, oz)], UNIT_ROWS)

        def plane(brick, ox, oy):
            chunks = chunk_rows(table[pl.ds(unit(brick, ox, oy, 0), UNIT_ROWS), :].astype(F32))
            after = table[pl.ds(unit(brick, ox, oy, 1), UNIT_ROWS), :].astype(F32)[0:8]
            before = table[pl.ds(unit(brick, ox, oy, -1), UNIT_ROWS), :].astype(F32)[24:32]
            return chunks + [jnp.where(low8, after, before)]

        for b2 in range(2):
            brick = pair * 2 + b2
            low64 = low_half((64, LANES))
            after = table[pl.ds(unit(brick, 0, 0, 1), Z_ROWS), :].astype(F32)
            before = table[pl.ds(unit(brick, 0, 0, -1), Z_ROWS), :].astype(F32)
            walls[b2] = jnp.where(low64, after, before)
            for side, oy in enumerate((-1, 1)):
                for i, part in enumerate(plane(brick, 0, oy)):
                    sides[b2, side, i] = part

        for ox in (-1, 1):
            per_brick = []
            for b2 in range(2):
                brick = pair * 2 + b2
                centre = plane(brick, ox, 0)
                lower = plane(brick, ox, -1)
                upper = plane(brick, ox, 1)
                per_brick.append(
                    [
                        [
                            pltpu.roll(jnp.where(bottom, l, c), 1, 0)
                            for l, c in zip(lower, centre)
                        ],
                        centre,
                        [
                            pltpu.roll(jnp.where(top, u, c), 7, 0)
                            for u, c in zip(upper, centre)
                        ],
                    ]
                )
            put(pair, 0 if ox < 0 else 9, per_brick)

        def one_x(x, carry):
            per_brick = []
            for b2 in range(2):
                brick = pair * 2 + b2
                block = source[brick, x].astype(F32)
                centre = [block[:, q * LANES : (q + 1) * LANES] for q in range(4)]
                centre.append(walls[b2, pl.ds(pl.multiple_of(x * 8, 8), 8), :])
                lower = [
                    jnp.broadcast_to(sides[b2, 0, i, pl.ds(x, 1), :], (8, LANES))
                    for i in range(5)
                ]
                upper = [
                    jnp.broadcast_to(sides[b2, 1, i, pl.ds(x, 1), :], (8, LANES))
                    for i in range(5)
                ]
                per_brick.append(
                    [
                        [jnp.where(top, l, pltpu.roll(c, 1, 0)) for l, c in zip(lower, centre)],
                        centre,
                        [
                            jnp.where(bottom, u, pltpu.roll(c, 7, 0))
                            for u, c in zip(upper, centre)
                        ],
                    ]
                )
            put(pair, x + 1, per_brick)
            return carry

        return lax.fori_loop(0, 8, one_x, carry)

    lax.fori_loop(0, windows.shape[2], one_pair, 0)


def weights_kernel(*refs, shard, groups):
    shards = refs[:groups]
    forward_out, backward_out, bias_out, gathered, flat, shifted = refs[groups:]
    me = lax.axis_index("dp")
    for m, part in enumerate(shards):
        gathered[m] = part[...]
    for k in range(groups):
        flat[:, k * shard : (k + 1) * shard] = gathered[me ^ k][:, 0:shard].astype(F32)
    total = groups * shard
    flat[:, total:] = jnp.zeros((64, flat.shape[1] - total), F32)
    shifted[:, :] = pltpu.roll(flat[...], flat.shape[1] - 64, 1)
    low = low_half((64, LANES))
    for ae in range(9):
        one = taps_pair(flat, shifted, 3 * ae)
        two = jnp.where(low, taps_pair(flat, shifted, 3 * ae + 2), 0.0)
        late = jnp.concatenate([one, two], axis=1)
        forward_out[ae, 64:128, :] = late.astype(BF16)
        forward_out[ae, 0:64, :] = pltpu.roll(late, 192, 1).astype(BF16)
    for ae in range(9):
        m = 3 * (8 - ae)
        first = taps_pair(flat, shifted, m)
        second = taps_pair(flat, shifted, m + 1)
        third = taps_pair(flat, shifted, m + 2)
        backward_out[ae, 0:64, :] = second.astype(BF16)
        backward_out[ae, 64:128, :] = first.astype(BF16)
        backward_out[ae, 128:192, :] = jnp.where(low, 0.0, pltpu.roll(first, 64, 1)).astype(BF16)
        backward_out[ae, 192:256, :] = jnp.where(low, third, 0.0).astype(BF16)

    lane = lax.broadcasted_iota(jnp.int32, (8, LANES), 1)
    bias_lane = shard % LANES
    bias_tile = shard - bias_lane
    count = 64 // groups
    bias_row = jnp.zeros((8, LANES), F32)
    for k in range(groups):
        tile = gathered[me ^ k][0:16, bias_tile : bias_tile + LANES].astype(F32)[0:8]
        moved = pltpu.roll(tile, (count * k - bias_lane) % LANES, 1)
        bias_row += jnp.where((lane >= count * k) & (lane < count * (k + 1)), moved, 0.0)
    bias_out[...] = bias_row + pltpu.roll(bias_row, 64, 1)


def taps_pair(flat, shifted, first):
    if first % 2 == 0:
        return flat[:, first * 64 : first * 64 + LANES]
    return shifted[:, (first - 1) * 64 : (first - 1) * 64 + LANES]


def forward_kernel(
    masked, mask, cotangent, toeplitz, bias, rows, send, r0, r1, r2, r3, r4,
    block_out, grad_out, u0, u1, u2, u3, u4, *rest, shard,
):
    chunk_outs = rest[:-8]
    table, windows, sides, walls, flat, shifted, values, flipped = rest[-8:]
    groups = len(chunk_outs)
    bricks = masked.shape[0]
    pairs = bricks // 2
    gather_units(table, (r0, r1, r2, r3, r4))
    assemble(masked, table, rows, windows, sides, walls)
    bias_lane = shard % LANES
    bias_tile = shard - bias_lane
    bias_row = bias[0:1, :]
    values[:, bricks * 64 :, :] = jnp.zeros((4, 64, LANES), F32)

    def one_chunk(q, bias_sum):
        total = jnp.zeros((pairs * LANES, LANES), F32)
        for a in range(3):
            for e in range(3):
                window = windows[e, q, :, a : a + 8].reshape(pairs * LANES, 256)
                total += lax.dot_general(
                    window, toeplitz[3 * a + e], DN_NT, preferred_element_type=F32
                )
        pre = (total + bias_row).reshape(pairs, 8, 2, 8, LANES)
        lanes = pl.ds(pl.multiple_of(q * LANES, LANES), LANES)
        for brick in range(bricks):
            p = pre[brick // 2, :, brick % 2]
            active = mask[brick, :, :, lanes].astype(F32)
            sig = jax.nn.sigmoid(p)
            block_out[brick, :, :, lanes] = (p * sig * active).astype(BF16)
            grad = (
                cotangent[brick, :, :, lanes].astype(F32)
                * sig
                * (1.0 + p * (1.0 - sig))
                * active
            ).astype(BF16)
            grad_out[brick, :, :, lanes] = grad
            wide = grad.astype(F32).reshape(64, LANES)
            values[q, brick * 64 : (brick + 1) * 64, :] = wide
            bias_sum += jnp.sum(wide.reshape(8, 8, LANES), axis=0)
        return bias_sum

    bias_sum = lax.fori_loop(0, 4, one_chunk, jnp.zeros((8, LANES), F32))
    pack_units(values, send, (u0, u1, u2, u3, u4))

    for q in range(4):
        for pair in range(pairs):
            by_x = []
            for x in range(8):
                for b2 in range(2):
                    at = (pair * 2 + b2) * 64 + x * 8
                    by_x.append(values[q, at : at + 8, :])
            flipped[q, :, pair * LANES : (pair + 1) * LANES] = jnp.transpose(
                jnp.concatenate(by_x, axis=0)
            ).astype(BF16)
    for ae in range(9):
        a, e = ae // 3, ae % 3
        total = jnp.zeros((LANES, 256), F32)
        for q in range(4):
            window = windows[e, q, :, a : a + 8].reshape(pairs * LANES, 256)
            total += jnp.dot(flipped[q], window, preferred_element_type=F32)
        flat[:, 192 * ae : 192 * ae + 256] = total[64:128] + pltpu.roll(total[0:64], 64, 1)

    width = chunk_outs[0].shape[1]
    bias_all = jnp.sum(bias_sum, axis=0, keepdims=True)
    bias_all = jnp.broadcast_to(bias_all, (8, LANES))
    bias_all = bias_all + pltpu.roll(bias_all, 64, 1)
    bias_all = pltpu.roll(bias_all, bias_lane, 1)
    row8 = lax.broadcasted_iota(jnp.int32, (8, LANES), 0)
    lane8 = lax.broadcasted_iota(jnp.int32, (8, LANES), 1)
    keep = (row8 == 0) & (lane8 >= bias_lane) & (lane8 < bias_lane + 64)
    me = lax.axis_index("dp")
    for k in range(groups):
        part = flat[:, k * shard : (k + 1) * shard]
        shifted[:, 0:shard] = part
        shifted[:, shard:width] = jnp.zeros((64, width - shard), F32)
        tile = shifted[0:8, bias_tile : bias_tile + LANES]
        shifted[0:8, bias_tile : bias_tile + LANES] = jnp.where(keep, bias_all, tile)
        block = shifted[:, 0:width].astype(BF16)
        for m in range(groups):

            @pl.when(me ^ m == k)
            def _(m=m, block=block):
                chunk_outs[m][...] = block


def assemble_kernel(grad, rows, r0, r1, r2, r3, r4, after, windows, table, sides, walls):
    del after
    gather_units(table, (r0, r1, r2, r3, r4))
    assemble(grad, table, rows, windows, sides, walls)


def sum_kernel(*refs, terms):
    total = refs[0][...].astype(F32)
    for share in refs[1:terms]:
        total += share[...].astype(F32)
    refs[terms + 4][...] = total.astype(BF16)


def backward_kernel(windows, mask, toeplitz, after, out):
    del after
    bricks = mask.shape[0]
    pairs = bricks // 2

    def one_chunk(q, carry):
        total = jnp.zeros((pairs * LANES, LANES), F32)
        for a in range(3):
            for e in range(3):
                window = windows[e, q, :, a : a + 8].reshape(pairs * LANES, 256)
                total += jnp.dot(window, toeplitz[3 * a + e], preferred_element_type=F32)
        total = total.reshape(pairs, 8, 2, 8, LANES)
        lanes = pl.ds(pl.multiple_of(q * LANES, LANES), LANES)
        for brick in range(bricks):
            active = mask[brick, :, :, lanes].astype(F32)
            out[brick, :, :, lanes] = (total[brick // 2, :, brick % 2] * active).astype(BF16)
        return carry

    lax.fori_loop(0, 4, one_chunk, 0)


def finish_kernel(mine, other, weight_out, bias_out):
    shard = weight_out.shape[1]
    count = bias_out.shape[1]
    total = mine[...].astype(F32) + other[...].astype(F32)
    weight_out[...] = total[:, 0:shard]
    bias_lane = shard % LANES
    bias_tile = shard - bias_lane
    tile = total[0:8, bias_tile : bias_tile + LANES]
    me = lax.axis_index("dp")
    moved = pltpu.roll(tile, 2 * LANES - bias_lane - me * count, 1)
    bias_out[...] = moved[0:1, 0:count]


def swapped(block, axis, bit):
    return lax.ppermute(block, axis, [(i, i ^ bit) for i in range(lax.axis_size(axis))])


def exchanged(number, unit):
    distance, turn = SWAPS[number - 1]
    route = []
    for low in range(lax.axis_size("space") - distance):
        if low // distance % 2 == turn:
            route += [(low, low + distance), (low + distance, low)]
    return lax.ppermute(unit, "space", route)


def body(features, occupancy, counts, send_units, neighbours, weight, conv_bias, cotangent):
    grid_shape = features.shape[1:]
    bricks = grid_shape[0]
    pairs = bricks // 2
    spread, links = send_units.shape[2:]
    shard, channels = weight.shape
    groups = lax.axis_size("dp")
    count = conv_bias.shape[0]
    width = -(-(shard + channels) // LANES) * LANES
    unit_rows = 8 * UNIT_ROWS + 2 * Z_ROWS
    units_type = jax.ShapeDtypeStruct((unit_rows, LANES), BF16)
    grid_type = jax.ShapeDtypeStruct(grid_shape, BF16)
    shard_type = jax.ShapeDtypeStruct((channels, width), BF16)
    params = pltpu.CompilerParams(vmem_limit_bytes=48 * 1024 * 1024)
    rows_shape = neighbours.shape[1:]
    send_shape = (spread, 1, links)

    masked, mask, rows, send, own_shard, *units = pl.pallas_call(
        prepare_kernel,
        name="prepare",
        out_shape=[
            grid_type,
            grid_type,
            jax.ShapeDtypeStruct(rows_shape, jnp.int32),
            jax.ShapeDtypeStruct(send_shape, jnp.int32),
            shard_type,
        ]
        + [units_type] * spread,
        in_specs=[pl.BlockSpec(memory_space=pltpu.HBM)] * 6 + [smem()],
        out_specs=[vmem(), vmem(), smem(), smem(), vmem()] + [vmem()] * spread,
        scratch_shapes=[
            pltpu.VMEM((4, (bricks + 1) * 64, LANES), F32),
            pltpu.VMEM(grid_shape, BF16),
            pltpu.VMEM(occupancy.shape[1:], jnp.int32),
            pltpu.VMEM(rows_shape, jnp.int32),
            pltpu.VMEM((channels, shard), BF16),
            pltpu.VMEM((1, count), BF16),
            pltpu.VMEM(rows_shape, jnp.int32),
            pltpu.SemaphoreType.DMA((7,)),
        ],
        compiler_params=params,
    )(
        *(
            pltpu.with_memory_space_constraint(operand, pltpu.HBM)
            for operand in (
                features[0],
                occupancy[0],
                send_units.transpose(0, 2, 1, 3).reshape(send_shape),
                neighbours[0],
                weight.T,
                conv_bias.reshape(1, count),
            )
        ),
        counts,
    )

    shards = [own_shard] + [swapped(own_shard, "dp", m) for m in range(1, groups)]
    received = units[:1] + [exchanged(number, units[number]) for number in range(1, spread)]

    flat = pltpu.VMEM((channels, 28 * 64), F32)
    band_forward, band_backward, bias = pl.pallas_call(
        functools.partial(weights_kernel, shard=shard, groups=groups),
        name="weights",
        out_shape=[
            jax.ShapeDtypeStruct((9, LANES, 256), BF16),
            jax.ShapeDtypeStruct((9, 256, LANES), BF16),
            jax.ShapeDtypeStruct((8, LANES), F32),
        ],
        in_specs=[vmem()] * groups,
        out_specs=[vmem()] * 3,
        scratch_shapes=[pltpu.VMEM((groups, channels, width), BF16), flat, flat],
        compiler_params=params,
    )(*shards)

    table = pltpu.VMEM((spread * unit_rows + Z_ROWS, LANES), BF16)
    windows = pltpu.VMEM((3, 4, pairs, 10, 16, 256), BF16)
    sides = pltpu.VMEM((2, 2, 5, 8, LANES), F32)
    walls = pltpu.VMEM((2, 64, LANES), F32)
    block_output, grad, *rest = pl.pallas_call(
        functools.partial(forward_kernel, shard=shard),
        name="forward",
        out_shape=[grid_type, grid_type] + [units_type] * spread + [shard_type] * groups,
        in_specs=[vmem()] * 5 + [smem(), smem()] + [vmem()] * spread,
        out_specs=[vmem()] * (2 + spread + groups),
        scratch_shapes=[
            table,
            windows,
            sides,
            walls,
            flat,
            flat,
            pltpu.VMEM((4, (bricks + 1) * 64, LANES), F32),
            pltpu.VMEM((4, LANES, pairs * LANES), BF16),
        ],
        compiler_params=params,
    )(masked, mask, cotangent[0], band_forward, bias, rows, send, *received)
    grad_units, blocks = rest[:spread], rest[spread:]

    shares = [blocks[0]] + [swapped(blocks[m], "dp", m) for m in range(1, groups)]
    grad_received = grad_units[:1] + [exchanged(n, grad_units[n]) for n in range(1, 3)]
    total, *later = pl.pallas_call(
        functools.partial(sum_kernel, terms=groups),
        name="sum",
        out_shape=[shard_type, units_type, units_type],
        in_specs=[vmem()] * groups + [untouched()] * 4,
        out_specs=[vmem(), untouched(), untouched()],
        input_output_aliases={groups: 1, groups + 1: 2},
        compiler_params=params,
    )(*shares, *grad_units[3:], *grad_received[1:])
    steps = []
    bit = 1
    while bit < lax.axis_size("space"):
        steps.append(bit)
        bit *= 2

    def stepped(total, bit):
        return (total.astype(F32) + swapped(total, "space", bit).astype(F32)).astype(BF16)

    for bit in steps[:-1][:1]:
        total = stepped(total, bit)
    grad_received += [exchanged(n, unit) for n, unit in zip(range(3, spread), later)]

    padded_grad = pl.pallas_call(
        assemble_kernel,
        name="assemble",
        out_shape=jax.ShapeDtypeStruct(windows.shape, BF16),
        in_specs=[vmem()] + [smem()] + [vmem()] * spread + [untouched()],
        out_specs=vmem(),
        scratch_shapes=[table, sides, walls],
        compiler_params=params,
    )(grad, rows, *grad_received, total)

    for bit in steps[1:-1]:
        total = stepped(total, bit)
    grad_input = pl.pallas_call(
        backward_kernel,
        name="backward",
        out_shape=grid_type,
        in_specs=[vmem()] * 3 + [untouched()],
        out_specs=vmem(),
        compiler_params=params,
    )(padded_grad, mask, band_backward, total)

    weight_share, bias_share = pl.pallas_call(
        finish_kernel,
        name="finish",
        out_shape=[
            jax.ShapeDtypeStruct((channels, shard), F32),
            jax.ShapeDtypeStruct((1, count), F32),
        ],
        in_specs=[vmem()] * 2,
        out_specs=[vmem()] * 2,
        compiler_params=params,
    )(total, swapped(total, "space", steps[-1]))
    return (
        block_output[None],
        grad_input[None],
        weight_share.T,
        bias_share.reshape(count),
    )


def solution(mesh):
    placed = (
        P("dp", "space", None, None, None),
        P("dp", "space", None),
        P("dp", "space"),
        P("dp", "space", None, None),
        P("dp", "space", None),
        P("dp", None),
        P("dp"),
        P("dp", "space", None, None, None),
    )
    return jax.shard_map(
        body,
        mesh=mesh,
        in_specs=placed,
        out_specs=(
            P("dp", "space", None, None, None),
            P("dp", "space", None, None, None),
            P("dp", None),
            P("dp"),
        ),
        check_vma=False,
    )
```

```python
import functools

import jax
import jax.numpy as jnp
from jax import lax
from jax.experimental import pallas as pl
from jax.experimental.pallas import tpu as pltpu
from jax.sharding import PartitionSpec as P

F32 = jnp.float32
BF16 = jnp.bfloat16
LANES = 128
UNIT_ROWS = 32
Z_ROWS = 64
SWAPS = (
    ((1, 0), (2, 0), (2, 1), (1, 1)),
    ((2, 0), (1, 0), (1, 1), (2, 1)),
)
DN_NT = (((1,), (1,)), ((), ()))
DN_NN = (((1,), (0,)), ((), ()))


def vmem():
    return pl.BlockSpec(memory_space=pltpu.VMEM)


def smem():
    return pl.BlockSpec(memory_space=pltpu.SMEM)


def untouched():
    return pl.BlockSpec(memory_space=pl.ANY)


def offset_number(ox, oy, oz):
    flat = (ox + 1) * 9 + (oy + 1) * 3 + (oz + 1)
    return flat if flat < 13 else flat - 1


def low_half(shape):
    return lax.broadcasted_iota(jnp.int32, shape, len(shape) - 1) % LANES < 64


def chunk_rows(block):
    return [block[8 * q : 8 * q + 8] for q in range(4)]


def upward(device, distance):
    return lax.rem(lax.div(device, distance), 2)


def pack_units(values, send, outs):
    slots = values.shape[1] // 64 - 1
    reach = len(outs) // 2
    low = low_half((64, LANES))
    device = lax.axis_index("space")
    odd = lax.rem(lax.axis_index("dp"), 2)
    for number, out in enumerate(outs):
        column = reach
        if number > 0:
            columns = []
            for distance, turn in (SWAPS[0][number - 1], SWAPS[1][number - 1]):
                up = upward(device, distance) == turn
                columns.append(jnp.where(up, reach + distance, reach - distance))
            column = jnp.where(odd == 0, columns[0], columns[1])

        def base(link):
            unit = send[column, 0, link]
            slot = jnp.where(unit < 0, slots, (unit * 43) >> 8)
            return pl.multiple_of(slot * 64, 64)

        for half in range(2):
            for face in range(4):
                start = base(half * 6 + face)
                if face < 2:
                    where = pl.ds(start + 56 * face, 8)
                else:
                    where = pl.ds(start + 7 * (face - 2), 8, stride=8)
                packed = jnp.concatenate([values[q, where, :] for q in range(4)], axis=0)
                at = (half * 4 + face) * UNIT_ROWS
                out[at : at + UNIT_ROWS, :] = packed.astype(BF16)
            first = values[0, pl.ds(base(half * 6 + 4), 64), :]
            last = values[3, pl.ds(base(half * 6 + 5), 64), :]
            at = 8 * UNIT_ROWS + half * Z_ROWS
            out[at : at + Z_ROWS, :] = jnp.where(low, first, last).astype(BF16)


def prepare_kernel(
    features_hbm, occupancy_hbm, send_hbm, listing_hbm, weight_hbm, bias_hbm, counts,
    masked_out, mask_out, rows_out, send_out, shard_out, u0, u1, u2, u3, u4,
    values, features, occupancy, listing, weight_t, bias, rows, sems,
):
    copies = [
        pltpu.make_async_copy(src, dst, sems.at[i])
        for i, (src, dst) in enumerate(
            (
                (occupancy_hbm, occupancy),
                (features_hbm, features),
                (send_hbm, send_out),
                (listing_hbm, listing),
                (weight_hbm, weight_t),
                (bias_hbm, bias),
            )
        )
    ]
    for copy in copies:
        copy.start()
    bricks = features.shape[0]
    shard_out[...] = jnp.zeros(shard_out.shape, BF16)
    values[:, bricks * 64 :, :] = jnp.zeros((4, 64, LANES), F32)
    row = lax.broadcasted_iota(jnp.int32, (64, 512), 0)
    col = lax.broadcasted_iota(jnp.int32, (64, 512), 1)
    same = (col >> 3) == row
    z_row = lax.broadcasted_iota(jnp.int32, (512, 512), 0) & 7
    z_col = lax.broadcasted_iota(jnp.int32, (512, 512), 1) >> 6
    expand = jnp.where(z_row == z_col, 1.0, 0.0).astype(BF16)

    copies[0].wait()
    live = lax.broadcasted_iota(jnp.int32, (bricks, 512), 0) < counts[0, 0]
    occ = jnp.where(live, occupancy[...], 0).astype(F32)
    spread = jnp.concatenate(
        [jnp.where(same, occ[b : b + 1, :], 0.0) for b in range(bricks)], axis=0
    ).astype(BF16)
    mask = jnp.dot(spread, expand, preferred_element_type=F32)
    mask_out[...] = mask.astype(BF16).reshape(mask_out.shape)
    copies[1].wait()
    value = features[...].astype(F32).reshape(bricks * 64, 512) * mask
    masked_out[...] = value.astype(BF16).reshape(masked_out.shape)
    for q in range(4):
        values[q, 0 : bricks * 64, :] = value[:, q * LANES : (q + 1) * LANES]
    copies[2].wait()
    pack_units(values, send_out, (u0, u1, u2, u3, u4))

    copies[3].wait()
    device = lax.axis_index("space")
    number = listing[...]
    column = (number * 43) >> 9
    link = number - column * 12
    half = (link >= 6).astype(jnp.int32)
    face = link - 6 * half
    block = jnp.zeros(number.shape, jnp.int32)
    odd = lax.rem(lax.axis_index("dp"), 2)
    for distance in (1, 2):
        up = upward(device, distance)
        first, second = (
            jnp.where(
                odd == 0,
                SWAPS[0].index((distance, turn)) + 1,
                SWAPS[1].index((distance, turn)) + 1,
            )
            for turn in range(2)
        )
        block = jnp.where(column == 2 - distance, jnp.where(up == 0, first, second), block)
        block = jnp.where(column == 2 + distance, jnp.where(up == 0, second, first), block)
    base = block * (8 * UNIT_ROWS + 2 * Z_ROWS)
    plain = base + (half * 4 + face) * UNIT_ROWS
    paired = base + 8 * UNIT_ROWS + half * Z_ROWS
    none = 5 * (8 * UNIT_ROWS + 2 * Z_ROWS)
    rows[...] = jnp.where(number < 0, none, jnp.where(face < 4, plain, paired))
    last = pltpu.make_async_copy(rows, rows_out, sems.at[len(copies)])
    last.start()

    copies[4].wait()
    copies[5].wait()
    shard = weight_t.shape[1]
    lead = shard // LANES * LANES
    count = bias.shape[1]
    shard_out[:, 0:lead] = weight_t[:, 0:lead]
    tile = jnp.concatenate(
        [weight_t[:, lead:shard].astype(F32), jnp.zeros((64, lead + LANES - shard), F32)], axis=1
    )
    offset = shard - lead
    behind = jnp.concatenate(
        [bias[...].astype(F32), jnp.zeros((1, LANES - count), F32)], axis=1
    )
    behind = pltpu.roll(jnp.broadcast_to(behind, (64, LANES)), offset, 1)
    first = lax.broadcasted_iota(jnp.int32, (64, LANES), 0) == 0
    lane = lax.broadcasted_iota(jnp.int32, (64, LANES), 1)
    behind = jnp.where(first & (lane >= offset) & (lane < offset + count), behind, 0.0)
    shard_out[:, lead : lead + LANES] = (tile + behind).astype(BF16)
    last.wait()


def gather_units(table, received):
    at = 0
    for part in received:
        table[at : at + part.shape[0], :] = part[...]
        at += part.shape[0]
    table[at:, :] = jnp.zeros((table.shape[0] - at, LANES), BF16)


def assemble(source, table, rows, windows, sides, walls):
    low8 = low_half((8, LANES))
    sub = lax.broadcasted_iota(jnp.int32, (8, LANES), 0)
    top, bottom = sub == 0, sub == 7

    def put(pair, xp, per_brick):
        for e in range(3):
            stacked = [
                jnp.concatenate([per_brick[0][e][i], per_brick[1][e][i]], axis=0)
                for i in range(5)
            ]
            low16 = low_half((16, LANES))
            before = [stacked[4]] + stacked[:3]
            after = stacked[1:4] + [stacked[4]]
            for q in range(4):
                windows[e, q, pair, xp, :, 0:LANES] = stacked[q].astype(BF16)
                windows[e, q, pair, xp, :, LANES:] = jnp.where(
                    low16, after[q], before[q]
                ).astype(BF16)

    def one_pair(pair, carry):
        def unit(brick, ox, oy, oz):
            return pl.multiple_of(rows[brick, offset_number(ox, oy, oz)], UNIT_ROWS)

        def plane(brick, ox, oy):
            chunks = chunk_rows(table[pl.ds(unit(brick, ox, oy, 0), UNIT_ROWS), :].astype(F32))
            after = table[pl.ds(unit(brick, ox, oy, 1), UNIT_ROWS), :].astype(F32)[0:8]
            before = table[pl.ds(unit(brick, ox, oy, -1), UNIT_ROWS), :].astype(F32)[24:32]
            return chunks + [jnp.where(low8, after, before)]

        for b2 in range(2):
            brick = pair * 2 + b2
            low64 = low_half((64, LANES))
            after = table[pl.ds(unit(brick, 0, 0, 1), Z_ROWS), :].astype(F32)
            before = table[pl.ds(unit(brick, 0, 0, -1), Z_ROWS), :].astype(F32)
            walls[b2] = jnp.where(low64, after, before)
            for side, oy in enumerate((-1, 1)):
                for i, part in enumerate(plane(brick, 0, oy)):
                    sides[b2, side, i] = part

        for ox in (-1, 1):
            per_brick = []
            for b2 in range(2):
                brick = pair * 2 + b2
                centre = plane(brick, ox, 0)
                lower = plane(brick, ox, -1)
                upper = plane(brick, ox, 1)
                per_brick.append(
                    [
                        [
                            pltpu.roll(jnp.where(bottom, l, c), 1, 0)
                            for l, c in zip(lower, centre)
                        ],
                        centre,
                        [
                            pltpu.roll(jnp.where(top, u, c), 7, 0)
                            for u, c in zip(upper, centre)
                        ],
                    ]
                )
            put(pair, 0 if ox < 0 else 9, per_brick)

        def one_x(x, carry):
            per_brick = []
            for b2 in range(2):
                brick = pair * 2 + b2
                block = source[brick, x].astype(F32)
                centre = [block[:, q * LANES : (q + 1) * LANES] for q in range(4)]
                centre.append(walls[b2, pl.ds(pl.multiple_of(x * 8, 8), 8), :])
                lower = [
                    jnp.broadcast_to(sides[b2, 0, i, pl.ds(x, 1), :], (8, LANES))
                    for i in range(5)
                ]
                upper = [
                    jnp.broadcast_to(sides[b2, 1, i, pl.ds(x, 1), :], (8, LANES))
                    for i in range(5)
                ]
                per_brick.append(
                    [
                        [jnp.where(top, l, pltpu.roll(c, 1, 0)) for l, c in zip(lower, centre)],
                        centre,
                        [
                            jnp.where(bottom, u, pltpu.roll(c, 7, 0))
                            for u, c in zip(upper, centre)
                        ],
                    ]
                )
            put(pair, x + 1, per_brick)
            return carry

        return lax.fori_loop(0, 8, one_x, carry)

    lax.fori_loop(0, windows.shape[2], one_pair, 0)


def weights_kernel(*refs, shard, groups):
    shards = refs[:groups]
    forward_out, backward_out, bias_out, gathered, flat, shifted = refs[groups:]
    me = lax.axis_index("dp")
    for m, part in enumerate(shards):
        gathered[m] = part[...]
    for k in range(groups):
        flat[:, k * shard : (k + 1) * shard] = gathered[me ^ k][:, 0:shard].astype(F32)
    total = groups * shard
    flat[:, total:] = jnp.zeros((64, flat.shape[1] - total), F32)
    shifted[:, :] = pltpu.roll(flat[...], flat.shape[1] - 64, 1)
    low = low_half((64, LANES))
    for ae in range(9):
        one = taps_pair(flat, shifted, 3 * ae)
        two = jnp.where(low, taps_pair(flat, shifted, 3 * ae + 2), 0.0)
        late = jnp.concatenate([one, two], axis=1)
        forward_out[ae, 64:128, :] = late.astype(BF16)
        forward_out[ae, 0:64, :] = pltpu.roll(late, 192, 1).astype(BF16)
    for ae in range(9):
        m = 3 * (8 - ae)
        first = taps_pair(flat, shifted, m)
        second = taps_pair(flat, shifted, m + 1)
        third = taps_pair(flat, shifted, m + 2)
        backward_out[ae, 0:64, :] = second.astype(BF16)
        backward_out[ae, 64:128, :] = first.astype(BF16)
        backward_out[ae, 128:192, :] = jnp.where(low, 0.0, pltpu.roll(first, 64, 1)).astype(BF16)
        backward_out[ae, 192:256, :] = jnp.where(low, third, 0.0).astype(BF16)

    lane = lax.broadcasted_iota(jnp.int32, (8, LANES), 1)
    bias_lane = shard % LANES
    bias_tile = shard - bias_lane
    count = 64 // groups
    bias_row = jnp.zeros((8, LANES), F32)
    for k in range(groups):
        tile = gathered[me ^ k][0:16, bias_tile : bias_tile + LANES].astype(F32)[0:8]
        moved = pltpu.roll(tile, (count * k - bias_lane) % LANES, 1)
        bias_row += jnp.where((lane >= count * k) & (lane < count * (k + 1)), moved, 0.0)
    bias_out[...] = bias_row + pltpu.roll(bias_row, 64, 1)


def taps_pair(flat, shifted, first):
    if first % 2 == 0:
        return flat[:, first * 64 : first * 64 + LANES]
    return shifted[:, (first - 1) * 64 : (first - 1) * 64 + LANES]


def forward_kernel(
    masked, mask, cotangent_hbm, toeplitz, bias, rows, send, r0, r1, r2, r3, r4,
    block_out, grad_out, keep_out, give_out, u0, u1, u2, u3, u4,
    table, windows, sides, walls, flat, shifted, values, flipped, cotangent, sem, *, shard,
):
    fetch = pltpu.make_async_copy(cotangent_hbm, cotangent, sem)
    fetch.start()
    groups = 2 * keep_out.shape[0]
    bricks = masked.shape[0]
    pairs = bricks // 2
    gather_units(table, (r0, r1, r2, r3, r4))
    assemble(masked, table, rows, windows, sides, walls)
    bias_lane = shard % LANES
    bias_tile = shard - bias_lane
    bias_row = bias[0:1, :]
    fetch.wait()
    values[:, bricks * 64 :, :] = jnp.zeros((4, 64, LANES), F32)

    def one_chunk(q, bias_sum):
        total = jnp.zeros((pairs * LANES, LANES), F32)
        for a in range(3):
            for e in range(3):
                window = windows[e, q, :, a : a + 8].reshape(pairs * LANES, 256)
                total += lax.dot_general(
                    window, toeplitz[3 * a + e], DN_NT, preferred_element_type=F32
                )
        pre = (total + bias_row).reshape(pairs, 8, 2, 8, LANES)
        lanes = pl.ds(pl.multiple_of(q * LANES, LANES), LANES)
        for brick in range(bricks):
            p = pre[brick // 2, :, brick % 2]
            active = mask[brick, :, :, lanes].astype(F32)
            sig = jax.nn.sigmoid(p)
            block_out[brick, :, :, lanes] = (p * sig * active).astype(BF16)
            grad = (
                cotangent[brick, :, :, lanes].astype(F32)
                * sig
                * (1.0 + p * (1.0 - sig))
                * active
            ).astype(BF16)
            grad_out[brick, :, :, lanes] = grad
            wide = grad.astype(F32).reshape(64, LANES)
            values[q, brick * 64 : (brick + 1) * 64, :] = wide
            bias_sum += jnp.sum(wide.reshape(8, 8, LANES), axis=0)
        return bias_sum

    bias_sum = lax.fori_loop(0, 4, one_chunk, jnp.zeros((8, LANES), F32))
    pack_units(values, send, (u0, u1, u2, u3, u4))

    for q in range(4):
        for pair in range(pairs):
            by_x = []
            for x in range(8):
                for b2 in range(2):
                    at = (pair * 2 + b2) * 64 + x * 8
                    by_x.append(values[q, at : at + 8, :])
            flipped[q, :, pair * LANES : (pair + 1) * LANES] = jnp.transpose(
                jnp.concatenate(by_x, axis=0)
            ).astype(BF16)
    for ae in range(9):
        a, e = ae // 3, ae % 3
        total = jnp.zeros((LANES, 256), F32)
        for q in range(4):
            window = windows[e, q, :, a : a + 8].reshape(pairs * LANES, 256)
            total += jnp.dot(flipped[q], window, preferred_element_type=F32)
        flat[:, 192 * ae : 192 * ae + 256] = total[64:128] + pltpu.roll(total[0:64], 64, 1)

    width = keep_out.shape[2]
    bias_all = jnp.sum(bias_sum, axis=0, keepdims=True)
    bias_all = jnp.broadcast_to(bias_all, (8, LANES))
    bias_all = bias_all + pltpu.roll(bias_all, 64, 1)
    bias_all = pltpu.roll(bias_all, bias_lane, 1)
    row8 = lax.broadcasted_iota(jnp.int32, (8, LANES), 0)
    lane8 = lax.broadcasted_iota(jnp.int32, (8, LANES), 1)
    keep = (row8 == 0) & (lane8 >= bias_lane) & (lane8 < bias_lane + 64)
    me = lax.axis_index("dp")
    for k in range(groups):
        part = flat[:, k * shard : (k + 1) * shard]
        shifted[:, 0:shard] = part
        shifted[:, shard:width] = jnp.zeros((64, width - shard), F32)
        tile = shifted[0:8, bias_tile : bias_tile + LANES]
        shifted[0:8, bias_tile : bias_tile + LANES] = jnp.where(keep, bias_all, tile)
        block = shifted[:, 0:width].astype(BF16)
        for m in range(groups):

            @pl.when(me ^ m == k)
            def _(m=m, block=block):
                (give_out if m % 2 else keep_out)[m // 2] = block


def assemble_kernel(grad, rows, r0, r1, r2, r3, r4, after, windows, table, sides, walls):
    del after
    gather_units(table, (r0, r1, r2, r3, r4))
    assemble(grad, table, rows, windows, sides, walls)


def sum_kernel(*refs):
    refs[-1][...] = (refs[0][...].astype(F32) + refs[1][...].astype(F32)).astype(BF16)


def sum_after(mine, other, after):
    return pl.pallas_call(
        sum_kernel,
        name="sum",
        out_shape=jax.ShapeDtypeStruct(mine.shape, mine.dtype),
        in_specs=[vmem()] * 2 + [untouched()] * len(after),
        out_specs=vmem(),
        compiler_params=pltpu.CompilerParams(vmem_limit_bytes=1024 * 1024),
    )(mine, other, *after)


def backward_kernel(windows, mask, toeplitz, after, out, done):
    del after
    done[...] = jnp.zeros(done.shape, F32)
    bricks = mask.shape[0]
    pairs = bricks // 2

    def one_chunk(q, carry):
        total = jnp.zeros((pairs * LANES, LANES), F32)
        for a in range(3):
            for e in range(3):
                window = windows[e, q, :, a : a + 8].reshape(pairs * LANES, 256)
                total += jnp.dot(window, toeplitz[3 * a + e], preferred_element_type=F32)
        total = total.reshape(pairs, 8, 2, 8, LANES)
        lanes = pl.ds(pl.multiple_of(q * LANES, LANES), LANES)
        for brick in range(bricks):
            active = mask[brick, :, :, lanes].astype(F32)
            out[brick, :, :, lanes] = (total[brick // 2, :, brick % 2] * active).astype(BF16)
        return carry

    lax.fori_loop(0, 4, one_chunk, 0)


def finish_kernel(mine, other, weight_out, bias_out):
    shard = weight_out.shape[1]
    count = bias_out.shape[1]
    total = mine[...].astype(F32) + other[...].astype(F32)
    weight_out[...] = total[:, 0:shard]
    bias_lane = shard % LANES
    bias_tile = shard - bias_lane
    tile = total[0:8, bias_tile : bias_tile + LANES]
    me = lax.axis_index("dp")
    moved = pltpu.roll(tile, 2 * LANES - bias_lane - me * count, 1)
    bias_out[...] = moved[0:1, 0:count]


def swapped(block, axis, bit):
    return lax.ppermute(block, axis, [(i, i ^ bit) for i in range(lax.axis_size(axis))])


def by_parity(block, routes):
    groups = lax.axis_size("dp")
    pairs = [
        (source * groups + group, target * groups + group)
        for group in range(groups)
        for source, target in routes[group % 2]
    ]
    return lax.ppermute(block, ("space", "dp"), pairs)


def exchanged(number, unit):
    routes = []
    for swaps in SWAPS:
        distance, turn = swaps[number - 1]
        route = []
        for low in range(lax.axis_size("space") - distance):
            if low // distance % 2 == turn:
                route += [(low, low + distance), (low + distance, low)]
        routes.append(route)
    return by_parity(unit, routes)


def space_steps():
    bits = []
    while 2 ** len(bits) < lax.axis_size("space"):
        bits.append(2 ** len(bits))
    return list(zip(bits, bits[1:] + bits[:1]))


def stepped(total, step):
    devices = range(lax.axis_size("space"))
    return by_parity(total, [[(i, i ^ bit) for i in devices] for bit in step])


def body(features, occupancy, counts, send_units, neighbours, weight, conv_bias, cotangent):
    grid_shape = features.shape[1:]
    bricks = grid_shape[0]
    pairs = bricks // 2
    spread, links = send_units.shape[2:]
    shard, channels = weight.shape
    groups = lax.axis_size("dp")
    count = conv_bias.shape[0]
    width = -(-(shard + channels) // LANES) * LANES
    unit_rows = 8 * UNIT_ROWS + 2 * Z_ROWS
    units_type = jax.ShapeDtypeStruct((unit_rows, LANES), BF16)
    grid_type = jax.ShapeDtypeStruct(grid_shape, BF16)
    shard_type = jax.ShapeDtypeStruct((channels, width), BF16)
    params = pltpu.CompilerParams(vmem_limit_bytes=48 * 1024 * 1024)
    rows_shape = neighbours.shape[1:]
    send_shape = (spread, 1, links)

    masked, mask, rows, send, own_shard, *units = pl.pallas_call(
        prepare_kernel,
        name="prepare",
        out_shape=[
            grid_type,
            grid_type,
            jax.ShapeDtypeStruct(rows_shape, jnp.int32),
            jax.ShapeDtypeStruct(send_shape, jnp.int32),
            shard_type,
        ]
        + [units_type] * spread,
        in_specs=[pl.BlockSpec(memory_space=pltpu.HBM)] * 6 + [smem()],
        out_specs=[vmem(), vmem(), smem(), smem(), vmem()] + [vmem()] * spread,
        scratch_shapes=[
            pltpu.VMEM((4, (bricks + 1) * 64, LANES), F32),
            pltpu.VMEM(grid_shape, BF16),
            pltpu.VMEM(occupancy.shape[1:], jnp.int32),
            pltpu.VMEM(rows_shape, jnp.int32),
            pltpu.VMEM((channels, shard), BF16),
            pltpu.VMEM((1, count), BF16),
            pltpu.VMEM(rows_shape, jnp.int32),
            pltpu.SemaphoreType.DMA((7,)),
        ],
        compiler_params=params,
    )(
        *(
            pltpu.with_memory_space_constraint(operand, pltpu.HBM)
            for operand in (
                features[0],
                occupancy[0],
                send_units.transpose(0, 2, 1, 3).reshape(send_shape),
                neighbours[0],
                weight.T,
                conv_bias.reshape(1, count),
            )
        ),
        counts,
    )

    shards = {0: own_shard}
    bit = groups // 2
    while bit:
        for m in list(shards):
            shards[m | bit] = swapped(shards[m], "dp", bit)
        bit //= 2
    received = units[:1] + [exchanged(number, units[number]) for number in range(1, spread)]

    flat = pltpu.VMEM((channels, 28 * 64), F32)
    band_forward, band_backward, bias = pl.pallas_call(
        functools.partial(weights_kernel, shard=shard, groups=groups),
        name="weights",
        out_shape=[
            jax.ShapeDtypeStruct((9, LANES, 256), BF16),
            jax.ShapeDtypeStruct((9, 256, LANES), BF16),
            jax.ShapeDtypeStruct((8, LANES), F32),
        ],
        in_specs=[vmem()] * groups,
        out_specs=[vmem()] * 3,
        scratch_shapes=[pltpu.VMEM((groups, channels, width), BF16), flat, flat],
        compiler_params=params,
    )(*(shards[m] for m in range(groups)))

    table = pltpu.VMEM((spread * unit_rows + Z_ROWS, LANES), BF16)
    windows = pltpu.VMEM((3, 4, pairs, 10, 16, 256), BF16)
    sides = pltpu.VMEM((2, 2, 5, 8, LANES), F32)
    walls = pltpu.VMEM((2, 64, LANES), F32)
    half_type = jax.ShapeDtypeStruct((groups // 2, channels, width), BF16)
    block_output, grad, keep, give, *grad_units = pl.pallas_call(
        functools.partial(forward_kernel, shard=shard),
        name="forward",
        out_shape=[grid_type, grid_type, half_type, half_type] + [units_type] * spread,
        in_specs=[vmem(), vmem(), pl.BlockSpec(memory_space=pltpu.HBM), vmem(), vmem()]
        + [smem(), smem()]
        + [vmem()] * spread,
        out_specs=[vmem()] * (4 + spread),
        scratch_shapes=[
            table,
            windows,
            sides,
            walls,
            flat,
            flat,
            pltpu.VMEM((4, (bricks + 1) * 64, LANES), F32),
            pltpu.VMEM((4, LANES, pairs * LANES), BF16),
            pltpu.VMEM(grid_shape, BF16),
            pltpu.SemaphoreType.DMA,
        ],
        compiler_params=params,
    )(
        masked,
        mask,
        pltpu.with_memory_space_constraint(cotangent[0], pltpu.HBM),
        band_forward,
        bias,
        rows,
        send,
        *received,
    )

    grad_received = grad_units[:1] + [exchanged(n, grad_units[n]) for n in range(1, 3)]
    total = sum_after(keep, swapped(give, "dp", 1), grad_received[1:])
    grad_received += [exchanged(n, grad_units[n]) for n in range(3, spread)]
    bit = 2
    while bit < groups:
        far = swapped(total[1::2], "dp", bit)
        total = sum_after(total[0::2], far, grad_received[3:] if 2 * bit >= groups else [])
        bit *= 2
    total = total[0]

    steps = space_steps()
    other = stepped(total, steps[0])
    padded_grad = pl.pallas_call(
        assemble_kernel,
        name="assemble",
        out_shape=jax.ShapeDtypeStruct(windows.shape, BF16),
        in_specs=[vmem()] + [smem()] + [vmem()] * spread + [untouched()],
        out_specs=vmem(),
        scratch_shapes=[table, sides, walls],
        compiler_params=params,
    )(grad, rows, *grad_received, total)

    if len(steps) > 1:
        total = sum_after(total, other, [padded_grad])
        other = stepped(total, steps[1])

    grad_input, done = pl.pallas_call(
        backward_kernel,
        name="backward",
        out_shape=[grid_type, jax.ShapeDtypeStruct((8, LANES), F32)],
        in_specs=[vmem()] * 3 + [untouched()],
        out_specs=[vmem()] * 2,
        compiler_params=params,
    )(padded_grad, mask, band_backward, total)

    for number, step in enumerate(steps[2:]):
        total = sum_after(total, other, [done] if number == 0 else [])
        other = stepped(total, step)
    weight_share, bias_share = pl.pallas_call(
        finish_kernel,
        name="finish",
        out_shape=[
            jax.ShapeDtypeStruct((channels, shard), F32),
            jax.ShapeDtypeStruct((1, count), F32),
        ],
        in_specs=[vmem()] * 2,
        out_specs=[vmem()] * 2,
        compiler_params=params,
    )(total, other)
    return (
        block_output[None],
        grad_input[None],
        weight_share.T,
        bias_share.reshape(count),
    )


def solution(mesh):
    placed = (
        P("dp", "space", None, None, None),
        P("dp", "space", None),
        P("dp", "space"),
        P("dp", "space", None, None),
        P("dp", "space", None),
        P("dp", None),
        P("dp"),
        P("dp", "space", None, None, None),
    )
    return jax.shard_map(
        body,
        mesh=mesh,
        in_specs=placed,
        out_specs=(
            P("dp", "space", None, None, None),
            P("dp", "space", None, None, None),
            P("dp", None),
            P("dp"),
        ),
        check_vma=False,
    )
```

```python
import functools

import jax
import jax.numpy as jnp
from jax import lax
from jax.experimental import pallas as pl
from jax.experimental.pallas import tpu as pltpu
from jax.sharding import PartitionSpec as P

F32 = jnp.float32
BF16 = jnp.bfloat16
LANES = 128
UNIT_ROWS = 32
Z_ROWS = 64
SWAPS = (
    ((1, 0), (2, 0), (2, 1), (1, 1)),
    ((2, 0), (1, 0), (1, 1), (2, 1)),
)
DN_NT = (((1,), (1,)), ((), ()))
DN_NN = (((1,), (0,)), ((), ()))


def vmem():
    return pl.BlockSpec(memory_space=pltpu.VMEM)


def smem():
    return pl.BlockSpec(memory_space=pltpu.SMEM)


def untouched():
    return pl.BlockSpec(memory_space=pl.ANY)


def offset_number(ox, oy, oz):
    flat = (ox + 1) * 9 + (oy + 1) * 3 + (oz + 1)
    return flat if flat < 13 else flat - 1


def low_half(shape):
    return lax.broadcasted_iota(jnp.int32, shape, len(shape) - 1) % LANES < 64


def chunk_rows(block):
    return [block[8 * q : 8 * q + 8] for q in range(4)]


def upward(device, distance):
    return lax.rem(lax.div(device, distance), 2)


def pack_units(values, send, outs):
    slots = values.shape[1] // 64 - 1
    reach = len(outs) // 2
    low = low_half((64, LANES))
    device = lax.axis_index("space")
    odd = lax.rem(lax.axis_index("dp"), 2)
    for number, out in enumerate(outs):
        column = reach
        if number > 0:
            columns = []
            for distance, turn in (SWAPS[0][number - 1], SWAPS[1][number - 1]):
                up = upward(device, distance) == turn
                columns.append(jnp.where(up, reach + distance, reach - distance))
            column = jnp.where(odd == 0, columns[0], columns[1])

        def base(link):
            unit = send[column, 0, link]
            slot = jnp.where(unit < 0, slots, (unit * 43) >> 8)
            return pl.multiple_of(slot * 64, 64)

        for half in range(2):
            for face in range(4):
                start = base(half * 6 + face)
                if face < 2:
                    where = pl.ds(start + 56 * face, 8)
                else:
                    where = pl.ds(start + 7 * (face - 2), 8, stride=8)
                packed = jnp.concatenate([values[q, where, :] for q in range(4)], axis=0)
                at = (half * 4 + face) * UNIT_ROWS
                out[at : at + UNIT_ROWS, :] = packed.astype(BF16)
            first = values[0, pl.ds(base(half * 6 + 4), 64), :]
            last = values[3, pl.ds(base(half * 6 + 5), 64), :]
            at = 8 * UNIT_ROWS + half * Z_ROWS
            out[at : at + Z_ROWS, :] = jnp.where(low, first, last).astype(BF16)


def prepare_kernel(
    features_hbm, occupancy_hbm, send_hbm, listing_hbm, weight_hbm, bias_hbm, counts,
    masked_out, mask_out, rows_out, send_out, shard_out, u0, u1, u2, u3, u4,
    values, features, occupancy, listing, weight_t, bias, rows, sems,
):
    copies = [
        pltpu.make_async_copy(src, dst, sems.at[i])
        for i, (src, dst) in enumerate(
            (
                (occupancy_hbm, occupancy),
                (features_hbm, features),
                (send_hbm, send_out),
                (listing_hbm, listing),
                (weight_hbm, weight_t),
                (bias_hbm, bias),
            )
        )
    ]
    for copy in copies:
        copy.start()
    bricks = features.shape[0]
    shard_out[...] = jnp.zeros(shard_out.shape, BF16)
    values[:, bricks * 64 :, :] = jnp.zeros((4, 64, LANES), F32)
    row = lax.broadcasted_iota(jnp.int32, (64, 512), 0)
    col = lax.broadcasted_iota(jnp.int32, (64, 512), 1)
    same = (col >> 3) == row
    z_row = lax.broadcasted_iota(jnp.int32, (512, 512), 0) & 7
    z_col = lax.broadcasted_iota(jnp.int32, (512, 512), 1) >> 6
    expand = jnp.where(z_row == z_col, 1.0, 0.0).astype(BF16)

    copies[0].wait()
    live = lax.broadcasted_iota(jnp.int32, (bricks, 512), 0) < counts[0, 0]
    occ = jnp.where(live, occupancy[...], 0).astype(F32)
    spread = jnp.concatenate(
        [jnp.where(same, occ[b : b + 1, :], 0.0) for b in range(bricks)], axis=0
    ).astype(BF16)
    mask = jnp.dot(spread, expand, preferred_element_type=F32)
    mask_out[...] = mask.astype(BF16).reshape(mask_out.shape)
    copies[1].wait()
    value = features[...].astype(F32).reshape(bricks * 64, 512) * mask
    masked_out[...] = value.astype(BF16).reshape(masked_out.shape)
    for q in range(4):
        values[q, 0 : bricks * 64, :] = value[:, q * LANES : (q + 1) * LANES]
    copies[2].wait()
    pack_units(values, send_out, (u0, u1, u2, u3, u4))

    copies[3].wait()
    device = lax.axis_index("space")
    number = listing[...]
    column = (number * 43) >> 9
    link = number - column * 12
    half = (link >= 6).astype(jnp.int32)
    face = link - 6 * half
    block = jnp.zeros(number.shape, jnp.int32)
    odd = lax.rem(lax.axis_index("dp"), 2)
    for distance in (1, 2):
        up = upward(device, distance)
        first, second = (
            jnp.where(
                odd == 0,
                SWAPS[0].index((distance, turn)) + 1,
                SWAPS[1].index((distance, turn)) + 1,
            )
            for turn in range(2)
        )
        block = jnp.where(column == 2 - distance, jnp.where(up == 0, first, second), block)
        block = jnp.where(column == 2 + distance, jnp.where(up == 0, second, first), block)
    base = block * (8 * UNIT_ROWS + 2 * Z_ROWS)
    plain = base + (half * 4 + face) * UNIT_ROWS
    paired = base + 8 * UNIT_ROWS + half * Z_ROWS
    none = 5 * (8 * UNIT_ROWS + 2 * Z_ROWS)
    rows[...] = jnp.where(number < 0, none, jnp.where(face < 4, plain, paired))
    last = pltpu.make_async_copy(rows, rows_out, sems.at[len(copies)])
    last.start()

    copies[4].wait()
    copies[5].wait()
    shard = weight_t.shape[1]
    lead = shard // LANES * LANES
    count = bias.shape[1]
    shard_out[:, 0:lead] = weight_t[:, 0:lead]
    tile = jnp.concatenate(
        [weight_t[:, lead:shard].astype(F32), jnp.zeros((64, lead + LANES - shard), F32)], axis=1
    )
    offset = shard - lead
    behind = jnp.concatenate(
        [bias[...].astype(F32), jnp.zeros((1, LANES - count), F32)], axis=1
    )
    behind = pltpu.roll(jnp.broadcast_to(behind, (64, LANES)), offset, 1)
    first = lax.broadcasted_iota(jnp.int32, (64, LANES), 0) == 0
    lane = lax.broadcasted_iota(jnp.int32, (64, LANES), 1)
    behind = jnp.where(first & (lane >= offset) & (lane < offset + count), behind, 0.0)
    shard_out[:, lead : lead + LANES] = (tile + behind).astype(BF16)
    last.wait()


def gather_units(table, received):
    at = 0
    for part in received:
        table[at : at + part.shape[0], :] = part[...]
        at += part.shape[0]
    table[at:, :] = jnp.zeros((table.shape[0] - at, LANES), BF16)


def assemble(source, table, rows, windows, sides, walls):
    low8 = low_half((8, LANES))
    sub = lax.broadcasted_iota(jnp.int32, (8, LANES), 0)
    top, bottom = sub == 0, sub == 7

    def put(pair, xp, per_brick):
        for e in range(3):
            stacked = [
                jnp.concatenate([per_brick[0][e][i], per_brick[1][e][i]], axis=0)
                for i in range(5)
            ]
            low16 = low_half((16, LANES))
            before = [stacked[4]] + stacked[:3]
            after = stacked[1:4] + [stacked[4]]
            for q in range(4):
                windows[e, q, pair, xp, :, 0:LANES] = stacked[q].astype(BF16)
                windows[e, q, pair, xp, :, LANES:] = jnp.where(
                    low16, after[q], before[q]
                ).astype(BF16)

    def one_pair(pair, carry):
        def unit(brick, ox, oy, oz):
            return pl.multiple_of(rows[brick, offset_number(ox, oy, oz)], UNIT_ROWS)

        def plane(brick, ox, oy):
            chunks = chunk_rows(table[pl.ds(unit(brick, ox, oy, 0), UNIT_ROWS), :].astype(F32))
            after = table[pl.ds(unit(brick, ox, oy, 1), UNIT_ROWS), :].astype(F32)[0:8]
            before = table[pl.ds(unit(brick, ox, oy, -1), UNIT_ROWS), :].astype(F32)[24:32]
            return chunks + [jnp.where(low8, after, before)]

        for b2 in range(2):
            brick = pair * 2 + b2
            low64 = low_half((64, LANES))
            after = table[pl.ds(unit(brick, 0, 0, 1), Z_ROWS), :].astype(F32)
            before = table[pl.ds(unit(brick, 0, 0, -1), Z_ROWS), :].astype(F32)
            walls[b2] = jnp.where(low64, after, before)
            for side, oy in enumerate((-1, 1)):
                for i, part in enumerate(plane(brick, 0, oy)):
                    sides[b2, side, i] = part

        for ox in (-1, 1):
            per_brick = []
            for b2 in range(2):
                brick = pair * 2 + b2
                centre = plane(brick, ox, 0)
                lower = plane(brick, ox, -1)
                upper = plane(brick, ox, 1)
                per_brick.append(
                    [
                        [
                            pltpu.roll(jnp.where(bottom, l, c), 1, 0)
                            for l, c in zip(lower, centre)
                        ],
                        centre,
                        [
                            pltpu.roll(jnp.where(top, u, c), 7, 0)
                            for u, c in zip(upper, centre)
                        ],
                    ]
                )
            put(pair, 0 if ox < 0 else 9, per_brick)

        def one_x(x, carry):
            per_brick = []
            for b2 in range(2):
                brick = pair * 2 + b2
                block = source[brick, x].astype(F32)
                centre = [block[:, q * LANES : (q + 1) * LANES] for q in range(4)]
                centre.append(walls[b2, pl.ds(pl.multiple_of(x * 8, 8), 8), :])
                lower = [
                    jnp.broadcast_to(sides[b2, 0, i, pl.ds(x, 1), :], (8, LANES))
                    for i in range(5)
                ]
                upper = [
                    jnp.broadcast_to(sides[b2, 1, i, pl.ds(x, 1), :], (8, LANES))
                    for i in range(5)
                ]
                per_brick.append(
                    [
                        [jnp.where(top, l, pltpu.roll(c, 1, 0)) for l, c in zip(lower, centre)],
                        centre,
                        [
                            jnp.where(bottom, u, pltpu.roll(c, 7, 0))
                            for u, c in zip(upper, centre)
                        ],
                    ]
                )
            put(pair, x + 1, per_brick)
            return carry

        return lax.fori_loop(0, 8, one_x, carry)

    lax.fori_loop(0, windows.shape[2], one_pair, 0)


def weights_kernel(*refs, shard, groups):
    shards = refs[:groups]
    forward_out, backward_out, bias_out, gathered, flat, shifted = refs[groups:]
    me = lax.axis_index("dp")
    for m, part in enumerate(shards):
        gathered[m] = part[...]
    for k in range(groups):
        flat[:, k * shard : (k + 1) * shard] = gathered[me ^ k][:, 0:shard].astype(F32)
    total = groups * shard
    flat[:, total:] = jnp.zeros((64, flat.shape[1] - total), F32)
    shifted[:, :] = pltpu.roll(flat[...], flat.shape[1] - 64, 1)
    low = low_half((64, LANES))
    for ae in range(9):
        one = taps_pair(flat, shifted, 3 * ae)
        two = jnp.where(low, taps_pair(flat, shifted, 3 * ae + 2), 0.0)
        late = jnp.concatenate([one, two], axis=1)
        forward_out[ae, 64:128, :] = late.astype(BF16)
        forward_out[ae, 0:64, :] = pltpu.roll(late, 192, 1).astype(BF16)
    for ae in range(9):
        m = 3 * (8 - ae)
        first = taps_pair(flat, shifted, m)
        second = taps_pair(flat, shifted, m + 1)
        third = taps_pair(flat, shifted, m + 2)
        backward_out[ae, 0:64, :] = second.astype(BF16)
        backward_out[ae, 64:128, :] = first.astype(BF16)
        backward_out[ae, 128:192, :] = jnp.where(low, 0.0, pltpu.roll(first, 64, 1)).astype(BF16)
        backward_out[ae, 192:256, :] = jnp.where(low, third, 0.0).astype(BF16)

    lane = lax.broadcasted_iota(jnp.int32, (8, LANES), 1)
    bias_lane = shard % LANES
    bias_tile = shard - bias_lane
    count = 64 // groups
    bias_row = jnp.zeros((8, LANES), F32)
    for k in range(groups):
        tile = gathered[me ^ k][0:16, bias_tile : bias_tile + LANES].astype(F32)[0:8]
        moved = pltpu.roll(tile, (count * k - bias_lane) % LANES, 1)
        bias_row += jnp.where((lane >= count * k) & (lane < count * (k + 1)), moved, 0.0)
    bias_out[...] = bias_row + pltpu.roll(bias_row, 64, 1)


def taps_pair(flat, shifted, first):
    if first % 2 == 0:
        return flat[:, first * 64 : first * 64 + LANES]
    return shifted[:, (first - 1) * 64 : (first - 1) * 64 + LANES]


def forward_kernel(
    masked, mask, cotangent_hbm, toeplitz, bias, rows, send, r0, r1, r2, r3, r4,
    block_out, grad_out, keep_out, give_out, u0, u1, u2, u3, u4,
    table, windows, sides, walls, flat, shifted, values, flipped, cotangent, sem, *, shard,
):
    fetch = pltpu.make_async_copy(cotangent_hbm, cotangent, sem)
    fetch.start()
    groups = 2 * keep_out.shape[0]
    bricks = masked.shape[0]
    pairs = bricks // 2
    gather_units(table, (r0, r1, r2, r3, r4))
    assemble(masked, table, rows, windows, sides, walls)
    bias_lane = shard % LANES
    bias_tile = shard - bias_lane
    bias_row = bias[0:1, :]
    fetch.wait()
    values[:, bricks * 64 :, :] = jnp.zeros((4, 64, LANES), F32)

    def one_chunk(q, bias_sum):
        total = jnp.zeros((pairs * LANES, LANES), F32)
        for a in range(3):
            for e in range(3):
                window = windows[e, q, :, a : a + 8].reshape(pairs * LANES, 256)
                total += lax.dot_general(
                    window, toeplitz[3 * a + e], DN_NT, preferred_element_type=F32
                )
        pre = (total + bias_row).reshape(pairs, 8, 2, 8, LANES)
        lanes = pl.ds(pl.multiple_of(q * LANES, LANES), LANES)
        for brick in range(bricks):
            p = pre[brick // 2, :, brick % 2]
            active = mask[brick, :, :, lanes].astype(F32)
            sig = jax.nn.sigmoid(p)
            block_out[brick, :, :, lanes] = (p * sig * active).astype(BF16)
            grad = (
                cotangent[brick, :, :, lanes].astype(F32)
                * sig
                * (1.0 + p * (1.0 - sig))
                * active
            ).astype(BF16)
            grad_out[brick, :, :, lanes] = grad
            wide = grad.astype(F32).reshape(64, LANES)
            values[q, brick * 64 : (brick + 1) * 64, :] = wide
            bias_sum += jnp.sum(wide.reshape(8, 8, LANES), axis=0)
        return bias_sum

    bias_sum = lax.fori_loop(0, 4, one_chunk, jnp.zeros((8, LANES), F32))
    pack_units(values, send, (u0, u1, u2, u3, u4))

    for q in range(4):
        for pair in range(pairs):
            by_x = []
            for x in range(8):
                for b2 in range(2):
                    at = (pair * 2 + b2) * 64 + x * 8
                    by_x.append(values[q, at : at + 8, :])
            flipped[q, :, pair * LANES : (pair + 1) * LANES] = jnp.transpose(
                jnp.concatenate(by_x, axis=0)
            ).astype(BF16)
    for ae in range(9):
        a, e = ae // 3, ae % 3
        total = jnp.zeros((LANES, 256), F32)
        for q in range(4):
            window = windows[e, q, :, a : a + 8].reshape(pairs * LANES, 256)
            total += jnp.dot(flipped[q], window, preferred_element_type=F32)
        flat[:, 192 * ae : 192 * ae + 256] = total[64:128] + pltpu.roll(total[0:64], 64, 1)

    width = keep_out.shape[2]
    bias_all = jnp.sum(bias_sum, axis=0, keepdims=True)
    bias_all = jnp.broadcast_to(bias_all, (8, LANES))
    bias_all = bias_all + pltpu.roll(bias_all, 64, 1)
    bias_all = pltpu.roll(bias_all, bias_lane, 1)
    row8 = lax.broadcasted_iota(jnp.int32, (8, LANES), 0)
    lane8 = lax.broadcasted_iota(jnp.int32, (8, LANES), 1)
    keep = (row8 == 0) & (lane8 >= bias_lane) & (lane8 < bias_lane + 64)
    me = lax.axis_index("dp")
    for k in range(groups):
        part = flat[:, k * shard : (k + 1) * shard]
        shifted[:, 0:shard] = part
        shifted[:, shard:width] = jnp.zeros((64, width - shard), F32)
        tile = shifted[0:8, bias_tile : bias_tile + LANES]
        shifted[0:8, bias_tile : bias_tile + LANES] = jnp.where(keep, bias_all, tile)
        block = shifted[:, 0:width].astype(BF16)
        for m in range(groups):

            @pl.when(me ^ m == k)
            def _(m=m, block=block):
                (give_out if m % 2 else keep_out)[m // 2] = block


def assemble_kernel(grad, rows, r0, r1, r2, r3, r4, windows, table, sides, walls):
    gather_units(table, (r0, r1, r2, r3, r4))
    assemble(grad, table, rows, windows, sides, walls)


def sum_kernel(*refs):
    refs[-1][...] = (refs[0][...].astype(F32) + refs[1][...].astype(F32)).astype(BF16)


def sum_after(mine, other, after):
    return pl.pallas_call(
        sum_kernel,
        name="sum",
        out_shape=jax.ShapeDtypeStruct(mine.shape, mine.dtype),
        in_specs=[vmem()] * 2 + [untouched()] * len(after),
        out_specs=vmem(),
        compiler_params=pltpu.CompilerParams(vmem_limit_bytes=1024 * 1024),
    )(mine, other, *after)


def backward_kernel(windows, mask, toeplitz, out):
    bricks = mask.shape[0]
    pairs = bricks // 2

    def one_chunk(q, carry):
        total = jnp.zeros((pairs * LANES, LANES), F32)
        for a in range(3):
            for e in range(3):
                window = windows[e, q, :, a : a + 8].reshape(pairs * LANES, 256)
                total += jnp.dot(window, toeplitz[3 * a + e], preferred_element_type=F32)
        total = total.reshape(pairs, 8, 2, 8, LANES)
        lanes = pl.ds(pl.multiple_of(q * LANES, LANES), LANES)
        for brick in range(bricks):
            active = mask[brick, :, :, lanes].astype(F32)
            out[brick, :, :, lanes] = (total[brick // 2, :, brick % 2] * active).astype(BF16)
        return carry

    lax.fori_loop(0, 4, one_chunk, 0)


def finish_kernel(terms, weight_out, bias_out):
    shard = weight_out.shape[1]
    count = bias_out.shape[1]
    total = jnp.zeros(terms.shape[1:], F32)
    for number in range(terms.shape[0]):
        total += terms[number].astype(F32)
    weight_out[...] = total[:, 0:shard]
    bias_lane = shard % LANES
    bias_tile = shard - bias_lane
    tile = total[0:8, bias_tile : bias_tile + LANES]
    me = lax.axis_index("dp")
    moved = pltpu.roll(tile, 2 * LANES - bias_lane - me * count, 1)
    bias_out[...] = moved[0:1, 0:count]


def swapped(block, axis, bit):
    return lax.ppermute(block, axis, [(i, i ^ bit) for i in range(lax.axis_size(axis))])


def by_parity(block, routes):
    groups = lax.axis_size("dp")
    pairs = [
        (source * groups + group, target * groups + group)
        for group in range(groups)
        for source, target in routes[group % 2]
    ]
    return lax.ppermute(block, ("space", "dp"), pairs)


def exchanged(number, unit):
    routes = []
    for swaps in SWAPS:
        distance, turn = swaps[number - 1]
        route = []
        for low in range(lax.axis_size("space") - distance):
            if low // distance % 2 == turn:
                route += [(low, low + distance), (low + distance, low)]
        routes.append(route)
    return by_parity(unit, routes)


def body(features, occupancy, counts, send_units, neighbours, weight, conv_bias, cotangent):
    grid_shape = features.shape[1:]
    bricks = grid_shape[0]
    pairs = bricks // 2
    spread, links = send_units.shape[2:]
    shard, channels = weight.shape
    groups = lax.axis_size("dp")
    count = conv_bias.shape[0]
    width = -(-(shard + channels) // LANES) * LANES
    unit_rows = 8 * UNIT_ROWS + 2 * Z_ROWS
    units_type = jax.ShapeDtypeStruct((unit_rows, LANES), BF16)
    grid_type = jax.ShapeDtypeStruct(grid_shape, BF16)
    shard_type = jax.ShapeDtypeStruct((channels, width), BF16)
    params = pltpu.CompilerParams(vmem_limit_bytes=48 * 1024 * 1024)
    rows_shape = neighbours.shape[1:]
    send_shape = (spread, 1, links)

    masked, mask, rows, send, own_shard, *units = pl.pallas_call(
        prepare_kernel,
        name="prepare",
        out_shape=[
            grid_type,
            grid_type,
            jax.ShapeDtypeStruct(rows_shape, jnp.int32),
            jax.ShapeDtypeStruct(send_shape, jnp.int32),
            shard_type,
        ]
        + [units_type] * spread,
        in_specs=[pl.BlockSpec(memory_space=pltpu.HBM)] * 6 + [smem()],
        out_specs=[vmem(), vmem(), smem(), smem(), vmem()] + [vmem()] * spread,
        scratch_shapes=[
            pltpu.VMEM((4, (bricks + 1) * 64, LANES), F32),
            pltpu.VMEM(grid_shape, BF16),
            pltpu.VMEM(occupancy.shape[1:], jnp.int32),
            pltpu.VMEM(rows_shape, jnp.int32),
            pltpu.VMEM((channels, shard), BF16),
            pltpu.VMEM((1, count), BF16),
            pltpu.VMEM(rows_shape, jnp.int32),
            pltpu.SemaphoreType.DMA((7,)),
        ],
        compiler_params=params,
    )(
        *(
            pltpu.with_memory_space_constraint(operand, pltpu.HBM)
            for operand in (
                features[0],
                occupancy[0],
                send_units.transpose(0, 2, 1, 3).reshape(send_shape),
                neighbours[0],
                weight.T,
                conv_bias.reshape(1, count),
            )
        ),
        counts,
    )

    shards = {0: own_shard}
    bit = groups // 2
    while bit:
        for m in list(shards):
            shards[m | bit] = swapped(shards[m], "dp", bit)
        bit //= 2
    received = units[:1] + [exchanged(number, units[number]) for number in range(1, spread)]

    flat = pltpu.VMEM((channels, 28 * 64), F32)
    band_forward, band_backward, bias = pl.pallas_call(
        functools.partial(weights_kernel, shard=shard, groups=groups),
        name="weights",
        out_shape=[
            jax.ShapeDtypeStruct((9, LANES, 256), BF16),
            jax.ShapeDtypeStruct((9, 256, LANES), BF16),
            jax.ShapeDtypeStruct((8, LANES), F32),
        ],
        in_specs=[vmem()] * groups,
        out_specs=[vmem()] * 3,
        scratch_shapes=[pltpu.VMEM((groups, channels, width), BF16), flat, flat],
        compiler_params=params,
    )(*(shards[m] for m in range(groups)))

    table = pltpu.VMEM((spread * unit_rows + Z_ROWS, LANES), BF16)
    windows = pltpu.VMEM((3, 4, pairs, 10, 16, 256), BF16)
    sides = pltpu.VMEM((2, 2, 5, 8, LANES), F32)
    walls = pltpu.VMEM((2, 64, LANES), F32)
    half_type = jax.ShapeDtypeStruct((groups // 2, channels, width), BF16)
    block_output, grad, keep, give, *grad_units = pl.pallas_call(
        functools.partial(forward_kernel, shard=shard),
        name="forward",
        out_shape=[grid_type, grid_type, half_type, half_type] + [units_type] * spread,
        in_specs=[vmem(), vmem(), pl.BlockSpec(memory_space=pltpu.HBM), vmem(), vmem()]
        + [smem(), smem()]
        + [vmem()] * spread,
        out_specs=[vmem()] * (4 + spread),
        scratch_shapes=[
            table,
            windows,
            sides,
            walls,
            flat,
            flat,
            pltpu.VMEM((4, (bricks + 1) * 64, LANES), F32),
            pltpu.VMEM((4, LANES, pairs * LANES), BF16),
            pltpu.VMEM(grid_shape, BF16),
            pltpu.SemaphoreType.DMA,
        ],
        compiler_params=params,
    )(
        masked,
        mask,
        pltpu.with_memory_space_constraint(cotangent[0], pltpu.HBM),
        band_forward,
        bias,
        rows,
        send,
        *received,
    )

    grad_received = grad_units[:1] + [exchanged(n, grad_units[n]) for n in range(1, 3)]
    total = sum_after(keep, swapped(give, "dp", 1), [])
    grad_received += [exchanged(n, grad_units[n]) for n in range(3, spread)]
    bit = 2
    while bit < groups:
        total = sum_after(total[0::2], swapped(total[1::2], "dp", bit), [])
        bit *= 2
    total = total[0]

    terms = lax.all_gather(total, "space", axis=0)

    padded_grad = pl.pallas_call(
        assemble_kernel,
        name="assemble",
        out_shape=jax.ShapeDtypeStruct(windows.shape, BF16),
        in_specs=[vmem()] + [smem()] + [vmem()] * spread,
        out_specs=vmem(),
        scratch_shapes=[table, sides, walls],
        compiler_params=params,
    )(grad, rows, *grad_received)

    grad_input = pl.pallas_call(
        backward_kernel,
        name="backward",
        out_shape=grid_type,
        in_specs=[vmem()] * 3,
        out_specs=vmem(),
        compiler_params=params,
    )(padded_grad, mask, band_backward)

    weight_share, bias_share = pl.pallas_call(
        finish_kernel,
        name="finish",
        out_shape=[
            jax.ShapeDtypeStruct((channels, shard), F32),
            jax.ShapeDtypeStruct((1, count), F32),
        ],
        in_specs=[vmem()],
        out_specs=[vmem()] * 2,
        compiler_params=params,
    )(terms)
    return (
        block_output[None],
        grad_input[None],
        weight_share.T,
        bias_share.reshape(count),
    )


def solution(mesh):
    placed = (
        P("dp", "space", None, None, None),
        P("dp", "space", None),
        P("dp", "space"),
        P("dp", "space", None, None),
        P("dp", "space", None),
        P("dp", None),
        P("dp"),
        P("dp", "space", None, None, None),
    )
    return jax.shard_map(
        body,
        mesh=mesh,
        in_specs=placed,
        out_specs=(
            P("dp", "space", None, None, None),
            P("dp", "space", None, None, None),
            P("dp", None),
            P("dp"),
        ),
        check_vma=False,
    )
```

```python
import functools

import jax
import jax.numpy as jnp
from jax import lax
from jax.experimental import pallas as pl
from jax.experimental.pallas import tpu as pltpu
from jax.sharding import PartitionSpec as P

F32 = jnp.float32
BF16 = jnp.bfloat16
LANES = 128
UNIT_ROWS = 32
Z_ROWS = 64
SWAPS = (
    ((1, 1), (2, 1), (1, 0), (2, 0)),
    ((2, 1), (1, 1), (2, 0), (1, 0)),
)
DN_NT = (((1,), (1,)), ((), ()))
DN_NN = (((1,), (0,)), ((), ()))


def vmem():
    return pl.BlockSpec(memory_space=pltpu.VMEM)


def smem():
    return pl.BlockSpec(memory_space=pltpu.SMEM)


def untouched():
    return pl.BlockSpec(memory_space=pl.ANY)


def offset_number(ox, oy, oz):
    flat = (ox + 1) * 9 + (oy + 1) * 3 + (oz + 1)
    return flat if flat < 13 else flat - 1


def low_half(shape):
    return lax.broadcasted_iota(jnp.int32, shape, len(shape) - 1) % LANES < 64


def chunk_rows(block):
    return [block[8 * q : 8 * q + 8] for q in range(4)]


def upward(device, distance):
    return lax.rem(lax.div(device, distance), 2)


def pack_units(values, send, outs):
    slots = values.shape[1] // 64 - 1
    reach = len(outs) // 2
    low = low_half((64, LANES))
    device = lax.axis_index("space")
    odd = lax.rem(lax.axis_index("dp"), 2)
    for number, out in enumerate(outs):
        column = reach
        if number > 0:
            columns = []
            for distance, turn in (SWAPS[0][number - 1], SWAPS[1][number - 1]):
                up = upward(device, distance) == turn
                columns.append(jnp.where(up, reach + distance, reach - distance))
            column = jnp.where(odd == 0, columns[0], columns[1])

        def base(link):
            unit = send[column, 0, link]
            slot = jnp.where(unit < 0, slots, (unit * 43) >> 8)
            return pl.multiple_of(slot * 64, 64)

        for half in range(2):
            for face in range(4):
                start = base(half * 6 + face)
                if face < 2:
                    where = pl.ds(start + 56 * face, 8)
                else:
                    where = pl.ds(start + 7 * (face - 2), 8, stride=8)
                packed = jnp.concatenate([values[q, where, :] for q in range(4)], axis=0)
                at = (half * 4 + face) * UNIT_ROWS
                out[at : at + UNIT_ROWS, :] = packed.astype(BF16)
            first = values[0, pl.ds(base(half * 6 + 4), 64), :]
            last = values[3, pl.ds(base(half * 6 + 5), 64), :]
            at = 8 * UNIT_ROWS + half * Z_ROWS
            out[at : at + Z_ROWS, :] = jnp.where(low, first, last).astype(BF16)


def prepare_kernel(
    features_hbm, occupancy_hbm, send_hbm, listing_hbm, weight_hbm, bias_hbm, counts,
    masked_out, mask_out, rows_out, send_out, shard_out, u0, u1, u2, u3, u4,
    values, features, occupancy, listing, weight_t, bias, rows, sems,
):
    copies = [
        pltpu.make_async_copy(src, dst, sems.at[i])
        for i, (src, dst) in enumerate(
            (
                (occupancy_hbm, occupancy),
                (features_hbm, features),
                (send_hbm, send_out),
                (listing_hbm, listing),
                (weight_hbm, weight_t),
                (bias_hbm, bias),
            )
        )
    ]
    for copy in copies:
        copy.start()
    bricks = features.shape[0]
    shard_out[...] = jnp.zeros(shard_out.shape, BF16)
    values[:, bricks * 64 :, :] = jnp.zeros((4, 64, LANES), F32)
    row = lax.broadcasted_iota(jnp.int32, (64, 512), 0)
    col = lax.broadcasted_iota(jnp.int32, (64, 512), 1)
    same = (col >> 3) == row
    z_row = lax.broadcasted_iota(jnp.int32, (512, 512), 0) & 7
    z_col = lax.broadcasted_iota(jnp.int32, (512, 512), 1) >> 6
    expand = jnp.where(z_row == z_col, 1.0, 0.0).astype(BF16)

    copies[0].wait()
    live = lax.broadcasted_iota(jnp.int32, (bricks, 512), 0) < counts[0, 0]
    occ = jnp.where(live, occupancy[...], 0).astype(F32)
    spread = jnp.concatenate(
        [jnp.where(same, occ[b : b + 1, :], 0.0) for b in range(bricks)], axis=0
    ).astype(BF16)
    mask = jnp.dot(spread, expand, preferred_element_type=F32)
    mask_out[...] = mask.astype(BF16).reshape(mask_out.shape)
    copies[1].wait()
    value = features[...].astype(F32).reshape(bricks * 64, 512) * mask
    masked_out[...] = value.astype(BF16).reshape(masked_out.shape)
    for q in range(4):
        values[q, 0 : bricks * 64, :] = value[:, q * LANES : (q + 1) * LANES]
    copies[2].wait()
    pack_units(values, send_out, (u0, u1, u2, u3, u4))

    copies[3].wait()
    device = lax.axis_index("space")
    number = listing[...]
    column = (number * 43) >> 9
    link = number - column * 12
    half = (link >= 6).astype(jnp.int32)
    face = link - 6 * half
    block = jnp.zeros(number.shape, jnp.int32)
    odd = lax.rem(lax.axis_index("dp"), 2)
    for distance in (1, 2):
        up = upward(device, distance)
        first, second = (
            jnp.where(
                odd == 0,
                SWAPS[0].index((distance, turn)) + 1,
                SWAPS[1].index((distance, turn)) + 1,
            )
            for turn in range(2)
        )
        block = jnp.where(column == 2 - distance, jnp.where(up == 0, first, second), block)
        block = jnp.where(column == 2 + distance, jnp.where(up == 0, second, first), block)
    base = block * (8 * UNIT_ROWS + 2 * Z_ROWS)
    plain = base + (half * 4 + face) * UNIT_ROWS
    paired = base + 8 * UNIT_ROWS + half * Z_ROWS
    none = 5 * (8 * UNIT_ROWS + 2 * Z_ROWS)
    rows[...] = jnp.where(number < 0, none, jnp.where(face < 4, plain, paired))
    last = pltpu.make_async_copy(rows, rows_out, sems.at[len(copies)])
    last.start()

    copies[4].wait()
    copies[5].wait()
    shard = weight_t.shape[1]
    lead = shard // LANES * LANES
    count = bias.shape[1]
    shard_out[:, 0:lead] = weight_t[:, 0:lead]
    tile = jnp.concatenate(
        [weight_t[:, lead:shard].astype(F32), jnp.zeros((64, lead + LANES - shard), F32)], axis=1
    )
    offset = shard - lead
    behind = jnp.concatenate(
        [bias[...].astype(F32), jnp.zeros((1, LANES - count), F32)], axis=1
    )
    behind = pltpu.roll(jnp.broadcast_to(behind, (64, LANES)), offset, 1)
    first = lax.broadcasted_iota(jnp.int32, (64, LANES), 0) == 0
    lane = lax.broadcasted_iota(jnp.int32, (64, LANES), 1)
    behind = jnp.where(first & (lane >= offset) & (lane < offset + count), behind, 0.0)
    shard_out[:, lead : lead + LANES] = (tile + behind).astype(BF16)
    last.wait()


def gather_units(table, received):
    at = 0
    for part in received:
        table[at : at + part.shape[0], :] = part[...]
        at += part.shape[0]
    table[at:, :] = jnp.zeros((table.shape[0] - at, LANES), BF16)


def assemble(source, table, rows, windows, sides, walls):
    low8 = low_half((8, LANES))
    sub = lax.broadcasted_iota(jnp.int32, (8, LANES), 0)
    top, bottom = sub == 0, sub == 7

    def put(pair, xp, per_brick):
        for e in range(3):
            stacked = [
                jnp.concatenate([per_brick[0][e][i], per_brick[1][e][i]], axis=0)
                for i in range(5)
            ]
            low16 = low_half((16, LANES))
            before = [stacked[4]] + stacked[:3]
            after = stacked[1:4] + [stacked[4]]
            for q in range(4):
                windows[e, q, pair, xp, :, 0:LANES] = stacked[q].astype(BF16)
                windows[e, q, pair, xp, :, LANES:] = jnp.where(
                    low16, after[q], before[q]
                ).astype(BF16)

    def one_pair(pair, carry):
        def unit(brick, ox, oy, oz):
            return pl.multiple_of(rows[brick, offset_number(ox, oy, oz)], UNIT_ROWS)

        def plane(brick, ox, oy):
            chunks = chunk_rows(table[pl.ds(unit(brick, ox, oy, 0), UNIT_ROWS), :].astype(F32))
            after = table[pl.ds(unit(brick, ox, oy, 1), UNIT_ROWS), :].astype(F32)[0:8]
            before = table[pl.ds(unit(brick, ox, oy, -1), UNIT_ROWS), :].astype(F32)[24:32]
            return chunks + [jnp.where(low8, after, before)]

        for b2 in range(2):
            brick = pair * 2 + b2
            low64 = low_half((64, LANES))
            after = table[pl.ds(unit(brick, 0, 0, 1), Z_ROWS), :].astype(F32)
            before = table[pl.ds(unit(brick, 0, 0, -1), Z_ROWS), :].astype(F32)
            walls[b2] = jnp.where(low64, after, before)
            for side, oy in enumerate((-1, 1)):
                for i, part in enumerate(plane(brick, 0, oy)):
                    sides[b2, side, i] = part

        for ox in (-1, 1):
            per_brick = []
            for b2 in range(2):
                brick = pair * 2 + b2
                centre = plane(brick, ox, 0)
                lower = plane(brick, ox, -1)
                upper = plane(brick, ox, 1)
                per_brick.append(
                    [
                        [
                            pltpu.roll(jnp.where(bottom, l, c), 1, 0)
                            for l, c in zip(lower, centre)
                        ],
                        centre,
                        [
                            pltpu.roll(jnp.where(top, u, c), 7, 0)
                            for u, c in zip(upper, centre)
                        ],
                    ]
                )
            put(pair, 0 if ox < 0 else 9, per_brick)

        def one_x(x, carry):
            per_brick = []
            for b2 in range(2):
                brick = pair * 2 + b2
                block = source[brick, x].astype(F32)
                centre = [block[:, q * LANES : (q + 1) * LANES] for q in range(4)]
                centre.append(walls[b2, pl.ds(pl.multiple_of(x * 8, 8), 8), :])
                lower = [
                    jnp.broadcast_to(sides[b2, 0, i, pl.ds(x, 1), :], (8, LANES))
                    for i in range(5)
                ]
                upper = [
                    jnp.broadcast_to(sides[b2, 1, i, pl.ds(x, 1), :], (8, LANES))
                    for i in range(5)
                ]
                per_brick.append(
                    [
                        [jnp.where(top, l, pltpu.roll(c, 1, 0)) for l, c in zip(lower, centre)],
                        centre,
                        [
                            jnp.where(bottom, u, pltpu.roll(c, 7, 0))
                            for u, c in zip(upper, centre)
                        ],
                    ]
                )
            put(pair, x + 1, per_brick)
            return carry

        return lax.fori_loop(0, 8, one_x, carry)

    lax.fori_loop(0, windows.shape[2], one_pair, 0)


def weights_kernel(*refs, shard, groups):
    shards = refs[:groups]
    forward_out, backward_out, bias_out, gathered, flat, shifted = refs[groups:]
    me = lax.axis_index("dp")
    for m, part in enumerate(shards):
        gathered[m] = part[...]
    for k in range(groups):
        flat[:, k * shard : (k + 1) * shard] = gathered[me ^ k][:, 0:shard].astype(F32)
    total = groups * shard
    flat[:, total:] = jnp.zeros((64, flat.shape[1] - total), F32)
    shifted[:, :] = pltpu.roll(flat[...], flat.shape[1] - 64, 1)
    low = low_half((64, LANES))
    for ae in range(9):
        one = taps_pair(flat, shifted, 3 * ae)
        two = jnp.where(low, taps_pair(flat, shifted, 3 * ae + 2), 0.0)
        late = jnp.concatenate([one, two], axis=1)
        forward_out[ae, 64:128, :] = late.astype(BF16)
        forward_out[ae, 0:64, :] = pltpu.roll(late, 192, 1).astype(BF16)
    for ae in range(9):
        m = 3 * (8 - ae)
        first = taps_pair(flat, shifted, m)
        second = taps_pair(flat, shifted, m + 1)
        third = taps_pair(flat, shifted, m + 2)
        backward_out[ae, 0:64, :] = second.astype(BF16)
        backward_out[ae, 64:128, :] = first.astype(BF16)
        backward_out[ae, 128:192, :] = jnp.where(low, 0.0, pltpu.roll(first, 64, 1)).astype(BF16)
        backward_out[ae, 192:256, :] = jnp.where(low, third, 0.0).astype(BF16)

    lane = lax.broadcasted_iota(jnp.int32, (8, LANES), 1)
    bias_lane = shard % LANES
    bias_tile = shard - bias_lane
    count = 64 // groups
    bias_row = jnp.zeros((8, LANES), F32)
    for k in range(groups):
        tile = gathered[me ^ k][0:16, bias_tile : bias_tile + LANES].astype(F32)[0:8]
        moved = pltpu.roll(tile, (count * k - bias_lane) % LANES, 1)
        bias_row += jnp.where((lane >= count * k) & (lane < count * (k + 1)), moved, 0.0)
    bias_out[...] = bias_row + pltpu.roll(bias_row, 64, 1)


def taps_pair(flat, shifted, first):
    if first % 2 == 0:
        return flat[:, first * 64 : first * 64 + LANES]
    return shifted[:, (first - 1) * 64 : (first - 1) * 64 + LANES]


def forward_kernel(
    masked, mask, cotangent_hbm, toeplitz, bias, rows, send, r0, r1, r2, r3, r4,
    block_out, grad_out, keep_out, give_out, u0, u1, u2, u3, u4,
    table, windows, sides, walls, flat, shifted, values, flipped, cotangent, sem, *, shard,
):
    fetch = pltpu.make_async_copy(cotangent_hbm, cotangent, sem)
    fetch.start()
    groups = 2 * keep_out.shape[0]
    bricks = masked.shape[0]
    pairs = bricks // 2
    gather_units(table, (r0, r1, r2, r3, r4))
    assemble(masked, table, rows, windows, sides, walls)
    bias_lane = shard % LANES
    bias_tile = shard - bias_lane
    bias_row = bias[0:1, :]
    fetch.wait()
    values[:, bricks * 64 :, :] = jnp.zeros((4, 64, LANES), F32)

    def one_chunk(q, bias_sum):
        total = jnp.zeros((pairs * LANES, LANES), F32)
        for a in range(3):
            for e in range(3):
                window = windows[e, q, :, a : a + 8].reshape(pairs * LANES, 256)
                total += lax.dot_general(
                    window, toeplitz[3 * a + e], DN_NT, preferred_element_type=F32
                )
        pre = (total + bias_row).reshape(pairs, 8, 2, 8, LANES)
        lanes = pl.ds(pl.multiple_of(q * LANES, LANES), LANES)
        for brick in range(bricks):
            p = pre[brick // 2, :, brick % 2]
            active = mask[brick, :, :, lanes].astype(F32)
            sig = jax.nn.sigmoid(p)
            block_out[brick, :, :, lanes] = (p * sig * active).astype(BF16)
            grad = (
                cotangent[brick, :, :, lanes].astype(F32)
                * sig
                * (1.0 + p * (1.0 - sig))
                * active
            ).astype(BF16)
            grad_out[brick, :, :, lanes] = grad
            wide = grad.astype(F32).reshape(64, LANES)
            values[q, brick * 64 : (brick + 1) * 64, :] = wide
            bias_sum += jnp.sum(wide.reshape(8, 8, LANES), axis=0)
        return bias_sum

    bias_sum = lax.fori_loop(0, 4, one_chunk, jnp.zeros((8, LANES), F32))
    pack_units(values, send, (u0, u1, u2, u3, u4))

    for q in range(4):
        for pair in range(pairs):
            by_x = []
            for x in range(8):
                for b2 in range(2):
                    at = (pair * 2 + b2) * 64 + x * 8
                    by_x.append(values[q, at : at + 8, :])
            flipped[q, :, pair * LANES : (pair + 1) * LANES] = jnp.transpose(
                jnp.concatenate(by_x, axis=0)
            ).astype(BF16)
    for ae in range(9):
        a, e = ae // 3, ae % 3
        total = jnp.zeros((LANES, 256), F32)
        for q in range(4):
            window = windows[e, q, :, a : a + 8].reshape(pairs * LANES, 256)
            total += jnp.dot(flipped[q], window, preferred_element_type=F32)
        flat[:, 192 * ae : 192 * ae + 256] = total[64:128] + pltpu.roll(total[0:64], 64, 1)

    width = keep_out.shape[2]
    bias_all = jnp.sum(bias_sum, axis=0, keepdims=True)
    bias_all = jnp.broadcast_to(bias_all, (8, LANES))
    bias_all = bias_all + pltpu.roll(bias_all, 64, 1)
    bias_all = pltpu.roll(bias_all, bias_lane, 1)
    row8 = lax.broadcasted_iota(jnp.int32, (8, LANES), 0)
    lane8 = lax.broadcasted_iota(jnp.int32, (8, LANES), 1)
    keep = (row8 == 0) & (lane8 >= bias_lane) & (lane8 < bias_lane + 64)
    me = lax.axis_index("dp")
    for k in range(groups):
        part = flat[:, k * shard : (k + 1) * shard]
        shifted[:, 0:shard] = part
        shifted[:, shard:width] = jnp.zeros((64, width - shard), F32)
        tile = shifted[0:8, bias_tile : bias_tile + LANES]
        shifted[0:8, bias_tile : bias_tile + LANES] = jnp.where(keep, bias_all, tile)
        block = shifted[:, 0:width].astype(BF16)
        for m in range(groups):

            @pl.when(me ^ m == k)
            def _(m=m, block=block):
                (give_out if m % 2 else keep_out)[m // 2] = block


def assemble_kernel(grad, rows, r0, r1, r2, r3, r4, after, windows, table, sides, walls):
    del after
    gather_units(table, (r0, r1, r2, r3, r4))
    assemble(grad, table, rows, windows, sides, walls)


def sum_kernel(*refs, operands):
    refs[operands][...] = (refs[0][...].astype(F32) + refs[1][...].astype(F32)).astype(BF16)


def sum_after(mine, other, after, through=()):
    operands = 2 + len(after) + len(through)
    total, *passed = pl.pallas_call(
        functools.partial(sum_kernel, operands=operands),
        name="sum",
        out_shape=[jax.ShapeDtypeStruct(x.shape, x.dtype) for x in (mine, *through)],
        in_specs=[vmem()] * 2 + [untouched()] * (operands - 2),
        out_specs=[vmem()] + [untouched()] * len(through),
        input_output_aliases={2 + len(after) + i: 1 + i for i in range(len(through))},
        compiler_params=pltpu.CompilerParams(vmem_limit_bytes=1024 * 1024),
    )(mine, other, *after, *through)
    return total, passed


def backward_kernel(windows, mask, toeplitz, after, out):
    del after
    bricks = mask.shape[0]
    pairs = bricks // 2

    def one_chunk(q, carry):
        total = jnp.zeros((pairs * LANES, LANES), F32)
        for a in range(3):
            for e in range(3):
                window = windows[e, q, :, a : a + 8].reshape(pairs * LANES, 256)
                total += jnp.dot(window, toeplitz[3 * a + e], preferred_element_type=F32)
        total = total.reshape(pairs, 8, 2, 8, LANES)
        lanes = pl.ds(pl.multiple_of(q * LANES, LANES), LANES)
        for brick in range(bricks):
            active = mask[brick, :, :, lanes].astype(F32)
            out[brick, :, :, lanes] = (total[brick // 2, :, brick % 2] * active).astype(BF16)
        return carry

    lax.fori_loop(0, 4, one_chunk, 0)


def finish_kernel(mine, other, weight_out, bias_out):
    shard = weight_out.shape[1]
    count = bias_out.shape[1]
    total = mine[...].astype(F32) + other[...].astype(F32)
    weight_out[...] = total[:, 0:shard]
    bias_lane = shard % LANES
    bias_tile = shard - bias_lane
    tile = total[0:8, bias_tile : bias_tile + LANES]
    me = lax.axis_index("dp")
    moved = pltpu.roll(tile, 2 * LANES - bias_lane - me * count, 1)
    bias_out[...] = moved[0:1, 0:count]


def swapped(block, axis, bit):
    return lax.ppermute(block, axis, [(i, i ^ bit) for i in range(lax.axis_size(axis))])


def by_parity(block, routes):
    groups = lax.axis_size("dp")
    pairs = [
        (source * groups + group, target * groups + group)
        for group in range(groups)
        for source, target in routes[group % 2]
    ]
    return lax.ppermute(block, ("space", "dp"), pairs)


def exchanged(number, unit):
    routes = []
    for swaps in SWAPS:
        distance, turn = swaps[number - 1]
        route = []
        for low in range(lax.axis_size("space") - distance):
            if low // distance % 2 == turn:
                route += [(low, low + distance), (low + distance, low)]
        routes.append(route)
    return by_parity(unit, routes)


def space_steps():
    bits = []
    while 2 ** len(bits) < lax.axis_size("space"):
        bits.append(2 ** len(bits))
    return list(zip(bits, bits[1:] + bits[:1]))


def stepped(total, step):
    devices = range(lax.axis_size("space"))
    return by_parity(total, [[(i, i ^ bit) for i in devices] for bit in step])


def body(features, occupancy, counts, send_units, neighbours, weight, conv_bias, cotangent):
    grid_shape = features.shape[1:]
    bricks = grid_shape[0]
    pairs = bricks // 2
    spread, links = send_units.shape[2:]
    shard, channels = weight.shape
    groups = lax.axis_size("dp")
    count = conv_bias.shape[0]
    width = -(-(shard + channels) // LANES) * LANES
    unit_rows = 8 * UNIT_ROWS + 2 * Z_ROWS
    units_type = jax.ShapeDtypeStruct((unit_rows, LANES), BF16)
    grid_type = jax.ShapeDtypeStruct(grid_shape, BF16)
    shard_type = jax.ShapeDtypeStruct((channels, width), BF16)
    params = pltpu.CompilerParams(vmem_limit_bytes=48 * 1024 * 1024)
    rows_shape = neighbours.shape[1:]
    send_shape = (spread, 1, links)

    masked, mask, rows, send, own_shard, *units = pl.pallas_call(
        prepare_kernel,
        name="prepare",
        out_shape=[
            grid_type,
            grid_type,
            jax.ShapeDtypeStruct(rows_shape, jnp.int32),
            jax.ShapeDtypeStruct(send_shape, jnp.int32),
            shard_type,
        ]
        + [units_type] * spread,
        in_specs=[pl.BlockSpec(memory_space=pltpu.HBM)] * 6 + [smem()],
        out_specs=[vmem(), vmem(), smem(), smem(), vmem()] + [vmem()] * spread,
        scratch_shapes=[
            pltpu.VMEM((4, (bricks + 1) * 64, LANES), F32),
            pltpu.VMEM(grid_shape, BF16),
            pltpu.VMEM(occupancy.shape[1:], jnp.int32),
            pltpu.VMEM(rows_shape, jnp.int32),
            pltpu.VMEM((channels, shard), BF16),
            pltpu.VMEM((1, count), BF16),
            pltpu.VMEM(rows_shape, jnp.int32),
            pltpu.SemaphoreType.DMA((7,)),
        ],
        compiler_params=params,
    )(
        *(
            pltpu.with_memory_space_constraint(operand, pltpu.HBM)
            for operand in (
                features[0],
                occupancy[0],
                send_units.transpose(0, 2, 1, 3).reshape(send_shape),
                neighbours[0],
                weight.T,
                conv_bias.reshape(1, count),
            )
        ),
        counts,
    )

    shards = {0: own_shard}
    bit = groups // 2
    while bit:
        for m in list(shards):
            shards[m | bit] = swapped(shards[m], "dp", bit)
        bit //= 2
    received = units[:1] + [exchanged(number, units[number]) for number in range(1, spread)]

    flat = pltpu.VMEM((channels, 28 * 64), F32)
    band_forward, band_backward, bias = pl.pallas_call(
        functools.partial(weights_kernel, shard=shard, groups=groups),
        name="weights",
        out_shape=[
            jax.ShapeDtypeStruct((9, LANES, 256), BF16),
            jax.ShapeDtypeStruct((9, 256, LANES), BF16),
            jax.ShapeDtypeStruct((8, LANES), F32),
        ],
        in_specs=[vmem()] * groups,
        out_specs=[vmem()] * 3,
        scratch_shapes=[pltpu.VMEM((groups, channels, width), BF16), flat, flat],
        compiler_params=params,
    )(*(shards[m] for m in range(groups)))

    table = pltpu.VMEM((spread * unit_rows + Z_ROWS, LANES), BF16)
    windows = pltpu.VMEM((3, 4, pairs, 10, 16, 256), BF16)
    sides = pltpu.VMEM((2, 2, 5, 8, LANES), F32)
    walls = pltpu.VMEM((2, 64, LANES), F32)
    half_type = jax.ShapeDtypeStruct((groups // 2, channels, width), BF16)
    block_output, grad, keep, give, *grad_units = pl.pallas_call(
        functools.partial(forward_kernel, shard=shard),
        name="forward",
        out_shape=[grid_type, grid_type, half_type, half_type] + [units_type] * spread,
        in_specs=[vmem(), vmem(), pl.BlockSpec(memory_space=pltpu.HBM), vmem(), vmem()]
        + [smem(), smem()]
        + [vmem()] * spread,
        out_specs=[vmem()] * (4 + spread),
        scratch_shapes=[
            table,
            windows,
            sides,
            walls,
            flat,
            flat,
            pltpu.VMEM((4, (bricks + 1) * 64, LANES), F32),
            pltpu.VMEM((4, LANES, pairs * LANES), BF16),
            pltpu.VMEM(grid_shape, BF16),
            pltpu.SemaphoreType.DMA,
        ],
        compiler_params=params,
    )(
        masked,
        mask,
        pltpu.with_memory_space_constraint(cotangent[0], pltpu.HBM),
        band_forward,
        bias,
        rows,
        send,
        *received,
    )

    grad_received = grad_units[:1] + [exchanged(n, grad_units[n]) for n in range(1, 3)]
    total, _ = sum_after(keep, swapped(give, "dp", 1), [])
    later = grad_units[3:]
    bit = 2
    while bit < groups:
        far = swapped(total[1::2], "dp", bit)
        last = 2 * bit >= groups
        total, later = sum_after(
            total[0::2], far, grad_received[1:3] if last else [], later if last else []
        )
        bit *= 2
    total = total[0]

    steps = space_steps()
    other = stepped(total, steps[0])
    grad_received += [exchanged(n, unit) for n, unit in zip(range(3, spread), later)]
    if len(steps) > 1:
        total, _ = sum_after(total, other, grad_received[3:4])
        other = stepped(total, steps[1])

    padded_grad = pl.pallas_call(
        assemble_kernel,
        name="assemble",
        out_shape=jax.ShapeDtypeStruct(windows.shape, BF16),
        in_specs=[vmem()] + [smem()] + [vmem()] * spread + [untouched()],
        out_specs=vmem(),
        scratch_shapes=[table, sides, walls],
        compiler_params=params,
    )(grad, rows, *grad_received, total)

    for number, step in enumerate(steps[2:]):
        total, _ = sum_after(total, other, [] if number else [padded_grad])
        other = stepped(total, step)

    grad_input = pl.pallas_call(
        backward_kernel,
        name="backward",
        out_shape=grid_type,
        in_specs=[vmem()] * 3 + [untouched()],
        out_specs=vmem(),
        compiler_params=params,
    )(padded_grad, mask, band_backward, total)

    weight_share, bias_share = pl.pallas_call(
        finish_kernel,
        name="finish",
        out_shape=[
            jax.ShapeDtypeStruct((channels, shard), F32),
            jax.ShapeDtypeStruct((1, count), F32),
        ],
        in_specs=[vmem()] * 2,
        out_specs=[vmem()] * 2,
        compiler_params=params,
    )(total, other)
    return (
        block_output[None],
        grad_input[None],
        weight_share.T,
        bias_share.reshape(count),
    )


def solution(mesh):
    placed = (
        P("dp", "space", None, None, None),
        P("dp", "space", None),
        P("dp", "space"),
        P("dp", "space", None, None),
        P("dp", "space", None),
        P("dp", None),
        P("dp"),
        P("dp", "space", None, None, None),
    )
    return jax.shard_map(
        body,
        mesh=mesh,
        in_specs=placed,
        out_specs=(
            P("dp", "space", None, None, None),
            P("dp", "space", None, None, None),
            P("dp", None),
            P("dp"),
        ),
        check_vma=False,
    )
```

```python
import functools

import jax
import jax.numpy as jnp
from jax import lax
from jax.experimental import pallas as pl
from jax.experimental.pallas import tpu as pltpu
from jax.sharding import PartitionSpec as P

F32 = jnp.float32
BF16 = jnp.bfloat16
LANES = 128
UNIT_ROWS = 32
Z_ROWS = 64
SWAPS = (
    ((1, 1), (2, 1), (1, 0), (2, 0)),
    ((2, 1), (1, 1), (2, 0), (1, 0)),
)
DN_NT = (((1,), (1,)), ((), ()))
DN_NN = (((1,), (0,)), ((), ()))


def vmem():
    return pl.BlockSpec(memory_space=pltpu.VMEM)


def smem():
    return pl.BlockSpec(memory_space=pltpu.SMEM)


def untouched():
    return pl.BlockSpec(memory_space=pl.ANY)


def offset_number(ox, oy, oz):
    flat = (ox + 1) * 9 + (oy + 1) * 3 + (oz + 1)
    return flat if flat < 13 else flat - 1


def low_half(shape):
    return lax.broadcasted_iota(jnp.int32, shape, len(shape) - 1) % LANES < 64


def chunk_rows(block):
    return [block[8 * q : 8 * q + 8] for q in range(4)]


def upward(device, distance):
    return lax.rem(lax.div(device, distance), 2)


def pack_units(values, send, outs):
    slots = values.shape[1] // 64 - 1
    reach = len(outs) // 2
    low = low_half((64, LANES))
    device = lax.axis_index("space")
    odd = lax.rem(lax.axis_index("dp"), 2)
    for number, out in enumerate(outs):
        column = reach
        if number > 0:
            columns = []
            for distance, turn in (SWAPS[0][number - 1], SWAPS[1][number - 1]):
                up = upward(device, distance) == turn
                columns.append(jnp.where(up, reach + distance, reach - distance))
            column = jnp.where(odd == 0, columns[0], columns[1])

        def base(link):
            unit = send[column, 0, link]
            slot = jnp.where(unit < 0, slots, (unit * 43) >> 8)
            return pl.multiple_of(slot * 64, 64)

        for half in range(2):
            for face in range(4):
                start = base(half * 6 + face)
                if face < 2:
                    where = pl.ds(start + 56 * face, 8)
                else:
                    where = pl.ds(start + 7 * (face - 2), 8, stride=8)
                packed = jnp.concatenate([values[q, where, :] for q in range(4)], axis=0)
                at = (half * 4 + face) * UNIT_ROWS
                out[at : at + UNIT_ROWS, :] = packed.astype(BF16)
            first = values[0, pl.ds(base(half * 6 + 4), 64), :]
            last = values[3, pl.ds(base(half * 6 + 5), 64), :]
            at = 8 * UNIT_ROWS + half * Z_ROWS
            out[at : at + Z_ROWS, :] = jnp.where(low, first, last).astype(BF16)


def prepare_kernel(
    features_hbm, occupancy_hbm, send_hbm, listing_hbm, weight_hbm, bias_hbm, counts,
    masked_out, mask_out, rows_out, send_out, shard_out, u0, u1, u2, u3, u4,
    values, features, occupancy, listing, weight_t, bias, rows, sems,
):
    copies = [
        pltpu.make_async_copy(src, dst, sems.at[i])
        for i, (src, dst) in enumerate(
            (
                (occupancy_hbm, occupancy),
                (features_hbm, features),
                (send_hbm, send_out),
                (listing_hbm, listing),
                (weight_hbm, weight_t),
                (bias_hbm, bias),
            )
        )
    ]
    for copy in copies:
        copy.start()
    bricks = features.shape[0]
    shard_out[...] = jnp.zeros(shard_out.shape, BF16)
    values[:, bricks * 64 :, :] = jnp.zeros((4, 64, LANES), F32)
    row = lax.broadcasted_iota(jnp.int32, (64, 512), 0)
    col = lax.broadcasted_iota(jnp.int32, (64, 512), 1)
    same = (col >> 3) == row
    z_row = lax.broadcasted_iota(jnp.int32, (512, 512), 0) & 7
    z_col = lax.broadcasted_iota(jnp.int32, (512, 512), 1) >> 6
    expand = jnp.where(z_row == z_col, 1.0, 0.0).astype(BF16)

    copies[0].wait()
    live = lax.broadcasted_iota(jnp.int32, (bricks, 512), 0) < counts[0, 0]
    occ = jnp.where(live, occupancy[...], 0).astype(F32)
    spread = jnp.concatenate(
        [jnp.where(same, occ[b : b + 1, :], 0.0) for b in range(bricks)], axis=0
    ).astype(BF16)
    mask = jnp.dot(spread, expand, preferred_element_type=F32)
    mask_out[...] = mask.astype(BF16).reshape(mask_out.shape)
    copies[1].wait()
    value = features[...].astype(F32).reshape(bricks * 64, 512) * mask
    masked_out[...] = value.astype(BF16).reshape(masked_out.shape)
    for q in range(4):
        values[q, 0 : bricks * 64, :] = value[:, q * LANES : (q + 1) * LANES]
    copies[2].wait()
    pack_units(values, send_out, (u0, u1, u2, u3, u4))

    copies[3].wait()
    device = lax.axis_index("space")
    number = listing[...]
    column = (number * 43) >> 9
    link = number - column * 12
    half = (link >= 6).astype(jnp.int32)
    face = link - 6 * half
    block = jnp.zeros(number.shape, jnp.int32)
    odd = lax.rem(lax.axis_index("dp"), 2)
    for distance in (1, 2):
        up = upward(device, distance)
        first, second = (
            jnp.where(
                odd == 0,
                SWAPS[0].index((distance, turn)) + 1,
                SWAPS[1].index((distance, turn)) + 1,
            )
            for turn in range(2)
        )
        block = jnp.where(column == 2 - distance, jnp.where(up == 0, first, second), block)
        block = jnp.where(column == 2 + distance, jnp.where(up == 0, second, first), block)
    base = block * (8 * UNIT_ROWS + 2 * Z_ROWS)
    plain = base + (half * 4 + face) * UNIT_ROWS
    paired = base + 8 * UNIT_ROWS + half * Z_ROWS
    none = 5 * (8 * UNIT_ROWS + 2 * Z_ROWS)
    rows[...] = jnp.where(number < 0, none, jnp.where(face < 4, plain, paired))
    last = pltpu.make_async_copy(rows, rows_out, sems.at[len(copies)])
    last.start()

    copies[4].wait()
    copies[5].wait()
    shard = weight_t.shape[1]
    lead = shard // LANES * LANES
    count = bias.shape[1]
    shard_out[:, 0:lead] = weight_t[:, 0:lead]
    tile = jnp.concatenate(
        [weight_t[:, lead:shard].astype(F32), jnp.zeros((64, lead + LANES - shard), F32)], axis=1
    )
    offset = shard - lead
    behind = jnp.concatenate(
        [bias[...].astype(F32), jnp.zeros((1, LANES - count), F32)], axis=1
    )
    behind = pltpu.roll(jnp.broadcast_to(behind, (64, LANES)), offset, 1)
    first = lax.broadcasted_iota(jnp.int32, (64, LANES), 0) == 0
    lane = lax.broadcasted_iota(jnp.int32, (64, LANES), 1)
    behind = jnp.where(first & (lane >= offset) & (lane < offset + count), behind, 0.0)
    shard_out[:, lead : lead + LANES] = (tile + behind).astype(BF16)
    last.wait()


def gather_units(table, received):
    at = 0
    for part in received:
        table[at : at + part.shape[0], :] = part[...]
        at += part.shape[0]
    table[at:, :] = jnp.zeros((table.shape[0] - at, LANES), BF16)


def assemble(source, table, rows, windows, sides, walls):
    low8 = low_half((8, LANES))
    sub = lax.broadcasted_iota(jnp.int32, (8, LANES), 0)
    top, bottom = sub == 0, sub == 7

    def put(pair, half, bit, per_brick):
        for e in range(3):
            stacked = [
                jnp.concatenate([per_brick[0][e][i], per_brick[1][e][i]], axis=0)
                for i in range(5)
            ]
            low16 = low_half((16, LANES))
            before = [stacked[4]] + stacked[:3]
            after = stacked[1:4] + [stacked[4]]
            for q in range(4):
                windows[e, q, pair, half, bit, :, 0:LANES] = stacked[q].astype(BF16)
                windows[e, q, pair, half, bit, :, LANES:] = jnp.where(
                    low16, after[q], before[q]
                ).astype(BF16)

    def one_pair(pair, carry):
        def unit(brick, ox, oy, oz):
            return pl.multiple_of(rows[brick, offset_number(ox, oy, oz)], UNIT_ROWS)

        def plane(brick, ox, oy):
            chunks = chunk_rows(table[pl.ds(unit(brick, ox, oy, 0), UNIT_ROWS), :].astype(F32))
            after = table[pl.ds(unit(brick, ox, oy, 1), UNIT_ROWS), :].astype(F32)[0:8]
            before = table[pl.ds(unit(brick, ox, oy, -1), UNIT_ROWS), :].astype(F32)[24:32]
            return chunks + [jnp.where(low8, after, before)]

        for b2 in range(2):
            brick = pair * 2 + b2
            low64 = low_half((64, LANES))
            after = table[pl.ds(unit(brick, 0, 0, 1), Z_ROWS), :].astype(F32)
            before = table[pl.ds(unit(brick, 0, 0, -1), Z_ROWS), :].astype(F32)
            walls[b2] = jnp.where(low64, after, before)
            for side, oy in enumerate((-1, 1)):
                for i, part in enumerate(plane(brick, 0, oy)):
                    sides[b2, side, i] = part

        for ox in (-1, 1):
            per_brick = []
            for b2 in range(2):
                brick = pair * 2 + b2
                centre = plane(brick, ox, 0)
                lower = plane(brick, ox, -1)
                upper = plane(brick, ox, 1)
                per_brick.append(
                    [
                        [
                            pltpu.roll(jnp.where(bottom, l, c), 1, 0)
                            for l, c in zip(lower, centre)
                        ],
                        centre,
                        [
                            pltpu.roll(jnp.where(top, u, c), 7, 0)
                            for u, c in zip(upper, centre)
                        ],
                    ]
                )
            put(pair, 0 if ox < 0 else 4, 0 if ox < 0 else 1, per_brick)

        def two_x(i, carry):
            for bit in range(2):
                x = 2 * i + bit
                per_brick = []
                for b2 in range(2):
                    brick = pair * 2 + b2
                    block = source[brick, i, bit].astype(F32)
                    centre = [block[:, q * LANES : (q + 1) * LANES] for q in range(4)]
                    centre.append(walls[b2, pl.ds(pl.multiple_of(x * 8, 8), 8), :])
                    lower = [
                        jnp.broadcast_to(sides[b2, 0, n, pl.ds(x, 1), :], (8, LANES))
                        for n in range(5)
                    ]
                    upper = [
                        jnp.broadcast_to(sides[b2, 1, n, pl.ds(x, 1), :], (8, LANES))
                        for n in range(5)
                    ]
                    per_brick.append(
                        [
                            [
                                jnp.where(top, l, pltpu.roll(c, 1, 0))
                                for l, c in zip(lower, centre)
                            ],
                            centre,
                            [
                                jnp.where(bottom, u, pltpu.roll(c, 7, 0))
                                for u, c in zip(upper, centre)
                            ],
                        ]
                    )
                put(pair, i + bit, 1 - bit, per_brick)
            return carry

        return lax.fori_loop(0, 4, two_x, carry)

    lax.fori_loop(0, windows.shape[2], one_pair, 0)


def lane_block(d, e):
    return slice((3 * d + e) * 256, (3 * d + e + 1) * 256)


def tap_rows(windows, d, e):
    block = windows[e, :, :, d // 2 : d // 2 + 4, d % 2]
    return block.reshape(-1, block.shape[-1])


def all_taps(windows):
    return jnp.concatenate(
        [tap_rows(windows, d, e) for d in range(4) for e in range(3)], axis=1
    )


def chunk_places(bricks):
    return [(2 * pair + b2, i) for pair in range(bricks // 2) for i in range(4) for b2 in range(2)]


def chunk_of(ref, q):
    lanes = slice(q * LANES, (q + 1) * LANES)
    return jnp.concatenate(
        [
            jnp.concatenate([ref[b, i, x, :, lanes].astype(F32) for x in range(2)], axis=1)
            for b, i in chunk_places(ref.shape[0])
        ],
        axis=0,
    )


def put_chunk(ref, q, value):
    for n, (b, i) in enumerate(chunk_places(ref.shape[0])):
        for x in range(2):
            part = value[8 * n : 8 * n + 8, x * LANES : (x + 1) * LANES]
            ref[b, i, x, :, q * LANES : (q + 1) * LANES] = part.astype(ref.dtype)


def weights_kernel(*refs, shard, groups):
    shards = refs[:groups]
    forward_out, backward_out, bias_out, gathered, flat, shifted = refs[groups:]
    me = lax.axis_index("dp")
    for m, part in enumerate(shards):
        gathered[m] = part[...]
    for k in range(groups):
        flat[:, k * shard : (k + 1) * shard] = gathered[me ^ k][:, 0:shard].astype(F32)
    total = groups * shard
    flat[:, total:] = jnp.zeros((64, flat.shape[1] - total), F32)
    shifted[:, :] = pltpu.roll(flat[...], flat.shape[1] - 64, 1)
    low = low_half((64, LANES))
    for e in range(3):
        for x in range(2):
            half = slice(x * LANES, (x + 1) * LANES)
            forward_out[half, lane_block(3 * (1 - x), e)] = jnp.zeros((LANES, 256), BF16)
            backward_out[lane_block(3 * (1 - x), e), half] = jnp.zeros((256, LANES), BF16)
    for ae in range(9):
        a, e = ae // 3, ae % 3
        one = taps_pair(flat, shifted, 3 * ae)
        two = jnp.where(low, taps_pair(flat, shifted, 3 * ae + 2), 0.0)
        late = jnp.concatenate([one, two], axis=1)
        band = jnp.concatenate([pltpu.roll(late, 192, 1), late], axis=0).astype(BF16)
        for x in range(2):
            forward_out[x * LANES : (x + 1) * LANES, lane_block(a + x, e)] = band
    for ae in range(9):
        a, e = ae // 3, ae % 3
        m = 3 * (8 - ae)
        first = taps_pair(flat, shifted, m)
        second = taps_pair(flat, shifted, m + 1)
        third = taps_pair(flat, shifted, m + 2)
        band = jnp.concatenate(
            [
                second,
                first,
                jnp.where(low, 0.0, pltpu.roll(first, 64, 1)),
                jnp.where(low, third, 0.0),
            ],
            axis=0,
        ).astype(BF16)
        for x in range(2):
            backward_out[lane_block(a + x, e), x * LANES : (x + 1) * LANES] = band

    lane = lax.broadcasted_iota(jnp.int32, (8, LANES), 1)
    bias_lane = shard % LANES
    bias_tile = shard - bias_lane
    count = 64 // groups
    bias_row = jnp.zeros((8, LANES), F32)
    for k in range(groups):
        tile = gathered[me ^ k][0:16, bias_tile : bias_tile + LANES].astype(F32)[0:8]
        moved = pltpu.roll(tile, (count * k - bias_lane) % LANES, 1)
        bias_row += jnp.where((lane >= count * k) & (lane < count * (k + 1)), moved, 0.0)
    bias_out[...] = bias_row + pltpu.roll(bias_row, 64, 1)


def taps_pair(flat, shifted, first):
    if first % 2 == 0:
        return flat[:, first * 64 : first * 64 + LANES]
    return shifted[:, (first - 1) * 64 : (first - 1) * 64 + LANES]


def forward_kernel(
    masked, mask, cotangent_hbm, toeplitz, bias, rows, send, r0, r1, r2, r3, r4,
    block_out, grad_out, keep_out, give_out, u0, u1, u2, u3, u4,
    table, windows, sides, walls, flat, shifted, values, flipped, cotangent, sem, *, shard,
):
    fetch = pltpu.make_async_copy(cotangent_hbm, cotangent, sem)
    fetch.start()
    groups = 2 * keep_out.shape[0]
    bricks = masked.shape[0]
    pairs = bricks // 2
    gather_units(table, (r0, r1, r2, r3, r4))
    assemble(masked, table, rows, windows, sides, walls)
    bias_lane = shard % LANES
    bias_tile = shard - bias_lane
    bias_row = bias[0:1, :]
    fetch.wait()
    values[:, bricks * 64 :, :] = jnp.zeros((4, 64, LANES), F32)

    bias_row = jnp.concatenate([bias_row, bias_row], axis=1)
    total = lax.dot_general(all_taps(windows), toeplitz[...], DN_NT, preferred_element_type=F32)
    rows_of_chunk = total.shape[0] // 4
    bias_sum = jnp.zeros((8, 256), F32)
    for q in range(4):
        p = total[q * rows_of_chunk : (q + 1) * rows_of_chunk] + bias_row
        active = chunk_of(mask, q)
        sig = jax.nn.sigmoid(p)
        put_chunk(block_out, q, p * sig * active)
        grad = (chunk_of(cotangent, q) * sig * (1.0 + p * (1.0 - sig)) * active).astype(BF16)
        wide = grad.astype(F32)
        put_chunk(grad_out, q, wide)
        for n, (brick, i) in enumerate(chunk_places(bricks)):
            for x in range(2):
                at = brick * 64 + (2 * i + x) * 8
                values[q, at : at + 8, :] = wide[
                    8 * n : 8 * n + 8, x * LANES : (x + 1) * LANES
                ]
        flipped[:, q * rows_of_chunk : (q + 1) * rows_of_chunk] = jnp.transpose(wide).astype(BF16)
        bias_sum += jnp.sum(wide.reshape(-1, 8, 256), axis=0)
    bias_sum = bias_sum[:, 0:LANES] + bias_sum[:, LANES:]
    pack_units(values, send, (u0, u1, u2, u3, u4))

    for e in range(3):
        products = [
            jnp.dot(flipped[...], tap_rows(windows, d, e), preferred_element_type=F32)
            for d in range(4)
        ]
        for a in range(3):
            both = products[a][0:LANES] + products[a + 1][LANES:]
            shifted[64 * a : 64 * a + 64, 256 * e : 256 * e + 256] = both[64:] + pltpu.roll(
                both[0:64], 64, 1
            )
    for a in range(3):
        for e in range(3):
            at = 192 * (3 * a + e)
            flat[:, at : at + 256] = shifted[64 * a : 64 * a + 64, 256 * e : 256 * e + 256]

    width = keep_out.shape[2]
    bias_all = jnp.sum(bias_sum, axis=0, keepdims=True)
    bias_all = jnp.broadcast_to(bias_all, (8, LANES))
    bias_all = bias_all + pltpu.roll(bias_all, 64, 1)
    bias_all = pltpu.roll(bias_all, bias_lane, 1)
    row8 = lax.broadcasted_iota(jnp.int32, (8, LANES), 0)
    lane8 = lax.broadcasted_iota(jnp.int32, (8, LANES), 1)
    keep = (row8 == 0) & (lane8 >= bias_lane) & (lane8 < bias_lane + 64)
    me = lax.axis_index("dp")
    for k in range(groups):
        part = flat[:, k * shard : (k + 1) * shard]
        shifted[0:64, 0:shard] = part
        shifted[0:64, shard:width] = jnp.zeros((64, width - shard), F32)
        tile = shifted[0:8, bias_tile : bias_tile + LANES]
        shifted[0:8, bias_tile : bias_tile + LANES] = jnp.where(keep, bias_all, tile)
        block = shifted[0:64, 0:width].astype(BF16)
        for m in range(groups):

            @pl.when(me ^ m == k)
            def _(m=m, block=block):
                (give_out if m % 2 else keep_out)[m // 2] = block


def assemble_kernel(grad, rows, r0, r1, r2, r3, r4, after, windows, table, sides, walls):
    del after
    gather_units(table, (r0, r1, r2, r3, r4))
    assemble(grad, table, rows, windows, sides, walls)


def sum_kernel(*refs, operands):
    refs[operands][...] = (refs[0][...].astype(F32) + refs[1][...].astype(F32)).astype(BF16)


def sum_after(mine, other, after, through=()):
    operands = 2 + len(after) + len(through)
    total, *passed = pl.pallas_call(
        functools.partial(sum_kernel, operands=operands),
        name="sum",
        out_shape=[jax.ShapeDtypeStruct(x.shape, x.dtype) for x in (mine, *through)],
        in_specs=[vmem()] * 2 + [untouched()] * (operands - 2),
        out_specs=[vmem()] + [untouched()] * len(through),
        input_output_aliases={2 + len(after) + i: 1 + i for i in range(len(through))},
        compiler_params=pltpu.CompilerParams(vmem_limit_bytes=1024 * 1024),
    )(mine, other, *after, *through)
    return total, passed


def backward_kernel(windows, mask, toeplitz, after, out):
    del after
    total = jnp.dot(all_taps(windows), toeplitz[...], preferred_element_type=F32)
    rows_of_chunk = total.shape[0] // 4
    for q in range(4):
        part = total[q * rows_of_chunk : (q + 1) * rows_of_chunk]
        put_chunk(out, q, part * chunk_of(mask, q))


def finish_kernel(mine, other, weight_out, bias_out):
    shard = weight_out.shape[1]
    count = bias_out.shape[1]
    total = mine[...].astype(F32) + other[...].astype(F32)
    weight_out[...] = total[:, 0:shard]
    bias_lane = shard % LANES
    bias_tile = shard - bias_lane
    tile = total[0:8, bias_tile : bias_tile + LANES]
    me = lax.axis_index("dp")
    moved = pltpu.roll(tile, 2 * LANES - bias_lane - me * count, 1)
    bias_out[...] = moved[0:1, 0:count]


def swapped(block, axis, bit):
    return lax.ppermute(block, axis, [(i, i ^ bit) for i in range(lax.axis_size(axis))])


def by_parity(block, routes):
    groups = lax.axis_size("dp")
    pairs = [
        (source * groups + group, target * groups + group)
        for group in range(groups)
        for source, target in routes[group % 2]
    ]
    return lax.ppermute(block, ("space", "dp"), pairs)


def exchanged(number, unit):
    routes = []
    for swaps in SWAPS:
        distance, turn = swaps[number - 1]
        route = []
        for low in range(lax.axis_size("space") - distance):
            if low // distance % 2 == turn:
                route += [(low, low + distance), (low + distance, low)]
        routes.append(route)
    return by_parity(unit, routes)


def space_steps():
    bits = []
    while 2 ** len(bits) < lax.axis_size("space"):
        bits.append(2 ** len(bits))
    return list(zip(bits, bits[1:] + bits[:1]))


def stepped(total, step):
    devices = range(lax.axis_size("space"))
    return by_parity(total, [[(i, i ^ bit) for i in devices] for bit in step])


def body(features, occupancy, counts, send_units, neighbours, weight, conv_bias, cotangent):
    bricks, edge, _, lanes = features.shape[1:]
    grid_shape = (bricks, edge // 2, 2, edge, lanes)
    pairs = bricks // 2
    spread, links = send_units.shape[2:]
    shard, channels = weight.shape
    groups = lax.axis_size("dp")
    count = conv_bias.shape[0]
    width = -(-(shard + channels) // LANES) * LANES
    unit_rows = 8 * UNIT_ROWS + 2 * Z_ROWS
    units_type = jax.ShapeDtypeStruct((unit_rows, LANES), BF16)
    grid_type = jax.ShapeDtypeStruct(grid_shape, BF16)
    shard_type = jax.ShapeDtypeStruct((channels, width), BF16)
    params = pltpu.CompilerParams(vmem_limit_bytes=48 * 1024 * 1024)
    rows_shape = neighbours.shape[1:]
    send_shape = (spread, 1, links)

    masked, mask, rows, send, own_shard, *units = pl.pallas_call(
        prepare_kernel,
        name="prepare",
        out_shape=[
            grid_type,
            grid_type,
            jax.ShapeDtypeStruct(rows_shape, jnp.int32),
            jax.ShapeDtypeStruct(send_shape, jnp.int32),
            shard_type,
        ]
        + [units_type] * spread,
        in_specs=[pl.BlockSpec(memory_space=pltpu.HBM)] * 6 + [smem()],
        out_specs=[vmem(), vmem(), smem(), smem(), vmem()] + [vmem()] * spread,
        scratch_shapes=[
            pltpu.VMEM((4, (bricks + 1) * 64, LANES), F32),
            pltpu.VMEM(grid_shape, BF16),
            pltpu.VMEM(occupancy.shape[1:], jnp.int32),
            pltpu.VMEM(rows_shape, jnp.int32),
            pltpu.VMEM((channels, shard), BF16),
            pltpu.VMEM((1, count), BF16),
            pltpu.VMEM(rows_shape, jnp.int32),
            pltpu.SemaphoreType.DMA((7,)),
        ],
        compiler_params=params,
    )(
        *(
            pltpu.with_memory_space_constraint(operand, pltpu.HBM)
            for operand in (
                features.reshape(grid_shape),
                occupancy[0],
                send_units.transpose(0, 2, 1, 3).reshape(send_shape),
                neighbours[0],
                weight.T,
                conv_bias.reshape(1, count),
            )
        ),
        counts,
    )

    shards = {0: own_shard}
    bit = groups // 2
    while bit:
        for m in list(shards):
            shards[m | bit] = swapped(shards[m], "dp", bit)
        bit //= 2
    received = units[:1] + [exchanged(number, units[number]) for number in range(1, spread)]

    flat = pltpu.VMEM((channels, 28 * 64), F32)
    band_forward, band_backward, bias = pl.pallas_call(
        functools.partial(weights_kernel, shard=shard, groups=groups),
        name="weights",
        out_shape=[
            jax.ShapeDtypeStruct((256, 12 * 256), BF16),
            jax.ShapeDtypeStruct((12 * 256, 256), BF16),
            jax.ShapeDtypeStruct((8, LANES), F32),
        ],
        in_specs=[vmem()] * groups,
        out_specs=[vmem()] * 3,
        scratch_shapes=[pltpu.VMEM((groups, channels, width), BF16), flat, flat],
        compiler_params=params,
    )(*(shards[m] for m in range(groups)))

    table = pltpu.VMEM((spread * unit_rows + Z_ROWS, LANES), BF16)
    windows = pltpu.VMEM((3, 4, pairs, 5, 2, 16, 256), BF16)
    sides = pltpu.VMEM((2, 2, 5, 8, LANES), F32)
    walls = pltpu.VMEM((2, 64, LANES), F32)
    half_type = jax.ShapeDtypeStruct((groups // 2, channels, width), BF16)
    block_output, grad, keep, give, *grad_units = pl.pallas_call(
        functools.partial(forward_kernel, shard=shard),
        name="forward",
        out_shape=[grid_type, grid_type, half_type, half_type] + [units_type] * spread,
        in_specs=[vmem(), vmem(), pl.BlockSpec(memory_space=pltpu.HBM), vmem(), vmem()]
        + [smem(), smem()]
        + [vmem()] * spread,
        out_specs=[vmem()] * (4 + spread),
        scratch_shapes=[
            table,
            windows,
            sides,
            walls,
            flat,
            pltpu.VMEM((192, 3 * 256), F32),
            pltpu.VMEM((4, (bricks + 1) * 64, LANES), F32),
            pltpu.VMEM((256, bricks * LANES), BF16),
            pltpu.VMEM(grid_shape, BF16),
            pltpu.SemaphoreType.DMA,
        ],
        compiler_params=params,
    )(
        masked,
        mask,
        pltpu.with_memory_space_constraint(cotangent.reshape(grid_shape), pltpu.HBM),
        band_forward,
        bias,
        rows,
        send,
        *received,
    )

    grad_received = grad_units[:1] + [exchanged(n, grad_units[n]) for n in range(1, 3)]
    total, _ = sum_after(keep, swapped(give, "dp", 1), [])
    later = grad_units[3:]
    bit = 2
    while bit < groups:
        far = swapped(total[1::2], "dp", bit)
        last = 2 * bit >= groups
        total, later = sum_after(
            total[0::2], far, grad_received[1:3] if last else [], later if last else []
        )
        bit *= 2
    total = total[0]

    steps = space_steps()
    other = stepped(total, steps[0])
    grad_received += [exchanged(n, unit) for n, unit in zip(range(3, spread), later)]
    if len(steps) > 1:
        total, _ = sum_after(total, other, grad_received[3:4])
        other = stepped(total, steps[1])

    padded_grad = pl.pallas_call(
        assemble_kernel,
        name="assemble",
        out_shape=jax.ShapeDtypeStruct(windows.shape, BF16),
        in_specs=[vmem()] + [smem()] + [vmem()] * spread + [untouched()],
        out_specs=vmem(),
        scratch_shapes=[table, sides, walls],
        compiler_params=params,
    )(grad, rows, *grad_received, total)

    for number, step in enumerate(steps[2:]):
        total, _ = sum_after(total, other, [] if number else [padded_grad])
        other = stepped(total, step)

    grad_input = pl.pallas_call(
        backward_kernel,
        name="backward",
        out_shape=grid_type,
        in_specs=[vmem()] * 3 + [untouched()],
        out_specs=vmem(),
        compiler_params=params,
    )(padded_grad, mask, band_backward, total)

    weight_share, bias_share = pl.pallas_call(
        finish_kernel,
        name="finish",
        out_shape=[
            jax.ShapeDtypeStruct((channels, shard), F32),
            jax.ShapeDtypeStruct((1, count), F32),
        ],
        in_specs=[vmem()] * 2,
        out_specs=[vmem()] * 2,
        compiler_params=params,
    )(total, other)
    return (
        block_output.reshape(features.shape),
        grad_input.reshape(features.shape),
        weight_share.T,
        bias_share.reshape(count),
    )


def solution(mesh):
    placed = (
        P("dp", "space", None, None, None),
        P("dp", "space", None),
        P("dp", "space"),
        P("dp", "space", None, None),
        P("dp", "space", None),
        P("dp", None),
        P("dp"),
        P("dp", "space", None, None, None),
    )
    return jax.shard_map(
        body,
        mesh=mesh,
        in_specs=placed,
        out_specs=(
            P("dp", "space", None, None, None),
            P("dp", "space", None, None, None),
            P("dp", None),
            P("dp"),
        ),
        check_vma=False,
    )
```

```python
import functools

import jax
import jax.numpy as jnp
from jax import lax
from jax.experimental import pallas as pl
from jax.experimental.pallas import tpu as pltpu
from jax.sharding import PartitionSpec as P

F32 = jnp.float32
BF16 = jnp.bfloat16
LANES = 128
UNIT_ROWS = 32
Z_ROWS = 64
SWAPS = (
    ((1, 1), (2, 1), (1, 0), (2, 0)),
    ((2, 1), (1, 1), (2, 0), (1, 0)),
)


def vmem():
    return pl.BlockSpec(memory_space=pltpu.VMEM)


def smem():
    return pl.BlockSpec(memory_space=pltpu.SMEM)


def untouched():
    return pl.BlockSpec(memory_space=pl.ANY)


def offset_number(ox, oy, oz):
    flat = (ox + 1) * 9 + (oy + 1) * 3 + (oz + 1)
    return flat if flat < 13 else flat - 1


def low_half(shape):
    return lax.broadcasted_iota(jnp.int32, shape, len(shape) - 1) % LANES < 64


def chunk_rows(block):
    return [block[8 * q : 8 * q + 8] for q in range(4)]


def upward(device, distance):
    return lax.rem(lax.div(device, distance), 2)


def pack_units(values, send, outs):
    slots = values.shape[1] // 64 - 1
    reach = len(outs) // 2
    low = low_half((64, LANES))
    device = lax.axis_index("space")
    odd = lax.rem(lax.axis_index("dp"), 2)
    for number, out in enumerate(outs):
        column = reach
        if number > 0:
            columns = []
            for distance, turn in (SWAPS[0][number - 1], SWAPS[1][number - 1]):
                up = upward(device, distance) == turn
                columns.append(jnp.where(up, reach + distance, reach - distance))
            column = jnp.where(odd == 0, columns[0], columns[1])

        def base(link):
            unit = send[column, 0, link]
            slot = jnp.where(unit < 0, slots, (unit * 43) >> 8)
            return pl.multiple_of(slot * 64, 64)

        for half in range(2):
            for face in range(4):
                start = base(half * 6 + face)
                if face < 2:
                    where = pl.ds(start + 56 * face, 8)
                else:
                    where = pl.ds(start + 7 * (face - 2), 8, stride=8)
                packed = jnp.concatenate([values[q, where, :] for q in range(4)], axis=0)
                at = (half * 4 + face) * UNIT_ROWS
                out[at : at + UNIT_ROWS, :] = packed.astype(BF16)
            first = values[0, pl.ds(base(half * 6 + 4), 64), :]
            last = values[3, pl.ds(base(half * 6 + 5), 64), :]
            at = 8 * UNIT_ROWS + half * Z_ROWS
            out[at : at + Z_ROWS, :] = jnp.where(low, first, last).astype(BF16)


def prepare_kernel(
    features_hbm, occupancy_hbm, send_hbm, listing_hbm, weight_hbm, bias_hbm, counts,
    masked_out, mask_out, rows_out, send_out, shard_out, u0, u1, u2, u3, u4,
    values, features, occupancy, listing, weight_t, bias, rows, sems,
):
    copies = [
        pltpu.make_async_copy(src, dst, sems.at[i])
        for i, (src, dst) in enumerate(
            (
                (occupancy_hbm, occupancy),
                (features_hbm, features),
                (send_hbm, send_out),
                (listing_hbm, listing),
                (weight_hbm, weight_t),
                (bias_hbm, bias),
            )
        )
    ]
    for copy in copies:
        copy.start()
    bricks = features.shape[0]
    shard_out[...] = jnp.zeros(shard_out.shape, BF16)
    values[:, bricks * 64 :, :] = jnp.zeros((4, 64, LANES), F32)
    row = lax.broadcasted_iota(jnp.int32, (64, 512), 0)
    col = lax.broadcasted_iota(jnp.int32, (64, 512), 1)
    same = (col >> 3) == row
    z_row = lax.broadcasted_iota(jnp.int32, (512, 512), 0) & 7
    z_col = lax.broadcasted_iota(jnp.int32, (512, 512), 1) >> 6
    expand = jnp.where(z_row == z_col, 1.0, 0.0).astype(BF16)

    copies[3].wait()
    device = lax.axis_index("space")
    number = listing[...]
    column = (number * 43) >> 9
    link = number - column * 12
    half = (link >= 6).astype(jnp.int32)
    face = link - 6 * half
    block = jnp.zeros(number.shape, jnp.int32)
    odd = lax.rem(lax.axis_index("dp"), 2)
    for distance in (1, 2):
        up = upward(device, distance)
        first, second = (
            jnp.where(
                odd == 0,
                SWAPS[0].index((distance, turn)) + 1,
                SWAPS[1].index((distance, turn)) + 1,
            )
            for turn in range(2)
        )
        block = jnp.where(column == 2 - distance, jnp.where(up == 0, first, second), block)
        block = jnp.where(column == 2 + distance, jnp.where(up == 0, second, first), block)
    base = block * (8 * UNIT_ROWS + 2 * Z_ROWS)
    plain = base + (half * 4 + face) * UNIT_ROWS
    paired = base + 8 * UNIT_ROWS + half * Z_ROWS
    none = 5 * (8 * UNIT_ROWS + 2 * Z_ROWS)
    rows[...] = jnp.where(number < 0, none, jnp.where(face < 4, plain, paired))
    last = pltpu.make_async_copy(rows, rows_out, sems.at[len(copies)])
    last.start()

    copies[0].wait()
    live = lax.broadcasted_iota(jnp.int32, (bricks, 512), 0) < counts[0, 0]
    occ = jnp.where(live, occupancy[...], 0).astype(F32)
    spread = jnp.concatenate(
        [jnp.where(same, occ[b : b + 1, :], 0.0) for b in range(bricks)], axis=0
    ).astype(BF16)
    mask = jnp.dot(spread, expand, preferred_element_type=F32)
    mask_out[...] = mask.astype(BF16).reshape(mask_out.shape)
    copies[1].wait()
    value = features[...].astype(F32).reshape(bricks * 64, 512) * mask
    masked_out[...] = value.astype(BF16).reshape(masked_out.shape)
    for q in range(4):
        values[q, 0 : bricks * 64, :] = value[:, q * LANES : (q + 1) * LANES]
    copies[2].wait()
    pack_units(values, send_out, (u0, u1, u2, u3, u4))

    copies[4].wait()
    copies[5].wait()
    shard = weight_t.shape[1]
    lead = shard // LANES * LANES
    count = bias.shape[1]
    shard_out[:, 0:lead] = weight_t[:, 0:lead]
    tile = jnp.concatenate(
        [weight_t[:, lead:shard].astype(F32), jnp.zeros((64, lead + LANES - shard), F32)], axis=1
    )
    offset = shard - lead
    behind = jnp.concatenate(
        [bias[...].astype(F32), jnp.zeros((1, LANES - count), F32)], axis=1
    )
    behind = pltpu.roll(jnp.broadcast_to(behind, (64, LANES)), offset, 1)
    first = lax.broadcasted_iota(jnp.int32, (64, LANES), 0) == 0
    lane = lax.broadcasted_iota(jnp.int32, (64, LANES), 1)
    behind = jnp.where(first & (lane >= offset) & (lane < offset + count), behind, 0.0)
    shard_out[:, lead : lead + LANES] = (tile + behind).astype(BF16)
    last.wait()


def gather_units(table, received):
    at = 0
    for part in received:
        table[at : at + part.shape[0], :] = part[...]
        at += part.shape[0]
    table[at:, :] = jnp.zeros((table.shape[0] - at, LANES), BF16)


def assemble(source, table, rows, windows, sides, walls):
    low8 = low_half((8, LANES))
    sub = lax.broadcasted_iota(jnp.int32, (8, LANES), 0)
    top, bottom = sub == 0, sub == 7

    def put(pair, half, bit, per_brick):
        for e in range(3):
            stacked = [
                jnp.concatenate([per_brick[0][e][i], per_brick[1][e][i]], axis=0)
                for i in range(5)
            ]
            low16 = low_half((16, LANES))
            before = [stacked[4]] + stacked[:3]
            after = stacked[1:4] + [stacked[4]]
            for q in range(4):
                windows[e, q, pair, half, bit, :, 0:LANES] = stacked[q].astype(BF16)
                windows[e, q, pair, half, bit, :, LANES:] = jnp.where(
                    low16, after[q], before[q]
                ).astype(BF16)

    def one_pair(pair, carry):
        def unit(brick, ox, oy, oz):
            return pl.multiple_of(rows[brick, offset_number(ox, oy, oz)], UNIT_ROWS)

        def plane(brick, ox, oy):
            chunks = chunk_rows(table[pl.ds(unit(brick, ox, oy, 0), UNIT_ROWS), :].astype(F32))
            after = table[pl.ds(unit(brick, ox, oy, 1), UNIT_ROWS), :].astype(F32)[0:8]
            before = table[pl.ds(unit(brick, ox, oy, -1), UNIT_ROWS), :].astype(F32)[24:32]
            return chunks + [jnp.where(low8, after, before)]

        for b2 in range(2):
            brick = pair * 2 + b2
            low64 = low_half((64, LANES))
            after = table[pl.ds(unit(brick, 0, 0, 1), Z_ROWS), :].astype(F32)
            before = table[pl.ds(unit(brick, 0, 0, -1), Z_ROWS), :].astype(F32)
            walls[b2] = jnp.where(low64, after, before)
            for side, oy in enumerate((-1, 1)):
                for i, part in enumerate(plane(brick, 0, oy)):
                    sides[b2, side, i] = part

        for ox in (-1, 1):
            per_brick = []
            for b2 in range(2):
                brick = pair * 2 + b2
                centre = plane(brick, ox, 0)
                lower = plane(brick, ox, -1)
                upper = plane(brick, ox, 1)
                per_brick.append(
                    [
                        [
                            pltpu.roll(jnp.where(bottom, l, c), 1, 0)
                            for l, c in zip(lower, centre)
                        ],
                        centre,
                        [
                            pltpu.roll(jnp.where(top, u, c), 7, 0)
                            for u, c in zip(upper, centre)
                        ],
                    ]
                )
            put(pair, 0 if ox < 0 else 4, 0 if ox < 0 else 1, per_brick)

        def two_x(i, carry):
            for bit in range(2):
                x = 2 * i + bit
                per_brick = []
                for b2 in range(2):
                    brick = pair * 2 + b2
                    block = source[brick, i, bit].astype(F32)
                    centre = [block[:, q * LANES : (q + 1) * LANES] for q in range(4)]
                    centre.append(walls[b2, pl.ds(pl.multiple_of(x * 8, 8), 8), :])
                    lower = [
                        jnp.broadcast_to(sides[b2, 0, n, pl.ds(x, 1), :], (8, LANES))
                        for n in range(5)
                    ]
                    upper = [
                        jnp.broadcast_to(sides[b2, 1, n, pl.ds(x, 1), :], (8, LANES))
                        for n in range(5)
                    ]
                    per_brick.append(
                        [
                            [
                                jnp.where(top, l, pltpu.roll(c, 1, 0))
                                for l, c in zip(lower, centre)
                            ],
                            centre,
                            [
                                jnp.where(bottom, u, pltpu.roll(c, 7, 0))
                                for u, c in zip(upper, centre)
                            ],
                        ]
                    )
                put(pair, i + bit, 1 - bit, per_brick)
            return carry

        return lax.fori_loop(0, 4, two_x, carry)

    lax.fori_loop(0, windows.shape[2], one_pair, 0)


def row_block(d, e):
    return slice((3 * d + e) * 256, (3 * d + e + 1) * 256)


def tap_rows(windows, d, e):
    block = windows[e, :, :, d // 2 : d // 2 + 4, d % 2]
    return block.reshape(-1, block.shape[-1])


def all_taps(windows):
    return jnp.concatenate(
        [tap_rows(windows, d, e) for d in range(4) for e in range(3)], axis=1
    )


def chunk_places(bricks):
    return [(2 * pair + b2, i) for pair in range(bricks // 2) for i in range(4) for b2 in range(2)]


def chunk_of(ref, q):
    lanes = slice(q * LANES, (q + 1) * LANES)
    return jnp.concatenate(
        [
            jnp.concatenate([ref[b, i, x, :, lanes].astype(F32) for x in range(2)], axis=1)
            for b, i in chunk_places(ref.shape[0])
        ],
        axis=0,
    )


def put_chunk(ref, q, value):
    for n, (b, i) in enumerate(chunk_places(ref.shape[0])):
        for x in range(2):
            part = value[8 * n : 8 * n + 8, x * LANES : (x + 1) * LANES]
            ref[b, i, x, :, q * LANES : (q + 1) * LANES] = part.astype(ref.dtype)


def weights_kernel(*refs, shard, groups):
    shards = refs[:groups]
    forward_out, backward_out, bias_out, gathered, flat, shifted = refs[groups:]
    me = lax.axis_index("dp")
    for m, part in enumerate(shards):
        gathered[m] = part[...]
    for k in range(groups):
        flat[:, k * shard : (k + 1) * shard] = gathered[me ^ k][:, 0:shard].astype(F32)
    total = groups * shard
    flat[:, total:] = jnp.zeros((64, flat.shape[1] - total), F32)
    shifted[:, :] = pltpu.roll(flat[...], flat.shape[1] - 64, 1)
    low = low_half((64, LANES))
    for e in range(3):
        for x in range(2):
            half = slice(x * LANES, (x + 1) * LANES)
            for out in (forward_out, backward_out):
                out[row_block(3 * (1 - x), e), half] = jnp.zeros((256, LANES), BF16)
    for ae in range(9):
        a, e = ae // 3, ae % 3
        one = taps_pair(flat, shifted, 3 * ae)
        two = jnp.where(low, taps_pair(flat, shifted, 3 * ae + 2), 0.0)
        late = jnp.concatenate([one, two], axis=1)
        band = jnp.transpose(jnp.concatenate([pltpu.roll(late, 192, 1), late], axis=0)).astype(BF16)
        for x in range(2):
            forward_out[row_block(a + x, e), x * LANES : (x + 1) * LANES] = band
    for ae in range(9):
        a, e = ae // 3, ae % 3
        m = 3 * (8 - ae)
        first = taps_pair(flat, shifted, m)
        second = taps_pair(flat, shifted, m + 1)
        third = taps_pair(flat, shifted, m + 2)
        band = jnp.concatenate(
            [
                second,
                first,
                jnp.where(low, 0.0, pltpu.roll(first, 64, 1)),
                jnp.where(low, third, 0.0),
            ],
            axis=0,
        ).astype(BF16)
        for x in range(2):
            backward_out[row_block(a + x, e), x * LANES : (x + 1) * LANES] = band

    lane = lax.broadcasted_iota(jnp.int32, (8, LANES), 1)
    bias_lane = shard % LANES
    bias_tile = shard - bias_lane
    count = 64 // groups
    bias_row = jnp.zeros((8, LANES), F32)
    for k in range(groups):
        tile = gathered[me ^ k][0:16, bias_tile : bias_tile + LANES].astype(F32)[0:8]
        moved = pltpu.roll(tile, (count * k - bias_lane) % LANES, 1)
        bias_row += jnp.where((lane >= count * k) & (lane < count * (k + 1)), moved, 0.0)
    bias_out[...] = bias_row + pltpu.roll(bias_row, 64, 1)


def taps_pair(flat, shifted, first):
    if first % 2 == 0:
        return flat[:, first * 64 : first * 64 + LANES]
    return shifted[:, (first - 1) * 64 : (first - 1) * 64 + LANES]


def forward_kernel(
    masked, mask, cotangent_hbm, toeplitz, bias, rows, send, r0, r1, r2, r3, r4,
    block_out, grad_out, keep_out, give_out, u0, u1, u2, u3, u4,
    table, windows, sides, walls, flat, shifted, values, flipped, cotangent, sem, *, shard,
):
    fetch = pltpu.make_async_copy(cotangent_hbm, cotangent, sem)
    fetch.start()
    groups = 2 * keep_out.shape[0]
    bricks = masked.shape[0]
    pairs = bricks // 2
    gather_units(table, (r0, r1, r2, r3, r4))
    assemble(masked, table, rows, windows, sides, walls)
    bias_lane = shard % LANES
    bias_tile = shard - bias_lane
    bias_row = bias[0:1, :]
    fetch.wait()
    values[:, bricks * 64 :, :] = jnp.zeros((4, 64, LANES), F32)

    bias_row = jnp.concatenate([bias_row, bias_row], axis=1)
    total = jnp.dot(all_taps(windows), toeplitz[...], preferred_element_type=F32)
    rows_of_chunk = total.shape[0] // 4
    bias_sum = jnp.zeros((8, 256), F32)
    for q in range(4):
        p = total[q * rows_of_chunk : (q + 1) * rows_of_chunk] + bias_row
        active = chunk_of(mask, q)
        sig = jax.nn.sigmoid(p)
        put_chunk(block_out, q, p * sig * active)
        grad = (chunk_of(cotangent, q) * sig * (1.0 + p * (1.0 - sig)) * active).astype(BF16)
        wide = grad.astype(F32)
        put_chunk(grad_out, q, wide)
        for n, (brick, i) in enumerate(chunk_places(bricks)):
            for x in range(2):
                at = brick * 64 + (2 * i + x) * 8
                values[q, at : at + 8, :] = wide[
                    8 * n : 8 * n + 8, x * LANES : (x + 1) * LANES
                ]
        flipped[:, q * rows_of_chunk : (q + 1) * rows_of_chunk] = jnp.transpose(wide).astype(BF16)
        bias_sum += jnp.sum(wide.reshape(-1, 8, 256), axis=0)
    bias_sum = bias_sum[:, 0:LANES] + bias_sum[:, LANES:]
    pack_units(values, send, (u0, u1, u2, u3, u4))

    for e in range(3):
        products = [
            jnp.dot(flipped[...], tap_rows(windows, d, e), preferred_element_type=F32)
            for d in range(4)
        ]
        for a in range(3):
            both = products[a][0:LANES] + products[a + 1][LANES:]
            shifted[64 * a : 64 * a + 64, 256 * e : 256 * e + 256] = both[64:] + pltpu.roll(
                both[0:64], 64, 1
            )
    for a in range(3):
        for e in range(3):
            at = 192 * (3 * a + e)
            flat[:, at : at + 256] = shifted[64 * a : 64 * a + 64, 256 * e : 256 * e + 256]

    width = keep_out.shape[2]
    bias_all = jnp.sum(bias_sum, axis=0, keepdims=True)
    bias_all = jnp.broadcast_to(bias_all, (8, LANES))
    bias_all = bias_all + pltpu.roll(bias_all, 64, 1)
    bias_all = pltpu.roll(bias_all, bias_lane, 1)
    row8 = lax.broadcasted_iota(jnp.int32, (8, LANES), 0)
    lane8 = lax.broadcasted_iota(jnp.int32, (8, LANES), 1)
    keep = (row8 == 0) & (lane8 >= bias_lane) & (lane8 < bias_lane + 64)
    me = lax.axis_index("dp")
    for k in range(groups):
        part = flat[:, k * shard : (k + 1) * shard]
        shifted[0:64, 0:shard] = part
        shifted[0:64, shard:width] = jnp.zeros((64, width - shard), F32)
        tile = shifted[0:8, bias_tile : bias_tile + LANES]
        shifted[0:8, bias_tile : bias_tile + LANES] = jnp.where(keep, bias_all, tile)
        block = shifted[0:64, 0:width].astype(BF16)
        for m in range(groups):

            @pl.when(me ^ m == k)
            def _(m=m, block=block):
                (give_out if m % 2 else keep_out)[m // 2] = block


def assemble_kernel(grad, rows, r0, r1, r2, r3, r4, after, windows, table, sides, walls):
    del after
    gather_units(table, (r0, r1, r2, r3, r4))
    assemble(grad, table, rows, windows, sides, walls)


def sum_kernel(*refs, operands, parts):
    total = (refs[0][...].astype(F32) + refs[1][...].astype(F32)).astype(BF16)
    for part in range(parts):
        for row in range(part, total.shape[0], parts):
            refs[operands + part][row // parts] = total[row]


def sum_after(mine, other, after=(), through=(), parts=1):
    operands = 2 + len(after) + len(through)
    share = jax.ShapeDtypeStruct((mine.shape[0] // parts, *mine.shape[1:]), mine.dtype)
    outs = pl.pallas_call(
        functools.partial(sum_kernel, operands=operands, parts=parts),
        name="sum",
        out_shape=[share] * parts + [jax.ShapeDtypeStruct(x.shape, x.dtype) for x in through],
        in_specs=[vmem()] * 2 + [untouched()] * (operands - 2),
        out_specs=[vmem()] * parts + [untouched()] * len(through),
        input_output_aliases={2 + len(after) + i: parts + i for i in range(len(through))},
        compiler_params=pltpu.CompilerParams(vmem_limit_bytes=1024 * 1024),
    )(mine, other, *after, *through)
    return list(outs[:parts]), list(outs[parts:])


def backward_kernel(windows, mask, toeplitz, after, out):
    del after
    total = jnp.dot(all_taps(windows), toeplitz[...], preferred_element_type=F32)
    rows_of_chunk = total.shape[0] // 4
    for q in range(4):
        part = total[q * rows_of_chunk : (q + 1) * rows_of_chunk]
        put_chunk(out, q, part * chunk_of(mask, q))


def finish_kernel(mine, other, weight_out, bias_out):
    shard = weight_out.shape[1]
    count = bias_out.shape[1]
    total = mine[...].astype(F32) + other[...].astype(F32)
    weight_out[...] = total[:, 0:shard]
    bias_lane = shard % LANES
    bias_tile = shard - bias_lane
    tile = total[0:8, bias_tile : bias_tile + LANES]
    me = lax.axis_index("dp")
    moved = pltpu.roll(tile, 2 * LANES - bias_lane - me * count, 1)
    bias_out[...] = moved[0:1, 0:count]


def swapped(block, axis, bit):
    return lax.ppermute(block, axis, [(i, i ^ bit) for i in range(lax.axis_size(axis))])


def by_parity(block, routes):
    groups = lax.axis_size("dp")
    pairs = [
        (source * groups + group, target * groups + group)
        for group in range(groups)
        for source, target in routes[group % 2]
    ]
    return lax.ppermute(block, ("space", "dp"), pairs)


def exchanged(number, unit):
    routes = []
    for swaps in SWAPS:
        distance, turn = swaps[number - 1]
        route = []
        for low in range(lax.axis_size("space") - distance):
            if low // distance % 2 == turn:
                route += [(low, low + distance), (low + distance, low)]
        routes.append(route)
    return by_parity(unit, routes)


def space_steps():
    bits = []
    while 2 ** len(bits) < lax.axis_size("space"):
        bits.append(2 ** len(bits))
    return list(zip(bits, bits[1:] + bits[:1]))


def stepped(total, step):
    devices = range(lax.axis_size("space"))
    return by_parity(total, [[(i, i ^ bit) for i in devices] for bit in step])


def body(features, occupancy, counts, send_units, neighbours, weight, conv_bias, cotangent):
    bricks, edge, _, lanes = features.shape[1:]
    grid_shape = (bricks, edge // 2, 2, edge, lanes)
    pairs = bricks // 2
    spread, links = send_units.shape[2:]
    shard, channels = weight.shape
    groups = lax.axis_size("dp")
    count = conv_bias.shape[0]
    width = -(-(shard + channels) // LANES) * LANES
    unit_rows = 8 * UNIT_ROWS + 2 * Z_ROWS
    units_type = jax.ShapeDtypeStruct((unit_rows, LANES), BF16)
    grid_type = jax.ShapeDtypeStruct(grid_shape, BF16)
    shard_type = jax.ShapeDtypeStruct((channels, width), BF16)
    params = pltpu.CompilerParams(vmem_limit_bytes=48 * 1024 * 1024)
    rows_shape = neighbours.shape[1:]
    send_shape = (spread, 1, links)

    masked, mask, rows, send, own_shard, *units = pl.pallas_call(
        prepare_kernel,
        name="prepare",
        out_shape=[
            grid_type,
            grid_type,
            jax.ShapeDtypeStruct(rows_shape, jnp.int32),
            jax.ShapeDtypeStruct(send_shape, jnp.int32),
            shard_type,
        ]
        + [units_type] * spread,
        in_specs=[pl.BlockSpec(memory_space=pltpu.HBM)] * 6 + [smem()],
        out_specs=[vmem(), vmem(), smem(), smem(), vmem()] + [vmem()] * spread,
        scratch_shapes=[
            pltpu.VMEM((4, (bricks + 1) * 64, LANES), F32),
            pltpu.VMEM(grid_shape, BF16),
            pltpu.VMEM(occupancy.shape[1:], jnp.int32),
            pltpu.VMEM(rows_shape, jnp.int32),
            pltpu.VMEM((channels, shard), BF16),
            pltpu.VMEM((1, count), BF16),
            pltpu.VMEM(rows_shape, jnp.int32),
            pltpu.SemaphoreType.DMA((7,)),
        ],
        compiler_params=params,
    )(
        *(
            pltpu.with_memory_space_constraint(operand, pltpu.HBM)
            for operand in (
                features.reshape(grid_shape),
                occupancy[0],
                send_units.transpose(0, 2, 1, 3).reshape(send_shape),
                neighbours[0],
                weight.T,
                conv_bias.reshape(1, count),
            )
        ),
        counts,
    )

    shards = {0: own_shard}
    bit = groups // 2
    while bit:
        for m in list(shards):
            shards[m | bit] = swapped(shards[m], "dp", bit)
        bit //= 2
    received = units[:1] + [exchanged(number, units[number]) for number in range(1, spread)]

    flat = pltpu.VMEM((channels, 28 * 64), F32)
    band_forward, band_backward, bias = pl.pallas_call(
        functools.partial(weights_kernel, shard=shard, groups=groups),
        name="weights",
        out_shape=[
            jax.ShapeDtypeStruct((12 * 256, 256), BF16),
            jax.ShapeDtypeStruct((12 * 256, 256), BF16),
            jax.ShapeDtypeStruct((8, LANES), F32),
        ],
        in_specs=[vmem()] * groups,
        out_specs=[vmem()] * 3,
        scratch_shapes=[pltpu.VMEM((groups, channels, width), BF16), flat, flat],
        compiler_params=params,
    )(*(shards[m] for m in range(groups)))

    table = pltpu.VMEM((spread * unit_rows + Z_ROWS, LANES), BF16)
    windows = pltpu.VMEM((3, 4, pairs, 5, 2, 16, 256), BF16)
    sides = pltpu.VMEM((2, 2, 5, 8, LANES), F32)
    walls = pltpu.VMEM((2, 64, LANES), F32)
    half_type = jax.ShapeDtypeStruct((groups // 2, channels, width), BF16)
    block_output, grad, keep, give, *grad_units = pl.pallas_call(
        functools.partial(forward_kernel, shard=shard),
        name="forward",
        out_shape=[grid_type, grid_type, half_type, half_type] + [units_type] * spread,
        in_specs=[vmem(), vmem(), pl.BlockSpec(memory_space=pltpu.HBM), vmem(), vmem()]
        + [smem(), smem()]
        + [vmem()] * spread,
        out_specs=[vmem()] * (4 + spread),
        scratch_shapes=[
            table,
            windows,
            sides,
            walls,
            flat,
            pltpu.VMEM((192, 3 * 256), F32),
            pltpu.VMEM((4, (bricks + 1) * 64, LANES), F32),
            pltpu.VMEM((256, bricks * LANES), BF16),
            pltpu.VMEM(grid_shape, BF16),
            pltpu.SemaphoreType.DMA,
        ],
        compiler_params=params,
    )(
        masked,
        mask,
        pltpu.with_memory_space_constraint(cotangent.reshape(grid_shape), pltpu.HBM),
        band_forward,
        bias,
        rows,
        send,
        *received,
    )

    later = grad_units[2:]
    bit = 1
    while 2 * bit < groups:
        first = later[:1] if bit == 1 else []
        (keep, give), first = sum_after(keep, swapped(give, "dp", bit), through=first, parts=2)
        later = first + later[1:] if bit == 1 else later
        bit *= 2
    grad_received = [grad_units[0], exchanged(1, grad_units[1])]
    (total,), last = sum_after(keep, swapped(give, "dp", bit), grad_received[1:], later[1:])
    for number, unit in enumerate([later[0], *last], 2):
        grad_received.append(exchanged(number, unit))

    steps = space_steps()
    other = stepped(total, steps[0])
    if len(steps) > 1:
        (total,), _ = sum_after(total, other, grad_received[3:4])
        other = stepped(total, steps[1])

    padded_grad = pl.pallas_call(
        assemble_kernel,
        name="assemble",
        out_shape=jax.ShapeDtypeStruct(windows.shape, BF16),
        in_specs=[vmem()] + [smem()] + [vmem()] * spread + [untouched()],
        out_specs=vmem(),
        scratch_shapes=[table, sides, walls],
        compiler_params=params,
    )(grad, rows, *grad_received, total)

    for number, step in enumerate(steps[2:]):
        (total,), _ = sum_after(total, other, [] if number else [padded_grad])
        other = stepped(total, step)

    grad_input = pl.pallas_call(
        backward_kernel,
        name="backward",
        out_shape=grid_type,
        in_specs=[vmem()] * 3 + [untouched()],
        out_specs=vmem(),
        compiler_params=params,
    )(padded_grad, mask, band_backward, total)

    weight_share, bias_share = pl.pallas_call(
        finish_kernel,
        name="finish",
        out_shape=[
            jax.ShapeDtypeStruct((channels, shard), F32),
            jax.ShapeDtypeStruct((1, count), F32),
        ],
        in_specs=[vmem()] * 2,
        out_specs=[vmem()] * 2,
        compiler_params=params,
    )(total[0], other[0])
    return (
        block_output.reshape(features.shape),
        grad_input.reshape(features.shape),
        weight_share.T,
        bias_share.reshape(count),
    )


def solution(mesh):
    placed = (
        P("dp", "space", None, None, None),
        P("dp", "space", None),
        P("dp", "space"),
        P("dp", "space", None, None),
        P("dp", "space", None),
        P("dp", None),
        P("dp"),
        P("dp", "space", None, None, None),
    )
    return jax.shard_map(
        body,
        mesh=mesh,
        in_specs=placed,
        out_specs=(
            P("dp", "space", None, None, None),
            P("dp", "space", None, None, None),
            P("dp", None),
            P("dp"),
        ),
        check_vma=False,
    )
```

```python
import functools

import jax
import jax.numpy as jnp
from jax import lax
from jax.experimental import pallas as pl
from jax.experimental.pallas import tpu as pltpu
from jax.sharding import PartitionSpec as P

F32 = jnp.float32
BF16 = jnp.bfloat16
LANES = 128
BIAS_LANE = 96
UNIT_ROWS = 32
Z_ROWS = 64
SWAPS = (
    ((1, 1), (2, 1), (1, 0), (2, 0)),
    ((2, 1), (1, 1), (2, 0), (1, 0)),
)


def vmem():
    return pl.BlockSpec(memory_space=pltpu.VMEM)


def smem():
    return pl.BlockSpec(memory_space=pltpu.SMEM)


def untouched():
    return pl.BlockSpec(memory_space=pl.ANY)


def offset_number(ox, oy, oz):
    flat = (ox + 1) * 9 + (oy + 1) * 3 + (oz + 1)
    return flat if flat < 13 else flat - 1


def low_half(shape):
    return lax.broadcasted_iota(jnp.int32, shape, len(shape) - 1) % LANES < 64


def chunk_rows(block):
    return [block[8 * q : 8 * q + 8] for q in range(4)]


def upward(device, distance):
    return lax.rem(lax.div(device, distance), 2)


def pack_units(values, send, outs):
    slots = values.shape[1] // 64 - 1
    reach = len(outs) // 2
    low = low_half((64, LANES))
    device = lax.axis_index("space")
    odd = lax.rem(lax.axis_index("dp"), 2)
    for number, out in enumerate(outs):
        column = reach
        if number > 0:
            columns = []
            for distance, turn in (SWAPS[0][number - 1], SWAPS[1][number - 1]):
                up = upward(device, distance) == turn
                columns.append(jnp.where(up, reach + distance, reach - distance))
            column = jnp.where(odd == 0, columns[0], columns[1])

        def base(link):
            unit = send[column, 0, link]
            slot = jnp.where(unit < 0, slots, (unit * 43) >> 8)
            return pl.multiple_of(slot * 64, 64)

        for half in range(2):
            for face in range(4):
                start = base(half * 6 + face)
                if face < 2:
                    where = pl.ds(start + 56 * face, 8)
                else:
                    where = pl.ds(start + 7 * (face - 2), 8, stride=8)
                packed = jnp.concatenate([values[q, where, :] for q in range(4)], axis=0)
                at = (half * 4 + face) * UNIT_ROWS
                out[at : at + UNIT_ROWS, :] = packed.astype(BF16)
            first = values[0, pl.ds(base(half * 6 + 4), 64), :]
            last = values[3, pl.ds(base(half * 6 + 5), 64), :]
            at = 8 * UNIT_ROWS + half * Z_ROWS
            out[at : at + Z_ROWS, :] = jnp.where(low, first, last).astype(BF16)


def prepare_kernel(
    features_hbm, occupancy_hbm, send_hbm, listing_hbm, weight_hbm, bias_hbm, counts,
    masked_out, mask_out, rows_out, send_out, shard_out, u0, u1, u2, u3, u4,
    values, features, occupancy, listing, weight_t, bias, rows, sems,
):
    copies = [
        pltpu.make_async_copy(src, dst, sems.at[i])
        for i, (src, dst) in enumerate(
            (
                (occupancy_hbm, occupancy),
                (features_hbm, features),
                (send_hbm, send_out),
                (listing_hbm, listing),
                (weight_hbm, weight_t),
                (bias_hbm, bias),
            )
        )
    ]
    for copy in copies:
        copy.start()
    bricks = features.shape[0]
    values[:, bricks * 64 :, :] = jnp.zeros((4, 64, LANES), F32)
    row = lax.broadcasted_iota(jnp.int32, (64, 512), 0)
    col = lax.broadcasted_iota(jnp.int32, (64, 512), 1)
    same = (col >> 3) == row
    z_row = lax.broadcasted_iota(jnp.int32, (512, 512), 0) & 7
    z_col = lax.broadcasted_iota(jnp.int32, (512, 512), 1) >> 6
    expand = jnp.where(z_row == z_col, 1.0, 0.0).astype(BF16)

    copies[3].wait()
    device = lax.axis_index("space")
    number = listing[...]
    column = (number * 43) >> 9
    link = number - column * 12
    half = (link >= 6).astype(jnp.int32)
    face = link - 6 * half
    block = jnp.zeros(number.shape, jnp.int32)
    odd = lax.rem(lax.axis_index("dp"), 2)
    for distance in (1, 2):
        up = upward(device, distance)
        first, second = (
            jnp.where(
                odd == 0,
                SWAPS[0].index((distance, turn)) + 1,
                SWAPS[1].index((distance, turn)) + 1,
            )
            for turn in range(2)
        )
        block = jnp.where(column == 2 - distance, jnp.where(up == 0, first, second), block)
        block = jnp.where(column == 2 + distance, jnp.where(up == 0, second, first), block)
    base = block * (8 * UNIT_ROWS + 2 * Z_ROWS)
    plain = base + (half * 4 + face) * UNIT_ROWS
    paired = base + 8 * UNIT_ROWS + half * Z_ROWS
    none = 5 * (8 * UNIT_ROWS + 2 * Z_ROWS)
    rows[...] = jnp.where(number < 0, none, jnp.where(face < 4, plain, paired))
    last = pltpu.make_async_copy(rows, rows_out, sems.at[len(copies)])
    last.start()

    copies[0].wait()
    live = lax.broadcasted_iota(jnp.int32, (bricks, 512), 0) < counts[0, 0]
    occ = jnp.where(live, occupancy[...], 0).astype(F32)
    spread = jnp.concatenate(
        [jnp.where(same, occ[b : b + 1, :], 0.0) for b in range(bricks)], axis=0
    ).astype(BF16)
    mask = jnp.dot(spread, expand, preferred_element_type=F32)
    mask_out[...] = mask.astype(BF16).reshape(mask_out.shape)
    copies[1].wait()
    value = features[...].astype(F32).reshape(bricks * 64, 512) * mask
    masked_out[...] = value.astype(BF16).reshape(masked_out.shape)
    for q in range(4):
        values[q, 0 : bricks * 64, :] = value[:, q * LANES : (q + 1) * LANES]
    copies[2].wait()
    pack_units(values, send_out, (u0, u1, u2, u3, u4))

    copies[4].wait()
    copies[5].wait()
    shard = weight_t.shape[1]
    lead = shard // LANES * LANES
    count = bias.shape[1]
    tail = jnp.concatenate(
        [weight_t[:, lead:shard].astype(F32), jnp.zeros((64, lead + LANES - shard), F32)], axis=1
    )
    behind = jnp.concatenate(
        [bias[...].astype(F32), jnp.zeros((1, LANES - count), F32)], axis=1
    )
    behind = pltpu.roll(jnp.broadcast_to(behind, (32, LANES)), BIAS_LANE, 1)
    packed = pack_shard(weight_t[:, 0:lead].astype(F32), (tail, shard - lead), behind, 0.0)
    shard_out[...] = packed.astype(BF16)
    last.wait()


def pack_shard(block, rest, bias_low, bias_high):
    tail, count = rest
    tiles = [block[:, i : i + LANES] for i in range(0, block.shape[1], LANES)]
    beside = tail[0:32] + pltpu.roll(tail[32:64], count, 1)
    row = lax.broadcasted_iota(jnp.int32, (32, LANES), 0)
    lane = lax.broadcasted_iota(jnp.int32, (32, LANES), 1)
    behind = jnp.where(row == 0, bias_low, bias_high)
    beside = jnp.where((lane >= BIAS_LANE) & (row < 2), behind, beside)
    return jnp.concatenate(tiles + [beside], axis=0)


def unpack_shard(rows, shard):
    lead = shard // LANES
    tiles = [rows[64 * i : 64 * i + 64] for i in range(lead)]
    beside = rows[64 * lead :]
    count = shard - lead * LANES
    tail = jnp.concatenate([beside, pltpu.roll(beside, LANES - count, 1)], axis=0)
    return jnp.concatenate(tiles + [tail[:, 0:count]], axis=1)


def unpack_bias(rows):
    edge = rows[rows.shape[0] - 32 : rows.shape[0] - 24]
    lane = lax.broadcasted_iota(jnp.int32, (1, LANES), 1)
    low = pltpu.roll(edge, LANES - BIAS_LANE, 1)[0:1]
    high = pltpu.roll(edge, 2 * (LANES - BIAS_LANE), 1)[1:2]
    return jnp.where(lane < 32, low, jnp.where(lane < 64, high, 0.0))


def gather_units(table, received):
    at = 0
    for part in received:
        table[at : at + part.shape[0], :] = part[...]
        at += part.shape[0]
    table[at:, :] = jnp.zeros((table.shape[0] - at, LANES), BF16)


def assemble(source, table, rows, windows, sides, walls):
    low8 = low_half((8, LANES))
    sub = lax.broadcasted_iota(jnp.int32, (8, LANES), 0)
    top, bottom = sub == 0, sub == 7

    def put(pair, half, bit, per_brick):
        for e in range(3):
            stacked = [
                jnp.concatenate([per_brick[0][e][i], per_brick[1][e][i]], axis=0)
                for i in range(5)
            ]
            low16 = low_half((16, LANES))
            before = [stacked[4]] + stacked[:3]
            after = stacked[1:4] + [stacked[4]]
            for q in range(4):
                windows[e, q, pair, half, bit, :, 0:LANES] = stacked[q].astype(BF16)
                windows[e, q, pair, half, bit, :, LANES:] = jnp.where(
                    low16, after[q], before[q]
                ).astype(BF16)

    def one_pair(pair, carry):
        def unit(brick, ox, oy, oz):
            return pl.multiple_of(rows[brick, offset_number(ox, oy, oz)], UNIT_ROWS)

        def plane(brick, ox, oy):
            chunks = chunk_rows(table[pl.ds(unit(brick, ox, oy, 0), UNIT_ROWS), :].astype(F32))
            after = table[pl.ds(unit(brick, ox, oy, 1), UNIT_ROWS), :].astype(F32)[0:8]
            before = table[pl.ds(unit(brick, ox, oy, -1), UNIT_ROWS), :].astype(F32)[24:32]
            return chunks + [jnp.where(low8, after, before)]

        for b2 in range(2):
            brick = pair * 2 + b2
            low64 = low_half((64, LANES))
            after = table[pl.ds(unit(brick, 0, 0, 1), Z_ROWS), :].astype(F32)
            before = table[pl.ds(unit(brick, 0, 0, -1), Z_ROWS), :].astype(F32)
            walls[b2] = jnp.where(low64, after, before)
            for side, oy in enumerate((-1, 1)):
                for i, part in enumerate(plane(brick, 0, oy)):
                    sides[b2, side, i] = part

        for ox in (-1, 1):
            per_brick = []
            for b2 in range(2):
                brick = pair * 2 + b2
                centre = plane(brick, ox, 0)
                lower = plane(brick, ox, -1)
                upper = plane(brick, ox, 1)
                per_brick.append(
                    [
                        [
                            pltpu.roll(jnp.where(bottom, l, c), 1, 0)
                            for l, c in zip(lower, centre)
                        ],
                        centre,
                        [
                            pltpu.roll(jnp.where(top, u, c), 7, 0)
                            for u, c in zip(upper, centre)
                        ],
                    ]
                )
            put(pair, 0 if ox < 0 else 4, 0 if ox < 0 else 1, per_brick)

        def two_x(i, carry):
            for bit in range(2):
                x = 2 * i + bit
                per_brick = []
                for b2 in range(2):
                    brick = pair * 2 + b2
                    block = source[brick, i, bit].astype(F32)
                    centre = [block[:, q * LANES : (q + 1) * LANES] for q in range(4)]
                    centre.append(walls[b2, pl.ds(pl.multiple_of(x * 8, 8), 8), :])
                    lower = [
                        jnp.broadcast_to(sides[b2, 0, n, pl.ds(x, 1), :], (8, LANES))
                        for n in range(5)
                    ]
                    upper = [
                        jnp.broadcast_to(sides[b2, 1, n, pl.ds(x, 1), :], (8, LANES))
                        for n in range(5)
                    ]
                    per_brick.append(
                        [
                            [
                                jnp.where(top, l, pltpu.roll(c, 1, 0))
                                for l, c in zip(lower, centre)
                            ],
                            centre,
                            [
                                jnp.where(bottom, u, pltpu.roll(c, 7, 0))
                                for u, c in zip(upper, centre)
                            ],
                        ]
                    )
                put(pair, i + bit, 1 - bit, per_brick)
            return carry

        return lax.fori_loop(0, 4, two_x, carry)

    lax.fori_loop(0, windows.shape[2], one_pair, 0)


def row_block(d, e):
    return slice((3 * d + e) * 256, (3 * d + e + 1) * 256)


def tap_rows(windows, d, e):
    block = windows[e, :, :, d // 2 : d // 2 + 4, d % 2]
    return block.reshape(-1, block.shape[-1])


def all_taps(windows):
    return jnp.concatenate(
        [tap_rows(windows, d, e) for d in range(4) for e in range(3)], axis=1
    )


def chunk_places(bricks):
    return [(2 * pair + b2, i) for pair in range(bricks // 2) for i in range(4) for b2 in range(2)]


def chunk_of(ref, q):
    lanes = slice(q * LANES, (q + 1) * LANES)
    return jnp.concatenate(
        [
            jnp.concatenate([ref[b, i, x, :, lanes].astype(F32) for x in range(2)], axis=1)
            for b, i in chunk_places(ref.shape[0])
        ],
        axis=0,
    )


def put_chunk(ref, q, value):
    for n, (b, i) in enumerate(chunk_places(ref.shape[0])):
        for x in range(2):
            part = value[8 * n : 8 * n + 8, x * LANES : (x + 1) * LANES]
            ref[b, i, x, :, q * LANES : (q + 1) * LANES] = part.astype(ref.dtype)


def weights_kernel(*refs, shard, groups):
    shards = refs[:groups]
    forward_out, backward_out, bias_out, gathered, flat, shifted = refs[groups:]
    me = lax.axis_index("dp")
    for m, part in enumerate(shards):
        gathered[m] = part[...]
    for k in range(groups):
        rows = gathered[me ^ k].astype(F32)
        flat[:, k * shard : (k + 1) * shard] = unpack_shard(rows, shard)
    total = groups * shard
    flat[:, total:] = jnp.zeros((64, flat.shape[1] - total), F32)
    shifted[:, :] = pltpu.roll(flat[...], flat.shape[1] - 64, 1)
    low = low_half((64, LANES))
    for e in range(3):
        for x in range(2):
            half = slice(x * LANES, (x + 1) * LANES)
            for out in (forward_out, backward_out):
                out[row_block(3 * (1 - x), e), half] = jnp.zeros((256, LANES), BF16)
    for ae in range(9):
        a, e = ae // 3, ae % 3
        one = taps_pair(flat, shifted, 3 * ae)
        two = jnp.where(low, taps_pair(flat, shifted, 3 * ae + 2), 0.0)
        late = jnp.concatenate([one, two], axis=1)
        band = jnp.transpose(jnp.concatenate([pltpu.roll(late, 192, 1), late], axis=0)).astype(BF16)
        for x in range(2):
            forward_out[row_block(a + x, e), x * LANES : (x + 1) * LANES] = band
    for ae in range(9):
        a, e = ae // 3, ae % 3
        m = 3 * (8 - ae)
        first = taps_pair(flat, shifted, m)
        second = taps_pair(flat, shifted, m + 1)
        third = taps_pair(flat, shifted, m + 2)
        band = jnp.concatenate(
            [
                second,
                first,
                jnp.where(low, 0.0, pltpu.roll(first, 64, 1)),
                jnp.where(low, third, 0.0),
            ],
            axis=0,
        ).astype(BF16)
        for x in range(2):
            backward_out[row_block(a + x, e), x * LANES : (x + 1) * LANES] = band

    lane = lax.broadcasted_iota(jnp.int32, (8, LANES), 1)
    count = 64 // groups
    bias_row = jnp.zeros((8, LANES), F32)
    for k in range(groups):
        row = unpack_bias(gathered[me ^ k].astype(F32))
        moved = pltpu.roll(jnp.broadcast_to(row, (8, LANES)), count * k, 1)
        bias_row += jnp.where((lane >= count * k) & (lane < count * (k + 1)), moved, 0.0)
    bias_out[...] = bias_row + pltpu.roll(bias_row, 64, 1)


def taps_pair(flat, shifted, first):
    if first % 2 == 0:
        return flat[:, first * 64 : first * 64 + LANES]
    return shifted[:, (first - 1) * 64 : (first - 1) * 64 + LANES]


def forward_kernel(
    masked, mask, cotangent_hbm, toeplitz, bias, rows, send, r0, r1, r2, r3, r4,
    block_out, grad_out, keep_out, give_out, u0, u1, u2, u3, u4,
    table, windows, sides, walls, flat, shifted, values, flipped, cotangent, product, sem,
    *, shard,
):
    fetch = pltpu.make_async_copy(cotangent_hbm, cotangent, sem)
    fetch.start()
    groups = 2 * keep_out.shape[0]
    bricks = masked.shape[0]
    pairs = bricks // 2
    gather_units(table, (r0, r1, r2, r3, r4))
    assemble(masked, table, rows, windows, sides, walls)
    bias_row = bias[0:1, :]
    fetch.wait()
    values[:, bricks * 64 :, :] = jnp.zeros((4, 64, LANES), F32)

    bias_row = jnp.concatenate([bias_row, bias_row], axis=1)
    product[...] = jnp.dot(all_taps(windows), toeplitz[...], preferred_element_type=F32)
    rows_of_chunk = product.shape[0] // 4

    def one_chunk(q, bias_sum):
        lanes = pl.ds(pl.multiple_of(q * LANES, LANES), LANES)
        for pair in range(pairs):
            for i in range(4):
                at = pl.multiple_of(q * rows_of_chunk + (pair * 4 + i) * 16, 16)
                p = product[pl.ds(at, 16), :] + bias_row

                def both(ref, i=i, pair=pair):
                    return jnp.concatenate(
                        [
                            jnp.concatenate(
                                [ref[2 * pair + b, i, x, :, lanes].astype(F32) for b in range(2)],
                                axis=0,
                            )
                            for x in range(2)
                        ],
                        axis=1,
                    )

                active = both(mask)
                sig = jax.nn.sigmoid(p)
                out = p * sig * active
                grad = both(cotangent) * sig * (1.0 + p * (1.0 - sig)) * active
                wide = grad.astype(BF16).astype(F32)
                product[pl.ds(at, 16), :] = wide
                bias_sum += wide[0:8] + wide[8:16]
                for b in range(2):
                    brick = 2 * pair + b
                    for x in range(2):
                        rows_, half = slice(8 * b, 8 * b + 8), slice(x * LANES, (x + 1) * LANES)
                        block_out[brick, i, x, :, lanes] = out[rows_, half].astype(BF16)
                        grad_out[brick, i, x, :, lanes] = wide[rows_, half].astype(BF16)
                        to = brick * 64 + (2 * i + x) * 8
                        values[q, to : to + 8, :] = wide[rows_, half]
        return bias_sum

    bias_sum = lax.fori_loop(0, 4, one_chunk, jnp.zeros((8, 256), F32))
    bias_sum = bias_sum[:, 0:LANES] + bias_sum[:, LANES:]
    pack_units(values, send, (u0, u1, u2, u3, u4))
    for q in range(4):
        rows_of_q = slice(q * rows_of_chunk, (q + 1) * rows_of_chunk)
        flipped[:, rows_of_q] = jnp.transpose(product[rows_of_q, :]).astype(BF16)

    for e in range(3):
        upper = None
        for d in range(4):
            terms = jnp.dot(flipped[...], tap_rows(windows, d, e), preferred_element_type=F32)
            if d > 0:
                both = upper + terms[LANES:]
                shifted[64 * d - 64 : 64 * d, 256 * e : 256 * e + 256] = both[64:] + pltpu.roll(
                    both[0:64], 64, 1
                )
            upper = terms[0:LANES]
    for a in range(3):
        for e in range(3):
            at = 192 * (3 * a + e)
            flat[:, at : at + 256] = shifted[64 * a : 64 * a + 64, 256 * e : 256 * e + 256]

    bias_all = jnp.sum(bias_sum, axis=0, keepdims=True)
    bias_all = jnp.broadcast_to(bias_all, (32, LANES))
    bias_all = bias_all + pltpu.roll(bias_all, 64, 1)
    bias_low = pltpu.roll(bias_all, BIAS_LANE, 1)
    bias_high = pltpu.roll(bias_all, BIAS_LANE - 32, 1)
    lead = shard // LANES * LANES
    me = lax.axis_index("dp")
    for k in range(groups):
        shifted[0:64, 0:shard] = flat[:, k * shard : (k + 1) * shard]
        shifted[0:64, shard : lead + LANES] = jnp.zeros((64, lead + LANES - shard), F32)
        tail = (shifted[0:64, lead : lead + LANES], shard - lead)
        block = pack_shard(shifted[0:64, 0:lead], tail, bias_low, bias_high).astype(BF16)
        for m in range(groups):

            @pl.when(me ^ m == k)
            def _(m=m, block=block):
                (give_out if m % 2 else keep_out)[m // 2] = block


def assemble_kernel(grad, rows, r0, r1, r2, r3, r4, after, windows, table, sides, walls):
    del after
    gather_units(table, (r0, r1, r2, r3, r4))
    assemble(grad, table, rows, windows, sides, walls)


def sum_kernel(*refs, operands, parts):
    total = (refs[0][...].astype(F32) + refs[1][...].astype(F32)).astype(BF16)
    for part in range(parts):
        for row in range(part, total.shape[0], parts):
            refs[operands + part][row // parts] = total[row]


def sum_after(mine, other, after=(), through=(), parts=1):
    operands = 2 + len(after) + len(through)
    share = jax.ShapeDtypeStruct((mine.shape[0] // parts, *mine.shape[1:]), mine.dtype)
    outs = pl.pallas_call(
        functools.partial(sum_kernel, operands=operands, parts=parts),
        name="sum",
        out_shape=[share] * parts + [jax.ShapeDtypeStruct(x.shape, x.dtype) for x in through],
        in_specs=[vmem()] * 2 + [untouched()] * (operands - 2),
        out_specs=[vmem()] * parts + [untouched()] * len(through),
        input_output_aliases={2 + len(after) + i: parts + i for i in range(len(through))},
        compiler_params=pltpu.CompilerParams(vmem_limit_bytes=1024 * 1024),
    )(mine, other, *after, *through)
    return list(outs[:parts]), list(outs[parts:])


def backward_kernel(windows, mask, toeplitz, after, out):
    del after
    total = jnp.dot(all_taps(windows), toeplitz[...], preferred_element_type=F32)
    rows_of_chunk = total.shape[0] // 4
    for q in range(4):
        part = total[q * rows_of_chunk : (q + 1) * rows_of_chunk]
        put_chunk(out, q, part * chunk_of(mask, q))


def finish_kernel(mine, other, weight_out, bias_out):
    total = mine[...].astype(F32) + other[...].astype(F32)
    weight_out[...] = unpack_shard(total, weight_out.shape[1])
    count = bias_out.shape[1]
    row = jnp.broadcast_to(unpack_bias(total), (8, LANES))
    bias_out[...] = pltpu.roll(row, LANES - lax.axis_index("dp") * count, 1)[0:1, 0:count]


def swapped(block, axis, bit):
    return lax.ppermute(block, axis, [(i, i ^ bit) for i in range(lax.axis_size(axis))])


def by_parity(block, routes):
    groups = lax.axis_size("dp")
    pairs = [
        (source * groups + group, target * groups + group)
        for group in range(groups)
        for source, target in routes[group % 2]
    ]
    return lax.ppermute(block, ("space", "dp"), pairs)


def exchanged(number, unit):
    routes = []
    for swaps in SWAPS:
        distance, turn = swaps[number - 1]
        route = []
        for low in range(lax.axis_size("space") - distance):
            if low // distance % 2 == turn:
                route += [(low, low + distance), (low + distance, low)]
        routes.append(route)
    return by_parity(unit, routes)


def space_steps():
    bits = []
    while 2 ** len(bits) < lax.axis_size("space"):
        bits.append(2 ** len(bits))
    return list(zip(bits, bits[1:] + bits[:1]))


def stepped(total, step):
    devices = range(lax.axis_size("space"))
    return by_parity(total, [[(i, i ^ bit) for i in devices] for bit in step])


def body(features, occupancy, counts, send_units, neighbours, weight, conv_bias, cotangent):
    bricks, edge, _, lanes = features.shape[1:]
    grid_shape = (bricks, edge // 2, 2, edge, lanes)
    pairs = bricks // 2
    spread, links = send_units.shape[2:]
    shard, channels = weight.shape
    groups = lax.axis_size("dp")
    count = conv_bias.shape[0]
    shard_rows = channels * (shard // LANES) + channels // 2
    unit_rows = 8 * UNIT_ROWS + 2 * Z_ROWS
    units_type = jax.ShapeDtypeStruct((unit_rows, LANES), BF16)
    grid_type = jax.ShapeDtypeStruct(grid_shape, BF16)
    shard_type = jax.ShapeDtypeStruct((shard_rows, LANES), BF16)
    params = pltpu.CompilerParams(vmem_limit_bytes=48 * 1024 * 1024)
    rows_shape = neighbours.shape[1:]
    send_shape = (spread, 1, links)

    masked, mask, rows, send, own_shard, *units = pl.pallas_call(
        prepare_kernel,
        name="prepare",
        out_shape=[
            grid_type,
            grid_type,
            jax.ShapeDtypeStruct(rows_shape, jnp.int32),
            jax.ShapeDtypeStruct(send_shape, jnp.int32),
            shard_type,
        ]
        + [units_type] * spread,
        in_specs=[pl.BlockSpec(memory_space=pltpu.HBM)] * 6 + [smem()],
        out_specs=[vmem(), vmem(), smem(), smem(), vmem()] + [vmem()] * spread,
        scratch_shapes=[
            pltpu.VMEM((4, (bricks + 1) * 64, LANES), F32),
            pltpu.VMEM(grid_shape, BF16),
            pltpu.VMEM(occupancy.shape[1:], jnp.int32),
            pltpu.VMEM(rows_shape, jnp.int32),
            pltpu.VMEM((channels, shard), BF16),
            pltpu.VMEM((1, count), BF16),
            pltpu.VMEM(rows_shape, jnp.int32),
            pltpu.SemaphoreType.DMA((7,)),
        ],
        compiler_params=params,
    )(
        *(
            pltpu.with_memory_space_constraint(operand, pltpu.HBM)
            for operand in (
                features.reshape(grid_shape),
                occupancy[0],
                send_units.transpose(0, 2, 1, 3).reshape(send_shape),
                neighbours[0],
                weight.T,
                conv_bias.reshape(1, count),
            )
        ),
        counts,
    )

    shards = {0: own_shard}
    bit = groups // 2
    while bit:
        for m in list(shards):
            shards[m | bit] = swapped(shards[m], "dp", bit)
        bit //= 2
    received = units[:1] + [exchanged(number, units[number]) for number in range(1, spread)]

    flat = pltpu.VMEM((channels, 28 * 64), F32)
    band_forward, band_backward, bias = pl.pallas_call(
        functools.partial(weights_kernel, shard=shard, groups=groups),
        name="weights",
        out_shape=[
            jax.ShapeDtypeStruct((12 * 256, 256), BF16),
            jax.ShapeDtypeStruct((12 * 256, 256), BF16),
            jax.ShapeDtypeStruct((8, LANES), F32),
        ],
        in_specs=[vmem()] * groups,
        out_specs=[vmem()] * 3,
        scratch_shapes=[pltpu.VMEM((groups, shard_rows, LANES), BF16), flat, flat],
        compiler_params=params,
    )(*(shards[m] for m in range(groups)))

    table = pltpu.VMEM((spread * unit_rows + Z_ROWS, LANES), BF16)
    windows = pltpu.VMEM((3, 4, pairs, 5, 2, 16, 256), BF16)
    sides = pltpu.VMEM((2, 2, 5, 8, LANES), F32)
    walls = pltpu.VMEM((2, 64, LANES), F32)
    half_type = jax.ShapeDtypeStruct((groups // 2, shard_rows, LANES), BF16)
    block_output, grad, keep, give, *grad_units = pl.pallas_call(
        functools.partial(forward_kernel, shard=shard),
        name="forward",
        out_shape=[grid_type, grid_type, half_type, half_type] + [units_type] * spread,
        in_specs=[vmem(), vmem(), pl.BlockSpec(memory_space=pltpu.HBM), vmem(), vmem()]
        + [smem(), smem()]
        + [vmem()] * spread,
        out_specs=[vmem()] * (4 + spread),
        scratch_shapes=[
            table,
            windows,
            sides,
            walls,
            flat,
            pltpu.VMEM((192, 3 * 256), F32),
            pltpu.VMEM((4, (bricks + 1) * 64, LANES), F32),
            pltpu.VMEM((256, bricks * LANES), BF16),
            pltpu.VMEM(grid_shape, BF16),
            pltpu.VMEM((bricks * LANES, 256), F32),
            pltpu.SemaphoreType.DMA,
        ],
        compiler_params=params,
    )(
        masked,
        mask,
        pltpu.with_memory_space_constraint(cotangent.reshape(grid_shape), pltpu.HBM),
        band_forward,
        bias,
        rows,
        send,
        *received,
    )

    later = grad_units[2:]
    bit = 1
    while 2 * bit < groups:
        first = later[:1] if bit == 1 else []
        (keep, give), first = sum_after(keep, swapped(give, "dp", bit), through=first, parts=2)
        later = first + later[1:] if bit == 1 else later
        bit *= 2
    grad_received = [grad_units[0], exchanged(1, grad_units[1])]
    (total,), last = sum_after(keep, swapped(give, "dp", bit), grad_received[1:], later[1:])
    for number, unit in enumerate([later[0], *last], 2):
        grad_received.append(exchanged(number, unit))

    steps = space_steps()
    other = stepped(total, steps[0])
    if len(steps) > 1:
        (total,), _ = sum_after(total, other, grad_received[3:4])
        other = stepped(total, steps[1])

    padded_grad = pl.pallas_call(
        assemble_kernel,
        name="assemble",
        out_shape=jax.ShapeDtypeStruct(windows.shape, BF16),
        in_specs=[vmem()] + [smem()] + [vmem()] * spread + [untouched()],
        out_specs=vmem(),
        scratch_shapes=[table, sides, walls],
        compiler_params=params,
    )(grad, rows, *grad_received, total)

    for number, step in enumerate(steps[2:]):
        (total,), _ = sum_after(total, other, [] if number else [padded_grad])
        other = stepped(total, step)

    grad_input = pl.pallas_call(
        backward_kernel,
        name="backward",
        out_shape=grid_type,
        in_specs=[vmem()] * 3 + [untouched()],
        out_specs=vmem(),
        compiler_params=params,
    )(padded_grad, mask, band_backward, total)

    weight_share, bias_share = pl.pallas_call(
        finish_kernel,
        name="finish",
        out_shape=[
            jax.ShapeDtypeStruct((channels, shard), F32),
            jax.ShapeDtypeStruct((1, count), F32),
        ],
        in_specs=[vmem()] * 2,
        out_specs=[vmem()] * 2,
        compiler_params=params,
    )(total[0], other[0])
    return (
        block_output.reshape(features.shape),
        grad_input.reshape(features.shape),
        weight_share.T,
        bias_share.reshape(count),
    )


def solution(mesh):
    placed = (
        P("dp", "space", None, None, None),
        P("dp", "space", None),
        P("dp", "space"),
        P("dp", "space", None, None),
        P("dp", "space", None),
        P("dp", None),
        P("dp"),
        P("dp", "space", None, None, None),
    )
    return jax.shard_map(
        body,
        mesh=mesh,
        in_specs=placed,
        out_specs=(
            P("dp", "space", None, None, None),
            P("dp", "space", None, None, None),
            P("dp", None),
            P("dp"),
        ),
        check_vma=False,
    )
```

```python
import functools

import jax
import jax.numpy as jnp
from jax import lax
from jax.experimental import pallas as pl
from jax.experimental.pallas import tpu as pltpu
from jax.sharding import PartitionSpec as P

F32 = jnp.float32
BF16 = jnp.bfloat16
LANES = 128
UNIT_ROWS = 32
Z_ROWS = 64
SWAPS = (
    ((1, 1), (2, 1), (1, 0), (2, 0)),
    ((2, 1), (1, 1), (2, 0), (1, 0)),
)


def vmem():
    return pl.BlockSpec(memory_space=pltpu.VMEM)


def smem():
    return pl.BlockSpec(memory_space=pltpu.SMEM)


def untouched():
    return pl.BlockSpec(memory_space=pl.ANY)


def offset_number(ox, oy, oz):
    flat = (ox + 1) * 9 + (oy + 1) * 3 + (oz + 1)
    return flat if flat < 13 else flat - 1


def low_half(shape):
    return lax.broadcasted_iota(jnp.int32, shape, len(shape) - 1) % LANES < 64


def chunk_rows(block):
    return [block[8 * q : 8 * q + 8] for q in range(4)]


def upward(device, distance):
    return lax.rem(lax.div(device, distance), 2)


def pack_units(values, send, outs):
    slots = values.shape[1] // 64 - 1
    reach = len(outs) // 2
    low = low_half((64, LANES))
    device = lax.axis_index("space")
    odd = lax.rem(lax.axis_index("dp"), 2)
    for number, out in enumerate(outs):
        column = reach
        if number > 0:
            columns = []
            for distance, turn in (SWAPS[0][number - 1], SWAPS[1][number - 1]):
                up = upward(device, distance) == turn
                columns.append(jnp.where(up, reach + distance, reach - distance))
            column = jnp.where(odd == 0, columns[0], columns[1])

        def base(link):
            unit = send[column, 0, link]
            slot = jnp.where(unit < 0, slots, (unit * 43) >> 8)
            return pl.multiple_of(slot * 64, 64)

        for half in range(2):
            for face in range(4):
                start = base(half * 6 + face)
                if face < 2:
                    where = pl.ds(start + 56 * face, 8)
                else:
                    where = pl.ds(start + 7 * (face - 2), 8, stride=8)
                packed = jnp.concatenate([values[q, where, :] for q in range(4)], axis=0)
                at = (half * 4 + face) * UNIT_ROWS
                out[at : at + UNIT_ROWS, :] = packed.astype(BF16)
            first = values[0, pl.ds(base(half * 6 + 4), 64), :]
            last = values[3, pl.ds(base(half * 6 + 5), 64), :]
            at = 8 * UNIT_ROWS + half * Z_ROWS
            out[at : at + Z_ROWS, :] = jnp.where(low, first, last).astype(BF16)


def prepare_kernel(
    features_hbm, occupancy_hbm, send_hbm, listing_hbm, weight_hbm, bias_hbm, counts,
    masked_out, mask_out, rows_out, send_out, shard_out, u0, u1, u2, u3, u4,
    values, features, occupancy, listing, weight_t, bias, rows, sems,
):
    copies = [
        pltpu.make_async_copy(src, dst, sems.at[i])
        for i, (src, dst) in enumerate(
            (
                (occupancy_hbm, occupancy),
                (features_hbm, features),
                (send_hbm, send_out),
                (listing_hbm, listing),
                (weight_hbm, weight_t),
                (bias_hbm, bias),
            )
        )
    ]
    for copy in copies:
        copy.start()
    bricks = features.shape[0]
    shard_out[...] = jnp.zeros(shard_out.shape, BF16)
    values[:, bricks * 64 :, :] = jnp.zeros((4, 64, LANES), F32)
    row = lax.broadcasted_iota(jnp.int32, (64, 512), 0)
    col = lax.broadcasted_iota(jnp.int32, (64, 512), 1)
    same = (col >> 3) == row
    z_row = lax.broadcasted_iota(jnp.int32, (512, 512), 0) & 7
    z_col = lax.broadcasted_iota(jnp.int32, (512, 512), 1) >> 6
    expand = jnp.where(z_row == z_col, 1.0, 0.0).astype(BF16)

    copies[3].wait()
    device = lax.axis_index("space")
    number = listing[...]
    column = (number * 43) >> 9
    link = number - column * 12
    half = (link >= 6).astype(jnp.int32)
    face = link - 6 * half
    block = jnp.zeros(number.shape, jnp.int32)
    odd = lax.rem(lax.axis_index("dp"), 2)
    for distance in (1, 2):
        up = upward(device, distance)
        first, second = (
            jnp.where(
                odd == 0,
                SWAPS[0].index((distance, turn)) + 1,
                SWAPS[1].index((distance, turn)) + 1,
            )
            for turn in range(2)
        )
        block = jnp.where(column == 2 - distance, jnp.where(up == 0, first, second), block)
        block = jnp.where(column == 2 + distance, jnp.where(up == 0, second, first), block)
    base = block * (8 * UNIT_ROWS + 2 * Z_ROWS)
    plain = base + (half * 4 + face) * UNIT_ROWS
    paired = base + 8 * UNIT_ROWS + half * Z_ROWS
    none = 5 * (8 * UNIT_ROWS + 2 * Z_ROWS)
    rows[...] = jnp.where(number < 0, none, jnp.where(face < 4, plain, paired))
    last = pltpu.make_async_copy(rows, rows_out, sems.at[len(copies)])
    last.start()

    copies[0].wait()
    live = lax.broadcasted_iota(jnp.int32, (bricks, 512), 0) < counts[0, 0]
    occ = jnp.where(live, occupancy[...], 0).astype(F32)
    spread = jnp.concatenate(
        [jnp.where(same, occ[b : b + 1, :], 0.0) for b in range(bricks)], axis=0
    ).astype(BF16)
    mask = jnp.dot(spread, expand, preferred_element_type=F32)
    mask_out[...] = mask.astype(BF16).reshape(mask_out.shape)
    copies[1].wait()
    value = features[...].astype(F32).reshape(bricks * 64, 512) * mask
    masked_out[...] = value.astype(BF16).reshape(masked_out.shape)
    for q in range(4):
        values[q, 0 : bricks * 64, :] = value[:, q * LANES : (q + 1) * LANES]
    copies[2].wait()
    pack_units(values, send_out, (u0, u1, u2, u3, u4))

    copies[4].wait()
    copies[5].wait()
    shard = weight_t.shape[1]
    lead = shard // LANES * LANES
    count = bias.shape[1]
    shard_out[:, 0:lead] = weight_t[:, 0:lead]
    tile = jnp.concatenate(
        [weight_t[:, lead:shard].astype(F32), jnp.zeros((64, lead + LANES - shard), F32)], axis=1
    )
    offset = shard - lead
    behind = jnp.concatenate(
        [bias[...].astype(F32), jnp.zeros((1, LANES - count), F32)], axis=1
    )
    behind = pltpu.roll(jnp.broadcast_to(behind, (64, LANES)), offset, 1)
    first = lax.broadcasted_iota(jnp.int32, (64, LANES), 0) == 0
    lane = lax.broadcasted_iota(jnp.int32, (64, LANES), 1)
    behind = jnp.where(first & (lane >= offset) & (lane < offset + count), behind, 0.0)
    shard_out[:, lead : lead + LANES] = (tile + behind).astype(BF16)
    last.wait()


def gather_units(table, received):
    at = 0
    for part in received:
        table[at : at + part.shape[0], :] = part[...]
        at += part.shape[0]
    table[at:, :] = jnp.zeros((table.shape[0] - at, LANES), BF16)


def assemble(source, table, rows, windows, sides, walls):
    low8 = low_half((8, LANES))
    sub = lax.broadcasted_iota(jnp.int32, (8, LANES), 0)
    top, bottom = sub == 0, sub == 7

    def put(pair, half, bit, per_brick):
        for e in range(3):
            stacked = [
                jnp.concatenate([per_brick[0][e][i], per_brick[1][e][i]], axis=0)
                for i in range(5)
            ]
            low16 = low_half((16, LANES))
            before = [stacked[4]] + stacked[:3]
            after = stacked[1:4] + [stacked[4]]
            for q in range(4):
                windows[e, q, pair, half, bit, :, 0:LANES] = stacked[q].astype(BF16)
                windows[e, q, pair, half, bit, :, LANES:] = jnp.where(
                    low16, after[q], before[q]
                ).astype(BF16)

    def one_pair(pair, carry):
        def unit(brick, ox, oy, oz):
            return pl.multiple_of(rows[brick, offset_number(ox, oy, oz)], UNIT_ROWS)

        def plane(brick, ox, oy):
            chunks = chunk_rows(table[pl.ds(unit(brick, ox, oy, 0), UNIT_ROWS), :].astype(F32))
            after = table[pl.ds(unit(brick, ox, oy, 1), UNIT_ROWS), :].astype(F32)[0:8]
            before = table[pl.ds(unit(brick, ox, oy, -1), UNIT_ROWS), :].astype(F32)[24:32]
            return chunks + [jnp.where(low8, after, before)]

        for b2 in range(2):
            brick = pair * 2 + b2
            low64 = low_half((64, LANES))
            after = table[pl.ds(unit(brick, 0, 0, 1), Z_ROWS), :].astype(F32)
            before = table[pl.ds(unit(brick, 0, 0, -1), Z_ROWS), :].astype(F32)
            walls[b2] = jnp.where(low64, after, before)
            for side, oy in enumerate((-1, 1)):
                for i, part in enumerate(plane(brick, 0, oy)):
                    sides[b2, side, i] = part

        for ox in (-1, 1):
            per_brick = []
            for b2 in range(2):
                brick = pair * 2 + b2
                centre = plane(brick, ox, 0)
                lower = plane(brick, ox, -1)
                upper = plane(brick, ox, 1)
                per_brick.append(
                    [
                        [
                            pltpu.roll(jnp.where(bottom, l, c), 1, 0)
                            for l, c in zip(lower, centre)
                        ],
                        centre,
                        [
                            pltpu.roll(jnp.where(top, u, c), 7, 0)
                            for u, c in zip(upper, centre)
                        ],
                    ]
                )
            put(pair, 0 if ox < 0 else 4, 0 if ox < 0 else 1, per_brick)

        def two_x(i, carry):
            for bit in range(2):
                x = 2 * i + bit
                per_brick = []
                for b2 in range(2):
                    brick = pair * 2 + b2
                    block = source[brick, i, bit].astype(F32)
                    centre = [block[:, q * LANES : (q + 1) * LANES] for q in range(4)]
                    centre.append(walls[b2, pl.ds(pl.multiple_of(x * 8, 8), 8), :])
                    lower = [
                        jnp.broadcast_to(sides[b2, 0, n, pl.ds(x, 1), :], (8, LANES))
                        for n in range(5)
                    ]
                    upper = [
                        jnp.broadcast_to(sides[b2, 1, n, pl.ds(x, 1), :], (8, LANES))
                        for n in range(5)
                    ]
                    per_brick.append(
                        [
                            [
                                jnp.where(top, l, pltpu.roll(c, 1, 0))
                                for l, c in zip(lower, centre)
                            ],
                            centre,
                            [
                                jnp.where(bottom, u, pltpu.roll(c, 7, 0))
                                for u, c in zip(upper, centre)
                            ],
                        ]
                    )
                put(pair, i + bit, 1 - bit, per_brick)
            return carry

        return lax.fori_loop(0, 4, two_x, carry)

    lax.fori_loop(0, windows.shape[2], one_pair, 0)


def row_block(d, e):
    return slice((3 * d + e) * 256, (3 * d + e + 1) * 256)


def tap_rows(windows, d, e):
    block = windows[e, :, :, d // 2 : d // 2 + 4, d % 2]
    return block.reshape(-1, block.shape[-1])


def all_taps(windows):
    return jnp.concatenate(
        [tap_rows(windows, d, e) for d in range(4) for e in range(3)], axis=1
    )


def chunk_places(bricks):
    return [(2 * pair + b2, i) for pair in range(bricks // 2) for i in range(4) for b2 in range(2)]


def chunk_of(ref, q):
    lanes = slice(q * LANES, (q + 1) * LANES)
    return jnp.concatenate(
        [
            jnp.concatenate([ref[b, i, x, :, lanes].astype(F32) for x in range(2)], axis=1)
            for b, i in chunk_places(ref.shape[0])
        ],
        axis=0,
    )


def put_chunk(ref, q, value):
    for n, (b, i) in enumerate(chunk_places(ref.shape[0])):
        for x in range(2):
            part = value[8 * n : 8 * n + 8, x * LANES : (x + 1) * LANES]
            ref[b, i, x, :, q * LANES : (q + 1) * LANES] = part.astype(ref.dtype)


def weights_kernel(*refs, shard, groups):
    shards = refs[:groups]
    forward_out, backward_out, bias_out, gathered, flat, shifted = refs[groups:]
    me = lax.axis_index("dp")
    for m, part in enumerate(shards):
        gathered[m] = part[...]
    for k in range(groups):
        flat[:, k * shard : (k + 1) * shard] = gathered[me ^ k][:, 0:shard].astype(F32)
    total = groups * shard
    flat[:, total:] = jnp.zeros((64, flat.shape[1] - total), F32)
    shifted[:, :] = pltpu.roll(flat[...], flat.shape[1] - 64, 1)
    low = low_half((64, LANES))
    for e in range(3):
        for x in range(2):
            half = slice(x * LANES, (x + 1) * LANES)
            for out in (forward_out, backward_out):
                out[row_block(3 * (1 - x), e), half] = jnp.zeros((256, LANES), BF16)
    for ae in range(9):
        a, e = ae // 3, ae % 3
        one = taps_pair(flat, shifted, 3 * ae)
        two = jnp.where(low, taps_pair(flat, shifted, 3 * ae + 2), 0.0)
        late = jnp.concatenate([one, two], axis=1)
        band = jnp.transpose(jnp.concatenate([pltpu.roll(late, 192, 1), late], axis=0)).astype(BF16)
        for x in range(2):
            forward_out[row_block(a + x, e), x * LANES : (x + 1) * LANES] = band
    for ae in range(9):
        a, e = ae // 3, ae % 3
        m = 3 * (8 - ae)
        first = taps_pair(flat, shifted, m)
        second = taps_pair(flat, shifted, m + 1)
        third = taps_pair(flat, shifted, m + 2)
        band = jnp.concatenate(
            [
                second,
                first,
                jnp.where(low, 0.0, pltpu.roll(first, 64, 1)),
                jnp.where(low, third, 0.0),
            ],
            axis=0,
        ).astype(BF16)
        for x in range(2):
            backward_out[row_block(a + x, e), x * LANES : (x + 1) * LANES] = band

    lane = lax.broadcasted_iota(jnp.int32, (8, LANES), 1)
    bias_lane = shard % LANES
    bias_tile = shard - bias_lane
    count = 64 // groups
    bias_row = jnp.zeros((8, LANES), F32)
    for k in range(groups):
        tile = gathered[me ^ k][0:16, bias_tile : bias_tile + LANES].astype(F32)[0:8]
        moved = pltpu.roll(tile, (count * k - bias_lane) % LANES, 1)
        bias_row += jnp.where((lane >= count * k) & (lane < count * (k + 1)), moved, 0.0)
    bias_out[...] = bias_row + pltpu.roll(bias_row, 64, 1)


def taps_pair(flat, shifted, first):
    if first % 2 == 0:
        return flat[:, first * 64 : first * 64 + LANES]
    return shifted[:, (first - 1) * 64 : (first - 1) * 64 + LANES]


def forward_kernel(
    masked, mask, cotangent_hbm, toeplitz, bias, rows, send, r0, r1, r2, r3, r4,
    block_out, grad_out, keep_out, give_out, u0, u1, u2, u3, u4,
    table, windows, sides, walls, flat, shifted, values, flipped, cotangent, sem, *, shard,
):
    fetch = pltpu.make_async_copy(cotangent_hbm, cotangent, sem)
    fetch.start()
    groups = 2 * keep_out.shape[0]
    bricks = masked.shape[0]
    pairs = bricks // 2
    gather_units(table, (r0, r1, r2, r3, r4))
    assemble(masked, table, rows, windows, sides, walls)
    bias_lane = shard % LANES
    bias_tile = shard - bias_lane
    bias_row = bias[0:1, :]
    fetch.wait()
    values[:, bricks * 64 :, :] = jnp.zeros((4, 64, LANES), F32)

    bias_row = jnp.concatenate([bias_row, bias_row], axis=1)
    total = jnp.dot(all_taps(windows), toeplitz[...], preferred_element_type=F32)
    rows_of_chunk = total.shape[0] // 4
    bias_sum = jnp.zeros((8, 256), F32)
    for q in range(4):
        p = total[q * rows_of_chunk : (q + 1) * rows_of_chunk] + bias_row
        active = chunk_of(mask, q)
        sig = jax.nn.sigmoid(p)
        put_chunk(block_out, q, p * sig * active)
        grad = (chunk_of(cotangent, q) * sig * (1.0 + p * (1.0 - sig)) * active).astype(BF16)
        wide = grad.astype(F32)
        put_chunk(grad_out, q, wide)
        for n, (brick, i) in enumerate(chunk_places(bricks)):
            for x in range(2):
                at = brick * 64 + (2 * i + x) * 8
                values[q, at : at + 8, :] = wide[
                    8 * n : 8 * n + 8, x * LANES : (x + 1) * LANES
                ]
        flipped[:, q * rows_of_chunk : (q + 1) * rows_of_chunk] = jnp.transpose(wide).astype(BF16)
        bias_sum += jnp.sum(wide.reshape(-1, 8, 256), axis=0)
    bias_sum = bias_sum[:, 0:LANES] + bias_sum[:, LANES:]
    pack_units(values, send, (u0, u1, u2, u3, u4))

    for ae in range(9):
        a, e = ae // 3, ae % 3
        both = jnp.zeros((LANES, 256), F32)
        for x in range(2):
            rows = tap_rows(windows, a + x, e)
            for part in range(0, rows.shape[0], 256):
                both += jnp.dot(
                    flipped[x * LANES : (x + 1) * LANES, part : part + 256],
                    rows[part : part + 256],
                    preferred_element_type=F32,
                )
        flat[:, 192 * ae : 192 * ae + 256] = both[64:] + pltpu.roll(both[0:64], 64, 1)

    width = keep_out.shape[2]
    bias_all = jnp.sum(bias_sum, axis=0, keepdims=True)
    bias_all = jnp.broadcast_to(bias_all, (8, LANES))
    bias_all = bias_all + pltpu.roll(bias_all, 64, 1)
    bias_all = pltpu.roll(bias_all, bias_lane, 1)
    row8 = lax.broadcasted_iota(jnp.int32, (8, LANES), 0)
    lane8 = lax.broadcasted_iota(jnp.int32, (8, LANES), 1)
    keep = (row8 == 0) & (lane8 >= bias_lane) & (lane8 < bias_lane + 64)
    me = lax.axis_index("dp")
    for k in range(groups):
        part = flat[:, k * shard : (k + 1) * shard]
        shifted[0:64, 0:shard] = part
        shifted[0:64, shard:width] = jnp.zeros((64, width - shard), F32)
        tile = shifted[0:8, bias_tile : bias_tile + LANES]
        shifted[0:8, bias_tile : bias_tile + LANES] = jnp.where(keep, bias_all, tile)
        block = shifted[0:64, 0:width].astype(BF16)
        for m in range(groups):

            @pl.when(me ^ m == k)
            def _(m=m, block=block):
                (give_out if m % 2 else keep_out)[m // 2] = block


def assemble_kernel(grad, rows, r0, r1, r2, r3, r4, after, windows, table, sides, walls):
    del after
    gather_units(table, (r0, r1, r2, r3, r4))
    assemble(grad, table, rows, windows, sides, walls)


def sum_kernel(*refs, operands, parts):
    total = (refs[0][...].astype(F32) + refs[1][...].astype(F32)).astype(BF16)
    for part in range(parts):
        for row in range(part, total.shape[0], parts):
            refs[operands + part][row // parts] = total[row]


def sum_after(mine, other, after=(), through=(), parts=1):
    operands = 2 + len(after) + len(through)
    share = jax.ShapeDtypeStruct((mine.shape[0] // parts, *mine.shape[1:]), mine.dtype)
    outs = pl.pallas_call(
        functools.partial(sum_kernel, operands=operands, parts=parts),
        name="sum",
        out_shape=[share] * parts + [jax.ShapeDtypeStruct(x.shape, x.dtype) for x in through],
        in_specs=[vmem()] * 2 + [untouched()] * (operands - 2),
        out_specs=[vmem()] * parts + [untouched()] * len(through),
        input_output_aliases={2 + len(after) + i: parts + i for i in range(len(through))},
        compiler_params=pltpu.CompilerParams(vmem_limit_bytes=1024 * 1024),
    )(mine, other, *after, *through)
    return list(outs[:parts]), list(outs[parts:])


def backward_kernel(windows, mask, toeplitz, after, out):
    del after
    total = jnp.dot(all_taps(windows), toeplitz[...], preferred_element_type=F32)
    rows_of_chunk = total.shape[0] // 4
    for q in range(4):
        part = total[q * rows_of_chunk : (q + 1) * rows_of_chunk]
        put_chunk(out, q, part * chunk_of(mask, q))


def finish_kernel(mine, other, weight_out, bias_out):
    shard = weight_out.shape[1]
    count = bias_out.shape[1]
    total = mine[...].astype(F32) + other[...].astype(F32)
    weight_out[...] = total[:, 0:shard]
    bias_lane = shard % LANES
    bias_tile = shard - bias_lane
    tile = total[0:8, bias_tile : bias_tile + LANES]
    me = lax.axis_index("dp")
    moved = pltpu.roll(tile, 2 * LANES - bias_lane - me * count, 1)
    bias_out[...] = moved[0:1, 0:count]


def swapped(block, axis, bit):
    return lax.ppermute(block, axis, [(i, i ^ bit) for i in range(lax.axis_size(axis))])


def by_parity(block, routes):
    groups = lax.axis_size("dp")
    pairs = [
        (source * groups + group, target * groups + group)
        for group in range(groups)
        for source, target in routes[group % 2]
    ]
    return lax.ppermute(block, ("space", "dp"), pairs)


def exchanged(number, unit):
    routes = []
    for swaps in SWAPS:
        distance, turn = swaps[number - 1]
        route = []
        for low in range(lax.axis_size("space") - distance):
            if low // distance % 2 == turn:
                route += [(low, low + distance), (low + distance, low)]
        routes.append(route)
    return by_parity(unit, routes)


def space_steps():
    bits = []
    while 2 ** len(bits) < lax.axis_size("space"):
        bits.append(2 ** len(bits))
    return list(zip(bits, bits[1:] + bits[:1]))


def stepped(total, step):
    devices = range(lax.axis_size("space"))
    return by_parity(total, [[(i, i ^ bit) for i in devices] for bit in step])


def body(features, occupancy, counts, send_units, neighbours, weight, conv_bias, cotangent):
    bricks, edge, _, lanes = features.shape[1:]
    grid_shape = (bricks, edge // 2, 2, edge, lanes)
    pairs = bricks // 2
    spread, links = send_units.shape[2:]
    shard, channels = weight.shape
    groups = lax.axis_size("dp")
    count = conv_bias.shape[0]
    width = -(-(shard + channels) // LANES) * LANES
    unit_rows = 8 * UNIT_ROWS + 2 * Z_ROWS
    units_type = jax.ShapeDtypeStruct((unit_rows, LANES), BF16)
    grid_type = jax.ShapeDtypeStruct(grid_shape, BF16)
    shard_type = jax.ShapeDtypeStruct((channels, width), BF16)
    params = pltpu.CompilerParams(vmem_limit_bytes=48 * 1024 * 1024)
    rows_shape = neighbours.shape[1:]
    send_shape = (spread, 1, links)

    masked, mask, rows, send, own_shard, *units = pl.pallas_call(
        prepare_kernel,
        name="prepare",
        out_shape=[
            grid_type,
            grid_type,
            jax.ShapeDtypeStruct(rows_shape, jnp.int32),
            jax.ShapeDtypeStruct(send_shape, jnp.int32),
            shard_type,
        ]
        + [units_type] * spread,
        in_specs=[pl.BlockSpec(memory_space=pltpu.HBM)] * 6 + [smem()],
        out_specs=[vmem(), vmem(), smem(), smem(), vmem()] + [vmem()] * spread,
        scratch_shapes=[
            pltpu.VMEM((4, (bricks + 1) * 64, LANES), F32),
            pltpu.VMEM(grid_shape, BF16),
            pltpu.VMEM(occupancy.shape[1:], jnp.int32),
            pltpu.VMEM(rows_shape, jnp.int32),
            pltpu.VMEM((channels, shard), BF16),
            pltpu.VMEM((1, count), BF16),
            pltpu.VMEM(rows_shape, jnp.int32),
            pltpu.SemaphoreType.DMA((7,)),
        ],
        compiler_params=params,
    )(
        *(
            pltpu.with_memory_space_constraint(operand, pltpu.HBM)
            for operand in (
                features.reshape(grid_shape),
                occupancy[0],
                send_units.transpose(0, 2, 1, 3).reshape(send_shape),
                neighbours[0],
                weight.T,
                conv_bias.reshape(1, count),
            )
        ),
        counts,
    )

    shards = {0: own_shard}
    bit = groups // 2
    while bit:
        for m in list(shards):
            shards[m | bit] = swapped(shards[m], "dp", bit)
        bit //= 2
    received = units[:1] + [exchanged(number, units[number]) for number in range(1, spread)]

    flat = pltpu.VMEM((channels, 28 * 64), F32)
    band_forward, band_backward, bias = pl.pallas_call(
        functools.partial(weights_kernel, shard=shard, groups=groups),
        name="weights",
        out_shape=[
            jax.ShapeDtypeStruct((12 * 256, 256), BF16),
            jax.ShapeDtypeStruct((12 * 256, 256), BF16),
            jax.ShapeDtypeStruct((8, LANES), F32),
        ],
        in_specs=[vmem()] * groups,
        out_specs=[vmem()] * 3,
        scratch_shapes=[pltpu.VMEM((groups, channels, width), BF16), flat, flat],
        compiler_params=params,
    )(*(shards[m] for m in range(groups)))

    table = pltpu.VMEM((spread * unit_rows + Z_ROWS, LANES), BF16)
    windows = pltpu.VMEM((3, 4, pairs, 5, 2, 16, 256), BF16)
    sides = pltpu.VMEM((2, 2, 5, 8, LANES), F32)
    walls = pltpu.VMEM((2, 64, LANES), F32)
    half_type = jax.ShapeDtypeStruct((groups // 2, channels, width), BF16)
    block_output, grad, keep, give, *grad_units = pl.pallas_call(
        functools.partial(forward_kernel, shard=shard),
        name="forward",
        out_shape=[grid_type, grid_type, half_type, half_type] + [units_type] * spread,
        in_specs=[vmem(), vmem(), pl.BlockSpec(memory_space=pltpu.HBM), vmem(), vmem()]
        + [smem(), smem()]
        + [vmem()] * spread,
        out_specs=[vmem()] * (4 + spread),
        scratch_shapes=[
            table,
            windows,
            sides,
            walls,
            flat,
            pltpu.VMEM((channels, 4 * LANES), F32),
            pltpu.VMEM((4, (bricks + 1) * 64, LANES), F32),
            pltpu.VMEM((256, bricks * LANES), BF16),
            pltpu.VMEM(grid_shape, BF16),
            pltpu.SemaphoreType.DMA,
        ],
        compiler_params=params,
    )(
        masked,
        mask,
        pltpu.with_memory_space_constraint(cotangent.reshape(grid_shape), pltpu.HBM),
        band_forward,
        bias,
        rows,
        send,
        *received,
    )

    later = grad_units[2:]
    bit = 1
    while 2 * bit < groups:
        first = later[:1] if bit == 1 else []
        (keep, give), first = sum_after(keep, swapped(give, "dp", bit), through=first, parts=2)
        later = first + later[1:] if bit == 1 else later
        bit *= 2
    grad_received = [grad_units[0], exchanged(1, grad_units[1])]
    (total,), last = sum_after(keep, swapped(give, "dp", bit), grad_received[1:], later[1:])
    for number, unit in enumerate([later[0], *last], 2):
        grad_received.append(exchanged(number, unit))

    steps = space_steps()
    other = stepped(total, steps[0])
    if len(steps) > 1:
        (total,), _ = sum_after(total, other, grad_received[3:4])
        other = stepped(total, steps[1])

    padded_grad = pl.pallas_call(
        assemble_kernel,
        name="assemble",
        out_shape=jax.ShapeDtypeStruct(windows.shape, BF16),
        in_specs=[vmem()] + [smem()] + [vmem()] * spread + [untouched()],
        out_specs=vmem(),
        scratch_shapes=[table, sides, walls],
        compiler_params=params,
    )(grad, rows, *grad_received, total)

    for number, step in enumerate(steps[2:]):
        (total,), _ = sum_after(total, other, [] if number else [padded_grad])
        other = stepped(total, step)

    grad_input = pl.pallas_call(
        backward_kernel,
        name="backward",
        out_shape=grid_type,
        in_specs=[vmem()] * 3 + [untouched()],
        out_specs=vmem(),
        compiler_params=params,
    )(padded_grad, mask, band_backward, total)

    weight_share, bias_share = pl.pallas_call(
        finish_kernel,
        name="finish",
        out_shape=[
            jax.ShapeDtypeStruct((channels, shard), F32),
            jax.ShapeDtypeStruct((1, count), F32),
        ],
        in_specs=[vmem()] * 2,
        out_specs=[vmem()] * 2,
        compiler_params=params,
    )(total[0], other[0])
    return (
        block_output.reshape(features.shape),
        grad_input.reshape(features.shape),
        weight_share.T,
        bias_share.reshape(count),
    )


def solution(mesh):
    placed = (
        P("dp", "space", None, None, None),
        P("dp", "space", None),
        P("dp", "space"),
        P("dp", "space", None, None),
        P("dp", "space", None),
        P("dp", None),
        P("dp"),
        P("dp", "space", None, None, None),
    )
    return jax.shard_map(
        body,
        mesh=mesh,
        in_specs=placed,
        out_specs=(
            P("dp", "space", None, None, None),
            P("dp", "space", None, None, None),
            P("dp", None),
            P("dp"),
        ),
        check_vma=False,
    )
```

```python
import functools

import jax
import jax.numpy as jnp
from jax import lax
from jax.experimental import pallas as pl
from jax.experimental.pallas import tpu as pltpu
from jax.sharding import PartitionSpec as P

F32 = jnp.float32
BF16 = jnp.bfloat16
LANES = 128
UNIT_ROWS = 32
Z_ROWS = 64
SWAPS = (
    ((1, 1), (2, 1), (1, 0), (2, 0)),
    ((2, 1), (1, 1), (2, 0), (1, 0)),
)


def vmem():
    return pl.BlockSpec(memory_space=pltpu.VMEM)


def smem():
    return pl.BlockSpec(memory_space=pltpu.SMEM)


def untouched():
    return pl.BlockSpec(memory_space=pl.ANY)


def offset_number(ox, oy, oz):
    flat = (ox + 1) * 9 + (oy + 1) * 3 + (oz + 1)
    return flat if flat < 13 else flat - 1


def low_half(shape):
    return lax.broadcasted_iota(jnp.int32, shape, len(shape) - 1) % LANES < 64


def chunk_rows(block):
    return [block[8 * q : 8 * q + 8] for q in range(4)]


def upward(device, distance):
    return lax.rem(lax.div(device, distance), 2)


def pack_units(values, send, outs):
    slots = values.shape[1] // 64 - 1
    reach = len(outs) // 2
    low = low_half((64, LANES))
    device = lax.axis_index("space")
    odd = lax.rem(lax.axis_index("dp"), 2)
    for number, out in enumerate(outs):
        column = reach
        if number > 0:
            columns = []
            for distance, turn in (SWAPS[0][number - 1], SWAPS[1][number - 1]):
                up = upward(device, distance) == turn
                columns.append(jnp.where(up, reach + distance, reach - distance))
            column = jnp.where(odd == 0, columns[0], columns[1])

        def base(link):
            unit = send[column, 0, link]
            slot = jnp.where(unit < 0, slots, (unit * 43) >> 8)
            return pl.multiple_of(slot * 64, 64)

        for half in range(2):
            for face in range(4):
                start = base(half * 6 + face)
                if face < 2:
                    where = pl.ds(start + 56 * face, 8)
                else:
                    where = pl.ds(start + 7 * (face - 2), 8, stride=8)
                packed = jnp.concatenate([values[q, where, :] for q in range(4)], axis=0)
                at = (half * 4 + face) * UNIT_ROWS
                out[at : at + UNIT_ROWS, :] = packed.astype(BF16)
            first = values[0, pl.ds(base(half * 6 + 4), 64), :]
            last = values[3, pl.ds(base(half * 6 + 5), 64), :]
            at = 8 * UNIT_ROWS + half * Z_ROWS
            out[at : at + Z_ROWS, :] = jnp.where(low, first, last).astype(BF16)


def prepare_kernel(
    features_hbm, occupancy_hbm, send_hbm, listing_hbm, weight_hbm, bias_hbm, counts,
    masked_out, mask_out, rows_out, send_out, shard_out, u0, u1, u2, u3, u4,
    values, features, occupancy, listing, weight_t, bias, rows, sems,
):
    copies = [
        pltpu.make_async_copy(src, dst, sems.at[i])
        for i, (src, dst) in enumerate(
            (
                (occupancy_hbm, occupancy),
                (features_hbm, features),
                (send_hbm, send_out),
                (listing_hbm, listing),
                (weight_hbm, weight_t),
                (bias_hbm, bias),
            )
        )
    ]
    for copy in copies:
        copy.start()
    bricks = features.shape[0]
    shard_out[...] = jnp.zeros(shard_out.shape, BF16)
    values[:, bricks * 64 :, :] = jnp.zeros((4, 64, LANES), F32)
    row = lax.broadcasted_iota(jnp.int32, (64, 512), 0)
    col = lax.broadcasted_iota(jnp.int32, (64, 512), 1)
    same = (col >> 3) == row
    z_row = lax.broadcasted_iota(jnp.int32, (512, 512), 0) & 7
    z_col = lax.broadcasted_iota(jnp.int32, (512, 512), 1) >> 6
    expand = jnp.where(z_row == z_col, 1.0, 0.0).astype(BF16)

    copies[3].wait()
    device = lax.axis_index("space")
    number = listing[...]
    column = (number * 43) >> 9
    link = number - column * 12
    half = (link >= 6).astype(jnp.int32)
    face = link - 6 * half
    block = jnp.zeros(number.shape, jnp.int32)
    odd = lax.rem(lax.axis_index("dp"), 2)
    for distance in (1, 2):
        up = upward(device, distance)
        first, second = (
            jnp.where(
                odd == 0,
                SWAPS[0].index((distance, turn)) + 1,
                SWAPS[1].index((distance, turn)) + 1,
            )
            for turn in range(2)
        )
        block = jnp.where(column == 2 - distance, jnp.where(up == 0, first, second), block)
        block = jnp.where(column == 2 + distance, jnp.where(up == 0, second, first), block)
    base = block * (8 * UNIT_ROWS + 2 * Z_ROWS)
    plain = base + (half * 4 + face) * UNIT_ROWS
    paired = base + 8 * UNIT_ROWS + half * Z_ROWS
    none = 5 * (8 * UNIT_ROWS + 2 * Z_ROWS)
    rows[...] = jnp.where(number < 0, none, jnp.where(face < 4, plain, paired))
    last = pltpu.make_async_copy(rows, rows_out, sems.at[len(copies)])
    last.start()

    copies[0].wait()
    live = lax.broadcasted_iota(jnp.int32, (bricks, 512), 0) < counts[0, 0]
    occ = jnp.where(live, occupancy[...], 0).astype(F32)
    spread = jnp.concatenate(
        [jnp.where(same, occ[b : b + 1, :], 0.0) for b in range(bricks)], axis=0
    ).astype(BF16)
    mask = jnp.dot(spread, expand, preferred_element_type=F32)
    mask_out[...] = mask.astype(BF16).reshape(mask_out.shape)
    copies[1].wait()
    value = features[...].astype(F32).reshape(bricks * 64, 512) * mask
    masked_out[...] = value.astype(BF16).reshape(masked_out.shape)
    for q in range(4):
        values[q, 0 : bricks * 64, :] = value[:, q * LANES : (q + 1) * LANES]
    copies[2].wait()
    pack_units(values, send_out, (u0, u1, u2, u3, u4))

    copies[4].wait()
    copies[5].wait()
    shard = weight_t.shape[1]
    lead = shard // LANES * LANES
    count = bias.shape[1]
    shard_out[:, 0:lead] = weight_t[:, 0:lead]
    tile = jnp.concatenate(
        [weight_t[:, lead:shard].astype(F32), jnp.zeros((64, lead + LANES - shard), F32)], axis=1
    )
    offset = shard - lead
    behind = jnp.concatenate(
        [bias[...].astype(F32), jnp.zeros((1, LANES - count), F32)], axis=1
    )
    behind = pltpu.roll(jnp.broadcast_to(behind, (64, LANES)), offset, 1)
    first = lax.broadcasted_iota(jnp.int32, (64, LANES), 0) == 0
    lane = lax.broadcasted_iota(jnp.int32, (64, LANES), 1)
    behind = jnp.where(first & (lane >= offset) & (lane < offset + count), behind, 0.0)
    shard_out[:, lead : lead + LANES] = (tile + behind).astype(BF16)
    last.wait()


def gather_units(table, received):
    at = 0
    for part in received:
        table[at : at + part.shape[0], :] = part[...]
        at += part.shape[0]
    table[at:, :] = jnp.zeros((table.shape[0] - at, LANES), BF16)


def assemble(source, table, rows, windows, sides, walls):
    low8 = low_half((8, LANES))
    sub = lax.broadcasted_iota(jnp.int32, (8, LANES), 0)
    top, bottom = sub == 0, sub == 7

    def put(pair, half, bit, per_brick):
        for e in range(3):
            stacked = [
                jnp.concatenate([per_brick[0][e][i], per_brick[1][e][i]], axis=0)
                for i in range(5)
            ]
            low16 = low_half((16, LANES))
            before = [stacked[4]] + stacked[:3]
            after = stacked[1:4] + [stacked[4]]
            for q in range(4):
                windows[e, q, pair, half, bit, :, 0:LANES] = stacked[q].astype(BF16)
                windows[e, q, pair, half, bit, :, LANES:] = jnp.where(
                    low16, after[q], before[q]
                ).astype(BF16)

    def one_pair(pair, carry):
        def unit(brick, ox, oy, oz):
            return pl.multiple_of(rows[brick, offset_number(ox, oy, oz)], UNIT_ROWS)

        def plane(brick, ox, oy):
            chunks = chunk_rows(table[pl.ds(unit(brick, ox, oy, 0), UNIT_ROWS), :].astype(F32))
            after = table[pl.ds(unit(brick, ox, oy, 1), UNIT_ROWS), :].astype(F32)[0:8]
            before = table[pl.ds(unit(brick, ox, oy, -1), UNIT_ROWS), :].astype(F32)[24:32]
            return chunks + [jnp.where(low8, after, before)]

        for b2 in range(2):
            brick = pair * 2 + b2
            low64 = low_half((64, LANES))
            after = table[pl.ds(unit(brick, 0, 0, 1), Z_ROWS), :].astype(F32)
            before = table[pl.ds(unit(brick, 0, 0, -1), Z_ROWS), :].astype(F32)
            walls[b2] = jnp.where(low64, after, before)
            for side, oy in enumerate((-1, 1)):
                for i, part in enumerate(plane(brick, 0, oy)):
                    sides[b2, side, i] = part

        for ox in (-1, 1):
            per_brick = []
            for b2 in range(2):
                brick = pair * 2 + b2
                centre = plane(brick, ox, 0)
                lower = plane(brick, ox, -1)
                upper = plane(brick, ox, 1)
                per_brick.append(
                    [
                        [
                            pltpu.roll(jnp.where(bottom, l, c), 1, 0)
                            for l, c in zip(lower, centre)
                        ],
                        centre,
                        [
                            pltpu.roll(jnp.where(top, u, c), 7, 0)
                            for u, c in zip(upper, centre)
                        ],
                    ]
                )
            put(pair, 0 if ox < 0 else 4, 0 if ox < 0 else 1, per_brick)

        def two_x(i, carry):
            for bit in range(2):
                x = 2 * i + bit
                per_brick = []
                for b2 in range(2):
                    brick = pair * 2 + b2
                    block = source[brick, i, bit].astype(F32)
                    centre = [block[:, q * LANES : (q + 1) * LANES] for q in range(4)]
                    centre.append(walls[b2, pl.ds(pl.multiple_of(x * 8, 8), 8), :])
                    lower = [
                        jnp.broadcast_to(sides[b2, 0, n, pl.ds(x, 1), :], (8, LANES))
                        for n in range(5)
                    ]
                    upper = [
                        jnp.broadcast_to(sides[b2, 1, n, pl.ds(x, 1), :], (8, LANES))
                        for n in range(5)
                    ]
                    per_brick.append(
                        [
                            [
                                jnp.where(top, l, pltpu.roll(c, 1, 0))
                                for l, c in zip(lower, centre)
                            ],
                            centre,
                            [
                                jnp.where(bottom, u, pltpu.roll(c, 7, 0))
                                for u, c in zip(upper, centre)
                            ],
                        ]
                    )
                put(pair, i + bit, 1 - bit, per_brick)
            return carry

        return lax.fori_loop(0, 4, two_x, carry)

    lax.fori_loop(0, windows.shape[2], one_pair, 0)


def row_block(d, e):
    return slice((3 * d + e) * 256, (3 * d + e + 1) * 256)


def tap_rows(windows, d, e):
    block = windows[e, :, :, d // 2 : d // 2 + 4, d % 2]
    return block.reshape(-1, block.shape[-1])


def all_taps(windows):
    return jnp.concatenate(
        [tap_rows(windows, d, e) for d in range(4) for e in range(3)], axis=1
    )


def chunk_places(bricks):
    return [(2 * pair + b2, i) for pair in range(bricks // 2) for i in range(4) for b2 in range(2)]


def chunk_of(ref, q):
    lanes = slice(q * LANES, (q + 1) * LANES)
    return jnp.concatenate(
        [
            jnp.concatenate([ref[b, i, x, :, lanes].astype(F32) for x in range(2)], axis=1)
            for b, i in chunk_places(ref.shape[0])
        ],
        axis=0,
    )


def put_chunk(ref, q, value):
    for n, (b, i) in enumerate(chunk_places(ref.shape[0])):
        for x in range(2):
            part = value[8 * n : 8 * n + 8, x * LANES : (x + 1) * LANES]
            ref[b, i, x, :, q * LANES : (q + 1) * LANES] = part.astype(ref.dtype)


def weights_kernel(*refs, shard, groups):
    shards = refs[:groups]
    forward_out, backward_out, bias_out, gathered, flat, shifted = refs[groups:]
    me = lax.axis_index("dp")
    for m, part in enumerate(shards):
        gathered[m] = part[...]
    for k in range(groups):
        flat[:, k * shard : (k + 1) * shard] = gathered[me ^ k][:, 0:shard].astype(F32)
    total = groups * shard
    flat[:, total:] = jnp.zeros((64, flat.shape[1] - total), F32)
    shifted[:, :] = pltpu.roll(flat[...], flat.shape[1] - 64, 1)
    low = low_half((64, LANES))
    for e in range(3):
        for x in range(2):
            half = slice(x * LANES, (x + 1) * LANES)
            for out in (forward_out, backward_out):
                out[row_block(3 * (1 - x), e), half] = jnp.zeros((256, LANES), BF16)
    for ae in range(9):
        a, e = ae // 3, ae % 3
        one = taps_pair(flat, shifted, 3 * ae)
        two = jnp.where(low, taps_pair(flat, shifted, 3 * ae + 2), 0.0)
        late = jnp.concatenate([one, two], axis=1)
        band = jnp.transpose(jnp.concatenate([pltpu.roll(late, 192, 1), late], axis=0)).astype(BF16)
        for x in range(2):
            forward_out[row_block(a + x, e), x * LANES : (x + 1) * LANES] = band
    for ae in range(9):
        a, e = ae // 3, ae % 3
        m = 3 * (8 - ae)
        first = taps_pair(flat, shifted, m)
        second = taps_pair(flat, shifted, m + 1)
        third = taps_pair(flat, shifted, m + 2)
        band = jnp.concatenate(
            [
                second,
                first,
                jnp.where(low, 0.0, pltpu.roll(first, 64, 1)),
                jnp.where(low, third, 0.0),
            ],
            axis=0,
        ).astype(BF16)
        for x in range(2):
            backward_out[row_block(a + x, e), x * LANES : (x + 1) * LANES] = band

    lane = lax.broadcasted_iota(jnp.int32, (8, LANES), 1)
    bias_lane = shard % LANES
    bias_tile = shard - bias_lane
    count = 64 // groups
    bias_row = jnp.zeros((8, LANES), F32)
    for k in range(groups):
        tile = gathered[me ^ k][0:16, bias_tile : bias_tile + LANES].astype(F32)[0:8]
        moved = pltpu.roll(tile, (count * k - bias_lane) % LANES, 1)
        bias_row += jnp.where((lane >= count * k) & (lane < count * (k + 1)), moved, 0.0)
    bias_out[...] = bias_row + pltpu.roll(bias_row, 64, 1)


def taps_pair(flat, shifted, first):
    if first % 2 == 0:
        return flat[:, first * 64 : first * 64 + LANES]
    return shifted[:, (first - 1) * 64 : (first - 1) * 64 + LANES]


def forward_kernel(
    masked, mask, cotangent_hbm, toeplitz, bias, rows, send, r0, r1, r2, r3, r4,
    block_out, grad_out, keep_out, give_out, u0, u1, u2, u3, u4,
    table, windows, sides, walls, flat, shifted, values, flipped, cotangent, sem, *, shard,
):
    fetch = pltpu.make_async_copy(cotangent_hbm, cotangent, sem)
    fetch.start()
    groups = 2 * keep_out.shape[0]
    bricks = masked.shape[0]
    pairs = bricks // 2
    gather_units(table, (r0, r1, r2, r3, r4))
    assemble(masked, table, rows, windows, sides, walls)
    bias_lane = shard % LANES
    bias_tile = shard - bias_lane
    bias_row = bias[0:1, :]
    fetch.wait()
    values[:, bricks * 64 :, :] = jnp.zeros((4, 64, LANES), F32)

    bias_row = jnp.concatenate([bias_row, bias_row], axis=1)
    total = jnp.dot(all_taps(windows), toeplitz[...], preferred_element_type=F32)
    rows_of_chunk = total.shape[0] // 4
    bias_sum = jnp.zeros((8, 256), F32)
    for q in range(4):
        p = total[q * rows_of_chunk : (q + 1) * rows_of_chunk] + bias_row
        active = chunk_of(mask, q)
        sig = jax.nn.sigmoid(p)
        put_chunk(block_out, q, p * sig * active)
        grad = (chunk_of(cotangent, q) * sig * (1.0 + p * (1.0 - sig)) * active).astype(BF16)
        wide = grad.astype(F32)
        put_chunk(grad_out, q, wide)
        for n, (brick, i) in enumerate(chunk_places(bricks)):
            for x in range(2):
                at = brick * 64 + (2 * i + x) * 8
                values[q, at : at + 8, :] = wide[
                    8 * n : 8 * n + 8, x * LANES : (x + 1) * LANES
                ]
        flipped[:, q * rows_of_chunk : (q + 1) * rows_of_chunk] = jnp.transpose(wide).astype(BF16)
        bias_sum += jnp.sum(wide.reshape(-1, 8, 256), axis=0)
    bias_sum = bias_sum[:, 0:LANES] + bias_sum[:, LANES:]
    pack_units(values, send, (u0, u1, u2, u3, u4))

    for ae in range(9):
        a, e = ae // 3, ae % 3
        both = jnp.zeros((LANES, 256), F32)
        for x in range(2):
            rows = tap_rows(windows, a + x, e)
            for part in range(0, rows.shape[0], 256):
                both += jnp.dot(
                    flipped[x * LANES : (x + 1) * LANES, part : part + 256],
                    rows[part : part + 256],
                    preferred_element_type=F32,
                )
        flat[:, 192 * ae : 192 * ae + 256] = both[64:] + pltpu.roll(both[0:64], 64, 1)

    width = keep_out.shape[2]
    bias_all = jnp.sum(bias_sum, axis=0, keepdims=True)
    bias_all = jnp.broadcast_to(bias_all, (8, LANES))
    bias_all = bias_all + pltpu.roll(bias_all, 64, 1)
    bias_all = pltpu.roll(bias_all, bias_lane, 1)
    row8 = lax.broadcasted_iota(jnp.int32, (8, LANES), 0)
    lane8 = lax.broadcasted_iota(jnp.int32, (8, LANES), 1)
    keep = (row8 == 0) & (lane8 >= bias_lane) & (lane8 < bias_lane + 64)
    me = lax.axis_index("dp")
    for k in range(groups):
        part = flat[:, k * shard : (k + 1) * shard]
        shifted[0:64, 0:shard] = part
        shifted[0:64, shard:width] = jnp.zeros((64, width - shard), F32)
        tile = shifted[0:8, bias_tile : bias_tile + LANES]
        shifted[0:8, bias_tile : bias_tile + LANES] = jnp.where(keep, bias_all, tile)
        block = shifted[0:64, 0:width].astype(BF16)
        for m in range(groups):

            @pl.when(me ^ m == k)
            def _(m=m, block=block):
                (give_out if m % 2 else keep_out)[m // 2] = block


def assemble_kernel(grad, rows, r0, r1, r2, r3, r4, after, windows, table, sides, walls):
    del after
    gather_units(table, (r0, r1, r2, r3, r4))
    assemble(grad, table, rows, windows, sides, walls)


def sum_kernel(*refs, operands, parts):
    total = (refs[0][...].astype(F32) + refs[1][...].astype(F32)).astype(BF16)
    for part in range(parts):
        for row in range(part, total.shape[0], parts):
            refs[operands + part][row // parts] = total[row]


def sum_after(mine, other, after=(), through=(), parts=1):
    operands = 2 + len(after) + len(through)
    share = jax.ShapeDtypeStruct((mine.shape[0] // parts, *mine.shape[1:]), mine.dtype)
    outs = pl.pallas_call(
        functools.partial(sum_kernel, operands=operands, parts=parts),
        name="sum",
        out_shape=[share] * parts + [jax.ShapeDtypeStruct(x.shape, x.dtype) for x in through],
        in_specs=[vmem()] * 2 + [untouched()] * (operands - 2),
        out_specs=[vmem()] * parts + [untouched()] * len(through),
        input_output_aliases={2 + len(after) + i: parts + i for i in range(len(through))},
        compiler_params=pltpu.CompilerParams(vmem_limit_bytes=1024 * 1024),
    )(mine, other, *after, *through)
    return list(outs[:parts]), list(outs[parts:])


def backward_kernel(windows, mask, toeplitz, after, out):
    del after
    total = jnp.dot(all_taps(windows), toeplitz[...], preferred_element_type=F32)
    rows_of_chunk = total.shape[0] // 4
    for q in range(4):
        part = total[q * rows_of_chunk : (q + 1) * rows_of_chunk]
        put_chunk(out, q, part * chunk_of(mask, q))


def finish_kernel(mine, other, weight_out, bias_out):
    shard = weight_out.shape[1]
    count = bias_out.shape[1]
    total = mine[...].astype(F32) + other[...].astype(F32)
    weight_out[...] = total[:, 0:shard]
    bias_lane = shard % LANES
    bias_tile = shard - bias_lane
    tile = total[0:8, bias_tile : bias_tile + LANES]
    me = lax.axis_index("dp")
    moved = pltpu.roll(tile, 2 * LANES - bias_lane - me * count, 1)
    bias_out[...] = moved[0:1, 0:count]


def swapped(block, axis, bit):
    return lax.ppermute(block, axis, [(i, i ^ bit) for i in range(lax.axis_size(axis))])


def by_parity(block, routes):
    groups = lax.axis_size("dp")
    pairs = [
        (source * groups + group, target * groups + group)
        for group in range(groups)
        for source, target in routes[group % 2]
    ]
    return lax.ppermute(block, ("space", "dp"), pairs)


def exchanged(number, unit):
    routes = []
    for swaps in SWAPS:
        distance, turn = swaps[number - 1]
        route = []
        for low in range(lax.axis_size("space") - distance):
            if low // distance % 2 == turn:
                route += [(low, low + distance), (low + distance, low)]
        routes.append(route)
    return by_parity(unit, routes)


def space_steps():
    bits = []
    while 2 ** len(bits) < lax.axis_size("space"):
        bits.append(2 ** len(bits))
    return list(zip(bits, bits[1:] + bits[:1]))


def stepped(total, step):
    devices = range(lax.axis_size("space"))
    return by_parity(total, [[(i, i ^ bit) for i in devices] for bit in step])


def body(features, occupancy, counts, send_units, neighbours, weight, conv_bias, cotangent):
    bricks, edge, _, lanes = features.shape[1:]
    grid_shape = (bricks, edge // 2, 2, edge, lanes)
    pairs = bricks // 2
    spread, links = send_units.shape[2:]
    shard, channels = weight.shape
    groups = lax.axis_size("dp")
    count = conv_bias.shape[0]
    width = -(-(shard + channels) // LANES) * LANES
    unit_rows = 8 * UNIT_ROWS + 2 * Z_ROWS
    units_type = jax.ShapeDtypeStruct((unit_rows, LANES), BF16)
    grid_type = jax.ShapeDtypeStruct(grid_shape, BF16)
    shard_type = jax.ShapeDtypeStruct((channels, width), BF16)
    params = pltpu.CompilerParams(vmem_limit_bytes=48 * 1024 * 1024)
    rows_shape = neighbours.shape[1:]
    send_shape = (spread, 1, links)

    masked, mask, rows, send, own_shard, *units = pl.pallas_call(
        prepare_kernel,
        name="prepare",
        out_shape=[
            grid_type,
            grid_type,
            jax.ShapeDtypeStruct(rows_shape, jnp.int32),
            jax.ShapeDtypeStruct(send_shape, jnp.int32),
            shard_type,
        ]
        + [units_type] * spread,
        in_specs=[pl.BlockSpec(memory_space=pltpu.HBM)] * 6 + [smem()],
        out_specs=[vmem(), vmem(), smem(), smem(), vmem()] + [vmem()] * spread,
        scratch_shapes=[
            pltpu.VMEM((4, (bricks + 1) * 64, LANES), F32),
            pltpu.VMEM(grid_shape, BF16),
            pltpu.VMEM(occupancy.shape[1:], jnp.int32),
            pltpu.VMEM(rows_shape, jnp.int32),
            pltpu.VMEM((channels, shard), BF16),
            pltpu.VMEM((1, count), BF16),
            pltpu.VMEM(rows_shape, jnp.int32),
            pltpu.SemaphoreType.DMA((7,)),
        ],
        compiler_params=params,
    )(
        *(
            pltpu.with_memory_space_constraint(operand, pltpu.HBM)
            for operand in (
                features.reshape(grid_shape),
                occupancy[0],
                send_units.transpose(0, 2, 1, 3).reshape(send_shape),
                neighbours[0],
                weight.T,
                conv_bias.reshape(1, count),
            )
        ),
        counts,
    )

    shards = {0: own_shard}
    bit = groups // 2
    while bit:
        for m in list(shards):
            shards[m | bit] = swapped(shards[m], "dp", bit)
        bit //= 2
    received = units[:1] + [exchanged(number, units[number]) for number in range(1, spread)]

    flat = pltpu.VMEM((channels, 28 * 64), F32)
    band_forward, band_backward, bias = pl.pallas_call(
        functools.partial(weights_kernel, shard=shard, groups=groups),
        name="weights",
        out_shape=[
            jax.ShapeDtypeStruct((12 * 256, 256), BF16),
            jax.ShapeDtypeStruct((12 * 256, 256), BF16),
            jax.ShapeDtypeStruct((8, LANES), F32),
        ],
        in_specs=[vmem()] * groups,
        out_specs=[vmem()] * 3,
        scratch_shapes=[pltpu.VMEM((groups, channels, width), BF16), flat, flat],
        compiler_params=params,
    )(*(shards[m] for m in range(groups)))

    table = pltpu.VMEM((spread * unit_rows + Z_ROWS, LANES), BF16)
    windows = pltpu.VMEM((3, 4, pairs, 5, 2, 16, 256), BF16)
    sides = pltpu.VMEM((2, 2, 5, 8, LANES), F32)
    walls = pltpu.VMEM((2, 64, LANES), F32)
    half_type = jax.ShapeDtypeStruct((groups // 2, channels, width), BF16)
    block_output, grad, keep, give, *grad_units = pl.pallas_call(
        functools.partial(forward_kernel, shard=shard),
        name="forward",
        out_shape=[grid_type, grid_type, half_type, half_type] + [units_type] * spread,
        in_specs=[vmem(), vmem(), pl.BlockSpec(memory_space=pltpu.HBM), vmem(), vmem()]
        + [smem(), smem()]
        + [vmem()] * spread,
        out_specs=[vmem()] * (4 + spread),
        scratch_shapes=[
            table,
            windows,
            sides,
            walls,
            flat,
            pltpu.VMEM((channels, 4 * LANES), F32),
            pltpu.VMEM((4, (bricks + 1) * 64, LANES), F32),
            pltpu.VMEM((256, bricks * LANES), BF16),
            pltpu.VMEM(grid_shape, BF16),
            pltpu.SemaphoreType.DMA,
        ],
        compiler_params=params,
    )(
        masked,
        mask,
        pltpu.with_memory_space_constraint(cotangent.reshape(grid_shape), pltpu.HBM),
        band_forward,
        bias,
        rows,
        send,
        *received,
    )

    early, late = 3, (1, 2, 4)
    grad_received = {0: grad_units[0]}
    unit = [grad_units[early]]
    bit = 1
    while 2 * bit < groups:
        (keep, give), unit = sum_after(keep, swapped(give, "dp", bit), through=unit, parts=2)
        bit *= 2
    far = swapped(give, "dp", bit)
    grad_received[early] = exchanged(early, unit[0])
    (total,), units_left = sum_after(
        keep, far, [grad_received[early]], [grad_units[n] for n in late]
    )

    steps = space_steps()
    other = stepped(total, steps[0])
    for number, unit in zip(late, units_left):
        grad_received[number] = exchanged(number, unit)
    grad_received = [grad_received[number] for number in range(spread)]
    if len(steps) > 1:
        (total,), _ = sum_after(total, other, [grad_received[late[0]]])
        other = stepped(total, steps[1])

    padded_grad = pl.pallas_call(
        assemble_kernel,
        name="assemble",
        out_shape=jax.ShapeDtypeStruct(windows.shape, BF16),
        in_specs=[vmem()] + [smem()] + [vmem()] * spread + [untouched()],
        out_specs=vmem(),
        scratch_shapes=[table, sides, walls],
        compiler_params=params,
    )(grad, rows, *grad_received, total)

    for number, step in enumerate(steps[2:]):
        (total,), _ = sum_after(total, other, [] if number else [padded_grad])
        other = stepped(total, step)

    grad_input = pl.pallas_call(
        backward_kernel,
        name="backward",
        out_shape=grid_type,
        in_specs=[vmem()] * 3 + [untouched()],
        out_specs=vmem(),
        compiler_params=params,
    )(padded_grad, mask, band_backward, total)

    weight_share, bias_share = pl.pallas_call(
        finish_kernel,
        name="finish",
        out_shape=[
            jax.ShapeDtypeStruct((channels, shard), F32),
            jax.ShapeDtypeStruct((1, count), F32),
        ],
        in_specs=[vmem()] * 2,
        out_specs=[vmem()] * 2,
        compiler_params=params,
    )(total[0], other[0])
    return (
        block_output.reshape(features.shape),
        grad_input.reshape(features.shape),
        weight_share.T,
        bias_share.reshape(count),
    )


def solution(mesh):
    placed = (
        P("dp", "space", None, None, None),
        P("dp", "space", None),
        P("dp", "space"),
        P("dp", "space", None, None),
        P("dp", "space", None),
        P("dp", None),
        P("dp"),
        P("dp", "space", None, None, None),
    )
    return jax.shard_map(
        body,
        mesh=mesh,
        in_specs=placed,
        out_specs=(
            P("dp", "space", None, None, None),
            P("dp", "space", None, None, None),
            P("dp", None),
            P("dp"),
        ),
        check_vma=False,
    )
```

```python
import functools

import jax
import jax.numpy as jnp
from jax import lax
from jax.experimental import pallas as pl
from jax.experimental.pallas import tpu as pltpu
from jax.sharding import PartitionSpec as P

F32 = jnp.float32
BF16 = jnp.bfloat16
LANES = 128
UNIT_ROWS = 32
Z_ROWS = 64
SWAPS = (
    ((1, 1), (2, 1), (1, 0), (2, 0)),
    ((2, 1), (1, 1), (2, 0), (1, 0)),
)


def vmem():
    return pl.BlockSpec(memory_space=pltpu.VMEM)


def smem():
    return pl.BlockSpec(memory_space=pltpu.SMEM)


def untouched():
    return pl.BlockSpec(memory_space=pl.ANY)


def offset_number(ox, oy, oz):
    flat = (ox + 1) * 9 + (oy + 1) * 3 + (oz + 1)
    return flat if flat < 13 else flat - 1


def low_half(shape):
    return lax.broadcasted_iota(jnp.int32, shape, len(shape) - 1) % LANES < 64


def chunk_rows(block):
    return [block[8 * q : 8 * q + 8] for q in range(4)]


def upward(device, distance):
    return lax.rem(lax.div(device, distance), 2)


def pack_units(values, send, outs):
    slots = values.shape[1] // 64 - 1
    reach = len(outs) // 2
    low = low_half((64, LANES))
    device = lax.axis_index("space")
    odd = lax.rem(lax.axis_index("dp"), 2)
    for number, out in enumerate(outs):
        column = reach
        if number > 0:
            columns = []
            for distance, turn in (SWAPS[0][number - 1], SWAPS[1][number - 1]):
                up = upward(device, distance) == turn
                columns.append(jnp.where(up, reach + distance, reach - distance))
            column = jnp.where(odd == 0, columns[0], columns[1])

        def base(link):
            unit = send[column, 0, link]
            slot = jnp.where(unit < 0, slots, (unit * 43) >> 8)
            return pl.multiple_of(slot * 64, 64)

        for half in range(2):
            for face in range(4):
                start = base(half * 6 + face)
                if face < 2:
                    where = pl.ds(start + 56 * face, 8)
                else:
                    where = pl.ds(start + 7 * (face - 2), 8, stride=8)
                packed = jnp.concatenate([values[q, where, :] for q in range(4)], axis=0)
                at = (half * 4 + face) * UNIT_ROWS
                out[at : at + UNIT_ROWS, :] = packed.astype(BF16)
            first = values[0, pl.ds(base(half * 6 + 4), 64), :]
            last = values[3, pl.ds(base(half * 6 + 5), 64), :]
            at = 8 * UNIT_ROWS + half * Z_ROWS
            out[at : at + Z_ROWS, :] = jnp.where(low, first, last).astype(BF16)


def prepare_kernel(
    features_hbm, occupancy_hbm, send_hbm, listing_hbm, weight_hbm, bias_hbm, counts,
    masked_out, mask_out, rows_out, send_out, shard_out, u0, u1, u2, u3, u4,
    values, features, occupancy, listing, weight_t, bias, rows, sems,
):
    copies = [
        pltpu.make_async_copy(src, dst, sems.at[i])
        for i, (src, dst) in enumerate(
            (
                (occupancy_hbm, occupancy),
                (features_hbm, features),
                (send_hbm, send_out),
                (listing_hbm, listing),
                (weight_hbm, weight_t),
                (bias_hbm, bias),
            )
        )
    ]
    for copy in copies:
        copy.start()
    bricks = features.shape[0]
    shard_out[...] = jnp.zeros(shard_out.shape, BF16)
    values[:, bricks * 64 :, :] = jnp.zeros((4, 64, LANES), F32)
    row = lax.broadcasted_iota(jnp.int32, (64, 512), 0)
    col = lax.broadcasted_iota(jnp.int32, (64, 512), 1)
    same = (col >> 3) == row
    z_row = lax.broadcasted_iota(jnp.int32, (512, 512), 0) & 7
    z_col = lax.broadcasted_iota(jnp.int32, (512, 512), 1) >> 6
    expand = jnp.where(z_row == z_col, 1.0, 0.0).astype(BF16)

    copies[3].wait()
    device = lax.axis_index("space")
    number = listing[...]
    column = (number * 43) >> 9
    link = number - column * 12
    half = (link >= 6).astype(jnp.int32)
    face = link - 6 * half
    block = jnp.zeros(number.shape, jnp.int32)
    odd = lax.rem(lax.axis_index("dp"), 2)
    for distance in (1, 2):
        up = upward(device, distance)
        first, second = (
            jnp.where(
                odd == 0,
                SWAPS[0].index((distance, turn)) + 1,
                SWAPS[1].index((distance, turn)) + 1,
            )
            for turn in range(2)
        )
        block = jnp.where(column == 2 - distance, jnp.where(up == 0, first, second), block)
        block = jnp.where(column == 2 + distance, jnp.where(up == 0, second, first), block)
    base = block * (8 * UNIT_ROWS + 2 * Z_ROWS)
    plain = base + (half * 4 + face) * UNIT_ROWS
    paired = base + 8 * UNIT_ROWS + half * Z_ROWS
    none = 5 * (8 * UNIT_ROWS + 2 * Z_ROWS)
    rows[...] = jnp.where(number < 0, none, jnp.where(face < 4, plain, paired))
    last = pltpu.make_async_copy(rows, rows_out, sems.at[len(copies)])
    last.start()

    copies[0].wait()
    live = lax.broadcasted_iota(jnp.int32, (bricks, 512), 0) < counts[0, 0]
    occ = jnp.where(live, occupancy[...], 0).astype(F32)
    spread = jnp.concatenate(
        [jnp.where(same, occ[b : b + 1, :], 0.0) for b in range(bricks)], axis=0
    ).astype(BF16)
    mask = jnp.dot(spread, expand, preferred_element_type=F32)
    mask_out[...] = mask.astype(BF16).reshape(mask_out.shape)
    copies[1].wait()
    value = features[...].astype(F32).reshape(bricks * 64, 512) * mask
    masked_out[...] = value.astype(BF16).reshape(masked_out.shape)
    for q in range(4):
        values[q, 0 : bricks * 64, :] = value[:, q * LANES : (q + 1) * LANES]
    copies[2].wait()
    pack_units(values, send_out, (u0, u1, u2, u3, u4))

    copies[4].wait()
    copies[5].wait()
    shard = weight_t.shape[1]
    lead = shard // LANES * LANES
    count = bias.shape[1]
    shard_out[:, 0:lead] = weight_t[:, 0:lead]
    tile = jnp.concatenate(
        [weight_t[:, lead:shard].astype(F32), jnp.zeros((64, lead + LANES - shard), F32)], axis=1
    )
    offset = shard - lead
    behind = jnp.concatenate(
        [bias[...].astype(F32), jnp.zeros((1, LANES - count), F32)], axis=1
    )
    behind = pltpu.roll(jnp.broadcast_to(behind, (64, LANES)), offset, 1)
    first = lax.broadcasted_iota(jnp.int32, (64, LANES), 0) == 0
    lane = lax.broadcasted_iota(jnp.int32, (64, LANES), 1)
    behind = jnp.where(first & (lane >= offset) & (lane < offset + count), behind, 0.0)
    shard_out[:, lead : lead + LANES] = (tile + behind).astype(BF16)
    last.wait()


def gather_units(table, received):
    at = 0
    for part in received:
        table[at : at + part.shape[0], :] = part[...]
        at += part.shape[0]
    table[at:, :] = jnp.zeros((table.shape[0] - at, LANES), BF16)


def assemble(source, table, rows, windows, sides, walls):
    low8 = low_half((8, LANES))
    sub = lax.broadcasted_iota(jnp.int32, (8, LANES), 0)
    top, bottom = sub == 0, sub == 7

    def put(pair, half, bit, per_brick):
        for e in range(3):
            stacked = [
                jnp.concatenate([per_brick[0][e][i], per_brick[1][e][i]], axis=0)
                for i in range(5)
            ]
            low16 = low_half((16, LANES))
            before = [stacked[4]] + stacked[:3]
            after = stacked[1:4] + [stacked[4]]
            for q in range(4):
                windows[e, q, pair, half, bit, :, 0:LANES] = stacked[q].astype(BF16)
                windows[e, q, pair, half, bit, :, LANES:] = jnp.where(
                    low16, after[q], before[q]
                ).astype(BF16)

    def one_pair(pair, carry):
        def unit(brick, ox, oy, oz):
            return pl.multiple_of(rows[brick, offset_number(ox, oy, oz)], UNIT_ROWS)

        def plane(brick, ox, oy):
            chunks = chunk_rows(table[pl.ds(unit(brick, ox, oy, 0), UNIT_ROWS), :].astype(F32))
            after = table[pl.ds(unit(brick, ox, oy, 1), UNIT_ROWS), :].astype(F32)[0:8]
            before = table[pl.ds(unit(brick, ox, oy, -1), UNIT_ROWS), :].astype(F32)[24:32]
            return chunks + [jnp.where(low8, after, before)]

        for b2 in range(2):
            brick = pair * 2 + b2
            low64 = low_half((64, LANES))
            after = table[pl.ds(unit(brick, 0, 0, 1), Z_ROWS), :].astype(F32)
            before = table[pl.ds(unit(brick, 0, 0, -1), Z_ROWS), :].astype(F32)
            walls[b2] = jnp.where(low64, after, before)
            for side, oy in enumerate((-1, 1)):
                for i, part in enumerate(plane(brick, 0, oy)):
                    sides[b2, side, i] = part

        for ox in (-1, 1):
            per_brick = []
            for b2 in range(2):
                brick = pair * 2 + b2
                centre = plane(brick, ox, 0)
                lower = plane(brick, ox, -1)
                upper = plane(brick, ox, 1)
                per_brick.append(
                    [
                        [
                            pltpu.roll(jnp.where(bottom, l, c), 1, 0)
                            for l, c in zip(lower, centre)
                        ],
                        centre,
                        [
                            pltpu.roll(jnp.where(top, u, c), 7, 0)
                            for u, c in zip(upper, centre)
                        ],
                    ]
                )
            put(pair, 0 if ox < 0 else 4, 0 if ox < 0 else 1, per_brick)

        def two_x(i, carry):
            for bit in range(2):
                x = 2 * i + bit
                per_brick = []
                for b2 in range(2):
                    brick = pair * 2 + b2
                    block = source[brick, i, bit].astype(F32)
                    centre = [block[:, q * LANES : (q + 1) * LANES] for q in range(4)]
                    centre.append(walls[b2, pl.ds(pl.multiple_of(x * 8, 8), 8), :])
                    lower = [
                        jnp.broadcast_to(sides[b2, 0, n, pl.ds(x, 1), :], (8, LANES))
                        for n in range(5)
                    ]
                    upper = [
                        jnp.broadcast_to(sides[b2, 1, n, pl.ds(x, 1), :], (8, LANES))
                        for n in range(5)
                    ]
                    per_brick.append(
                        [
                            [
                                jnp.where(top, l, pltpu.roll(c, 1, 0))
                                for l, c in zip(lower, centre)
                            ],
                            centre,
                            [
                                jnp.where(bottom, u, pltpu.roll(c, 7, 0))
                                for u, c in zip(upper, centre)
                            ],
                        ]
                    )
                put(pair, i + bit, 1 - bit, per_brick)
            return carry

        return lax.fori_loop(0, 4, two_x, carry)

    lax.fori_loop(0, windows.shape[2], one_pair, 0)


def row_block(d, e):
    return slice((3 * d + e) * 256, (3 * d + e + 1) * 256)


def tap_rows(windows, d, e):
    block = windows[e, :, :, d // 2 : d // 2 + 4, d % 2]
    return block.reshape(-1, block.shape[-1])


def all_taps(windows):
    return jnp.concatenate(
        [tap_rows(windows, d, e) for d in range(4) for e in range(3)], axis=1
    )


def chunk_places(bricks):
    return [(2 * pair + b2, i) for pair in range(bricks // 2) for i in range(4) for b2 in range(2)]


def chunk_of(ref, q):
    lanes = slice(q * LANES, (q + 1) * LANES)
    return jnp.concatenate(
        [
            jnp.concatenate([ref[b, i, x, :, lanes].astype(F32) for x in range(2)], axis=1)
            for b, i in chunk_places(ref.shape[0])
        ],
        axis=0,
    )


def put_chunk(ref, q, value):
    for n, (b, i) in enumerate(chunk_places(ref.shape[0])):
        for x in range(2):
            part = value[8 * n : 8 * n + 8, x * LANES : (x + 1) * LANES]
            ref[b, i, x, :, q * LANES : (q + 1) * LANES] = part.astype(ref.dtype)


def weights_kernel(*refs, shard, groups):
    shards = refs[:groups]
    forward_out, backward_out, bias_out, gathered, flat, shifted = refs[groups:]
    me = lax.axis_index("dp")
    for m, part in enumerate(shards):
        gathered[m] = part[...]
    for k in range(groups):
        flat[:, k * shard : (k + 1) * shard] = gathered[me ^ k][:, 0:shard].astype(F32)
    total = groups * shard
    flat[:, total:] = jnp.zeros((64, flat.shape[1] - total), F32)
    shifted[:, :] = pltpu.roll(flat[...], flat.shape[1] - 64, 1)
    low = low_half((64, LANES))
    for e in range(3):
        for x in range(2):
            half = slice(x * LANES, (x + 1) * LANES)
            for out in (forward_out, backward_out):
                out[row_block(3 * (1 - x), e), half] = jnp.zeros((256, LANES), BF16)
    for ae in range(9):
        a, e = ae // 3, ae % 3
        one = taps_pair(flat, shifted, 3 * ae)
        two = jnp.where(low, taps_pair(flat, shifted, 3 * ae + 2), 0.0)
        late = jnp.concatenate([one, two], axis=1)
        band = jnp.transpose(jnp.concatenate([pltpu.roll(late, 192, 1), late], axis=0)).astype(BF16)
        for x in range(2):
            forward_out[row_block(a + x, e), x * LANES : (x + 1) * LANES] = band
    for ae in range(9):
        a, e = ae // 3, ae % 3
        m = 3 * (8 - ae)
        first = taps_pair(flat, shifted, m)
        second = taps_pair(flat, shifted, m + 1)
        third = taps_pair(flat, shifted, m + 2)
        band = jnp.concatenate(
            [
                second,
                first,
                jnp.where(low, 0.0, pltpu.roll(first, 64, 1)),
                jnp.where(low, third, 0.0),
            ],
            axis=0,
        ).astype(BF16)
        for x in range(2):
            backward_out[row_block(a + x, e), x * LANES : (x + 1) * LANES] = band

    lane = lax.broadcasted_iota(jnp.int32, (8, LANES), 1)
    bias_lane = shard % LANES
    bias_tile = shard - bias_lane
    count = 64 // groups
    bias_row = jnp.zeros((8, LANES), F32)
    for k in range(groups):
        tile = gathered[me ^ k][0:16, bias_tile : bias_tile + LANES].astype(F32)[0:8]
        moved = pltpu.roll(tile, (count * k - bias_lane) % LANES, 1)
        bias_row += jnp.where((lane >= count * k) & (lane < count * (k + 1)), moved, 0.0)
    bias_out[...] = bias_row + pltpu.roll(bias_row, 64, 1)


def taps_pair(flat, shifted, first):
    if first % 2 == 0:
        return flat[:, first * 64 : first * 64 + LANES]
    return shifted[:, (first - 1) * 64 : (first - 1) * 64 + LANES]


def forward_kernel(
    masked, mask, cotangent_hbm, toeplitz, bias, rows, send, r0, r1, r2, r3, r4,
    block_out, grad_out, keep_out, give_out, u0, u1, u2, u3, u4,
    table, windows, sides, walls, flat, shifted, values, flipped, cotangent, sem, *, shard,
):
    fetch = pltpu.make_async_copy(cotangent_hbm, cotangent, sem)
    fetch.start()
    groups = 2 * keep_out.shape[0]
    bricks = masked.shape[0]
    pairs = bricks // 2
    gather_units(table, (r0, r1, r2, r3, r4))
    assemble(masked, table, rows, windows, sides, walls)
    bias_lane = shard % LANES
    bias_tile = shard - bias_lane
    bias_row = bias[0:1, :]
    fetch.wait()
    values[:, bricks * 64 :, :] = jnp.zeros((4, 64, LANES), F32)

    bias_row = jnp.concatenate([bias_row, bias_row], axis=1)
    total = jnp.dot(all_taps(windows), toeplitz[...], preferred_element_type=F32)
    rows_of_chunk = total.shape[0] // 4
    bias_sum = jnp.zeros((8, 256), F32)
    for q in range(4):
        p = total[q * rows_of_chunk : (q + 1) * rows_of_chunk] + bias_row
        active = chunk_of(mask, q)
        sig = jax.nn.sigmoid(p)
        put_chunk(block_out, q, p * sig * active)
        grad = (chunk_of(cotangent, q) * sig * (1.0 + p * (1.0 - sig)) * active).astype(BF16)
        wide = grad.astype(F32)
        put_chunk(grad_out, q, wide)
        for n, (brick, i) in enumerate(chunk_places(bricks)):
            for x in range(2):
                at = brick * 64 + (2 * i + x) * 8
                values[q, at : at + 8, :] = wide[
                    8 * n : 8 * n + 8, x * LANES : (x + 1) * LANES
                ]
        flipped[:, q * rows_of_chunk : (q + 1) * rows_of_chunk] = jnp.transpose(wide).astype(BF16)
        bias_sum += jnp.sum(wide.reshape(-1, 8, 256), axis=0)
    bias_sum = bias_sum[:, 0:LANES] + bias_sum[:, LANES:]
    pack_units(values, send, (u0, u1, u2, u3, u4))

    for ae in range(9):
        a, e = ae // 3, ae % 3
        both = jnp.zeros((LANES, 256), F32)
        for x in range(2):
            rows = tap_rows(windows, a + x, e)
            for part in range(0, rows.shape[0], 256):
                both += jnp.dot(
                    flipped[x * LANES : (x + 1) * LANES, part : part + 256],
                    rows[part : part + 256],
                    preferred_element_type=F32,
                )
        flat[:, 192 * ae : 192 * ae + 256] = both[64:] + pltpu.roll(both[0:64], 64, 1)

    width = keep_out.shape[2]
    bias_all = jnp.sum(bias_sum, axis=0, keepdims=True)
    bias_all = jnp.broadcast_to(bias_all, (8, LANES))
    bias_all = bias_all + pltpu.roll(bias_all, 64, 1)
    bias_all = pltpu.roll(bias_all, bias_lane, 1)
    row8 = lax.broadcasted_iota(jnp.int32, (8, LANES), 0)
    lane8 = lax.broadcasted_iota(jnp.int32, (8, LANES), 1)
    keep = (row8 == 0) & (lane8 >= bias_lane) & (lane8 < bias_lane + 64)
    me = lax.axis_index("dp")
    for k in range(groups):
        part = flat[:, k * shard : (k + 1) * shard]
        shifted[0:64, 0:shard] = part
        shifted[0:64, shard:width] = jnp.zeros((64, width - shard), F32)
        tile = shifted[0:8, bias_tile : bias_tile + LANES]
        shifted[0:8, bias_tile : bias_tile + LANES] = jnp.where(keep, bias_all, tile)
        block = shifted[0:64, 0:width].astype(BF16)
        for m in range(groups):

            @pl.when(me ^ m == k)
            def _(m=m, block=block):
                (give_out if m % 2 else keep_out)[m // 2] = block


def assemble_kernel(grad, rows, r0, r1, r2, r3, r4, after, windows, table, sides, walls):
    del after
    gather_units(table, (r0, r1, r2, r3, r4))
    assemble(grad, table, rows, windows, sides, walls)


def sum_kernel(*refs, operands, parts):
    total = (refs[0][...].astype(F32) + refs[1][...].astype(F32)).astype(BF16)
    for part in range(parts):
        for row in range(part, total.shape[0], parts):
            refs[operands + part][row // parts] = total[row]


def sum_after(mine, other, after=(), through=(), parts=1):
    operands = 2 + len(after) + len(through)
    share = jax.ShapeDtypeStruct((mine.shape[0] // parts, *mine.shape[1:]), mine.dtype)
    outs = pl.pallas_call(
        functools.partial(sum_kernel, operands=operands, parts=parts),
        name="sum",
        out_shape=[share] * parts + [jax.ShapeDtypeStruct(x.shape, x.dtype) for x in through],
        in_specs=[vmem()] * 2 + [untouched()] * (operands - 2),
        out_specs=[vmem()] * parts + [untouched()] * len(through),
        input_output_aliases={2 + len(after) + i: parts + i for i in range(len(through))},
        compiler_params=pltpu.CompilerParams(vmem_limit_bytes=1024 * 1024),
    )(mine, other, *after, *through)
    return list(outs[:parts]), list(outs[parts:])


def backward_kernel(windows, mask, toeplitz, after, out):
    del after
    total = jnp.dot(all_taps(windows), toeplitz[...], preferred_element_type=F32)
    rows_of_chunk = total.shape[0] // 4
    for q in range(4):
        part = total[q * rows_of_chunk : (q + 1) * rows_of_chunk]
        put_chunk(out, q, part * chunk_of(mask, q))


def finish_kernel(mine, other, weight_out, bias_out):
    shard = weight_out.shape[1]
    count = bias_out.shape[1]
    total = mine[...].astype(F32) + other[...].astype(F32)
    weight_out[...] = total[:, 0:shard]
    bias_lane = shard % LANES
    bias_tile = shard - bias_lane
    tile = total[0:8, bias_tile : bias_tile + LANES]
    me = lax.axis_index("dp")
    moved = pltpu.roll(tile, 2 * LANES - bias_lane - me * count, 1)
    bias_out[...] = moved[0:1, 0:count]


def swapped(block, axis, bit):
    return lax.ppermute(block, axis, [(i, i ^ bit) for i in range(lax.axis_size(axis))])


def by_parity(block, routes):
    groups = lax.axis_size("dp")
    pairs = [
        (source * groups + group, target * groups + group)
        for group in range(groups)
        for source, target in routes[group % 2]
    ]
    return lax.ppermute(block, ("space", "dp"), pairs)


def exchanged(number, unit):
    routes = []
    for swaps in SWAPS:
        distance, turn = swaps[number - 1]
        route = []
        for low in range(lax.axis_size("space") - distance):
            if low // distance % 2 == turn:
                route += [(low, low + distance), (low + distance, low)]
        routes.append(route)
    return by_parity(unit, routes)


def space_steps():
    bits = []
    while 2 ** len(bits) < lax.axis_size("space"):
        bits.append(2 ** len(bits))
    return list(zip(bits[1:] + bits[:1], bits))


def stepped(total, step):
    devices = range(lax.axis_size("space"))
    return by_parity(total, [[(i, i ^ bit) for i in devices] for bit in step])


def body(features, occupancy, counts, send_units, neighbours, weight, conv_bias, cotangent):
    bricks, edge, _, lanes = features.shape[1:]
    grid_shape = (bricks, edge // 2, 2, edge, lanes)
    pairs = bricks // 2
    spread, links = send_units.shape[2:]
    shard, channels = weight.shape
    groups = lax.axis_size("dp")
    count = conv_bias.shape[0]
    width = -(-(shard + channels) // LANES) * LANES
    unit_rows = 8 * UNIT_ROWS + 2 * Z_ROWS
    units_type = jax.ShapeDtypeStruct((unit_rows, LANES), BF16)
    grid_type = jax.ShapeDtypeStruct(grid_shape, BF16)
    shard_type = jax.ShapeDtypeStruct((channels, width), BF16)
    params = pltpu.CompilerParams(vmem_limit_bytes=48 * 1024 * 1024)
    rows_shape = neighbours.shape[1:]
    send_shape = (spread, 1, links)

    masked, mask, rows, send, own_shard, *units = pl.pallas_call(
        prepare_kernel,
        name="prepare",
        out_shape=[
            grid_type,
            grid_type,
            jax.ShapeDtypeStruct(rows_shape, jnp.int32),
            jax.ShapeDtypeStruct(send_shape, jnp.int32),
            shard_type,
        ]
        + [units_type] * spread,
        in_specs=[pl.BlockSpec(memory_space=pltpu.HBM)] * 6 + [smem()],
        out_specs=[vmem(), vmem(), smem(), smem(), vmem()] + [vmem()] * spread,
        scratch_shapes=[
            pltpu.VMEM((4, (bricks + 1) * 64, LANES), F32),
            pltpu.VMEM(grid_shape, BF16),
            pltpu.VMEM(occupancy.shape[1:], jnp.int32),
            pltpu.VMEM(rows_shape, jnp.int32),
            pltpu.VMEM((channels, shard), BF16),
            pltpu.VMEM((1, count), BF16),
            pltpu.VMEM(rows_shape, jnp.int32),
            pltpu.SemaphoreType.DMA((7,)),
        ],
        compiler_params=params,
    )(
        *(
            pltpu.with_memory_space_constraint(operand, pltpu.HBM)
            for operand in (
                features.reshape(grid_shape),
                occupancy[0],
                send_units.transpose(0, 2, 1, 3).reshape(send_shape),
                neighbours[0],
                weight.T,
                conv_bias.reshape(1, count),
            )
        ),
        counts,
    )

    shards = {0: own_shard}
    bit = groups // 2
    while bit:
        for m in list(shards):
            shards[m | bit] = swapped(shards[m], "dp", bit)
        bit //= 2
    received = units[:1] + [exchanged(number, units[number]) for number in range(1, spread)]

    flat = pltpu.VMEM((channels, 28 * 64), F32)
    band_forward, band_backward, bias = pl.pallas_call(
        functools.partial(weights_kernel, shard=shard, groups=groups),
        name="weights",
        out_shape=[
            jax.ShapeDtypeStruct((12 * 256, 256), BF16),
            jax.ShapeDtypeStruct((12 * 256, 256), BF16),
            jax.ShapeDtypeStruct((8, LANES), F32),
        ],
        in_specs=[vmem()] * groups,
        out_specs=[vmem()] * 3,
        scratch_shapes=[pltpu.VMEM((groups, channels, width), BF16), flat, flat],
        compiler_params=params,
    )(*(shards[m] for m in range(groups)))

    table = pltpu.VMEM((spread * unit_rows + Z_ROWS, LANES), BF16)
    windows = pltpu.VMEM((3, 4, pairs, 5, 2, 16, 256), BF16)
    sides = pltpu.VMEM((2, 2, 5, 8, LANES), F32)
    walls = pltpu.VMEM((2, 64, LANES), F32)
    half_type = jax.ShapeDtypeStruct((groups // 2, channels, width), BF16)
    block_output, grad, keep, give, *grad_units = pl.pallas_call(
        functools.partial(forward_kernel, shard=shard),
        name="forward",
        out_shape=[grid_type, grid_type, half_type, half_type] + [units_type] * spread,
        in_specs=[vmem(), vmem(), pl.BlockSpec(memory_space=pltpu.HBM), vmem(), vmem()]
        + [smem(), smem()]
        + [vmem()] * spread,
        out_specs=[vmem()] * (4 + spread),
        scratch_shapes=[
            table,
            windows,
            sides,
            walls,
            flat,
            pltpu.VMEM((channels, 4 * LANES), F32),
            pltpu.VMEM((4, (bricks + 1) * 64, LANES), F32),
            pltpu.VMEM((256, bricks * LANES), BF16),
            pltpu.VMEM(grid_shape, BF16),
            pltpu.SemaphoreType.DMA,
        ],
        compiler_params=params,
    )(
        masked,
        mask,
        pltpu.with_memory_space_constraint(cotangent.reshape(grid_shape), pltpu.HBM),
        band_forward,
        bias,
        rows,
        send,
        *received,
    )

    later = grad_units[2:]
    bit = 1
    while 2 * bit < groups:
        first = later[:1] if bit == 1 else []
        (keep, give), first = sum_after(keep, swapped(give, "dp", bit), through=first, parts=2)
        later = first + later[1:] if bit == 1 else later
        bit *= 2
    grad_received = [grad_units[0], exchanged(1, grad_units[1])]
    (total,), last = sum_after(keep, swapped(give, "dp", bit), grad_received[1:], later[1:])
    for number, unit in enumerate([later[0], *last], 2):
        grad_received.append(exchanged(number, unit))

    steps = space_steps()
    other = stepped(total, steps[0])
    if len(steps) > 1:
        (total,), _ = sum_after(total, other, grad_received[3:4])
        other = stepped(total, steps[1])

    padded_grad = pl.pallas_call(
        assemble_kernel,
        name="assemble",
        out_shape=jax.ShapeDtypeStruct(windows.shape, BF16),
        in_specs=[vmem()] + [smem()] + [vmem()] * spread + [untouched()],
        out_specs=vmem(),
        scratch_shapes=[table, sides, walls],
        compiler_params=params,
    )(grad, rows, *grad_received, total)

    for number, step in enumerate(steps[2:]):
        (total,), _ = sum_after(total, other, [] if number else [padded_grad])
        other = stepped(total, step)

    grad_input = pl.pallas_call(
        backward_kernel,
        name="backward",
        out_shape=grid_type,
        in_specs=[vmem()] * 3 + [untouched()],
        out_specs=vmem(),
        compiler_params=params,
    )(padded_grad, mask, band_backward, total)

    weight_share, bias_share = pl.pallas_call(
        finish_kernel,
        name="finish",
        out_shape=[
            jax.ShapeDtypeStruct((channels, shard), F32),
            jax.ShapeDtypeStruct((1, count), F32),
        ],
        in_specs=[vmem()] * 2,
        out_specs=[vmem()] * 2,
        compiler_params=params,
    )(total[0], other[0])
    return (
        block_output.reshape(features.shape),
        grad_input.reshape(features.shape),
        weight_share.T,
        bias_share.reshape(count),
    )


def solution(mesh):
    placed = (
        P("dp", "space", None, None, None),
        P("dp", "space", None),
        P("dp", "space"),
        P("dp", "space", None, None),
        P("dp", "space", None),
        P("dp", None),
        P("dp"),
        P("dp", "space", None, None, None),
    )
    return jax.shard_map(
        body,
        mesh=mesh,
        in_specs=placed,
        out_specs=(
            P("dp", "space", None, None, None),
            P("dp", "space", None, None, None),
            P("dp", None),
            P("dp"),
        ),
        check_vma=False,
    )
```

```python
import functools

import jax
import jax.numpy as jnp
from jax import lax
from jax.experimental import pallas as pl
from jax.experimental.pallas import tpu as pltpu
from jax.sharding import PartitionSpec as P

F32 = jnp.float32
BF16 = jnp.bfloat16
LANES = 128
UNIT_ROWS = 32
Z_ROWS = 64
SWAPS = (
    ((1, 1), (2, 1), (1, 0), (2, 0)),
    ((2, 1), (1, 1), (2, 0), (1, 0)),
)


def vmem():
    return pl.BlockSpec(memory_space=pltpu.VMEM)


def smem():
    return pl.BlockSpec(memory_space=pltpu.SMEM)


def untouched():
    return pl.BlockSpec(memory_space=pl.ANY)


def offset_number(ox, oy, oz):
    flat = (ox + 1) * 9 + (oy + 1) * 3 + (oz + 1)
    return flat if flat < 13 else flat - 1


def low_half(shape):
    return lax.broadcasted_iota(jnp.int32, shape, len(shape) - 1) % LANES < 64


def chunk_rows(block):
    return [block[8 * q : 8 * q + 8] for q in range(4)]


def upward(device, distance):
    return lax.rem(lax.div(device, distance), 2)


def pack_units(values, send, outs):
    slots = values.shape[1] // 64 - 1
    reach = len(outs) // 2
    low = low_half((64, LANES))
    device = lax.axis_index("space")
    odd = lax.rem(lax.axis_index("dp"), 2)
    for number, out in enumerate(outs):
        column = reach
        if number > 0:
            columns = []
            for distance, turn in (SWAPS[0][number - 1], SWAPS[1][number - 1]):
                up = upward(device, distance) == turn
                columns.append(jnp.where(up, reach + distance, reach - distance))
            column = jnp.where(odd == 0, columns[0], columns[1])

        def base(link):
            unit = send[column, 0, link]
            slot = jnp.where(unit < 0, slots, (unit * 43) >> 8)
            return pl.multiple_of(slot * 64, 64)

        for half in range(2):
            for face in range(4):
                start = base(half * 6 + face)
                if face < 2:
                    where = pl.ds(start + 56 * face, 8)
                else:
                    where = pl.ds(start + 7 * (face - 2), 8, stride=8)
                packed = jnp.concatenate([values[q, where, :] for q in range(4)], axis=0)
                at = (half * 4 + face) * UNIT_ROWS
                out[at : at + UNIT_ROWS, :] = packed.astype(BF16)
            first = values[0, pl.ds(base(half * 6 + 4), 64), :]
            last = values[3, pl.ds(base(half * 6 + 5), 64), :]
            at = 8 * UNIT_ROWS + half * Z_ROWS
            out[at : at + Z_ROWS, :] = jnp.where(low, first, last).astype(BF16)


def prepare_kernel(
    features_hbm, occupancy_hbm, send_hbm, listing_hbm, weight_hbm, bias_hbm, counts,
    masked_out, mask_out, rows_out, send_out, shard_out, u0, u1, u2, u3, u4,
    values, features, occupancy, listing, weight_t, bias, rows, sems,
):
    copies = [
        pltpu.make_async_copy(src, dst, sems.at[i])
        for i, (src, dst) in enumerate(
            (
                (occupancy_hbm, occupancy),
                (features_hbm, features),
                (send_hbm, send_out),
                (listing_hbm, listing),
                (weight_hbm, weight_t),
                (bias_hbm, bias),
            )
        )
    ]
    for copy in copies:
        copy.start()
    bricks = features.shape[0]
    shard_out[...] = jnp.zeros(shard_out.shape, BF16)
    values[:, bricks * 64 :, :] = jnp.zeros((4, 64, LANES), F32)
    row = lax.broadcasted_iota(jnp.int32, (64, 512), 0)
    col = lax.broadcasted_iota(jnp.int32, (64, 512), 1)
    same = (col >> 3) == row
    z_row = lax.broadcasted_iota(jnp.int32, (512, 512), 0) & 7
    z_col = lax.broadcasted_iota(jnp.int32, (512, 512), 1) >> 6
    expand = jnp.where(z_row == z_col, 1.0, 0.0).astype(BF16)

    copies[3].wait()
    device = lax.axis_index("space")
    number = listing[...]
    column = (number * 43) >> 9
    link = number - column * 12
    half = (link >= 6).astype(jnp.int32)
    face = link - 6 * half
    block = jnp.zeros(number.shape, jnp.int32)
    odd = lax.rem(lax.axis_index("dp"), 2)
    for distance in (1, 2):
        up = upward(device, distance)
        first, second = (
            jnp.where(
                odd == 0,
                SWAPS[0].index((distance, turn)) + 1,
                SWAPS[1].index((distance, turn)) + 1,
            )
            for turn in range(2)
        )
        block = jnp.where(column == 2 - distance, jnp.where(up == 0, first, second), block)
        block = jnp.where(column == 2 + distance, jnp.where(up == 0, second, first), block)
    base = block * (8 * UNIT_ROWS + 2 * Z_ROWS)
    plain = base + (half * 4 + face) * UNIT_ROWS
    paired = base + 8 * UNIT_ROWS + half * Z_ROWS
    none = 5 * (8 * UNIT_ROWS + 2 * Z_ROWS)
    rows[...] = jnp.where(number < 0, none, jnp.where(face < 4, plain, paired))
    last = pltpu.make_async_copy(rows, rows_out, sems.at[len(copies)])
    last.start()

    copies[0].wait()
    live = lax.broadcasted_iota(jnp.int32, (bricks, 512), 0) < counts[0, 0]
    occ = jnp.where(live, occupancy[...], 0).astype(F32)
    spread = jnp.concatenate(
        [jnp.where(same, occ[b : b + 1, :], 0.0) for b in range(bricks)], axis=0
    ).astype(BF16)
    mask = jnp.dot(spread, expand, preferred_element_type=F32)
    mask_out[...] = mask.astype(BF16).reshape(mask_out.shape)
    copies[1].wait()
    value = features[...].astype(F32).reshape(bricks * 64, 512) * mask
    masked_out[...] = value.astype(BF16).reshape(masked_out.shape)
    for q in range(4):
        values[q, 0 : bricks * 64, :] = value[:, q * LANES : (q + 1) * LANES]
    copies[2].wait()
    pack_units(values, send_out, (u0, u1, u2, u3, u4))

    copies[4].wait()
    copies[5].wait()
    shard = weight_t.shape[1]
    lead = shard // LANES * LANES
    count = bias.shape[1]
    shard_out[:, 0:lead] = weight_t[:, 0:lead]
    tile = jnp.concatenate(
        [weight_t[:, lead:shard].astype(F32), jnp.zeros((64, lead + LANES - shard), F32)], axis=1
    )
    offset = shard - lead
    behind = jnp.concatenate(
        [bias[...].astype(F32), jnp.zeros((1, LANES - count), F32)], axis=1
    )
    behind = pltpu.roll(jnp.broadcast_to(behind, (64, LANES)), offset, 1)
    first = lax.broadcasted_iota(jnp.int32, (64, LANES), 0) == 0
    lane = lax.broadcasted_iota(jnp.int32, (64, LANES), 1)
    behind = jnp.where(first & (lane >= offset) & (lane < offset + count), behind, 0.0)
    shard_out[:, lead : lead + LANES] = (tile + behind).astype(BF16)
    last.wait()


def gather_units(table, received):
    at = 0
    for part in received:
        table[at : at + part.shape[0], :] = part[...]
        at += part.shape[0]
    table[at:, :] = jnp.zeros((table.shape[0] - at, LANES), BF16)


def assemble(source, table, rows, windows, sides, walls):
    low8 = low_half((8, LANES))
    sub = lax.broadcasted_iota(jnp.int32, (8, LANES), 0)
    top, bottom = sub == 0, sub == 7

    def put(pair, half, bit, per_brick):
        for e in range(3):
            stacked = [
                jnp.concatenate([per_brick[0][e][i], per_brick[1][e][i]], axis=0)
                for i in range(5)
            ]
            low16 = low_half((16, LANES))
            before = [stacked[4]] + stacked[:3]
            after = stacked[1:4] + [stacked[4]]
            for q in range(4):
                windows[e, q, pair, half, bit, :, 0:LANES] = stacked[q].astype(BF16)
                windows[e, q, pair, half, bit, :, LANES:] = jnp.where(
                    low16, after[q], before[q]
                ).astype(BF16)

    def one_pair(pair, carry):
        def unit(brick, ox, oy, oz):
            return pl.multiple_of(rows[brick, offset_number(ox, oy, oz)], UNIT_ROWS)

        def plane(brick, ox, oy):
            chunks = chunk_rows(table[pl.ds(unit(brick, ox, oy, 0), UNIT_ROWS), :].astype(F32))
            after = table[pl.ds(unit(brick, ox, oy, 1), UNIT_ROWS), :].astype(F32)[0:8]
            before = table[pl.ds(unit(brick, ox, oy, -1), UNIT_ROWS), :].astype(F32)[24:32]
            return chunks + [jnp.where(low8, after, before)]

        for b2 in range(2):
            brick = pair * 2 + b2
            low64 = low_half((64, LANES))
            after = table[pl.ds(unit(brick, 0, 0, 1), Z_ROWS), :].astype(F32)
            before = table[pl.ds(unit(brick, 0, 0, -1), Z_ROWS), :].astype(F32)
            walls[b2] = jnp.where(low64, after, before)
            for side, oy in enumerate((-1, 1)):
                for i, part in enumerate(plane(brick, 0, oy)):
                    sides[b2, side, i] = part

        for ox in (-1, 1):
            per_brick = []
            for b2 in range(2):
                brick = pair * 2 + b2
                centre = plane(brick, ox, 0)
                lower = plane(brick, ox, -1)
                upper = plane(brick, ox, 1)
                per_brick.append(
                    [
                        [
                            pltpu.roll(jnp.where(bottom, l, c), 1, 0)
                            for l, c in zip(lower, centre)
                        ],
                        centre,
                        [
                            pltpu.roll(jnp.where(top, u, c), 7, 0)
                            for u, c in zip(upper, centre)
                        ],
                    ]
                )
            put(pair, 0 if ox < 0 else 4, 0 if ox < 0 else 1, per_brick)

        def two_x(i, carry):
            for bit in range(2):
                x = 2 * i + bit
                per_brick = []
                for b2 in range(2):
                    brick = pair * 2 + b2
                    block = source[brick, i, bit].astype(F32)
                    centre = [block[:, q * LANES : (q + 1) * LANES] for q in range(4)]
                    centre.append(walls[b2, pl.ds(pl.multiple_of(x * 8, 8), 8), :])
                    lower = [
                        jnp.broadcast_to(sides[b2, 0, n, pl.ds(x, 1), :], (8, LANES))
                        for n in range(5)
                    ]
                    upper = [
                        jnp.broadcast_to(sides[b2, 1, n, pl.ds(x, 1), :], (8, LANES))
                        for n in range(5)
                    ]
                    per_brick.append(
                        [
                            [
                                jnp.where(top, l, pltpu.roll(c, 1, 0))
                                for l, c in zip(lower, centre)
                            ],
                            centre,
                            [
                                jnp.where(bottom, u, pltpu.roll(c, 7, 0))
                                for u, c in zip(upper, centre)
                            ],
                        ]
                    )
                put(pair, i + bit, 1 - bit, per_brick)
            return carry

        return lax.fori_loop(0, 4, two_x, carry)

    lax.fori_loop(0, windows.shape[2], one_pair, 0)


def row_block(d, e):
    return slice((3 * d + e) * 256, (3 * d + e + 1) * 256)


def tap_rows(windows, d, e):
    block = windows[e, :, :, d // 2 : d // 2 + 4, d % 2]
    return block.reshape(-1, block.shape[-1])


def all_taps(windows):
    return jnp.concatenate(
        [tap_rows(windows, d, e) for d in range(4) for e in range(3)], axis=1
    )


def chunk_places(bricks):
    return [(2 * pair + b2, i) for pair in range(bricks // 2) for i in range(4) for b2 in range(2)]


def chunk_of(ref, q):
    lanes = slice(q * LANES, (q + 1) * LANES)
    return jnp.concatenate(
        [
            jnp.concatenate([ref[b, i, x, :, lanes].astype(F32) for x in range(2)], axis=1)
            for b, i in chunk_places(ref.shape[0])
        ],
        axis=0,
    )


def put_chunk(ref, q, value):
    for n, (b, i) in enumerate(chunk_places(ref.shape[0])):
        for x in range(2):
            part = value[8 * n : 8 * n + 8, x * LANES : (x + 1) * LANES]
            ref[b, i, x, :, q * LANES : (q + 1) * LANES] = part.astype(ref.dtype)


def weights_kernel(*refs, shard, groups):
    shards = refs[:groups]
    forward_out, backward_out, bias_out, gathered, flat, shifted = refs[groups:]
    me = lax.axis_index("dp")
    for m, part in enumerate(shards):
        gathered[m] = part[...]
    for k in range(groups):
        flat[:, k * shard : (k + 1) * shard] = gathered[me ^ k][:, 0:shard].astype(F32)
    total = groups * shard
    flat[:, total:] = jnp.zeros((64, flat.shape[1] - total), F32)
    shifted[:, :] = pltpu.roll(flat[...], flat.shape[1] - 64, 1)
    low = low_half((64, LANES))
    for e in range(3):
        for x in range(2):
            half = slice(x * LANES, (x + 1) * LANES)
            for out in (forward_out, backward_out):
                out[row_block(3 * (1 - x), e), half] = jnp.zeros((256, LANES), BF16)
    for ae in range(9):
        a, e = ae // 3, ae % 3
        one = taps_pair(flat, shifted, 3 * ae)
        two = jnp.where(low, taps_pair(flat, shifted, 3 * ae + 2), 0.0)
        late = jnp.concatenate([one, two], axis=1)
        band = jnp.transpose(jnp.concatenate([pltpu.roll(late, 192, 1), late], axis=0)).astype(BF16)
        for x in range(2):
            forward_out[row_block(a + x, e), x * LANES : (x + 1) * LANES] = band
    for ae in range(9):
        a, e = ae // 3, ae % 3
        m = 3 * (8 - ae)
        first = taps_pair(flat, shifted, m)
        second = taps_pair(flat, shifted, m + 1)
        third = taps_pair(flat, shifted, m + 2)
        band = jnp.concatenate(
            [
                second,
                first,
                jnp.where(low, 0.0, pltpu.roll(first, 64, 1)),
                jnp.where(low, third, 0.0),
            ],
            axis=0,
        ).astype(BF16)
        for x in range(2):
            backward_out[row_block(a + x, e), x * LANES : (x + 1) * LANES] = band

    lane = lax.broadcasted_iota(jnp.int32, (8, LANES), 1)
    bias_lane = shard % LANES
    bias_tile = shard - bias_lane
    count = 64 // groups
    bias_row = jnp.zeros((8, LANES), F32)
    for k in range(groups):
        tile = gathered[me ^ k][0:16, bias_tile : bias_tile + LANES].astype(F32)[0:8]
        moved = pltpu.roll(tile, (count * k - bias_lane) % LANES, 1)
        bias_row += jnp.where((lane >= count * k) & (lane < count * (k + 1)), moved, 0.0)
    bias_out[...] = bias_row + pltpu.roll(bias_row, 64, 1)


def taps_pair(flat, shifted, first):
    if first % 2 == 0:
        return flat[:, first * 64 : first * 64 + LANES]
    return shifted[:, (first - 1) * 64 : (first - 1) * 64 + LANES]


def forward_kernel(
    masked, mask, cotangent_hbm, toeplitz, bias, rows, send, r0, r1, r2, r3, r4,
    block_out, grad_out, keep_out, give_out, u0, u1, u2, u3, u4,
    table, windows, sides, walls, flat, shifted, values, flipped, cotangent, sem, *, shard,
):
    fetch = pltpu.make_async_copy(cotangent_hbm, cotangent, sem)
    fetch.start()
    groups = 2 * keep_out.shape[0]
    bricks = masked.shape[0]
    pairs = bricks // 2
    gather_units(table, (r0, r1, r2, r3, r4))
    assemble(masked, table, rows, windows, sides, walls)
    bias_lane = shard % LANES
    bias_tile = shard - bias_lane
    bias_row = bias[0:1, :]
    fetch.wait()
    values[:, bricks * 64 :, :] = jnp.zeros((4, 64, LANES), F32)

    bias_row = jnp.concatenate([bias_row, bias_row], axis=1)
    total = jnp.dot(all_taps(windows), toeplitz[...], preferred_element_type=F32)
    rows_of_chunk = total.shape[0] // 4
    bias_sum = jnp.zeros((8, 256), F32)
    for q in range(4):
        p = total[q * rows_of_chunk : (q + 1) * rows_of_chunk] + bias_row
        active = chunk_of(mask, q)
        sig = jax.nn.sigmoid(p)
        put_chunk(block_out, q, p * sig * active)
        grad = (chunk_of(cotangent, q) * sig * (1.0 + p * (1.0 - sig)) * active).astype(BF16)
        wide = grad.astype(F32)
        put_chunk(grad_out, q, wide)
        for n, (brick, i) in enumerate(chunk_places(bricks)):
            for x in range(2):
                at = brick * 64 + (2 * i + x) * 8
                values[q, at : at + 8, :] = wide[
                    8 * n : 8 * n + 8, x * LANES : (x + 1) * LANES
                ]
        flipped[:, q * rows_of_chunk : (q + 1) * rows_of_chunk] = jnp.transpose(wide).astype(BF16)
        bias_sum += jnp.sum(wide.reshape(-1, 8, 256), axis=0)
    bias_sum = bias_sum[:, 0:LANES] + bias_sum[:, LANES:]
    pack_units(values, send, (u0, u1, u2, u3, u4))

    for ae in range(9):
        a, e = ae // 3, ae % 3
        both = jnp.zeros((LANES, 256), F32)
        for x in range(2):
            rows = tap_rows(windows, a + x, e)
            for part in range(0, rows.shape[0], 256):
                both += jnp.dot(
                    flipped[x * LANES : (x + 1) * LANES, part : part + 256],
                    rows[part : part + 256],
                    preferred_element_type=F32,
                )
        flat[:, 192 * ae : 192 * ae + 256] = both[64:] + pltpu.roll(both[0:64], 64, 1)

    width = keep_out.shape[2]
    bias_all = jnp.sum(bias_sum, axis=0, keepdims=True)
    bias_all = jnp.broadcast_to(bias_all, (8, LANES))
    bias_all = bias_all + pltpu.roll(bias_all, 64, 1)
    bias_all = pltpu.roll(bias_all, bias_lane, 1)
    row8 = lax.broadcasted_iota(jnp.int32, (8, LANES), 0)
    lane8 = lax.broadcasted_iota(jnp.int32, (8, LANES), 1)
    keep = (row8 == 0) & (lane8 >= bias_lane) & (lane8 < bias_lane + 64)
    me = lax.axis_index("dp")
    for k in range(groups):
        part = flat[:, k * shard : (k + 1) * shard]
        shifted[0:64, 0:shard] = part
        shifted[0:64, shard:width] = jnp.zeros((64, width - shard), F32)
        tile = shifted[0:8, bias_tile : bias_tile + LANES]
        shifted[0:8, bias_tile : bias_tile + LANES] = jnp.where(keep, bias_all, tile)
        block = shifted[0:64, 0:width].astype(BF16)
        for m in range(groups):

            @pl.when(me ^ m == k)
            def _(m=m, block=block):
                (give_out if m % 2 else keep_out)[m // 2] = block


def assemble_kernel(grad, rows, r0, r1, r2, r3, r4, after, windows, table, sides, walls):
    del after
    gather_units(table, (r0, r1, r2, r3, r4))
    assemble(grad, table, rows, windows, sides, walls)


def sum_kernel(*refs, operands, parts):
    total = (refs[0][...].astype(F32) + refs[1][...].astype(F32)).astype(BF16)
    for part in range(parts):
        for row in range(part, total.shape[0], parts):
            refs[operands + part][row // parts] = total[row]


def sum_after(mine, other, after=(), through=(), parts=1):
    operands = 2 + len(after) + len(through)
    share = jax.ShapeDtypeStruct((mine.shape[0] // parts, *mine.shape[1:]), mine.dtype)
    outs = pl.pallas_call(
        functools.partial(sum_kernel, operands=operands, parts=parts),
        name="sum",
        out_shape=[share] * parts + [jax.ShapeDtypeStruct(x.shape, x.dtype) for x in through],
        in_specs=[vmem()] * 2 + [untouched()] * (operands - 2),
        out_specs=[vmem()] * parts + [untouched()] * len(through),
        input_output_aliases={2 + len(after) + i: parts + i for i in range(len(through))},
        compiler_params=pltpu.CompilerParams(vmem_limit_bytes=1024 * 1024),
    )(mine, other, *after, *through)
    return list(outs[:parts]), list(outs[parts:])


def backward_kernel(windows, mask, toeplitz, after, out):
    del after
    total = jnp.dot(all_taps(windows), toeplitz[...], preferred_element_type=F32)
    rows_of_chunk = total.shape[0] // 4
    for q in range(4):
        part = total[q * rows_of_chunk : (q + 1) * rows_of_chunk]
        put_chunk(out, q, part * chunk_of(mask, q))


def finish_kernel(mine, other, weight_out, bias_out):
    shard = weight_out.shape[1]
    count = bias_out.shape[1]
    total = mine[...].astype(F32) + other[...].astype(F32)
    weight_out[...] = total[:, 0:shard]
    bias_lane = shard % LANES
    bias_tile = shard - bias_lane
    tile = total[0:8, bias_tile : bias_tile + LANES]
    me = lax.axis_index("dp")
    moved = pltpu.roll(tile, 2 * LANES - bias_lane - me * count, 1)
    bias_out[...] = moved[0:1, 0:count]


def swapped(block, axis, bit):
    return lax.ppermute(block, axis, [(i, i ^ bit) for i in range(lax.axis_size(axis))])


def by_parity(block, routes):
    groups = lax.axis_size("dp")
    pairs = [
        (source * groups + group, target * groups + group)
        for group in range(groups)
        for source, target in routes[group % 2]
    ]
    return lax.ppermute(block, ("space", "dp"), pairs)


def exchanged(number, unit):
    routes = []
    for swaps in SWAPS:
        distance, turn = swaps[number - 1]
        route = []
        for low in range(lax.axis_size("space") - distance):
            if low // distance % 2 == turn:
                route += [(low, low + distance), (low + distance, low)]
        routes.append(route)
    return by_parity(unit, routes)


def space_steps():
    bits = []
    while 2 ** len(bits) < lax.axis_size("space"):
        bits.append(2 ** len(bits))
    return list(zip(bits[1:] + bits[:1], bits))


def stepped(total, step):
    devices = range(lax.axis_size("space"))
    return by_parity(total, [[(i, i ^ bit) for i in devices] for bit in step])


def body(features, occupancy, counts, send_units, neighbours, weight, conv_bias, cotangent):
    bricks, edge, _, lanes = features.shape[1:]
    grid_shape = (bricks, edge // 2, 2, edge, lanes)
    pairs = bricks // 2
    spread, links = send_units.shape[2:]
    shard, channels = weight.shape
    groups = lax.axis_size("dp")
    count = conv_bias.shape[0]
    width = -(-(shard + channels) // LANES) * LANES
    unit_rows = 8 * UNIT_ROWS + 2 * Z_ROWS
    units_type = jax.ShapeDtypeStruct((unit_rows, LANES), BF16)
    grid_type = jax.ShapeDtypeStruct(grid_shape, BF16)
    shard_type = jax.ShapeDtypeStruct((channels, width), BF16)
    params = pltpu.CompilerParams(vmem_limit_bytes=48 * 1024 * 1024)
    rows_shape = neighbours.shape[1:]
    send_shape = (spread, 1, links)

    masked, mask, rows, send, own_shard, *units = pl.pallas_call(
        prepare_kernel,
        name="prepare",
        out_shape=[
            grid_type,
            grid_type,
            jax.ShapeDtypeStruct(rows_shape, jnp.int32),
            jax.ShapeDtypeStruct(send_shape, jnp.int32),
            shard_type,
        ]
        + [units_type] * spread,
        in_specs=[pl.BlockSpec(memory_space=pltpu.HBM)] * 6 + [smem()],
        out_specs=[vmem(), vmem(), smem(), smem(), vmem()] + [vmem()] * spread,
        scratch_shapes=[
            pltpu.VMEM((4, (bricks + 1) * 64, LANES), F32),
            pltpu.VMEM(grid_shape, BF16),
            pltpu.VMEM(occupancy.shape[1:], jnp.int32),
            pltpu.VMEM(rows_shape, jnp.int32),
            pltpu.VMEM((channels, shard), BF16),
            pltpu.VMEM((1, count), BF16),
            pltpu.VMEM(rows_shape, jnp.int32),
            pltpu.SemaphoreType.DMA((7,)),
        ],
        compiler_params=params,
    )(
        *(
            pltpu.with_memory_space_constraint(operand, pltpu.HBM)
            for operand in (
                features.reshape(grid_shape),
                occupancy[0],
                send_units.transpose(0, 2, 1, 3).reshape(send_shape),
                neighbours[0],
                weight.T,
                conv_bias.reshape(1, count),
            )
        ),
        counts,
    )

    shards = {0: own_shard}
    bit = groups // 2
    while bit:
        for m in list(shards):
            shards[m | bit] = swapped(shards[m], "dp", bit)
        bit //= 2
    received = units[:1] + [exchanged(number, units[number]) for number in range(1, spread)]

    flat = pltpu.VMEM((channels, 28 * 64), F32)
    band_forward, band_backward, bias = pl.pallas_call(
        functools.partial(weights_kernel, shard=shard, groups=groups),
        name="weights",
        out_shape=[
            jax.ShapeDtypeStruct((12 * 256, 256), BF16),
            jax.ShapeDtypeStruct((12 * 256, 256), BF16),
            jax.ShapeDtypeStruct((8, LANES), F32),
        ],
        in_specs=[vmem()] * groups,
        out_specs=[vmem()] * 3,
        scratch_shapes=[pltpu.VMEM((groups, channels, width), BF16), flat, flat],
        compiler_params=params,
    )(*(shards[m] for m in range(groups)))

    table = pltpu.VMEM((spread * unit_rows + Z_ROWS, LANES), BF16)
    windows = pltpu.VMEM((3, 4, pairs, 5, 2, 16, 256), BF16)
    sides = pltpu.VMEM((2, 2, 5, 8, LANES), F32)
    walls = pltpu.VMEM((2, 64, LANES), F32)
    half_type = jax.ShapeDtypeStruct((groups // 2, channels, width), BF16)
    block_output, grad, keep, give, *grad_units = pl.pallas_call(
        functools.partial(forward_kernel, shard=shard),
        name="forward",
        out_shape=[grid_type, grid_type, half_type, half_type] + [units_type] * spread,
        in_specs=[vmem(), vmem(), pl.BlockSpec(memory_space=pltpu.HBM), vmem(), vmem()]
        + [smem(), smem()]
        + [vmem()] * spread,
        out_specs=[vmem()] * (4 + spread),
        scratch_shapes=[
            table,
            windows,
            sides,
            walls,
            flat,
            pltpu.VMEM((channels, 4 * LANES), F32),
            pltpu.VMEM((4, (bricks + 1) * 64, LANES), F32),
            pltpu.VMEM((256, bricks * LANES), BF16),
            pltpu.VMEM(grid_shape, BF16),
            pltpu.SemaphoreType.DMA,
        ],
        compiler_params=params,
    )(
        masked,
        mask,
        pltpu.with_memory_space_constraint(cotangent.reshape(grid_shape), pltpu.HBM),
        band_forward,
        bias,
        rows,
        send,
        *received,
    )

    later = grad_units[1:]
    bit = 1
    while 2 * bit < groups:
        (keep, give), _ = sum_after(keep, swapped(give, "dp", bit), parts=2)
        bit *= 2
    (total,), later = sum_after(keep, swapped(give, "dp", bit), through=later)
    grad_received = grad_units[:1]
    for number, unit in enumerate(later, 1):
        grad_received.append(exchanged(number, unit))

    steps = space_steps()
    other = stepped(total, steps[0])
    if len(steps) > 1:
        (total,), _ = sum_after(total, other, grad_received[3:4])
        other = stepped(total, steps[1])

    padded_grad = pl.pallas_call(
        assemble_kernel,
        name="assemble",
        out_shape=jax.ShapeDtypeStruct(windows.shape, BF16),
        in_specs=[vmem()] + [smem()] + [vmem()] * spread + [untouched()],
        out_specs=vmem(),
        scratch_shapes=[table, sides, walls],
        compiler_params=params,
    )(grad, rows, *grad_received, total)

    for number, step in enumerate(steps[2:]):
        (total,), _ = sum_after(total, other, [] if number else [padded_grad])
        other = stepped(total, step)

    grad_input = pl.pallas_call(
        backward_kernel,
        name="backward",
        out_shape=grid_type,
        in_specs=[vmem()] * 3 + [untouched()],
        out_specs=vmem(),
        compiler_params=params,
    )(padded_grad, mask, band_backward, total)

    weight_share, bias_share = pl.pallas_call(
        finish_kernel,
        name="finish",
        out_shape=[
            jax.ShapeDtypeStruct((channels, shard), F32),
            jax.ShapeDtypeStruct((1, count), F32),
        ],
        in_specs=[vmem()] * 2,
        out_specs=[vmem()] * 2,
        compiler_params=params,
    )(total[0], other[0])
    return (
        block_output.reshape(features.shape),
        grad_input.reshape(features.shape),
        weight_share.T,
        bias_share.reshape(count),
    )


def solution(mesh):
    placed = (
        P("dp", "space", None, None, None),
        P("dp", "space", None),
        P("dp", "space"),
        P("dp", "space", None, None),
        P("dp", "space", None),
        P("dp", None),
        P("dp"),
        P("dp", "space", None, None, None),
    )
    return jax.shard_map(
        body,
        mesh=mesh,
        in_specs=placed,
        out_specs=(
            P("dp", "space", None, None, None),
            P("dp", "space", None, None, None),
            P("dp", None),
            P("dp"),
        ),
        check_vma=False,
    )
```

```python
import functools

import jax
import jax.numpy as jnp
from jax import lax
from jax.experimental import pallas as pl
from jax.experimental.pallas import tpu as pltpu
from jax.sharding import PartitionSpec as P

F32 = jnp.float32
BF16 = jnp.bfloat16
LANES = 128
UNIT_ROWS = 32
Z_ROWS = 64
SWAPS = (
    ((1, 1), (2, 1), (1, 0), (2, 0)),
    ((2, 1), (1, 1), (2, 0), (1, 0)),
)


def vmem():
    return pl.BlockSpec(memory_space=pltpu.VMEM)


def smem():
    return pl.BlockSpec(memory_space=pltpu.SMEM)


def untouched():
    return pl.BlockSpec(memory_space=pl.ANY)


def offset_number(ox, oy, oz):
    flat = (ox + 1) * 9 + (oy + 1) * 3 + (oz + 1)
    return flat if flat < 13 else flat - 1


def low_half(shape):
    return lax.broadcasted_iota(jnp.int32, shape, len(shape) - 1) % LANES < 64


def chunk_rows(block):
    return [block[8 * q : 8 * q + 8] for q in range(4)]


def upward(device, distance):
    return lax.rem(lax.div(device, distance), 2)


def pack_units(values, send, outs):
    slots = values.shape[1] // 64 - 1
    reach = len(outs) // 2
    low = low_half((64, LANES))
    device = lax.axis_index("space")
    odd = lax.rem(lax.axis_index("dp"), 2)
    for number, out in enumerate(outs):
        column = reach
        if number > 0:
            columns = []
            for distance, turn in (SWAPS[0][number - 1], SWAPS[1][number - 1]):
                up = upward(device, distance) == turn
                columns.append(jnp.where(up, reach + distance, reach - distance))
            column = jnp.where(odd == 0, columns[0], columns[1])

        def base(link):
            unit = send[column, 0, link]
            slot = jnp.where(unit < 0, slots, (unit * 43) >> 8)
            return pl.multiple_of(slot * 64, 64)

        for half in range(2):
            for face in range(4):
                start = base(half * 6 + face)
                if face < 2:
                    where = pl.ds(start + 56 * face, 8)
                else:
                    where = pl.ds(start + 7 * (face - 2), 8, stride=8)
                packed = jnp.concatenate([values[q, where, :] for q in range(4)], axis=0)
                at = (half * 4 + face) * UNIT_ROWS
                out[at : at + UNIT_ROWS, :] = packed.astype(BF16)
            first = values[0, pl.ds(base(half * 6 + 4), 64), :]
            last = values[3, pl.ds(base(half * 6 + 5), 64), :]
            at = 8 * UNIT_ROWS + half * Z_ROWS
            out[at : at + Z_ROWS, :] = jnp.where(low, first, last).astype(BF16)


def prepare_kernel(
    features_hbm, occupancy_hbm, send_hbm, listing_hbm, weight_hbm, bias_hbm, counts,
    masked_out, mask_out, rows_out, send_out, shard_out, u0, u1, u2, u3, u4,
    values, features, occupancy, listing, weight_t, bias, rows, sems,
):
    copies = [
        pltpu.make_async_copy(src, dst, sems.at[i])
        for i, (src, dst) in enumerate(
            (
                (occupancy_hbm, occupancy),
                (features_hbm, features),
                (send_hbm, send_out),
                (listing_hbm, listing),
                (weight_hbm, weight_t),
                (bias_hbm, bias),
            )
        )
    ]
    for copy in copies:
        copy.start()
    bricks = features.shape[0]
    shard_out[...] = jnp.zeros(shard_out.shape, BF16)
    values[:, bricks * 64 :, :] = jnp.zeros((4, 64, LANES), F32)
    row = lax.broadcasted_iota(jnp.int32, (64, 512), 0)
    col = lax.broadcasted_iota(jnp.int32, (64, 512), 1)
    same = (col >> 3) == row
    z_row = lax.broadcasted_iota(jnp.int32, (512, 512), 0) & 7
    z_col = lax.broadcasted_iota(jnp.int32, (512, 512), 1) >> 6
    expand = jnp.where(z_row == z_col, 1.0, 0.0).astype(BF16)

    copies[3].wait()
    device = lax.axis_index("space")
    number = listing[...]
    column = (number * 43) >> 9
    link = number - column * 12
    half = (link >= 6).astype(jnp.int32)
    face = link - 6 * half
    block = jnp.zeros(number.shape, jnp.int32)
    odd = lax.rem(lax.axis_index("dp"), 2)
    for distance in (1, 2):
        up = upward(device, distance)
        first, second = (
            jnp.where(
                odd == 0,
                SWAPS[0].index((distance, turn)) + 1,
                SWAPS[1].index((distance, turn)) + 1,
            )
            for turn in range(2)
        )
        block = jnp.where(column == 2 - distance, jnp.where(up == 0, first, second), block)
        block = jnp.where(column == 2 + distance, jnp.where(up == 0, second, first), block)
    base = block * (8 * UNIT_ROWS + 2 * Z_ROWS)
    plain = base + (half * 4 + face) * UNIT_ROWS
    paired = base + 8 * UNIT_ROWS + half * Z_ROWS
    none = 5 * (8 * UNIT_ROWS + 2 * Z_ROWS)
    rows[...] = jnp.where(number < 0, none, jnp.where(face < 4, plain, paired))
    last = pltpu.make_async_copy(rows, rows_out, sems.at[len(copies)])
    last.start()

    copies[0].wait()
    live = lax.broadcasted_iota(jnp.int32, (bricks, 512), 0) < counts[0, 0]
    occ = jnp.where(live, occupancy[...], 0).astype(F32)
    spread = jnp.concatenate(
        [jnp.where(same, occ[b : b + 1, :], 0.0) for b in range(bricks)], axis=0
    ).astype(BF16)
    mask = jnp.dot(spread, expand, preferred_element_type=F32)
    mask_out[...] = mask.astype(BF16).reshape(mask_out.shape)
    copies[1].wait()
    value = features[...].astype(F32).reshape(bricks * 64, 512) * mask
    masked_out[...] = value.astype(BF16).reshape(masked_out.shape)
    for q in range(4):
        values[q, 0 : bricks * 64, :] = value[:, q * LANES : (q + 1) * LANES]
    copies[2].wait()
    pack_units(values, send_out, (u0, u1, u2, u3, u4))

    copies[4].wait()
    copies[5].wait()
    shard = weight_t.shape[1]
    lead = shard // LANES * LANES
    count = bias.shape[1]
    shard_out[:, 0:lead] = weight_t[:, 0:lead]
    tile = jnp.concatenate(
        [weight_t[:, lead:shard].astype(F32), jnp.zeros((64, lead + LANES - shard), F32)], axis=1
    )
    offset = shard - lead
    behind = jnp.concatenate(
        [bias[...].astype(F32), jnp.zeros((1, LANES - count), F32)], axis=1
    )
    behind = pltpu.roll(jnp.broadcast_to(behind, (64, LANES)), offset, 1)
    first = lax.broadcasted_iota(jnp.int32, (64, LANES), 0) == 0
    lane = lax.broadcasted_iota(jnp.int32, (64, LANES), 1)
    behind = jnp.where(first & (lane >= offset) & (lane < offset + count), behind, 0.0)
    shard_out[:, lead : lead + LANES] = (tile + behind).astype(BF16)
    last.wait()


def gather_units(table, received):
    at = 0
    for part in received:
        table[at : at + part.shape[0], :] = part[...]
        at += part.shape[0]
    table[at:, :] = jnp.zeros((table.shape[0] - at, LANES), BF16)


def assemble(source, table, rows, windows, sides, walls):
    low8 = low_half((8, LANES))
    sub = lax.broadcasted_iota(jnp.int32, (8, LANES), 0)
    top, bottom = sub == 0, sub == 7

    def put(pair, half, bit, per_brick):
        for e in range(3):
            stacked = [
                jnp.concatenate([per_brick[0][e][i], per_brick[1][e][i]], axis=0)
                for i in range(5)
            ]
            low16 = low_half((16, LANES))
            before = [stacked[4]] + stacked[:3]
            after = stacked[1:4] + [stacked[4]]
            for q in range(4):
                windows[e, q, pair, half, bit, :, 0:LANES] = stacked[q].astype(BF16)
                windows[e, q, pair, half, bit, :, LANES:] = jnp.where(
                    low16, after[q], before[q]
                ).astype(BF16)

    def one_pair(pair, carry):
        def unit(brick, ox, oy, oz):
            return pl.multiple_of(rows[brick, offset_number(ox, oy, oz)], UNIT_ROWS)

        def plane(brick, ox, oy):
            chunks = chunk_rows(table[pl.ds(unit(brick, ox, oy, 0), UNIT_ROWS), :].astype(F32))
            after = table[pl.ds(unit(brick, ox, oy, 1), UNIT_ROWS), :].astype(F32)[0:8]
            before = table[pl.ds(unit(brick, ox, oy, -1), UNIT_ROWS), :].astype(F32)[24:32]
            return chunks + [jnp.where(low8, after, before)]

        for b2 in range(2):
            brick = pair * 2 + b2
            low64 = low_half((64, LANES))
            after = table[pl.ds(unit(brick, 0, 0, 1), Z_ROWS), :].astype(F32)
            before = table[pl.ds(unit(brick, 0, 0, -1), Z_ROWS), :].astype(F32)
            walls[b2] = jnp.where(low64, after, before)
            for side, oy in enumerate((-1, 1)):
                for i, part in enumerate(plane(brick, 0, oy)):
                    sides[b2, side, i] = part

        for ox in (-1, 1):
            per_brick = []
            for b2 in range(2):
                brick = pair * 2 + b2
                centre = plane(brick, ox, 0)
                lower = plane(brick, ox, -1)
                upper = plane(brick, ox, 1)
                per_brick.append(
                    [
                        [
                            pltpu.roll(jnp.where(bottom, l, c), 1, 0)
                            for l, c in zip(lower, centre)
                        ],
                        centre,
                        [
                            pltpu.roll(jnp.where(top, u, c), 7, 0)
                            for u, c in zip(upper, centre)
                        ],
                    ]
                )
            put(pair, 0 if ox < 0 else 4, 0 if ox < 0 else 1, per_brick)

        def two_x(i, carry):
            for bit in range(2):
                x = 2 * i + bit
                per_brick = []
                for b2 in range(2):
                    brick = pair * 2 + b2
                    block = source[brick, i, bit].astype(F32)
                    centre = [block[:, q * LANES : (q + 1) * LANES] for q in range(4)]
                    centre.append(walls[b2, pl.ds(pl.multiple_of(x * 8, 8), 8), :])
                    lower = [
                        jnp.broadcast_to(sides[b2, 0, n, pl.ds(x, 1), :], (8, LANES))
                        for n in range(5)
                    ]
                    upper = [
                        jnp.broadcast_to(sides[b2, 1, n, pl.ds(x, 1), :], (8, LANES))
                        for n in range(5)
                    ]
                    per_brick.append(
                        [
                            [
                                jnp.where(top, l, pltpu.roll(c, 1, 0))
                                for l, c in zip(lower, centre)
                            ],
                            centre,
                            [
                                jnp.where(bottom, u, pltpu.roll(c, 7, 0))
                                for u, c in zip(upper, centre)
                            ],
                        ]
                    )
                put(pair, i + bit, 1 - bit, per_brick)
            return carry

        return lax.fori_loop(0, 4, two_x, carry)

    lax.fori_loop(0, windows.shape[2], one_pair, 0)


def row_block(d, e):
    return slice((3 * d + e) * 256, (3 * d + e + 1) * 256)


def tap_rows(windows, d, e):
    block = windows[e, :, :, d // 2 : d // 2 + 4, d % 2]
    return block.reshape(-1, block.shape[-1])


def all_taps(windows):
    return jnp.concatenate(
        [tap_rows(windows, d, e) for d in range(4) for e in range(3)], axis=1
    )


def chunk_places(bricks):
    return [(2 * pair + b2, i) for pair in range(bricks // 2) for i in range(4) for b2 in range(2)]


def chunk_of(ref, q):
    lanes = slice(q * LANES, (q + 1) * LANES)
    return jnp.concatenate(
        [
            jnp.concatenate([ref[b, i, x, :, lanes].astype(F32) for x in range(2)], axis=1)
            for b, i in chunk_places(ref.shape[0])
        ],
        axis=0,
    )


def put_chunk(ref, q, value):
    for n, (b, i) in enumerate(chunk_places(ref.shape[0])):
        for x in range(2):
            part = value[8 * n : 8 * n + 8, x * LANES : (x + 1) * LANES]
            ref[b, i, x, :, q * LANES : (q + 1) * LANES] = part.astype(ref.dtype)


def weights_kernel(*refs, shard, groups):
    shards = refs[:groups]
    forward_out, backward_out, bias_out, gathered, flat, shifted = refs[groups:]
    me = lax.axis_index("dp")
    for m, part in enumerate(shards):
        gathered[m] = part[...]
    for k in range(groups):
        flat[:, k * shard : (k + 1) * shard] = gathered[me ^ k][:, 0:shard].astype(F32)
    total = groups * shard
    flat[:, total:] = jnp.zeros((64, flat.shape[1] - total), F32)
    shifted[:, :] = pltpu.roll(flat[...], flat.shape[1] - 64, 1)
    low = low_half((64, LANES))
    for e in range(3):
        for x in range(2):
            half = slice(x * LANES, (x + 1) * LANES)
            for out in (forward_out, backward_out):
                out[row_block(3 * (1 - x), e), half] = jnp.zeros((256, LANES), BF16)
    for ae in range(9):
        a, e = ae // 3, ae % 3
        one = taps_pair(flat, shifted, 3 * ae)
        two = jnp.where(low, taps_pair(flat, shifted, 3 * ae + 2), 0.0)
        late = jnp.concatenate([one, two], axis=1)
        band = jnp.transpose(jnp.concatenate([pltpu.roll(late, 192, 1), late], axis=0)).astype(BF16)
        for x in range(2):
            forward_out[row_block(a + x, e), x * LANES : (x + 1) * LANES] = band
    for ae in range(9):
        a, e = ae // 3, ae % 3
        m = 3 * (8 - ae)
        first = taps_pair(flat, shifted, m)
        second = taps_pair(flat, shifted, m + 1)
        third = taps_pair(flat, shifted, m + 2)
        band = jnp.concatenate(
            [
                second,
                first,
                jnp.where(low, 0.0, pltpu.roll(first, 64, 1)),
                jnp.where(low, third, 0.0),
            ],
            axis=0,
        ).astype(BF16)
        for x in range(2):
            backward_out[row_block(a + x, e), x * LANES : (x + 1) * LANES] = band

    lane = lax.broadcasted_iota(jnp.int32, (8, LANES), 1)
    bias_lane = shard % LANES
    bias_tile = shard - bias_lane
    count = 64 // groups
    bias_row = jnp.zeros((8, LANES), F32)
    for k in range(groups):
        tile = gathered[me ^ k][0:16, bias_tile : bias_tile + LANES].astype(F32)[0:8]
        moved = pltpu.roll(tile, (count * k - bias_lane) % LANES, 1)
        bias_row += jnp.where((lane >= count * k) & (lane < count * (k + 1)), moved, 0.0)
    bias_out[...] = bias_row + pltpu.roll(bias_row, 64, 1)


def taps_pair(flat, shifted, first):
    if first % 2 == 0:
        return flat[:, first * 64 : first * 64 + LANES]
    return shifted[:, (first - 1) * 64 : (first - 1) * 64 + LANES]


def forward_kernel(
    masked, mask, cotangent_hbm, toeplitz, bias, rows, send, r0, r1, r2, r3, r4,
    block_out, grad_out, keep_out, give_out, u0, u1, u2, u3, u4,
    table, windows, sides, walls, flat, shifted, values, flipped, cotangent, product, sem,
    *, shard,
):
    fetch = pltpu.make_async_copy(cotangent_hbm, cotangent, sem)
    fetch.start()
    groups = 2 * keep_out.shape[0]
    bricks = masked.shape[0]
    pairs = bricks // 2
    gather_units(table, (r0, r1, r2, r3, r4))
    assemble(masked, table, rows, windows, sides, walls)
    bias_lane = shard % LANES
    bias_tile = shard - bias_lane
    bias_row = bias[0:1, :]
    fetch.wait()
    values[:, bricks * 64 :, :] = jnp.zeros((4, 64, LANES), F32)

    bias_row = jnp.concatenate([bias_row, bias_row], axis=1)
    product[...] = jnp.dot(all_taps(windows), toeplitz[...], preferred_element_type=F32)
    rows_of_chunk = product.shape[0] // 4

    def one_chunk(q, bias_sum):
        lanes = pl.ds(pl.multiple_of(q * LANES, LANES), LANES)
        for pair in range(pairs):
            for i in range(4):
                at = pl.multiple_of(q * rows_of_chunk + (pair * 4 + i) * 16, 16)
                p = product[pl.ds(at, 16), :] + bias_row

                def both(ref, i=i, pair=pair):
                    return jnp.concatenate(
                        [
                            jnp.concatenate(
                                [ref[2 * pair + b, i, x, :, lanes].astype(F32) for b in range(2)],
                                axis=0,
                            )
                            for x in range(2)
                        ],
                        axis=1,
                    )

                active = both(mask)
                sig = jax.nn.sigmoid(p)
                out = p * sig * active
                grad = both(cotangent) * sig * (1.0 + p * (1.0 - sig)) * active
                wide = grad.astype(BF16).astype(F32)
                product[pl.ds(at, 16), :] = wide
                bias_sum += wide[0:8] + wide[8:16]
                for b in range(2):
                    brick = 2 * pair + b
                    for x in range(2):
                        rows_, half = slice(8 * b, 8 * b + 8), slice(x * LANES, (x + 1) * LANES)
                        block_out[brick, i, x, :, lanes] = out[rows_, half].astype(BF16)
                        grad_out[brick, i, x, :, lanes] = wide[rows_, half].astype(BF16)
                        to = brick * 64 + (2 * i + x) * 8
                        values[q, to : to + 8, :] = wide[rows_, half]
        return bias_sum

    bias_sum = lax.fori_loop(0, 4, one_chunk, jnp.zeros((8, 256), F32))
    bias_sum = bias_sum[:, 0:LANES] + bias_sum[:, LANES:]
    pack_units(values, send, (u0, u1, u2, u3, u4))
    for q in range(4):
        rows_of_q = slice(q * rows_of_chunk, (q + 1) * rows_of_chunk)
        flipped[:, rows_of_q] = jnp.transpose(product[rows_of_q, :]).astype(BF16)

    for ae in range(9):
        a, e = ae // 3, ae % 3
        both = jnp.zeros((LANES, 256), F32)
        for x in range(2):
            rows = tap_rows(windows, a + x, e)
            for part in range(0, rows.shape[0], 256):
                both += jnp.dot(
                    flipped[x * LANES : (x + 1) * LANES, part : part + 256],
                    rows[part : part + 256],
                    preferred_element_type=F32,
                )
        flat[:, 192 * ae : 192 * ae + 256] = both[64:] + pltpu.roll(both[0:64], 64, 1)

    width = keep_out.shape[2]
    bias_all = jnp.sum(bias_sum, axis=0, keepdims=True)
    bias_all = jnp.broadcast_to(bias_all, (8, LANES))
    bias_all = bias_all + pltpu.roll(bias_all, 64, 1)
    bias_all = pltpu.roll(bias_all, bias_lane, 1)
    row8 = lax.broadcasted_iota(jnp.int32, (8, LANES), 0)
    lane8 = lax.broadcasted_iota(jnp.int32, (8, LANES), 1)
    keep = (row8 == 0) & (lane8 >= bias_lane) & (lane8 < bias_lane + 64)
    me = lax.axis_index("dp")
    for k in range(groups):
        part = flat[:, k * shard : (k + 1) * shard]
        shifted[0:64, 0:shard] = part
        shifted[0:64, shard:width] = jnp.zeros((64, width - shard), F32)
        tile = shifted[0:8, bias_tile : bias_tile + LANES]
        shifted[0:8, bias_tile : bias_tile + LANES] = jnp.where(keep, bias_all, tile)
        block = shifted[0:64, 0:width].astype(BF16)
        for m in range(groups):

            @pl.when(me ^ m == k)
            def _(m=m, block=block):
                (give_out if m % 2 else keep_out)[m // 2] = block


def assemble_kernel(grad, rows, r0, r1, r2, r3, r4, after, windows, table, sides, walls):
    del after
    gather_units(table, (r0, r1, r2, r3, r4))
    assemble(grad, table, rows, windows, sides, walls)


def sum_kernel(*refs, operands, parts):
    total = (refs[0][...].astype(F32) + refs[1][...].astype(F32)).astype(BF16)
    for part in range(parts):
        for row in range(part, total.shape[0], parts):
            refs[operands + part][row // parts] = total[row]


def sum_after(mine, other, after=(), through=(), parts=1):
    operands = 2 + len(after) + len(through)
    share = jax.ShapeDtypeStruct((mine.shape[0] // parts, *mine.shape[1:]), mine.dtype)
    outs = pl.pallas_call(
        functools.partial(sum_kernel, operands=operands, parts=parts),
        name="sum",
        out_shape=[share] * parts + [jax.ShapeDtypeStruct(x.shape, x.dtype) for x in through],
        in_specs=[vmem()] * 2 + [untouched()] * (operands - 2),
        out_specs=[vmem()] * parts + [untouched()] * len(through),
        input_output_aliases={2 + len(after) + i: parts + i for i in range(len(through))},
        compiler_params=pltpu.CompilerParams(vmem_limit_bytes=1024 * 1024),
    )(mine, other, *after, *through)
    return list(outs[:parts]), list(outs[parts:])


def backward_kernel(windows, mask, toeplitz, after, out):
    del after
    total = jnp.dot(all_taps(windows), toeplitz[...], preferred_element_type=F32)
    rows_of_chunk = total.shape[0] // 4
    for q in range(4):
        part = total[q * rows_of_chunk : (q + 1) * rows_of_chunk]
        put_chunk(out, q, part * chunk_of(mask, q))


def finish_kernel(mine, other, weight_out, bias_out):
    shard = weight_out.shape[1]
    count = bias_out.shape[1]
    total = mine[...].astype(F32) + other[...].astype(F32)
    weight_out[...] = total[:, 0:shard]
    bias_lane = shard % LANES
    bias_tile = shard - bias_lane
    tile = total[0:8, bias_tile : bias_tile + LANES]
    me = lax.axis_index("dp")
    moved = pltpu.roll(tile, 2 * LANES - bias_lane - me * count, 1)
    bias_out[...] = moved[0:1, 0:count]


def swapped(block, axis, bit):
    return lax.ppermute(block, axis, [(i, i ^ bit) for i in range(lax.axis_size(axis))])


def by_parity(block, routes):
    groups = lax.axis_size("dp")
    pairs = [
        (source * groups + group, target * groups + group)
        for group in range(groups)
        for source, target in routes[group % 2]
    ]
    return lax.ppermute(block, ("space", "dp"), pairs)


def exchanged(number, unit):
    routes = []
    for swaps in SWAPS:
        distance, turn = swaps[number - 1]
        route = []
        for low in range(lax.axis_size("space") - distance):
            if low // distance % 2 == turn:
                route += [(low, low + distance), (low + distance, low)]
        routes.append(route)
    return by_parity(unit, routes)


def space_steps():
    bits = []
    while 2 ** len(bits) < lax.axis_size("space"):
        bits.append(2 ** len(bits))
    return list(zip(bits, bits[1:] + bits[:1]))


def stepped(total, step):
    devices = range(lax.axis_size("space"))
    return by_parity(total, [[(i, i ^ bit) for i in devices] for bit in step])


def body(features, occupancy, counts, send_units, neighbours, weight, conv_bias, cotangent):
    bricks, edge, _, lanes = features.shape[1:]
    grid_shape = (bricks, edge // 2, 2, edge, lanes)
    pairs = bricks // 2
    spread, links = send_units.shape[2:]
    shard, channels = weight.shape
    groups = lax.axis_size("dp")
    count = conv_bias.shape[0]
    width = -(-(shard + channels) // LANES) * LANES
    unit_rows = 8 * UNIT_ROWS + 2 * Z_ROWS
    units_type = jax.ShapeDtypeStruct((unit_rows, LANES), BF16)
    grid_type = jax.ShapeDtypeStruct(grid_shape, BF16)
    shard_type = jax.ShapeDtypeStruct((channels, width), BF16)
    params = pltpu.CompilerParams(vmem_limit_bytes=48 * 1024 * 1024)
    rows_shape = neighbours.shape[1:]
    send_shape = (spread, 1, links)

    masked, mask, rows, send, own_shard, *units = pl.pallas_call(
        prepare_kernel,
        name="prepare",
        out_shape=[
            grid_type,
            grid_type,
            jax.ShapeDtypeStruct(rows_shape, jnp.int32),
            jax.ShapeDtypeStruct(send_shape, jnp.int32),
            shard_type,
        ]
        + [units_type] * spread,
        in_specs=[pl.BlockSpec(memory_space=pltpu.HBM)] * 6 + [smem()],
        out_specs=[vmem(), vmem(), smem(), smem(), vmem()] + [vmem()] * spread,
        scratch_shapes=[
            pltpu.VMEM((4, (bricks + 1) * 64, LANES), F32),
            pltpu.VMEM(grid_shape, BF16),
            pltpu.VMEM(occupancy.shape[1:], jnp.int32),
            pltpu.VMEM(rows_shape, jnp.int32),
            pltpu.VMEM((channels, shard), BF16),
            pltpu.VMEM((1, count), BF16),
            pltpu.VMEM(rows_shape, jnp.int32),
            pltpu.SemaphoreType.DMA((7,)),
        ],
        compiler_params=params,
    )(
        *(
            pltpu.with_memory_space_constraint(operand, pltpu.HBM)
            for operand in (
                features.reshape(grid_shape),
                occupancy[0],
                send_units.transpose(0, 2, 1, 3).reshape(send_shape),
                neighbours[0],
                weight.T,
                conv_bias.reshape(1, count),
            )
        ),
        counts,
    )

    shards = {0: own_shard}
    bit = groups // 2
    while bit:
        for m in list(shards):
            shards[m | bit] = swapped(shards[m], "dp", bit)
        bit //= 2
    received = units[:1] + [exchanged(number, units[number]) for number in range(1, spread)]

    flat = pltpu.VMEM((channels, 28 * 64), F32)
    band_forward, band_backward, bias = pl.pallas_call(
        functools.partial(weights_kernel, shard=shard, groups=groups),
        name="weights",
        out_shape=[
            jax.ShapeDtypeStruct((12 * 256, 256), BF16),
            jax.ShapeDtypeStruct((12 * 256, 256), BF16),
            jax.ShapeDtypeStruct((8, LANES), F32),
        ],
        in_specs=[vmem()] * groups,
        out_specs=[vmem()] * 3,
        scratch_shapes=[pltpu.VMEM((groups, channels, width), BF16), flat, flat],
        compiler_params=params,
    )(*(shards[m] for m in range(groups)))

    table = pltpu.VMEM((spread * unit_rows + Z_ROWS, LANES), BF16)
    windows = pltpu.VMEM((3, 4, pairs, 5, 2, 16, 256), BF16)
    sides = pltpu.VMEM((2, 2, 5, 8, LANES), F32)
    walls = pltpu.VMEM((2, 64, LANES), F32)
    half_type = jax.ShapeDtypeStruct((groups // 2, channels, width), BF16)
    block_output, grad, keep, give, *grad_units = pl.pallas_call(
        functools.partial(forward_kernel, shard=shard),
        name="forward",
        out_shape=[grid_type, grid_type, half_type, half_type] + [units_type] * spread,
        in_specs=[vmem(), vmem(), pl.BlockSpec(memory_space=pltpu.HBM), vmem(), vmem()]
        + [smem(), smem()]
        + [vmem()] * spread,
        out_specs=[vmem()] * (4 + spread),
        scratch_shapes=[
            table,
            windows,
            sides,
            walls,
            flat,
            pltpu.VMEM((channels, 4 * LANES), F32),
            pltpu.VMEM((4, (bricks + 1) * 64, LANES), F32),
            pltpu.VMEM((256, bricks * LANES), BF16),
            pltpu.VMEM(grid_shape, BF16),
            pltpu.VMEM((bricks * LANES, 256), F32),
            pltpu.SemaphoreType.DMA,
        ],
        compiler_params=params,
    )(
        masked,
        mask,
        pltpu.with_memory_space_constraint(cotangent.reshape(grid_shape), pltpu.HBM),
        band_forward,
        bias,
        rows,
        send,
        *received,
    )

    later = grad_units[2:]
    bit = 1
    while 2 * bit < groups:
        first = later[:1] if bit == 1 else []
        (keep, give), first = sum_after(keep, swapped(give, "dp", bit), through=first, parts=2)
        later = first + later[1:] if bit == 1 else later
        bit *= 2
    grad_received = [grad_units[0], exchanged(1, grad_units[1])]
    (total,), last = sum_after(keep, swapped(give, "dp", bit), grad_received[1:], later[1:])
    for number, unit in enumerate([later[0], *last], 2):
        grad_received.append(exchanged(number, unit))

    steps = space_steps()
    other = stepped(total, steps[0])
    if len(steps) > 1:
        (total,), _ = sum_after(total, other, grad_received[3:4])
        other = stepped(total, steps[1])

    padded_grad = pl.pallas_call(
        assemble_kernel,
        name="assemble",
        out_shape=jax.ShapeDtypeStruct(windows.shape, BF16),
        in_specs=[vmem()] + [smem()] + [vmem()] * spread + [untouched()],
        out_specs=vmem(),
        scratch_shapes=[table, sides, walls],
        compiler_params=params,
    )(grad, rows, *grad_received, total)

    for number, step in enumerate(steps[2:]):
        (total,), _ = sum_after(total, other, [] if number else [padded_grad])
        other = stepped(total, step)

    grad_input = pl.pallas_call(
        backward_kernel,
        name="backward",
        out_shape=grid_type,
        in_specs=[vmem()] * 3 + [untouched()],
        out_specs=vmem(),
        compiler_params=params,
    )(padded_grad, mask, band_backward, total)

    weight_share, bias_share = pl.pallas_call(
        finish_kernel,
        name="finish",
        out_shape=[
            jax.ShapeDtypeStruct((channels, shard), F32),
            jax.ShapeDtypeStruct((1, count), F32),
        ],
        in_specs=[vmem()] * 2,
        out_specs=[vmem()] * 2,
        compiler_params=params,
    )(total[0], other[0])
    return (
        block_output.reshape(features.shape),
        grad_input.reshape(features.shape),
        weight_share.T,
        bias_share.reshape(count),
    )


def solution(mesh):
    placed = (
        P("dp", "space", None, None, None),
        P("dp", "space", None),
        P("dp", "space"),
        P("dp", "space", None, None),
        P("dp", "space", None),
        P("dp", None),
        P("dp"),
        P("dp", "space", None, None, None),
    )
    return jax.shard_map(
        body,
        mesh=mesh,
        in_specs=placed,
        out_specs=(
            P("dp", "space", None, None, None),
            P("dp", "space", None, None, None),
            P("dp", None),
            P("dp"),
        ),
        check_vma=False,
    )
```

```python
import functools

import jax
import jax.numpy as jnp
from jax import lax
from jax.experimental import pallas as pl
from jax.experimental.pallas import tpu as pltpu
from jax.sharding import PartitionSpec as P

F32 = jnp.float32
BF16 = jnp.bfloat16
LANES = 128
UNIT_ROWS = 32
Z_ROWS = 64
SWAPS = (
    ((1, 1), (2, 1), (1, 0), (2, 0)),
    ((2, 1), (1, 1), (2, 0), (1, 0)),
)


def vmem():
    return pl.BlockSpec(memory_space=pltpu.VMEM)


def smem():
    return pl.BlockSpec(memory_space=pltpu.SMEM)


def untouched():
    return pl.BlockSpec(memory_space=pl.ANY)


def offset_number(ox, oy, oz):
    flat = (ox + 1) * 9 + (oy + 1) * 3 + (oz + 1)
    return flat if flat < 13 else flat - 1


def low_half(shape):
    return lax.broadcasted_iota(jnp.int32, shape, len(shape) - 1) % LANES < 64


def chunk_rows(block):
    return [block[8 * q : 8 * q + 8] for q in range(4)]


def upward(device, distance):
    return lax.rem(lax.div(device, distance), 2)


def pack_units(values, send, outs):
    slots = values.shape[1] // 64 - 1
    reach = len(outs) // 2
    low = low_half((64, LANES))
    device = lax.axis_index("space")
    odd = lax.rem(lax.axis_index("dp"), 2)
    for number, out in enumerate(outs):
        column = reach
        if number > 0:
            columns = []
            for distance, turn in (SWAPS[0][number - 1], SWAPS[1][number - 1]):
                up = upward(device, distance) == turn
                columns.append(jnp.where(up, reach + distance, reach - distance))
            column = jnp.where(odd == 0, columns[0], columns[1])

        def base(link):
            unit = send[column, 0, link]
            slot = jnp.where(unit < 0, slots, (unit * 43) >> 8)
            return pl.multiple_of(slot * 64, 64)

        for half in range(2):
            for face in range(4):
                start = base(half * 6 + face)
                if face < 2:
                    where = pl.ds(start + 56 * face, 8)
                else:
                    where = pl.ds(start + 7 * (face - 2), 8, stride=8)
                packed = jnp.concatenate([values[q, where, :] for q in range(4)], axis=0)
                at = (half * 4 + face) * UNIT_ROWS
                out[at : at + UNIT_ROWS, :] = packed.astype(BF16)
            first = values[0, pl.ds(base(half * 6 + 4), 64), :]
            last = values[3, pl.ds(base(half * 6 + 5), 64), :]
            at = 8 * UNIT_ROWS + half * Z_ROWS
            out[at : at + Z_ROWS, :] = jnp.where(low, first, last).astype(BF16)


def prepare_kernel(
    features_hbm, occupancy_hbm, send_hbm, listing_hbm, weight_hbm, bias_hbm, counts,
    masked_out, mask_out, rows_out, send_out, shard_out, u0, u1, u2, u3, u4,
    values, features, occupancy, listing, weight_t, bias, rows, sems,
):
    copies = [
        pltpu.make_async_copy(src, dst, sems.at[i])
        for i, (src, dst) in enumerate(
            (
                (occupancy_hbm, occupancy),
                (features_hbm, features),
                (send_hbm, send_out),
                (listing_hbm, listing),
                (weight_hbm, weight_t),
                (bias_hbm, bias),
            )
        )
    ]
    for copy in copies:
        copy.start()
    bricks = features.shape[0]
    shard_out[...] = jnp.zeros(shard_out.shape, BF16)
    values[:, bricks * 64 :, :] = jnp.zeros((4, 64, LANES), F32)
    row = lax.broadcasted_iota(jnp.int32, (64, 512), 0)
    col = lax.broadcasted_iota(jnp.int32, (64, 512), 1)
    same = (col >> 3) == row
    z_row = lax.broadcasted_iota(jnp.int32, (512, 512), 0) & 7
    z_col = lax.broadcasted_iota(jnp.int32, (512, 512), 1) >> 6
    expand = jnp.where(z_row == z_col, 1.0, 0.0).astype(BF16)

    copies[3].wait()
    device = lax.axis_index("space")
    number = listing[...]
    column = (number * 43) >> 9
    link = number - column * 12
    half = (link >= 6).astype(jnp.int32)
    face = link - 6 * half
    block = jnp.zeros(number.shape, jnp.int32)
    odd = lax.rem(lax.axis_index("dp"), 2)
    for distance in (1, 2):
        up = upward(device, distance)
        first, second = (
            jnp.where(
                odd == 0,
                SWAPS[0].index((distance, turn)) + 1,
                SWAPS[1].index((distance, turn)) + 1,
            )
            for turn in range(2)
        )
        block = jnp.where(column == 2 - distance, jnp.where(up == 0, first, second), block)
        block = jnp.where(column == 2 + distance, jnp.where(up == 0, second, first), block)
    base = block * (8 * UNIT_ROWS + 2 * Z_ROWS)
    plain = base + (half * 4 + face) * UNIT_ROWS
    paired = base + 8 * UNIT_ROWS + half * Z_ROWS
    none = 5 * (8 * UNIT_ROWS + 2 * Z_ROWS)
    rows[...] = jnp.where(number < 0, none, jnp.where(face < 4, plain, paired))
    last = pltpu.make_async_copy(rows, rows_out, sems.at[len(copies)])
    last.start()

    copies[0].wait()
    live = lax.broadcasted_iota(jnp.int32, (bricks, 512), 0) < counts[0, 0]
    occ = jnp.where(live, occupancy[...], 0).astype(F32)
    spread = jnp.concatenate(
        [jnp.where(same, occ[b : b + 1, :], 0.0) for b in range(bricks)], axis=0
    ).astype(BF16)
    mask = jnp.dot(spread, expand, preferred_element_type=F32)
    mask_out[...] = mask.astype(BF16).reshape(mask_out.shape)
    copies[1].wait()
    value = features[...].astype(F32).reshape(bricks * 64, 512) * mask
    masked_out[...] = value.astype(BF16).reshape(masked_out.shape)
    for q in range(4):
        values[q, 0 : bricks * 64, :] = value[:, q * LANES : (q + 1) * LANES]
    copies[2].wait()
    pack_units(values, send_out, (u0, u1, u2, u3, u4))

    copies[4].wait()
    copies[5].wait()
    shard = weight_t.shape[1]
    lead = shard // LANES * LANES
    count = bias.shape[1]
    shard_out[:, 0:lead] = weight_t[:, 0:lead]
    tile = jnp.concatenate(
        [weight_t[:, lead:shard].astype(F32), jnp.zeros((64, lead + LANES - shard), F32)], axis=1
    )
    offset = shard - lead
    behind = jnp.concatenate(
        [bias[...].astype(F32), jnp.zeros((1, LANES - count), F32)], axis=1
    )
    behind = pltpu.roll(jnp.broadcast_to(behind, (64, LANES)), offset, 1)
    first = lax.broadcasted_iota(jnp.int32, (64, LANES), 0) == 0
    lane = lax.broadcasted_iota(jnp.int32, (64, LANES), 1)
    behind = jnp.where(first & (lane >= offset) & (lane < offset + count), behind, 0.0)
    shard_out[:, lead : lead + LANES] = (tile + behind).astype(BF16)
    last.wait()


def gather_units(table, received):
    at = 0
    for part in received:
        table[at : at + part.shape[0], :] = part[...]
        at += part.shape[0]
    table[at:, :] = jnp.zeros((table.shape[0] - at, LANES), BF16)


def assemble(source, table, rows, windows, sides, walls):
    low8 = low_half((8, LANES))
    sub = lax.broadcasted_iota(jnp.int32, (8, LANES), 0)
    top, bottom = sub == 0, sub == 7

    def put(pair, half, bit, per_brick):
        for e in range(3):
            stacked = [
                jnp.concatenate([per_brick[0][e][i], per_brick[1][e][i]], axis=0)
                for i in range(5)
            ]
            low16 = low_half((16, LANES))
            before = [stacked[4]] + stacked[:3]
            after = stacked[1:4] + [stacked[4]]
            for q in range(4):
                windows[e, q, pair, half, bit, :, 0:LANES] = stacked[q].astype(BF16)
                windows[e, q, pair, half, bit, :, LANES:] = jnp.where(
                    low16, after[q], before[q]
                ).astype(BF16)

    def one_pair(pair, carry):
        def unit(brick, ox, oy, oz):
            return pl.multiple_of(rows[brick, offset_number(ox, oy, oz)], UNIT_ROWS)

        def plane(brick, ox, oy):
            chunks = chunk_rows(table[pl.ds(unit(brick, ox, oy, 0), UNIT_ROWS), :].astype(F32))
            after = table[pl.ds(unit(brick, ox, oy, 1), UNIT_ROWS), :].astype(F32)[0:8]
            before = table[pl.ds(unit(brick, ox, oy, -1), UNIT_ROWS), :].astype(F32)[24:32]
            return chunks + [jnp.where(low8, after, before)]

        for b2 in range(2):
            brick = pair * 2 + b2
            low64 = low_half((64, LANES))
            after = table[pl.ds(unit(brick, 0, 0, 1), Z_ROWS), :].astype(F32)
            before = table[pl.ds(unit(brick, 0, 0, -1), Z_ROWS), :].astype(F32)
            walls[b2] = jnp.where(low64, after, before)
            for side, oy in enumerate((-1, 1)):
                for i, part in enumerate(plane(brick, 0, oy)):
                    sides[b2, side, i] = part

        for ox in (-1, 1):
            per_brick = []
            for b2 in range(2):
                brick = pair * 2 + b2
                centre = plane(brick, ox, 0)
                lower = plane(brick, ox, -1)
                upper = plane(brick, ox, 1)
                per_brick.append(
                    [
                        [
                            pltpu.roll(jnp.where(bottom, l, c), 1, 0)
                            for l, c in zip(lower, centre)
                        ],
                        centre,
                        [
                            pltpu.roll(jnp.where(top, u, c), 7, 0)
                            for u, c in zip(upper, centre)
                        ],
                    ]
                )
            put(pair, 0 if ox < 0 else 4, 0 if ox < 0 else 1, per_brick)

        def two_x(i, carry):
            for bit in range(2):
                x = 2 * i + bit
                per_brick = []
                for b2 in range(2):
                    brick = pair * 2 + b2
                    block = source[brick, i, bit].astype(F32)
                    centre = [block[:, q * LANES : (q + 1) * LANES] for q in range(4)]
                    centre.append(walls[b2, pl.ds(pl.multiple_of(x * 8, 8), 8), :])
                    lower = [
                        jnp.broadcast_to(sides[b2, 0, n, pl.ds(x, 1), :], (8, LANES))
                        for n in range(5)
                    ]
                    upper = [
                        jnp.broadcast_to(sides[b2, 1, n, pl.ds(x, 1), :], (8, LANES))
                        for n in range(5)
                    ]
                    per_brick.append(
                        [
                            [
                                jnp.where(top, l, pltpu.roll(c, 1, 0))
                                for l, c in zip(lower, centre)
                            ],
                            centre,
                            [
                                jnp.where(bottom, u, pltpu.roll(c, 7, 0))
                                for u, c in zip(upper, centre)
                            ],
                        ]
                    )
                put(pair, i + bit, 1 - bit, per_brick)
            return carry

        return lax.fori_loop(0, 4, two_x, carry)

    lax.fori_loop(0, windows.shape[2], one_pair, 0)


def row_block(d, e):
    return slice((3 * d + e) * 256, (3 * d + e + 1) * 256)


def tap_rows(windows, d, e):
    block = windows[e, :, :, d // 2 : d // 2 + 4, d % 2]
    return block.reshape(-1, block.shape[-1])


def all_taps(windows):
    return jnp.concatenate(
        [tap_rows(windows, d, e) for d in range(4) for e in range(3)], axis=1
    )


def chunk_places(bricks):
    return [(2 * pair + b2, i) for pair in range(bricks // 2) for i in range(4) for b2 in range(2)]


def chunk_of(ref, q):
    lanes = slice(q * LANES, (q + 1) * LANES)
    return jnp.concatenate(
        [
            jnp.concatenate([ref[b, i, x, :, lanes].astype(F32) for x in range(2)], axis=1)
            for b, i in chunk_places(ref.shape[0])
        ],
        axis=0,
    )


def put_chunk(ref, q, value):
    for n, (b, i) in enumerate(chunk_places(ref.shape[0])):
        for x in range(2):
            part = value[8 * n : 8 * n + 8, x * LANES : (x + 1) * LANES]
            ref[b, i, x, :, q * LANES : (q + 1) * LANES] = part.astype(ref.dtype)


def weights_kernel(*refs, shard, groups):
    shards = refs[:groups]
    forward_out, backward_out, bias_out, gathered, flat, shifted = refs[groups:]
    me = lax.axis_index("dp")
    for m, part in enumerate(shards):
        gathered[m] = part[...]
    for k in range(groups):
        flat[:, k * shard : (k + 1) * shard] = gathered[me ^ k][:, 0:shard].astype(F32)
    total = groups * shard
    flat[:, total:] = jnp.zeros((64, flat.shape[1] - total), F32)
    shifted[:, :] = pltpu.roll(flat[...], flat.shape[1] - 64, 1)
    low = low_half((64, LANES))
    for e in range(3):
        for x in range(2):
            half = slice(x * LANES, (x + 1) * LANES)
            for out in (forward_out, backward_out):
                out[row_block(3 * (1 - x), e), half] = jnp.zeros((256, LANES), BF16)
    for ae in range(9):
        a, e = ae // 3, ae % 3
        one = taps_pair(flat, shifted, 3 * ae)
        two = jnp.where(low, taps_pair(flat, shifted, 3 * ae + 2), 0.0)
        late = jnp.concatenate([one, two], axis=1)
        band = jnp.transpose(jnp.concatenate([pltpu.roll(late, 192, 1), late], axis=0)).astype(BF16)
        for x in range(2):
            forward_out[row_block(a + x, e), x * LANES : (x + 1) * LANES] = band
    for ae in range(9):
        a, e = ae // 3, ae % 3
        m = 3 * (8 - ae)
        first = taps_pair(flat, shifted, m)
        second = taps_pair(flat, shifted, m + 1)
        third = taps_pair(flat, shifted, m + 2)
        band = jnp.concatenate(
            [
                second,
                first,
                jnp.where(low, 0.0, pltpu.roll(first, 64, 1)),
                jnp.where(low, third, 0.0),
            ],
            axis=0,
        ).astype(BF16)
        for x in range(2):
            backward_out[row_block(a + x, e), x * LANES : (x + 1) * LANES] = band

    lane = lax.broadcasted_iota(jnp.int32, (8, LANES), 1)
    bias_lane = shard % LANES
    bias_tile = shard - bias_lane
    count = 64 // groups
    bias_row = jnp.zeros((8, LANES), F32)
    for k in range(groups):
        tile = gathered[me ^ k][0:16, bias_tile : bias_tile + LANES].astype(F32)[0:8]
        moved = pltpu.roll(tile, (count * k - bias_lane) % LANES, 1)
        bias_row += jnp.where((lane >= count * k) & (lane < count * (k + 1)), moved, 0.0)
    bias_out[...] = bias_row + pltpu.roll(bias_row, 64, 1)


def taps_pair(flat, shifted, first):
    if first % 2 == 0:
        return flat[:, first * 64 : first * 64 + LANES]
    return shifted[:, (first - 1) * 64 : (first - 1) * 64 + LANES]


def forward_kernel(
    masked, mask, cotangent_hbm, toeplitz, bias, rows, send, r0, r1, r2, r3, r4,
    block_out, grad_out, keep_out, give_out, u0, u1, u2, u3, u4,
    table, windows, sides, walls, flat, shifted, values, flipped, cotangent, sem, *, shard,
):
    fetch = pltpu.make_async_copy(cotangent_hbm, cotangent, sem)
    fetch.start()
    groups = 2 * keep_out.shape[0]
    bricks = masked.shape[0]
    pairs = bricks // 2
    gather_units(table, (r0, r1, r2, r3, r4))
    assemble(masked, table, rows, windows, sides, walls)
    bias_lane = shard % LANES
    bias_tile = shard - bias_lane
    bias_row = bias[0:1, :]
    fetch.wait()
    values[:, bricks * 64 :, :] = jnp.zeros((4, 64, LANES), F32)

    bias_row = jnp.concatenate([bias_row, bias_row], axis=1)
    total = jnp.dot(all_taps(windows), toeplitz[...], preferred_element_type=F32)
    rows_of_chunk = total.shape[0] // 4
    bias_sum = jnp.zeros((8, 256), F32)
    for q in range(4):
        p = total[q * rows_of_chunk : (q + 1) * rows_of_chunk] + bias_row
        active = chunk_of(mask, q)
        sig = jax.nn.sigmoid(p)
        put_chunk(block_out, q, p * sig * active)
        grad = (chunk_of(cotangent, q) * sig * (1.0 + p * (1.0 - sig)) * active).astype(BF16)
        wide = grad.astype(F32)
        put_chunk(grad_out, q, wide)
        for n, (brick, i) in enumerate(chunk_places(bricks)):
            for x in range(2):
                at = brick * 64 + (2 * i + x) * 8
                values[q, at : at + 8, :] = wide[
                    8 * n : 8 * n + 8, x * LANES : (x + 1) * LANES
                ]
        flipped[:, q * rows_of_chunk : (q + 1) * rows_of_chunk] = jnp.transpose(wide).astype(BF16)
        bias_sum += jnp.sum(wide.reshape(-1, 8, 256), axis=0)
    bias_sum = bias_sum[:, 0:LANES] + bias_sum[:, LANES:]
    pack_units(values, send, (u0, u1, u2, u3, u4))

    for ae in range(9):
        a, e = ae // 3, ae % 3
        both = jnp.zeros((LANES, 256), F32)
        for x in range(2):
            rows = tap_rows(windows, a + x, e)
            for part in range(0, rows.shape[0], 256):
                both += jnp.dot(
                    flipped[x * LANES : (x + 1) * LANES, part : part + 256],
                    rows[part : part + 256],
                    preferred_element_type=F32,
                )
        flat[:, 192 * ae : 192 * ae + 256] = both[64:] + pltpu.roll(both[0:64], 64, 1)

    width = keep_out.shape[2]
    bias_all = jnp.sum(bias_sum, axis=0, keepdims=True)
    bias_all = jnp.broadcast_to(bias_all, (8, LANES))
    bias_all = bias_all + pltpu.roll(bias_all, 64, 1)
    bias_all = pltpu.roll(bias_all, bias_lane, 1)
    row8 = lax.broadcasted_iota(jnp.int32, (8, LANES), 0)
    lane8 = lax.broadcasted_iota(jnp.int32, (8, LANES), 1)
    keep = (row8 == 0) & (lane8 >= bias_lane) & (lane8 < bias_lane + 64)
    me = lax.axis_index("dp")
    for k in range(groups):
        part = flat[:, k * shard : (k + 1) * shard]
        shifted[0:64, 0:shard] = part
        shifted[0:64, shard:width] = jnp.zeros((64, width - shard), F32)
        tile = shifted[0:8, bias_tile : bias_tile + LANES]
        shifted[0:8, bias_tile : bias_tile + LANES] = jnp.where(keep, bias_all, tile)
        block = shifted[0:64, 0:width].astype(BF16)
        for m in range(groups):

            @pl.when(me ^ m == k)
            def _(m=m, block=block):
                (give_out if m % 2 else keep_out)[m // 2] = block


def assemble_kernel(grad, rows, r0, r1, r2, r3, r4, after, windows, table, sides, walls):
    del after
    gather_units(table, (r0, r1, r2, r3, r4))
    assemble(grad, table, rows, windows, sides, walls)


def sum_kernel(*refs, operands, parts):
    total = (refs[0][...].astype(F32) + refs[1][...].astype(F32)).astype(BF16)
    for part in range(parts):
        for row in range(part, total.shape[0], parts):
            refs[operands + part][row // parts] = total[row]


def sum_after(mine, other, after=(), through=(), parts=1):
    operands = 2 + len(after) + len(through)
    share = jax.ShapeDtypeStruct((mine.shape[0] // parts, *mine.shape[1:]), mine.dtype)
    outs = pl.pallas_call(
        functools.partial(sum_kernel, operands=operands, parts=parts),
        name="sum",
        out_shape=[share] * parts + [jax.ShapeDtypeStruct(x.shape, x.dtype) for x in through],
        in_specs=[vmem()] * 2 + [untouched()] * (operands - 2),
        out_specs=[vmem()] * parts + [untouched()] * len(through),
        input_output_aliases={2 + len(after) + i: parts + i for i in range(len(through))},
        compiler_params=pltpu.CompilerParams(vmem_limit_bytes=1024 * 1024),
    )(mine, other, *after, *through)
    return list(outs[:parts]), list(outs[parts:])


def backward_kernel(windows, mask, toeplitz, after, out):
    del after
    total = jnp.dot(all_taps(windows), toeplitz[...], preferred_element_type=F32)
    rows_of_chunk = total.shape[0] // 4
    for q in range(4):
        part = total[q * rows_of_chunk : (q + 1) * rows_of_chunk]
        put_chunk(out, q, part * chunk_of(mask, q))


def finish_kernel(mine, other, weight_out, bias_out):
    shard = weight_out.shape[1]
    count = bias_out.shape[1]
    total = mine[...].astype(F32) + other[...].astype(F32)
    weight_out[...] = total[:, 0:shard]
    bias_lane = shard % LANES
    bias_tile = shard - bias_lane
    tile = total[0:8, bias_tile : bias_tile + LANES]
    me = lax.axis_index("dp")
    moved = pltpu.roll(tile, 2 * LANES - bias_lane - me * count, 1)
    bias_out[...] = moved[0:1, 0:count]


def swapped(block, axis, bit):
    return lax.ppermute(block, axis, [(i, i ^ bit) for i in range(lax.axis_size(axis))])


def by_parity(block, routes):
    groups = lax.axis_size("dp")
    pairs = [
        (source * groups + group, target * groups + group)
        for group in range(groups)
        for source, target in routes[group % 2]
    ]
    return lax.ppermute(block, ("space", "dp"), pairs)


def exchanged(number, unit):
    routes = []
    for swaps in SWAPS:
        distance, turn = swaps[number - 1]
        route = []
        for low in range(lax.axis_size("space") - distance):
            if low // distance % 2 == turn:
                route += [(low, low + distance), (low + distance, low)]
        routes.append(route)
    return by_parity(unit, routes)


def space_steps():
    bits = []
    while 2 ** len(bits) < lax.axis_size("space"):
        bits.append(2 ** len(bits))
    return [(bit, bit) for bit in bits[1:] + bits[:1]]


def stepped(total, step):
    devices = range(lax.axis_size("space"))
    return by_parity(total, [[(i, i ^ bit) for i in devices] for bit in step])


def body(features, occupancy, counts, send_units, neighbours, weight, conv_bias, cotangent):
    bricks, edge, _, lanes = features.shape[1:]
    grid_shape = (bricks, edge // 2, 2, edge, lanes)
    pairs = bricks // 2
    spread, links = send_units.shape[2:]
    shard, channels = weight.shape
    groups = lax.axis_size("dp")
    count = conv_bias.shape[0]
    width = -(-(shard + channels) // LANES) * LANES
    unit_rows = 8 * UNIT_ROWS + 2 * Z_ROWS
    units_type = jax.ShapeDtypeStruct((unit_rows, LANES), BF16)
    grid_type = jax.ShapeDtypeStruct(grid_shape, BF16)
    shard_type = jax.ShapeDtypeStruct((channels, width), BF16)
    params = pltpu.CompilerParams(vmem_limit_bytes=48 * 1024 * 1024)
    rows_shape = neighbours.shape[1:]
    send_shape = (spread, 1, links)

    masked, mask, rows, send, own_shard, *units = pl.pallas_call(
        prepare_kernel,
        name="prepare",
        out_shape=[
            grid_type,
            grid_type,
            jax.ShapeDtypeStruct(rows_shape, jnp.int32),
            jax.ShapeDtypeStruct(send_shape, jnp.int32),
            shard_type,
        ]
        + [units_type] * spread,
        in_specs=[pl.BlockSpec(memory_space=pltpu.HBM)] * 6 + [smem()],
        out_specs=[vmem(), vmem(), smem(), smem(), vmem()] + [vmem()] * spread,
        scratch_shapes=[
            pltpu.VMEM((4, (bricks + 1) * 64, LANES), F32),
            pltpu.VMEM(grid_shape, BF16),
            pltpu.VMEM(occupancy.shape[1:], jnp.int32),
            pltpu.VMEM(rows_shape, jnp.int32),
            pltpu.VMEM((channels, shard), BF16),
            pltpu.VMEM((1, count), BF16),
            pltpu.VMEM(rows_shape, jnp.int32),
            pltpu.SemaphoreType.DMA((7,)),
        ],
        compiler_params=params,
    )(
        *(
            pltpu.with_memory_space_constraint(operand, pltpu.HBM)
            for operand in (
                features.reshape(grid_shape),
                occupancy[0],
                send_units.transpose(0, 2, 1, 3).reshape(send_shape),
                neighbours[0],
                weight.T,
                conv_bias.reshape(1, count),
            )
        ),
        counts,
    )

    shards = {0: own_shard}
    bit = groups // 2
    while bit:
        for m in list(shards):
            shards[m | bit] = swapped(shards[m], "dp", bit)
        bit //= 2
    received = units[:1] + [exchanged(number, units[number]) for number in range(1, spread)]

    flat = pltpu.VMEM((channels, 28 * 64), F32)
    band_forward, band_backward, bias = pl.pallas_call(
        functools.partial(weights_kernel, shard=shard, groups=groups),
        name="weights",
        out_shape=[
            jax.ShapeDtypeStruct((12 * 256, 256), BF16),
            jax.ShapeDtypeStruct((12 * 256, 256), BF16),
            jax.ShapeDtypeStruct((8, LANES), F32),
        ],
        in_specs=[vmem()] * groups,
        out_specs=[vmem()] * 3,
        scratch_shapes=[pltpu.VMEM((groups, channels, width), BF16), flat, flat],
        compiler_params=params,
    )(*(shards[m] for m in range(groups)))

    table = pltpu.VMEM((spread * unit_rows + Z_ROWS, LANES), BF16)
    windows = pltpu.VMEM((3, 4, pairs, 5, 2, 16, 256), BF16)
    sides = pltpu.VMEM((2, 2, 5, 8, LANES), F32)
    walls = pltpu.VMEM((2, 64, LANES), F32)
    half_type = jax.ShapeDtypeStruct((groups // 2, channels, width), BF16)
    block_output, grad, keep, give, *grad_units = pl.pallas_call(
        functools.partial(forward_kernel, shard=shard),
        name="forward",
        out_shape=[grid_type, grid_type, half_type, half_type] + [units_type] * spread,
        in_specs=[vmem(), vmem(), pl.BlockSpec(memory_space=pltpu.HBM), vmem(), vmem()]
        + [smem(), smem()]
        + [vmem()] * spread,
        out_specs=[vmem()] * (4 + spread),
        scratch_shapes=[
            table,
            windows,
            sides,
            walls,
            flat,
            pltpu.VMEM((channels, 4 * LANES), F32),
            pltpu.VMEM((4, (bricks + 1) * 64, LANES), F32),
            pltpu.VMEM((256, bricks * LANES), BF16),
            pltpu.VMEM(grid_shape, BF16),
            pltpu.SemaphoreType.DMA,
        ],
        compiler_params=params,
    )(
        masked,
        mask,
        pltpu.with_memory_space_constraint(cotangent.reshape(grid_shape), pltpu.HBM),
        band_forward,
        bias,
        rows,
        send,
        *received,
    )

    later = grad_units[2:]
    bit = 1
    while 2 * bit < groups:
        first = later[:1] if bit == 1 else []
        (keep, give), first = sum_after(keep, swapped(give, "dp", bit), through=first, parts=2)
        later = first + later[1:] if bit == 1 else later
        bit *= 2
    grad_received = [grad_units[0], exchanged(1, grad_units[1])]
    (total,), last = sum_after(keep, swapped(give, "dp", bit), grad_received[1:], later[1:])
    for number, unit in enumerate([later[0], *last], 2):
        grad_received.append(exchanged(number, unit))

    steps = space_steps()
    other = stepped(total, steps[0])
    if len(steps) > 1:
        (total,), _ = sum_after(total, other, grad_received[3:4])
        other = stepped(total, steps[1])

    padded_grad = pl.pallas_call(
        assemble_kernel,
        name="assemble",
        out_shape=jax.ShapeDtypeStruct(windows.shape, BF16),
        in_specs=[vmem()] + [smem()] + [vmem()] * spread + [untouched()],
        out_specs=vmem(),
        scratch_shapes=[table, sides, walls],
        compiler_params=params,
    )(grad, rows, *grad_received, total)

    for number, step in enumerate(steps[2:]):
        (total,), _ = sum_after(total, other, [] if number else [padded_grad])
        other = stepped(total, step)

    grad_input = pl.pallas_call(
        backward_kernel,
        name="backward",
        out_shape=grid_type,
        in_specs=[vmem()] * 3 + [untouched()],
        out_specs=vmem(),
        compiler_params=params,
    )(padded_grad, mask, band_backward, total)

    weight_share, bias_share = pl.pallas_call(
        finish_kernel,
        name="finish",
        out_shape=[
            jax.ShapeDtypeStruct((channels, shard), F32),
            jax.ShapeDtypeStruct((1, count), F32),
        ],
        in_specs=[vmem()] * 2,
        out_specs=[vmem()] * 2,
        compiler_params=params,
    )(total[0], other[0])
    return (
        block_output.reshape(features.shape),
        grad_input.reshape(features.shape),
        weight_share.T,
        bias_share.reshape(count),
    )


def solution(mesh):
    placed = (
        P("dp", "space", None, None, None),
        P("dp", "space", None),
        P("dp", "space"),
        P("dp", "space", None, None),
        P("dp", "space", None),
        P("dp", None),
        P("dp"),
        P("dp", "space", None, None, None),
    )
    return jax.shard_map(
        body,
        mesh=mesh,
        in_specs=placed,
        out_specs=(
            P("dp", "space", None, None, None),
            P("dp", "space", None, None, None),
            P("dp", None),
            P("dp"),
        ),
        check_vma=False,
    )
```
